32 devices in a mesh: grp: 4 (over z), dev: 8 (over y, x, core).
Axes of the slice: x: 2, y: 2, z: 4, core: 2. Of those that a mesh axis runs over, the one named last changes fastest.
Arguments:
- fields: float32 [128, 6, 16, 256], P(('grp', 'dev')), may hold values from 0 to 1
- swap_dev: int32 [32], P(('grp', 'dev')), may hold values from 0 to 1, as said below
- swap_grp: int32 [32], P(('grp', 'dev')), may hold values from 0 to 1, as said below
- neighbors: int32 [128, 6], P(('grp', 'dev')), may hold values from -1 to 127, as said below
- orient: int32 [128], P(('grp', 'dev')), may hold values from 0 to 7
Outputs:
- advanced: float32 [128, 6, 16, 256], P(('grp', 'dev'))
The draws below stay inside these ranges and needn't reach their ends.
Inputs may be any that keep to these rules, and one draw needn't show every extreme that they name: `swap_dev`: equal on devices 2i and 2i+1 of each group. `swap_grp`: equal on the devices of one dev index in groups 2j and 2j+1. `neighbors`: adjacency is mutual: b names n across a face exactly when n names b across the opposite face. Neighbours across -x and -y lie on the same device or the previous dev index of the same group, across +x and +y on the same device or the next dev index of the same group; across -z and +z on the same dev index of the previous and the next group.
All inputs are finite; a program needn't handle non-finite values.
Results may differ from the reference program's by a relative error of at most 0.0001.
Values sent between devices are 32-bit elements; how exact they have to be, the bound alone decides.
No kernel may reach another device: no remote copies, remote signals or barrier semaphores. Data moves between devices by JAX's collectives and lax.ppermute only.
A program may use at most 64 MiB of HBM per device.

```python
import math
import jax
import jax.numpy as jnp
from jax import lax

BS = 16
NPHASE = 4
NCONC = 2
NFIELD = 6
NORI = 8
STEPS = 2
SLOTS = 4
BLOCKS = 128
N_GRP = 4
N_DEV = 8


def draw_swap_dev(key, part):
    bits = jax.random.randint(jax.random.fold_in(key, 101), (N_GRP, N_DEV // 2), 0, 2)
    return jnp.repeat(bits, 2, axis=1).reshape(N_GRP * N_DEV).astype(jnp.int32)


def draw_swap_grp(key, part):
    bits = jax.random.randint(jax.random.fold_in(key, 202), (N_GRP // 2, N_DEV), 0, 2)
    return jnp.repeat(bits, 2, axis=0).reshape(N_GRP * N_DEV).astype(jnp.int32)


def draw_neighbors(key, part):
    group_rows = SLOTS * N_DEV
    order = jnp.arange(group_rows)
    base = (jnp.arange(N_GRP) * group_rows).reshape(N_GRP, 1)
    columns = []
    for number in range(2):
        step_size = jax.random.randint(jax.random.fold_in(key, 303 + number), (N_GRP, 1), 1, SLOTS + 1)
        lower = order.reshape(1, group_rows) - step_size
        upper = order.reshape(1, group_rows) + step_size
        columns.append(jnp.where(lower >= 0, base + lower, -1))
        columns.append(jnp.where(upper < group_rows, base + upper, -1))
    subkeys = jax.random.split(jax.random.fold_in(key, 404), N_GRP * N_DEV)
    forward = jax.vmap(lambda one: jax.random.permutation(one, SLOTS))(subkeys).reshape(N_GRP, N_DEV, SLOTS).astype(jnp.int32)
    backward = jnp.argsort(forward, axis=2).astype(jnp.int32)
    groups = jnp.arange(N_GRP).reshape(N_GRP, 1, 1)
    devices = jnp.arange(N_DEV).reshape(1, N_DEV, 1)
    upper_z = jnp.where(groups < N_GRP - 1, ((groups + 1) * N_DEV + devices) * SLOTS + forward, -1)
    shifted = jnp.concatenate([backward[:1], backward[:-1]], axis=0)
    lower_z = jnp.where(groups > 0, ((groups - 1) * N_DEV + devices) * SLOTS + shifted, -1)
    columns.append(lower_z.reshape(N_GRP, group_rows))
    columns.append(upper_z.reshape(N_GRP, group_rows))
    table = jnp.stack(columns, axis=-1)
    return table.reshape(N_GRP * group_rows, 6).astype(jnp.int32)


def with_ends(values, rng, least, high):
    extent = values.shape
    index_at = [jax.random.randint(jax.random.fold_in(rng, axis), (), 0, extent[axis]) for axis in range(len(extent))]
    values = values.at[tuple(index_at)].set(least)
    longest = extent.index(max(extent))
    index_at[longest] = (index_at[longest] + 1) % extent[longest]
    return values.at[tuple(index_at)].set(high)


def block_levels(own_key, extent, pieces, smallest, high):
    level, own = 1.0, jax.random.fold_in(own_key, 6)
    for position, parts in pieces:
        steps = jnp.exp(jax.random.uniform(jax.random.fold_in(own, position), (parts,), jnp.float32, smallest / len(pieces), high / len(pieces)))
        level = level * jnp.repeat(steps, extent[position] // parts).reshape([-1 if axis == position else 1 for axis in range(len(extent))])
    return level


def setup_inputs(seed: int = 0) -> dict:
    splits = jax.random.split(jax.random.key(seed), 6)
    fields = jnp.clip(1.0 * jax.random.uniform(splits[0], (BLOCKS, NFIELD, BS, BS * BS), jnp.float32) ** block_levels(splits[0], (BLOCKS, NFIELD, BS, BS * BS), ((0, 32),), -0.2, 0.2), 0.0, 1.0)
    swap_dev = draw_swap_dev(jax.random.fold_in(splits[5], 71), 0)
    swap_grp = draw_swap_grp(jax.random.fold_in(splits[5], 71), 0)
    neighbors = draw_neighbors(jax.random.fold_in(splits[5], 71), 0)
    orient = with_ends(jax.random.randint(splits[4], (BLOCKS,), 0, NORI), jax.random.fold_in(splits[4], 1), 0, NORI - 1).astype(jnp.int32)
    return dict(fields=fields, swap_dev=swap_dev, swap_grp=swap_grp, neighbors=neighbors, orient=orient)


phase_rate = 0.05
closure = 0.1
coupling = (0.5, -0.5, 1.0, -1.0)
conc_rates = (0.08, 0.04)


def coefficients(orient):
    theta = math.pi * orient.astype(jnp.float32) / NORI
    return 1.0 + 0.5 * jnp.cos(2.0 * theta), 1.0 - 0.5 * jnp.cos(2.0 * theta), 1.0 + 0.5 * jnp.sin(2.0 * theta)


def advance(inputs):
    block, ghosts, orient = inputs
    sums = []
    for axis in range(3):
        dim = 2 + axis
        lower = jnp.expand_dims(ghosts[2 * axis], dim)
        upper = jnp.expand_dims(ghosts[2 * axis + 1], dim)
        padded = jnp.concatenate([lower, block, upper], axis=dim)
        size = padded.shape[dim]
        sums.append(lax.slice_in_dim(padded, 2, size, axis=dim) + lax.slice_in_dim(padded, 0, size - 2, axis=dim))
    kx, ky, kz = coefficients(orient)
    kx = kx.reshape(-1, 1, 1, 1, 1)
    ky = ky.reshape(-1, 1, 1, 1, 1)
    kz = kz.reshape(-1, 1, 1, 1, 1)
    aniso = kx * (sums[0] - 2.0 * block) + ky * (sums[1] - 2.0 * block) + kz * (sums[2] - 2.0 * block)
    iso = sums[0] + sums[1] + sums[2] - 6.0 * block
    phases = block[:, :NPHASE]
    conc = block[:, NPHASE:]
    total = jnp.sum(phases, axis=1, keepdims=True)
    drive = conc[:, 0:1] - conc[:, 1:2]
    beta = jnp.array(coupling, jnp.float32).reshape(1, NPHASE, 1, 1, 1)
    rates = jnp.array(conc_rates, jnp.float32).reshape(1, NCONC, 1, 1, 1)
    well = phases * (1.0 - phases) * (1.0 - 2.0 * phases)
    new_phases = phases + phase_rate * (aniso[:, :NPHASE] - well + beta * drive * phases * (1.0 - phases) - closure * (total - 1.0))
    new_conc = conc + rates * iso[:, NPHASE:]
    return jnp.concatenate([new_phases, new_conc], axis=1)


def reference(fields, swap_dev, swap_grp, neighbors, orient):
    nfield = NPHASE + NCONC
    grid = fields.reshape(N_GRP, N_DEV, SLOTS, nfield, BS, BS * BS)
    flag_dev = swap_dev.reshape(N_GRP, N_DEV, 1, 1, 1)
    flag_grp = swap_grp.reshape(N_GRP, N_DEV, 1, 1, 1)
    index_dev = jnp.arange(N_DEV)
    partner_dev = index_dev + 1 - 2 * (index_dev % 2)
    index_grp = jnp.arange(N_GRP)
    partner_grp = index_grp + 1 - 2 * (index_grp % 2)
    last = grid[:, :, SLOTS - 1]
    last = jnp.where(flag_dev == 1, last[:, partner_dev], last)
    grid = grid.at[:, :, SLOTS - 1].set(last)
    first = grid[:, :, 0]
    first = jnp.where(flag_grp == 1, first[partner_grp], first)
    grid = grid.at[:, :, 0].set(first)
    blocks = grid.reshape(BLOCKS, nfield, BS, BS, BS)
    group_rows = SLOTS * N_DEV
    for step in range(STEPS):
        faces = [blocks[:, :, 0], blocks[:, :, BS - 1], blocks[:, :, :, 0], blocks[:, :, :, BS - 1], blocks[:, :, :, :, 0], blocks[:, :, :, :, BS - 1]]
        ghosts = []
        for face in range(6):
            opposite = face + 1 - 2 * (face % 2)
            target = neighbors[:, face]
            taken = faces[opposite][jnp.maximum(target, 0)]
            ghosts.append(jnp.where(target.reshape(-1, 1, 1, 1) < 0, faces[face], taken))
        stacked = jnp.stack(ghosts, axis=0).reshape(6, N_GRP, group_rows, nfield, BS, BS)
        stacked = jnp.moveaxis(stacked, 1, 0)
        result = lax.map(advance, (blocks.reshape(N_GRP, group_rows, nfield, BS, BS, BS), stacked, orient.reshape(N_GRP, group_rows)))
        blocks = result.reshape(BLOCKS, nfield, BS, BS, BS)
    return blocks.reshape(BLOCKS, nfield, BS, BS * BS)
```

```python
import functools
import math

import jax
import jax.numpy as jnp
from jax import lax
from jax.experimental import pallas as pl
from jax.experimental.pallas import tpu as pltpu
from jax.sharding import PartitionSpec as P

NPHASE = 4
NCONC = 2
NFIELD = NPHASE + NCONC
STEPS = 2
EDGE = 16
PLANE = EDGE * EDGE
HALF = PLANE // 2
SLOTS = 4

phase_rate = 0.05
closure = 0.1
coupling = (0.5, -0.5, 1.0, -1.0)
conc_rates = (0.08, 0.04)

FLAT = (SLOTS, EDGE, PLANE)
DEEP = (SLOTS // 2, EDGE, PLANE)


def pairing(count, offset, wrap):
    route = []
    for low in range(offset, count, 2):
        high = low + 1
        if high < count:
            route += [(low, high), (high, low)]
        elif wrap and high == count and offset == 1:
            route += [(low, 0), (0, low)]
    return route


def exchange(block, axis, offset, wrap=True):
    return lax.ppermute(block, axis, pairing(lax.axis_size(axis), offset, wrap))


def lane_ids(shape):
    return lax.broadcasted_iota(jnp.int32, shape, len(shape) - 1)


def row_ids(shape):
    return lax.broadcasted_iota(jnp.int32, shape, len(shape) - 2)


def pack_slot(fields, slot, flat_refs, deep_refs):
    lane = lane_ids((EDGE, HALF))
    for side in range(2):
        flat, deep = flat_refs[side], deep_refs[side]
        row = side * (EDGE - 1)
        y_face = None
        z_left = z_right = None
        for f, value in enumerate(fields):
            flat[slot, f : f + 1, :] = value[row : row + 1, :]
            half = value[:, :HALF] if side == 0 else value[:, HALF:]
            origin = side * (HALF - EDGE)
            shift = (EDGE * f - origin) % HALF
            moved = pltpu.roll(half, shift, 1) if shift else half
            y_face = moved if y_face is None else jnp.where(lane >= EDGE * f, moved, y_face)
            shift = (8 * (slot % 2) + f - side * (EDGE - 1)) % HALF
            left, right = value[:, :HALF], value[:, HALF:]
            if shift:
                left, right = pltpu.roll(left, shift, 1), pltpu.roll(right, shift, 1)
            place = lane % 8 >= f
            z_left = left if z_left is None else jnp.where(place, left, z_left)
            z_right = right if z_right is None else jnp.where(place, right, z_right)
        flat[slot, 8:16, :HALF] = y_face[:8]
        flat[slot, 8:16, HALF:] = y_face[8:]
        index = slot // 2
        if slot % 2 == 0:
            deep[index, :, :HALF] = z_left
            deep[index, :, HALF:] = z_right
        else:
            upper = lane % EDGE >= 8
            deep[index, :, :HALF] = jnp.where(upper, z_left, deep[index, :, :HALF])
            deep[index, :, HALF:] = jnp.where(upper, z_right, deep[index, :, HALF:])


def send_faces(flat_refs, deep_refs, outs):
    flat_a, flat_b, deep_a, deep_b = outs
    even = lax.rem(lax.axis_index("dev"), 2) == 0
    low, high = flat_refs[0][...], flat_refs[1][...]
    flat_a[...] = jnp.where(even, high, low)
    flat_b[...] = jnp.where(even, low, high)
    even = lax.rem(lax.axis_index("grp"), 2) == 0
    low, high = deep_refs[0][...], deep_refs[1][...]
    deep_a[...] = jnp.where(even, high, low)
    deep_b[...] = jnp.where(even, low, high)


def migrate_kernel(swap_dev, swap_grp, fields, last, first, state, *outs):
    flat_refs, deep_refs = outs[0:2], outs[2:4]
    for slot in range(SLOTS):
        values = []
        for f in range(NFIELD):
            value = fields[slot, f]
            if slot == 0:
                value = jnp.where(swap_grp[0] == 1, first[0, f], value)
            if slot == SLOTS - 1:
                value = jnp.where(swap_dev[0] == 1, last[0, f], value)
            state[slot, f] = value
            values.append(value)
        pack_slot(values, slot, flat_refs, deep_refs)
    send_faces(flat_refs, deep_refs, outs[4:8])


def cos_quarter(number):
    turn = number & 7
    size = jnp.where((turn & 3) == 0, 1.0, jnp.where((turn & 3) == 2, 0.0, math.sqrt(0.5)))
    return jnp.where((turn > 2) & (turn < 6), -size, size)


def step_kernel(last_step, neighbors, orient, state, *refs):
    own_flat, own_deep = refs[0:2], refs[2:4]
    got_flat, got_deep = refs[4:6], refs[6:8]
    new_state = refs[8]
    if last_step:
        flats, deeps = refs[9:11]
    else:
        flat_refs, deep_refs, sends = refs[9:11], refs[11:13], refs[13:17]
        flats, deeps = refs[17:19]
    for source, ref in enumerate((*own_flat, *got_flat)):
        flats[source * SLOTS : (source + 1) * SLOTS] = ref[...]
    pairs = SLOTS // 2
    for source, ref in enumerate((*own_deep, *got_deep)):
        deeps[source * pairs : (source + 1) * pairs] = ref[...]
    grp, dev = lax.axis_index("grp"), lax.axis_index("dev")
    rank = grp * lax.axis_size("dev") + dev
    lane = lane_ids((EDGE, HALF))
    row = row_ids((EDGE, PLANE))
    wide = lane_ids((EDGE, PLANE))
    for slot in range(SLOTS):
        flat_at, deep_at, deep_shift = [], [], []
        for face in range(6):
            target = neighbors[slot, face]
            side = face % 2
            position = dev if face < 4 else grp
            came = 2 + (lax.rem(position, 2) + side + 1) % 2
            where_from = jnp.where(target < 0, side, jnp.where(target // SLOTS == rank, 1 - side, came))
            number = jnp.where(target < 0, slot, target & (SLOTS - 1))
            if face < 4:
                flat_at.append(where_from * SLOTS + number)
            else:
                deep_at.append(where_from * pairs + number // 2)
                deep_shift.append((number & 1) * 8)
        angle = orient[slot]
        turn = 0.5 * cos_quarter(angle)
        lift = 0.5 * cos_quarter(angle + 6)
        kx, ky, kz = 1.0 + turn, 1.0 - turn, 1.0 + lift
        values = [state[slot, f] for f in range(NFIELD)]
        y_low = [flats[flat_at[2], 8:16, :HALF], flats[flat_at[2], 8:16, HALF:]]
        y_high = [flats[flat_at[3], 8:16, :HALF], flats[flat_at[3], 8:16, HALF:]]
        y_low, y_high = jnp.concatenate(y_low, axis=0), jnp.concatenate(y_high, axis=0)
        z_low = [pltpu.roll(deeps[deep_at[0], :, h * HALF : (h + 1) * HALF], (HALF - deep_shift[0]) % HALF, 1) for h in range(2)]
        z_high = [pltpu.roll(deeps[deep_at[1], :, h * HALF : (h + 1) * HALF], (HALF - deep_shift[1]) % HALF, 1) for h in range(2)]
        total = values[0] + values[1] + values[2] + values[3]
        drive = values[4] - values[5]
        tail = phase_rate * closure * (1.0 - total)
        fresh = []
        for f, value in enumerate(values):
            x_low = jnp.broadcast_to(flats[flat_at[0], f : f + 1, :], (EDGE, PLANE))
            x_high = jnp.broadcast_to(flats[flat_at[1], f : f + 1, :], (EDGE, PLANE))
            below = jnp.where(row == 0, x_low, pltpu.roll(value, 1, 0))
            above = jnp.where(row == EDGE - 1, x_high, pltpu.roll(value, EDGE - 1, 0))
            sum_x = below + above
            left, right = value[:, :HALF], value[:, HALF:]
            left_up, right_up = pltpu.roll(left, EDGE, 1), pltpu.roll(right, EDGE, 1)
            left_down, right_down = pltpu.roll(left, HALF - EDGE, 1), pltpu.roll(right, HALF - EDGE, 1)
            ghost_low = pltpu.roll(y_low, (HALF - EDGE * f) % HALF, 1) if f else y_low
            ghost_high = pltpu.roll(y_high, HALF - EDGE - EDGE * f, 1) if f != 7 else y_high
            start, end = lane < EDGE, lane >= HALF - EDGE
            sum_left = jnp.where(start, ghost_low, left_up) + jnp.where(end, right_down, left_down)
            sum_right = jnp.where(start, left_up, right_up) + jnp.where(end, ghost_high, right_down)
            start, end = lane % EDGE == 0, lane % EDGE == EDGE - 1
            deep = []
            for half, low, high in ((left, z_low[0], z_high[0]), (right, z_low[1], z_high[1])):
                low = pltpu.roll(low, HALF - f, 1) if f else low
                high = pltpu.roll(high, EDGE - 1 - f, 1)
                deep.append(
                    jnp.where(start, low, pltpu.roll(half, 1, 1))
                    + jnp.where(end, high, pltpu.roll(half, HALF - 1, 1))
                )
            sum_y = jnp.concatenate([sum_left, sum_right], axis=1)
            sum_z = jnp.concatenate(deep, axis=1)
            if f < NPHASE:
                flow = kx * sum_x + ky * sum_y + kz * sum_z - (2.0 * (kx + ky + kz)) * value
                gain = value * (1.0 - value) * (coupling[f] * drive + (2.0 * value - 1.0))
                result = value + phase_rate * (flow + gain) + tail
            else:
                result = value + conc_rates[f - NPHASE] * (sum_x + sum_y + sum_z - 6.0 * value)
            new_state[slot, f] = result
            fresh.append(result)
        if not last_step:
            pack_slot(fresh, slot, flat_refs, deep_refs)
    if not last_step:
        send_faces(flat_refs, deep_refs, sends)


def spec(space):
    return pl.BlockSpec(memory_space=space)


VECTOR, SCALAR = pltpu.VMEM, pltpu.SMEM
TABLES = (FLAT, FLAT, DEEP, DEEP, FLAT, FLAT, DEEP, DEEP)


def shaped(shape):
    return jax.ShapeDtypeStruct(shape, jnp.float32)


def body(fields, swap_dev, swap_grp, neighbors, orient):
    last = exchange(fields[SLOTS - 1 :], "dev", 0)
    first = exchange(fields[:1], "grp", 0)
    state, *tables = pl.pallas_call(
        migrate_kernel,
        name="migrate",
        out_shape=[shaped(fields.shape)] + [shaped(shape) for shape in TABLES],
        in_specs=[spec(SCALAR)] * 2 + [spec(VECTOR)] * 3,
        out_specs=[spec(VECTOR)] * 9,
    )(swap_dev, swap_grp, fields, last, first)
    for step in range(STEPS):
        last_step = step == STEPS - 1
        own, sends = tables[:4], tables[4:]
        got = [exchange(sends[number], "dev" if number < 2 else "grp", number % 2) for number in range(4)]
        outs = pl.pallas_call(
            functools.partial(step_kernel, last_step),
            name=f"step_{step}",
            out_shape=[shaped(fields.shape)] + ([] if last_step else [shaped(shape) for shape in TABLES]),
            in_specs=[spec(SCALAR)] * 2 + [spec(VECTOR)] * 9,
            out_specs=[spec(VECTOR)] * (1 if last_step else 9),
            scratch_shapes=[
                pltpu.VMEM((4 * SLOTS, EDGE, PLANE), jnp.float32),
                pltpu.VMEM((2 * SLOTS, EDGE, PLANE), jnp.float32),
            ],
        )(neighbors, orient, state, *own, *got)
        state, tables = outs[0], outs[1:]
    return state


def solution(mesh):
    in_specs = (
        P(("grp", "dev"), None, None, None),
        P(("grp", "dev")),
        P(("grp", "dev")),
        P(("grp", "dev"), None),
        P(("grp", "dev")),
    )
    out_specs = P(("grp", "dev"), None, None, None)
    return jax.shard_map(body, mesh=mesh, in_specs=in_specs, out_specs=out_specs, check_vma=False)
```

```python
import functools
import math

import jax
import jax.numpy as jnp
from jax import lax
from jax.experimental import pallas as pl
from jax.experimental.pallas import tpu as pltpu
from jax.sharding import PartitionSpec as P

NPHASE = 4
NCONC = 2
NFIELD = NPHASE + NCONC
STEPS = 2
EDGE = 16
PLANE = EDGE * EDGE
HALF = PLANE // 2
SLOTS = 4

phase_rate = 0.05
closure = 0.1
coupling = (0.5, -0.5, 1.0, -1.0)
conc_rates = (0.08, 0.04)

FLAT = (SLOTS, EDGE, PLANE)
DEEP = (SLOTS // 2, EDGE, PLANE)


def pairing(count, offset):
    route = []
    for index in range(count):
        partner = index + 1 if (index - offset) % 2 == 0 else index - 1
        route.append((index, partner if 0 <= partner < count else index))
    return route


def exchange(block, axis, offset):
    return lax.ppermute(block, axis, pairing(lax.axis_size(axis), offset))


def lane_ids(shape):
    return lax.broadcasted_iota(jnp.int32, shape, len(shape) - 1)


def row_ids(shape):
    return lax.broadcasted_iota(jnp.int32, shape, len(shape) - 2)


def pack_slot(fields, slot, flat_refs, deep_refs):
    lane = lane_ids((EDGE, HALF))
    for side in range(2):
        flat, deep = flat_refs[side], deep_refs[side]
        row = side * (EDGE - 1)
        y_face = None
        z_left = z_right = None
        for f, value in enumerate(fields):
            flat[slot, f : f + 1, :] = value[row : row + 1, :]
            half = value[:, :HALF] if side == 0 else value[:, HALF:]
            origin = side * (HALF - EDGE)
            shift = (EDGE * f - origin) % HALF
            moved = pltpu.roll(half, shift, 1) if shift else half
            y_face = moved if y_face is None else jnp.where(lane >= EDGE * f, moved, y_face)
            shift = (8 * (slot % 2) + f - side * (EDGE - 1)) % HALF
            left, right = value[:, :HALF], value[:, HALF:]
            if shift:
                left, right = pltpu.roll(left, shift, 1), pltpu.roll(right, shift, 1)
            place = lane % 8 >= f
            z_left = left if z_left is None else jnp.where(place, left, z_left)
            z_right = right if z_right is None else jnp.where(place, right, z_right)
        flat[slot, 8:16, :HALF] = y_face[:8]
        flat[slot, 8:16, HALF:] = y_face[8:]
        index = slot // 2
        if slot % 2 == 0:
            deep[index, :, :HALF] = z_left
            deep[index, :, HALF:] = z_right
        else:
            upper = lane % EDGE >= 8
            deep[index, :, :HALF] = jnp.where(upper, z_left, deep[index, :, :HALF])
            deep[index, :, HALF:] = jnp.where(upper, z_right, deep[index, :, HALF:])


def send_faces(flat_refs, deep_refs, outs):
    flat_a, flat_b, deep_a, deep_b = outs
    even = lax.rem(lax.axis_index("dev"), 2) == 0
    low, high = flat_refs[0][...], flat_refs[1][...]
    flat_a[...] = jnp.where(even, high, low)
    flat_b[...] = jnp.where(even, low, high)
    even = lax.rem(lax.axis_index("grp"), 2) == 0
    low, high = deep_refs[0][...], deep_refs[1][...]
    deep_a[...] = jnp.where(even, high, low)
    deep_b[...] = jnp.where(even, low, high)


def migrate_kernel(swap_dev, swap_grp, fields, last, first, state, *outs):
    flat_refs, deep_refs = outs[0:2], outs[2:4]
    for slot in range(SLOTS):
        values = []
        for f in range(NFIELD):
            value = fields[slot, f]
            if slot == 0:
                value = jnp.where(swap_grp[0] == 1, first[0, f], value)
            if slot == SLOTS - 1:
                value = jnp.where(swap_dev[0] == 1, last[0, f], value)
            state[slot, f] = value
            values.append(value)
        pack_slot(values, slot, flat_refs, deep_refs)
    send_faces(flat_refs, deep_refs, outs[4:8])


def cos_quarter(number):
    turn = number & 7
    size = jnp.where((turn & 3) == 0, 1.0, jnp.where((turn & 3) == 2, 0.0, math.sqrt(0.5)))
    return jnp.where((turn > 2) & (turn < 6), -size, size)


def step_kernel(last_step, neighbors, orient, state, *refs):
    own_flat, own_deep = refs[0:2], refs[2:4]
    got_flat, got_deep = refs[4:6], refs[6:8]
    new_state = refs[8]
    if last_step:
        flats, deeps = refs[9:11]
    else:
        flat_refs, deep_refs, sends = refs[9:11], refs[11:13], refs[13:17]
        flats, deeps = refs[17:19]
    for source, ref in enumerate((*own_flat, *got_flat)):
        flats[source * SLOTS : (source + 1) * SLOTS] = ref[...]
    pairs = SLOTS // 2
    for source, ref in enumerate((*own_deep, *got_deep)):
        deeps[source * pairs : (source + 1) * pairs] = ref[...]
    grp, dev = lax.axis_index("grp"), lax.axis_index("dev")
    rank = grp * lax.axis_size("dev") + dev
    lane = lane_ids((EDGE, HALF))
    row = row_ids((EDGE, PLANE))
    wide = lane_ids((EDGE, PLANE))
    for slot in range(SLOTS):
        flat_at, deep_at, deep_shift = [], [], []
        for face in range(6):
            target = neighbors[slot, face]
            side = face % 2
            position = dev if face < 4 else grp
            came = 2 + (lax.rem(position, 2) + side + 1) % 2
            where_from = jnp.where(target < 0, side, jnp.where(target // SLOTS == rank, 1 - side, came))
            number = jnp.where(target < 0, slot, target & (SLOTS - 1))
            if face < 4:
                flat_at.append(where_from * SLOTS + number)
            else:
                deep_at.append(where_from * pairs + number // 2)
                deep_shift.append((number & 1) * 8)
        angle = orient[slot]
        turn = 0.5 * cos_quarter(angle)
        lift = 0.5 * cos_quarter(angle + 6)
        kx, ky, kz = 1.0 + turn, 1.0 - turn, 1.0 + lift
        values = [state[slot, f] for f in range(NFIELD)]
        y_low = [flats[flat_at[2], 8:16, :HALF], flats[flat_at[2], 8:16, HALF:]]
        y_high = [flats[flat_at[3], 8:16, :HALF], flats[flat_at[3], 8:16, HALF:]]
        y_low, y_high = jnp.concatenate(y_low, axis=0), jnp.concatenate(y_high, axis=0)
        z_low = [pltpu.roll(deeps[deep_at[0], :, h * HALF : (h + 1) * HALF], (HALF - deep_shift[0]) % HALF, 1) for h in range(2)]
        z_high = [pltpu.roll(deeps[deep_at[1], :, h * HALF : (h + 1) * HALF], (HALF - deep_shift[1]) % HALF, 1) for h in range(2)]
        total = values[0] + values[1] + values[2] + values[3]
        drive = values[4] - values[5]
        tail = phase_rate * closure * (1.0 - total)
        fresh = []
        for f, value in enumerate(values):
            x_low = jnp.broadcast_to(flats[flat_at[0], f : f + 1, :], (EDGE, PLANE))
            x_high = jnp.broadcast_to(flats[flat_at[1], f : f + 1, :], (EDGE, PLANE))
            below = jnp.where(row == 0, x_low, pltpu.roll(value, 1, 0))
            above = jnp.where(row == EDGE - 1, x_high, pltpu.roll(value, EDGE - 1, 0))
            sum_x = below + above
            left, right = value[:, :HALF], value[:, HALF:]
            left_up, right_up = pltpu.roll(left, EDGE, 1), pltpu.roll(right, EDGE, 1)
            left_down, right_down = pltpu.roll(left, HALF - EDGE, 1), pltpu.roll(right, HALF - EDGE, 1)
            ghost_low = pltpu.roll(y_low, (HALF - EDGE * f) % HALF, 1) if f else y_low
            ghost_high = pltpu.roll(y_high, HALF - EDGE - EDGE * f, 1) if f != 7 else y_high
            start, end = lane < EDGE, lane >= HALF - EDGE
            sum_left = jnp.where(start, ghost_low, left_up) + jnp.where(end, right_down, left_down)
            sum_right = jnp.where(start, left_up, right_up) + jnp.where(end, ghost_high, right_down)
            start, end = lane % EDGE == 0, lane % EDGE == EDGE - 1
            deep = []
            for half, low, high in ((left, z_low[0], z_high[0]), (right, z_low[1], z_high[1])):
                low = pltpu.roll(low, HALF - f, 1) if f else low
                high = pltpu.roll(high, EDGE - 1 - f, 1)
                deep.append(
                    jnp.where(start, low, pltpu.roll(half, 1, 1))
                    + jnp.where(end, high, pltpu.roll(half, HALF - 1, 1))
                )
            sum_y = jnp.concatenate([sum_left, sum_right], axis=1)
            sum_z = jnp.concatenate(deep, axis=1)
            if f < NPHASE:
                flow = kx * sum_x + ky * sum_y + kz * sum_z - (2.0 * (kx + ky + kz)) * value
                gain = value * (1.0 - value) * (coupling[f] * drive + (2.0 * value - 1.0))
                result = value + phase_rate * (flow + gain) + tail
            else:
                result = value + conc_rates[f - NPHASE] * (sum_x + sum_y + sum_z - 6.0 * value)
            new_state[slot, f] = result
            fresh.append(result)
        if not last_step:
            pack_slot(fresh, slot, flat_refs, deep_refs)
    if not last_step:
        send_faces(flat_refs, deep_refs, sends)


def spec(space):
    return pl.BlockSpec(memory_space=space)


VECTOR, SCALAR = pltpu.VMEM, pltpu.SMEM
SMALL = pltpu.CompilerParams(vmem_limit_bytes=8 << 20)
TABLES = (FLAT, FLAT, DEEP, DEEP, FLAT, FLAT, DEEP, DEEP)


def shaped(shape):
    return jax.ShapeDtypeStruct(shape, jnp.float32)


def body(fields, swap_dev, swap_grp, neighbors, orient):
    first = exchange(fields[:1], "grp", 0)
    last = exchange(fields[SLOTS - 1 :], "dev", 0)
    state, *tables = pl.pallas_call(
        migrate_kernel,
        name="migrate",
        compiler_params=SMALL,
        out_shape=[shaped(fields.shape)] + [shaped(shape) for shape in TABLES],
        in_specs=[spec(SCALAR)] * 2 + [spec(VECTOR)] * 3,
        out_specs=[spec(VECTOR)] * 9,
    )(swap_dev, swap_grp, fields, last, first)
    for step in range(STEPS):
        last_step = step == STEPS - 1
        own, sends = tables[:4], tables[4:]
        got_deep = [exchange(sends[2 + number], "grp", number) for number in range(2)]
        got = [exchange(sends[number], "dev", number) for number in range(2)] + got_deep
        outs = pl.pallas_call(
            functools.partial(step_kernel, last_step),
            name=f"step_{step}",
            compiler_params=SMALL,
            out_shape=[shaped(fields.shape)] + ([] if last_step else [shaped(shape) for shape in TABLES]),
            in_specs=[spec(SCALAR)] * 2 + [spec(VECTOR)] * 9,
            out_specs=[spec(VECTOR)] * (1 if last_step else 9),
            scratch_shapes=[
                pltpu.VMEM((4 * SLOTS, EDGE, PLANE), jnp.float32),
                pltpu.VMEM((2 * SLOTS, EDGE, PLANE), jnp.float32),
            ],
        )(neighbors, orient, state, *own, *got)
        state, tables = outs[0], outs[1:]
    return state


def solution(mesh):
    in_specs = (
        P(("grp", "dev"), None, None, None),
        P(("grp", "dev")),
        P(("grp", "dev")),
        P(("grp", "dev"), None),
        P(("grp", "dev")),
    )
    out_specs = P(("grp", "dev"), None, None, None)
    return jax.shard_map(body, mesh=mesh, in_specs=in_specs, out_specs=out_specs, check_vma=False)
```

```python
import functools
import math

import jax
import jax.numpy as jnp
from jax import lax
from jax.experimental import pallas as pl
from jax.experimental.pallas import tpu as pltpu
from jax.sharding import PartitionSpec as P

NPHASE = 4
NCONC = 2
NFIELD = NPHASE + NCONC
STEPS = 2
EDGE = 16
PLANE = EDGE * EDGE
HALF = PLANE // 2
SLOTS = 4

phase_rate = 0.05
closure = 0.1
coupling = (0.5, -0.5, 1.0, -1.0)
conc_rates = (0.08, 0.04)

FLAT = (SLOTS, EDGE, PLANE)
DEEP = (SLOTS // 2, EDGE, PLANE)


def partners(axis, offset):
    sizes = (lax.axis_size("grp"), lax.axis_size("dev"))
    along = ("grp", "dev").index(axis)
    route = []
    for grp in range(sizes[0]):
        for dev in range(sizes[1]):
            own = (grp, dev)
            step = 1 if (own[along] - offset) % 2 == 0 else -1
            partner = list(own)
            partner[along] += step
            if not 0 <= partner[along] < sizes[along]:
                partner = list(own)
                partner[1 - along] ^= 1
                if partner[1 - along] >= sizes[1 - along]:
                    partner = list(own)
            route.append((grp * sizes[1] + dev, partner[0] * sizes[1] + partner[1]))
    return route


def exchange(block, axis, offset):
    return lax.ppermute(block, ("grp", "dev"), partners(axis, offset))


def lane_ids(shape):
    return lax.broadcasted_iota(jnp.int32, shape, len(shape) - 1)


def row_ids(shape):
    return lax.broadcasted_iota(jnp.int32, shape, len(shape) - 2)


def pack_slot(fields, slot, flat_refs, deep_refs):
    lane = lane_ids((EDGE, HALF))
    for side in range(2):
        flat, deep = flat_refs[side], deep_refs[side]
        row = side * (EDGE - 1)
        y_face = None
        z_left = z_right = None
        for f, value in enumerate(fields):
            flat[slot, f : f + 1, :] = value[row : row + 1, :]
            half = value[:, :HALF] if side == 0 else value[:, HALF:]
            origin = side * (HALF - EDGE)
            shift = (EDGE * f - origin) % HALF
            moved = pltpu.roll(half, shift, 1) if shift else half
            y_face = moved if y_face is None else jnp.where(lane >= EDGE * f, moved, y_face)
            shift = (8 * (slot % 2) + f - side * (EDGE - 1)) % HALF
            left, right = value[:, :HALF], value[:, HALF:]
            if shift:
                left, right = pltpu.roll(left, shift, 1), pltpu.roll(right, shift, 1)
            place = lane % 8 >= f
            z_left = left if z_left is None else jnp.where(place, left, z_left)
            z_right = right if z_right is None else jnp.where(place, right, z_right)
        flat[slot, 8:16, :HALF] = y_face[:8]
        flat[slot, 8:16, HALF:] = y_face[8:]
        index = slot // 2
        if slot % 2 == 0:
            deep[index, :, :HALF] = z_left
            deep[index, :, HALF:] = z_right
        else:
            upper = lane % EDGE >= 8
            deep[index, :, :HALF] = jnp.where(upper, z_left, deep[index, :, :HALF])
            deep[index, :, HALF:] = jnp.where(upper, z_right, deep[index, :, HALF:])


def send_faces(flat_refs, deep_refs, outs):
    flat_a, flat_b, deep_a, deep_b = outs
    even = lax.rem(lax.axis_index("dev"), 2) == 0
    low, high = flat_refs[0][...], flat_refs[1][...]
    flat_a[...] = jnp.where(even, high, low)
    flat_b[...] = jnp.where(even, low, high)
    even = lax.rem(lax.axis_index("grp"), 2) == 0
    low, high = deep_refs[0][...], deep_refs[1][...]
    deep_a[...] = jnp.where(even, high, low)
    deep_b[...] = jnp.where(even, low, high)


def migrate_kernel(swap_dev, swap_grp, fields, last, first, state, *outs):
    flat_refs, deep_refs = outs[0:2], outs[6:8]
    for slot in range(SLOTS):
        values = []
        for f in range(NFIELD):
            value = fields[slot, f]
            if slot == 0:
                value = jnp.where(swap_grp[0] == 1, first[0, f], value)
            if slot == SLOTS - 1:
                value = jnp.where(swap_dev[0] == 1, last[0, f], value)
            state[slot, f] = value
            values.append(value)
        pack_slot(values, slot, flat_refs, deep_refs)
    send_faces(flat_refs, deep_refs, outs[2:6])


def cos_quarter(number):
    turn = number & 7
    size = jnp.where((turn & 3) == 0, 1.0, jnp.where((turn & 3) == 2, 0.0, math.sqrt(0.5)))
    return jnp.where((turn > 2) & (turn < 6), -size, size)


def weights(angle):
    turn = 0.5 * cos_quarter(angle)
    lift = 0.5 * cos_quarter(angle + 6)
    return 1.0 + turn, 1.0 - turn, 1.0 + lift


def place():
    grp, dev = lax.axis_index("grp"), lax.axis_index("dev")
    return grp, dev, grp * lax.axis_size("dev") + dev


def y_rows(flats, at):
    return jnp.concatenate([flats[at, 8:16, :HALF], flats[at, 8:16, HALF:]], axis=0)


def inner_kernel(neighbors, orient, state, flat_low, flat_high, partial):
    _, _, rank = place()
    lane = lane_ids((EDGE, HALF))
    row = row_ids((EDGE, PLANE))
    for slot in range(SLOTS):
        number, same, local = [], [], []
        for face in range(6):
            target = neighbors[slot, face]
            number.append(target & (SLOTS - 1))
            same.append(target < 0)
            local.append((target >= 0) & (target // SLOTS == rank))
        opposite = (flat_high, flat_low)
        y_ghost = [y_rows(opposite[side], number[2 + side]) for side in range(2)]
        kx, ky, kz = weights(orient[slot])
        values = [state[slot, f] for f in range(NFIELD)]
        total = values[0] + values[1] + values[2] + values[3]
        drive = values[4] - values[5]
        tail = phase_rate * closure * (1.0 - total)
        y_ends = (lane < EDGE, lane >= HALF - EDGE)
        z_ends = (lane % EDGE == 0, lane % EDGE == EDGE - 1)
        for f, value in enumerate(values):
            left, right = value[:, :HALF], value[:, HALF:]

            def ghost(face, arrived, own):
                return jnp.where(same[face], own, jnp.where(local[face], arrived, 0.0))

            x_low = ghost(0, flat_high[number[0], f : f + 1, :], value[:1])
            x_high = ghost(1, flat_low[number[1], f : f + 1, :], value[EDGE - 1 :])
            below = jnp.where(row == 0, jnp.broadcast_to(x_low, (EDGE, PLANE)), pltpu.roll(value, 1, 0))
            above = jnp.where(row == EDGE - 1, jnp.broadcast_to(x_high, (EDGE, PLANE)), pltpu.roll(value, EDGE - 1, 0))
            sum_x = below + above
            left_up, right_up = pltpu.roll(left, EDGE, 1), pltpu.roll(right, EDGE, 1)
            left_down, right_down = pltpu.roll(left, HALF - EDGE, 1), pltpu.roll(right, HALF - EDGE, 1)
            y_low = ghost(2, pltpu.roll(y_ghost[0], (HALF - EDGE * f) % HALF, 1) if f else y_ghost[0], left)
            y_high = ghost(3, pltpu.roll(y_ghost[1], HALF - EDGE - EDGE * f, 1), right)
            sum_left = jnp.where(y_ends[0], y_low, left_up) + jnp.where(y_ends[1], right_down, left_down)
            sum_right = jnp.where(y_ends[0], left_up, right_up) + jnp.where(y_ends[1], y_high, right_down)
            deep = []
            for half in (left, right):
                deep.append(
                    jnp.where(z_ends[0], jnp.where(same[4], half, 0.0), pltpu.roll(half, 1, 1))
                    + jnp.where(z_ends[1], jnp.where(same[5], half, 0.0), pltpu.roll(half, HALF - 1, 1))
                )
            sum_y = jnp.concatenate([sum_left, sum_right], axis=1)
            sum_z = jnp.concatenate(deep, axis=1)
            if f < NPHASE:
                flow = kx * sum_x + ky * sum_y + kz * sum_z - (2.0 * (kx + ky + kz)) * value
                gain = value * (1.0 - value) * (coupling[f] * drive + (2.0 * value - 1.0))
                result = value + phase_rate * (flow + gain) + tail
            else:
                result = value + conc_rates[f - NPHASE] * (sum_x + sum_y + sum_z - 6.0 * value)
            partial[slot, f] = result


def finish_kernel(last_step, neighbors, orient, partial, *refs):
    got_flat, got_deep = refs[0:2], refs[2:4]
    if last_step:
        result, done, sent = refs[4:7]
    else:
        done, flat_refs, sends = refs[4], refs[5:7], refs[7:11]
        deep_refs = refs[11:13]
    grp, dev, rank = place()
    lane = lane_ids((EDGE, HALF))
    y_ends = (lane < EDGE, lane >= HALF - EDGE)
    z_ends = (lane % EDGE == 0, lane % EDGE == EDGE - 1)
    copies = []
    for slot in range(SLOTS):
        number, scale = [], []
        for face in range(6):
            target = neighbors[slot, face]
            number.append(target & (SLOTS - 1))
            scale.append(jnp.where((target >= 0) & (target // SLOTS != rank), 1.0, 0.0))
        even_dev, even_grp = lax.rem(dev, 2) == 0, lax.rem(grp, 2) == 0

        def pick(pair, even, side, cut):
            one, other = cut(pair[0]), cut(pair[1])
            return jnp.where(even, other if side == 0 else one, one if side == 0 else other)

        x_ghost = [pick(got_flat, even_dev, side, lambda ref, n=number[side]: ref[n, 0:8, :]) for side in range(2)]
        y_ghost = [pick(got_flat, even_dev, side, lambda ref, n=number[2 + side]: y_rows(ref, n)) for side in range(2)]
        z_ghost = []
        for side in range(2):
            at, shift = number[4 + side] // 2, (number[4 + side] & 1) * 8
            both = pick(got_deep, even_grp, side, lambda ref, n=at: ref[n])
            z_ghost.append([pltpu.roll(both[:, h * HALF : (h + 1) * HALF], (HALF - shift) % HALF, 1) for h in range(2)])
        spread = weights(orient[slot])
        fresh = []
        for f in range(NFIELD):
            value = partial[slot, f]
            left, right = value[:, :HALF], value[:, HALF:]
            if f < NPHASE:
                factor = [phase_rate * spread[face // 2] * scale[face] for face in range(6)]
            else:
                factor = [conc_rates[f - NPHASE] * scale[face] for face in range(6)]
            y_low = pltpu.roll(y_ghost[0], HALF - EDGE * f, 1) if f else y_ghost[0]
            y_high = pltpu.roll(y_ghost[1], HALF - EDGE - EDGE * f, 1)
            left = left + jnp.where(y_ends[0], factor[2] * y_low, 0.0)
            right = right + jnp.where(y_ends[1], factor[3] * y_high, 0.0)
            halves = []
            for h, half in enumerate((left, right)):
                low = pltpu.roll(z_ghost[0][h], HALF - f, 1) if f else z_ghost[0][h]
                high = pltpu.roll(z_ghost[1][h], EDGE - 1 - f, 1)
                halves.append(half + jnp.where(z_ends[0], factor[4] * low, jnp.where(z_ends[1], factor[5] * high, 0.0)))
            value = jnp.concatenate(halves, axis=1)
            row = row_ids((EDGE, PLANE))
            x_low = jnp.broadcast_to(factor[0] * x_ghost[0][f : f + 1], (EDGE, PLANE))
            x_high = jnp.broadcast_to(factor[1] * x_ghost[1][f : f + 1], (EDGE, PLANE))
            value = value + jnp.where(row == 0, x_low, jnp.where(row == EDGE - 1, x_high, 0.0))
            done[slot, f] = value
            fresh.append(value)
        if last_step:
            copy = pltpu.make_async_copy(done.at[slot], result.at[slot], sent.at[slot])
            copy.start()
            copies.append(copy)
        else:
            pack_slot(fresh, slot, flat_refs, deep_refs)
    for copy in copies:
        copy.wait()
    if not last_step:
        send_faces(flat_refs, deep_refs, sends)


def spec(space):
    return pl.BlockSpec(memory_space=space)


VECTOR, SCALAR = pltpu.VMEM, pltpu.SMEM
SMALL = pltpu.CompilerParams(vmem_limit_bytes=8 << 20)
TABLES = (FLAT, FLAT, FLAT, FLAT, DEEP, DEEP)
DEEP_PAIR = [pltpu.VMEM(DEEP, jnp.float32)] * 2


def shaped(shape):
    return jax.ShapeDtypeStruct(shape, jnp.float32)


def body(fields, swap_dev, swap_grp, neighbors, orient):
    first = exchange(fields[:1], "grp", 0)
    last = exchange(fields[SLOTS - 1 :], "dev", 0)
    state, *tables = pl.pallas_call(
        migrate_kernel,
        name="migrate",
        compiler_params=SMALL,
        out_shape=[shaped(fields.shape)] + [shaped(shape) for shape in TABLES],
        in_specs=[spec(SCALAR)] * 2 + [spec(VECTOR)] * 3,
        out_specs=[spec(VECTOR)] * 7,
        scratch_shapes=DEEP_PAIR,
    )(swap_dev, swap_grp, fields, last, first)
    for step in range(STEPS):
        last_step = step == STEPS - 1
        own, sends = tables[:2], tables[2:]
        got = [exchange(sends[number], "dev" if number < 2 else "grp", number % 2) for number in range(4)]
        partial = pl.pallas_call(
            inner_kernel,
            name=f"inner_{step}",
            compiler_params=SMALL,
            out_shape=shaped(fields.shape),
            in_specs=[spec(SCALAR)] * 2 + [spec(VECTOR)] * 3,
            out_specs=spec(VECTOR),
            cost_estimate=pl.CostEstimate(flops=4 << 20, bytes_accessed=2 << 20, transcendentals=0),
        )(neighbors, orient, state, *own)
        finish = functools.partial(finish_kernel, last_step)
        in_specs = [spec(SCALAR)] * 2 + [spec(VECTOR)] * 5
        if last_step:
            return pl.pallas_call(
                finish,
                name=f"finish_{step}",
                compiler_params=SMALL,
                out_shape=shaped(fields.shape),
                in_specs=in_specs,
                out_specs=spec(pl.ANY),
                scratch_shapes=[pltpu.VMEM(fields.shape, jnp.float32), pltpu.SemaphoreType.DMA((SLOTS,))],
            )(neighbors, orient, partial, *got)
        state, *tables = pl.pallas_call(
            finish,
            name=f"finish_{step}",
            compiler_params=SMALL,
            out_shape=[shaped(fields.shape)] + [shaped(shape) for shape in TABLES],
            in_specs=in_specs,
            out_specs=[spec(VECTOR)] * 7,
            scratch_shapes=DEEP_PAIR,
        )(neighbors, orient, partial, *got)


def solution(mesh):
    in_specs = (
        P(("grp", "dev"), None, None, None),
        P(("grp", "dev")),
        P(("grp", "dev")),
        P(("grp", "dev"), None),
        P(("grp", "dev")),
    )
    out_specs = P(("grp", "dev"), None, None, None)
    return jax.shard_map(body, mesh=mesh, in_specs=in_specs, out_specs=out_specs, check_vma=False)
```

```python
import functools
import math

import jax
import jax.numpy as jnp
from jax import lax
from jax.experimental import pallas as pl
from jax.experimental.pallas import tpu as pltpu
from jax.sharding import PartitionSpec as P

NPHASE = 4
NCONC = 2
NFIELD = NPHASE + NCONC
STEPS = 2
EDGE = 16
PLANE = EDGE * EDGE
HALF = PLANE // 2
SLOTS = 4

phase_rate = 0.05
closure = 0.1
coupling = (0.5, -0.5, 1.0, -1.0)
conc_rates = (0.08, 0.04)

FLAT = (SLOTS, EDGE, PLANE)
DEEP = (SLOTS // 2, EDGE, PLANE)


def partners(axis, offset):
    sizes = (lax.axis_size("grp"), lax.axis_size("dev"))
    along = ("grp", "dev").index(axis)
    route = []
    for grp in range(sizes[0]):
        for dev in range(sizes[1]):
            own = (grp, dev)
            step = 1 if (own[along] - offset) % 2 == 0 else -1
            partner = list(own)
            partner[along] += step
            if not 0 <= partner[along] < sizes[along]:
                partner = list(own)
                partner[1 - along] ^= 1
                if partner[1 - along] >= sizes[1 - along]:
                    partner = list(own)
            route.append((grp * sizes[1] + dev, partner[0] * sizes[1] + partner[1]))
    return route


def exchange(block, axis, offset):
    return lax.ppermute(block, ("grp", "dev"), partners(axis, offset))


def lane_ids(shape):
    return lax.broadcasted_iota(jnp.int32, shape, len(shape) - 1)


def row_ids(shape):
    return lax.broadcasted_iota(jnp.int32, shape, len(shape) - 2)


def pack_slot(fields, slot, flat_refs, deep_refs):
    lane = lane_ids((EDGE, HALF))
    for side in range(2):
        flat, deep = flat_refs[side], deep_refs[side]
        row = side * (EDGE - 1)
        y_face = None
        z_left = z_right = None
        for f, value in enumerate(fields):
            flat[slot, f : f + 1, :] = value[row : row + 1, :]
            half = value[:, :HALF] if side == 0 else value[:, HALF:]
            origin = side * (HALF - EDGE)
            shift = (EDGE * f - origin) % HALF
            moved = pltpu.roll(half, shift, 1) if shift else half
            y_face = moved if y_face is None else jnp.where(lane >= EDGE * f, moved, y_face)
            shift = (8 * (slot % 2) + f - side * (EDGE - 1)) % HALF
            left, right = value[:, :HALF], value[:, HALF:]
            if shift:
                left, right = pltpu.roll(left, shift, 1), pltpu.roll(right, shift, 1)
            place = lane % 8 >= f
            z_left = left if z_left is None else jnp.where(place, left, z_left)
            z_right = right if z_right is None else jnp.where(place, right, z_right)
        flat[slot, 8:16, :HALF] = y_face[:8]
        flat[slot, 8:16, HALF:] = y_face[8:]
        index = slot // 2
        if slot % 2 == 0:
            deep[index, :, :HALF] = z_left
            deep[index, :, HALF:] = z_right
        else:
            upper = lane % EDGE >= 8
            deep[index, :, :HALF] = jnp.where(upper, z_left, deep[index, :, :HALF])
            deep[index, :, HALF:] = jnp.where(upper, z_right, deep[index, :, HALF:])


def send_faces(flat_refs, deep_refs, outs):
    flat_a, flat_b, deep = outs
    even = lax.rem(lax.axis_index("dev"), 2) == 0
    low, high = flat_refs[0][...], flat_refs[1][...]
    flat_a[...] = jnp.where(even, high, low)
    flat_b[...] = jnp.where(even, low, high)
    deep[0], deep[1] = deep_refs[0][...], deep_refs[1][...]


def migrate_kernel(swap_dev, swap_grp, neighbors, orient, fields, last, first, state, *outs):
    del neighbors, orient
    flat_refs, deep_refs = outs[0:2], outs[5:7]
    for slot in range(SLOTS):
        values = []
        for f in range(NFIELD):
            value = fields[slot, f]
            if slot == 0:
                value = jnp.where(swap_grp[0] == 1, first[0, f], value)
            if slot == SLOTS - 1:
                value = jnp.where(swap_dev[0] == 1, last[0, f], value)
            state[slot, f] = value
            values.append(value)
        pack_slot(values, slot, flat_refs, deep_refs)
    send_faces(flat_refs, deep_refs, outs[2:5])


def cos_quarter(number):
    turn = number & 7
    size = jnp.where((turn & 3) == 0, 1.0, jnp.where((turn & 3) == 2, 0.0, math.sqrt(0.5)))
    return jnp.where((turn > 2) & (turn < 6), -size, size)


def weights(angle):
    turn = 0.5 * cos_quarter(angle)
    lift = 0.5 * cos_quarter(angle + 6)
    return 1.0 + turn, 1.0 - turn, 1.0 + lift


def place():
    grp, dev = lax.axis_index("grp"), lax.axis_index("dev")
    return grp, dev, grp * lax.axis_size("dev") + dev


def y_rows(flats, at):
    return jnp.concatenate([flats[at, 8:16, :HALF], flats[at, 8:16, HALF:]], axis=0)


def inner_kernel(neighbors, orient, state, flat_low, flat_high, partial):
    _, _, rank = place()
    lane = lane_ids((EDGE, HALF))
    row = row_ids((EDGE, PLANE))
    for slot in range(SLOTS):
        number, same, local = [], [], []
        for face in range(6):
            target = neighbors[slot, face]
            number.append(target & (SLOTS - 1))
            same.append(target < 0)
            local.append((target >= 0) & (target // SLOTS == rank))
        opposite = (flat_high, flat_low)
        y_ghost = [y_rows(opposite[side], number[2 + side]) for side in range(2)]
        kx, ky, kz = weights(orient[slot])
        values = [state[slot, f] for f in range(NFIELD)]
        total = values[0] + values[1] + values[2] + values[3]
        drive = values[4] - values[5]
        tail = phase_rate * closure * (1.0 - total)
        y_ends = (lane < EDGE, lane >= HALF - EDGE)
        z_ends = (lane % EDGE == 0, lane % EDGE == EDGE - 1)
        for f, value in enumerate(values):
            left, right = value[:, :HALF], value[:, HALF:]

            def ghost(face, arrived, own):
                return jnp.where(same[face], own, jnp.where(local[face], arrived, 0.0))

            x_low = ghost(0, flat_high[number[0], f : f + 1, :], value[:1])
            x_high = ghost(1, flat_low[number[1], f : f + 1, :], value[EDGE - 1 :])
            below = jnp.where(row == 0, jnp.broadcast_to(x_low, (EDGE, PLANE)), pltpu.roll(value, 1, 0))
            above = jnp.where(row == EDGE - 1, jnp.broadcast_to(x_high, (EDGE, PLANE)), pltpu.roll(value, EDGE - 1, 0))
            sum_x = below + above
            left_up, right_up = pltpu.roll(left, EDGE, 1), pltpu.roll(right, EDGE, 1)
            left_down, right_down = pltpu.roll(left, HALF - EDGE, 1), pltpu.roll(right, HALF - EDGE, 1)
            y_low = ghost(2, pltpu.roll(y_ghost[0], (HALF - EDGE * f) % HALF, 1) if f else y_ghost[0], left)
            y_high = ghost(3, pltpu.roll(y_ghost[1], HALF - EDGE - EDGE * f, 1), right)
            sum_left = jnp.where(y_ends[0], y_low, left_up) + jnp.where(y_ends[1], right_down, left_down)
            sum_right = jnp.where(y_ends[0], left_up, right_up) + jnp.where(y_ends[1], y_high, right_down)
            deep = []
            for half in (left, right):
                deep.append(
                    jnp.where(z_ends[0], jnp.where(same[4], half, 0.0), pltpu.roll(half, 1, 1))
                    + jnp.where(z_ends[1], jnp.where(same[5], half, 0.0), pltpu.roll(half, HALF - 1, 1))
                )
            sum_y = jnp.concatenate([sum_left, sum_right], axis=1)
            sum_z = jnp.concatenate(deep, axis=1)
            if f < NPHASE:
                flow = kx * sum_x + ky * sum_y + kz * sum_z - (2.0 * (kx + ky + kz)) * value
                gain = value * (1.0 - value) * (coupling[f] * drive + (2.0 * value - 1.0))
                result = value + phase_rate * (flow + gain) + tail
            else:
                result = value + conc_rates[f - NPHASE] * (sum_x + sum_y + sum_z - 6.0 * value)
            partial[slot, f] = result


def finish_kernel(last_step, neighbors, orient, partial, *refs):
    got_flat, got_deep = refs[0:2], refs[2]
    if last_step:
        result, done, sent = refs[3:6]
    else:
        done, flat_refs, sends = refs[3], refs[4:6], refs[6:9]
        deep_refs = refs[9:11]
    grp, dev, rank = place()
    lane = lane_ids((EDGE, HALF))
    y_ends = (lane < EDGE, lane >= HALF - EDGE)
    z_ends = (lane % EDGE == 0, lane % EDGE == EDGE - 1)
    copies = []
    for slot in range(SLOTS):
        number, scale = [], []
        for face in range(6):
            target = neighbors[slot, face]
            number.append(target & (SLOTS - 1))
            scale.append(jnp.where((target >= 0) & (target // SLOTS != rank), 1.0, 0.0))
        even_dev, even_grp = lax.rem(dev, 2) == 0, lax.rem(grp, 2) == 0

        def pick(pair, even, side, cut):
            one, other = cut(pair[0]), cut(pair[1])
            return jnp.where(even, other if side == 0 else one, one if side == 0 else other)

        x_ghost = [pick(got_flat, even_dev, side, lambda ref, n=number[side]: ref[n, 0:8, :]) for side in range(2)]
        y_ghost = [pick(got_flat, even_dev, side, lambda ref, n=number[2 + side]: y_rows(ref, n)) for side in range(2)]
        z_ghost = []
        for side in range(2):
            at, shift = number[4 + side] // 2, (number[4 + side] & 1) * 8
            group = jnp.clip(grp + 2 * side - 1, 0, got_deep.shape[0] - 1)
            both = got_deep[group, 1 - side, at]
            z_ghost.append([pltpu.roll(both[:, h * HALF : (h + 1) * HALF], (HALF - shift) % HALF, 1) for h in range(2)])
        spread = weights(orient[slot])
        fresh = []
        for f in range(NFIELD):
            value = partial[slot, f]
            left, right = value[:, :HALF], value[:, HALF:]
            if f < NPHASE:
                factor = [phase_rate * spread[face // 2] * scale[face] for face in range(6)]
            else:
                factor = [conc_rates[f - NPHASE] * scale[face] for face in range(6)]
            y_low = pltpu.roll(y_ghost[0], HALF - EDGE * f, 1) if f else y_ghost[0]
            y_high = pltpu.roll(y_ghost[1], HALF - EDGE - EDGE * f, 1)
            left = left + jnp.where(y_ends[0], factor[2] * y_low, 0.0)
            right = right + jnp.where(y_ends[1], factor[3] * y_high, 0.0)
            halves = []
            for h, half in enumerate((left, right)):
                low = pltpu.roll(z_ghost[0][h], HALF - f, 1) if f else z_ghost[0][h]
                high = pltpu.roll(z_ghost[1][h], EDGE - 1 - f, 1)
                halves.append(half + jnp.where(z_ends[0], factor[4] * low, jnp.where(z_ends[1], factor[5] * high, 0.0)))
            value = jnp.concatenate(halves, axis=1)
            row = row_ids((EDGE, PLANE))
            x_low = jnp.broadcast_to(factor[0] * x_ghost[0][f : f + 1], (EDGE, PLANE))
            x_high = jnp.broadcast_to(factor[1] * x_ghost[1][f : f + 1], (EDGE, PLANE))
            value = value + jnp.where(row == 0, x_low, jnp.where(row == EDGE - 1, x_high, 0.0))
            done[slot, f] = value
            fresh.append(value)
        if last_step:
            copy = pltpu.make_async_copy(done.at[slot], result.at[slot], sent.at[slot])
            copy.start()
            copies.append(copy)
        else:
            pack_slot(fresh, slot, flat_refs, deep_refs)
    for copy in copies:
        copy.wait()
    if not last_step:
        send_faces(flat_refs, deep_refs, sends)


def spec(space):
    return pl.BlockSpec(memory_space=space)


VECTOR, SCALAR = pltpu.VMEM, pltpu.SMEM
SMALL = pltpu.CompilerParams(vmem_limit_bytes=8 << 20)
TABLES = (FLAT, FLAT, FLAT, FLAT, (2, *DEEP))
DEEP_PAIR = [pltpu.VMEM(DEEP, jnp.float32)] * 2


def shaped(shape):
    return jax.ShapeDtypeStruct(shape, jnp.float32)


def body(fields, swap_dev, swap_grp, neighbors, orient):
    first = exchange(fields[:1], "grp", 0)
    last = exchange(fields[SLOTS - 1 :], "dev", 0)
    state, *tables = pl.pallas_call(
        migrate_kernel,
        name="migrate",
        compiler_params=SMALL,
        out_shape=[shaped(fields.shape)] + [shaped(shape) for shape in TABLES],
        in_specs=[spec(SCALAR)] * 4 + [spec(VECTOR)] * 3,
        out_specs=[spec(VECTOR)] * 6,
        scratch_shapes=DEEP_PAIR,
    )(swap_dev, swap_grp, neighbors, orient, fields, last, first)
    for step in range(STEPS):
        last_step = step == STEPS - 1
        own, sends = tables[:2], tables[2:]
        got = [lax.all_gather(sends[2], "grp")] + [exchange(sends[number], "dev", number) for number in range(2)]
        got = [got[1], got[2], got[0]]
        partial = pl.pallas_call(
            inner_kernel,
            name=f"inner_{step}",
            compiler_params=SMALL,
            out_shape=shaped(fields.shape),
            in_specs=[spec(SCALAR)] * 2 + [spec(VECTOR)] * 3,
            out_specs=spec(VECTOR),
            cost_estimate=pl.CostEstimate(flops=4 << 20, bytes_accessed=2 << 20, transcendentals=0),
        )(neighbors, orient, state, *own)
        finish = functools.partial(finish_kernel, last_step)
        in_specs = [spec(SCALAR)] * 2 + [spec(VECTOR)] * 4
        if last_step:
            return pl.pallas_call(
                finish,
                name=f"finish_{step}",
                compiler_params=SMALL,
                out_shape=shaped(fields.shape),
                in_specs=in_specs,
                out_specs=spec(pl.ANY),
                scratch_shapes=[pltpu.VMEM(fields.shape, jnp.float32), pltpu.SemaphoreType.DMA((SLOTS,))],
            )(neighbors, orient, partial, *got)
        state, *tables = pl.pallas_call(
            finish,
            name=f"finish_{step}",
            compiler_params=SMALL,
            out_shape=[shaped(fields.shape)] + [shaped(shape) for shape in TABLES],
            in_specs=in_specs,
            out_specs=[spec(VECTOR)] * 6,
            scratch_shapes=DEEP_PAIR,
        )(neighbors, orient, partial, *got)


def solution(mesh):
    in_specs = (
        P(("grp", "dev"), None, None, None),
        P(("grp", "dev")),
        P(("grp", "dev")),
        P(("grp", "dev"), None),
        P(("grp", "dev")),
    )
    out_specs = P(("grp", "dev"), None, None, None)
    return jax.shard_map(body, mesh=mesh, in_specs=in_specs, out_specs=out_specs, check_vma=False)
```

```python
import functools
import math

import jax
import jax.numpy as jnp
from jax import lax
from jax.experimental import pallas as pl
from jax.experimental.pallas import tpu as pltpu
from jax.sharding import PartitionSpec as P

NPHASE = 4
NCONC = 2
NFIELD = NPHASE + NCONC
STEPS = 2
EDGE = 16
PLANE = EDGE * EDGE
HALF = PLANE // 2
GROUPS = HALF // EDGE
SLOTS = 4
ROWS = NFIELD * SLOTS

phase_rate = 0.05
closure = 0.1
coupling = (0.5, -0.5, 1.0, -1.0)
conc_rates = (0.08, 0.04)

STATE = (2, EDGE * ROWS, HALF)
FACE = (ROWS, PLANE)
SIDE = (3, ROWS, PLANE)
SOURCES = 4


def partners(axis, offset):
    sizes = (lax.axis_size("grp"), lax.axis_size("dev"))
    along = ("grp", "dev").index(axis)
    route = []
    for grp in range(sizes[0]):
        for dev in range(sizes[1]):
            own = (grp, dev)
            step = 1 if (own[along] - offset) % 2 == 0 else -1
            partner = list(own)
            partner[along] += step
            if not 0 <= partner[along] < sizes[along]:
                partner = list(own)
                partner[1 - along] ^= 1
                if partner[1 - along] >= sizes[1 - along]:
                    partner = list(own)
            route.append((grp * sizes[1] + dev, partner[0] * sizes[1] + partner[1]))
    return route


def exchange(block, axis, offset):
    return lax.ppermute(block, ("grp", "dev"), partners(axis, offset))


def iota(shape, dim):
    return lax.broadcasted_iota(jnp.int32, shape, dim)


def plane_at(ref, x):
    rows = pl.ds(x * ROWS, ROWS)
    return ref[0, rows, :], ref[1, rows, :]


def turned(value, shift):
    shift %= HALF
    return pltpu.roll(value, shift, 1) if shift else value


class Packer:
    def __init__(self):
        lane = iota((ROWS, HALF), 1)
        self.lane, self.group, self.place = lane, lane // EDGE, lane % EDGE
        self.y = [[None, None], [None, None]]
        self.z = [[None, None], [None, None]]

    def add(self, x, left, right):
        odd, half, at = x % 2, x // GROUPS, x % GROUPS
        ends = turned(jnp.where(self.lane < EDGE, left, right), EDGE * at)
        taken = (self.group == at) | (self.group == (at + GROUPS - 1) % GROUPS)
        before = self.y[half][odd]
        self.y[half][odd] = ends if before is None else jnp.where(taken, ends, before)
        taken = (self.place == x) | (self.place == (x + EDGE - 1) % EDGE)
        for h, value in enumerate((left, right)):
            moved = turned(value, x)
            before = self.z[h][odd]
            self.z[h][odd] = moved if before is None else jnp.where(taken, moved, before)

    def tables(self, h):
        even_group, even_place = self.group % 2 == 0, self.place % 2 == 0
        (y_even, y_odd), (z_even, z_odd) = self.y[h], self.z[h]
        low = (jnp.where(even_group, y_even, y_odd), jnp.where(even_place, z_even, z_odd))
        y_high, z_high = jnp.where(even_group, y_odd, y_even), jnp.where(even_place, z_odd, z_even)
        return low, (turned(y_high, EDGE), turned(z_high, 1 - EDGE))


def emit_faces(packer, state, own, sends):
    low, high = own
    for h in range(2):
        lanes = pl.ds(h * HALF, HALF)
        for ref, x in ((low, 0), (high, EDGE - 1)):
            ref[0, :, lanes] = state[h, pl.ds(x * ROWS, ROWS), :]
        for ref, (y_table, z_table) in zip(own, packer.tables(h)):
            ref[1, :, lanes] = y_table
            ref[2, :, lanes] = z_table
    flat_a, flat_b, deep_a, deep_b = sends
    even = lax.rem(lax.axis_index("dev"), 2) == 0
    for face in range(2):
        flat_a[face] = jnp.where(even, high[face], low[face])
        flat_b[face] = jnp.where(even, low[face], high[face])
    even = lax.rem(lax.axis_index("grp"), 2) == 0
    deep_a[...] = jnp.where(even, high[2], low[2])
    deep_b[...] = jnp.where(even, low[2], high[2])


def migrate_kernel(swap_dev, swap_grp, scale, fields, last, first, state, *outs):
    del scale
    own, sends = outs[0:2], outs[2:6]
    for slot in range(SLOTS):
        for f in range(NFIELD):
            value = fields[slot, f]
            if slot == 0:
                value = jnp.where(swap_grp[0] == 1, first[0, f], value)
            if slot == SLOTS - 1:
                value = jnp.where(swap_dev[0] == 1, last[0, f], value)
            for h in range(2):
                state[h, pl.ds(f * SLOTS + slot, EDGE, stride=ROWS), :] = value[:, h * HALF : (h + 1) * HALF]
    packer = Packer()
    for x in range(EDGE):
        packer.add(x, *plane_at(state, x))
    emit_faces(packer, state, own, sends)


def cos_quarter(number):
    turn = number & 7
    size = jnp.where((turn & 3) == 0, 1.0, jnp.where((turn & 3) == 2, 0.0, math.sqrt(0.5)))
    return jnp.where((turn > 2) & (turn < 6), -size, size)


def plan_kernel(neighbors, orient, scale, select):
    shape = (ROWS, HALF)
    slot, field, column = iota(shape, 0) % SLOTS, iota(shape, 0) // SLOTS, iota(shape, 1)
    grp, dev = lax.axis_index("grp"), lax.axis_index("dev")
    rank = grp * lax.axis_size("dev") + dev

    def by_slot(values):
        rows = values[0]
        for number in range(1, SLOTS):
            rows = jnp.where(slot == number, values[number], rows)
        return rows

    spread = []
    for number in range(SLOTS):
        turn = 0.5 * cos_quarter(orient[number])
        lift = 0.5 * cos_quarter(orient[number] + 6)
        spread.append((1.0 + turn, 1.0 - turn, 1.0 + lift))
    conc = jnp.where(field == NPHASE, conc_rates[0], conc_rates[1])
    weights = [jnp.where(field < NPHASE, phase_rate * by_slot([own[axis] for own in spread]), conc) for axis in range(3)]
    for axis in range(3):
        scale[axis] = weights[axis]
    scale[3] = 1.0 - 2.0 * (weights[0] + weights[1] + weights[2])
    for face in range(6):
        first = []
        came = 2 + lax.rem(lax.rem(dev if face < 4 else grp, 2) + face % 2 + 1, 2)
        for number in range(SLOTS):
            target = neighbors[number, face]
            source = jnp.where(target < 0, 0, jnp.where(target // SLOTS == rank, 1, came))
            first.append(source * ROWS + jnp.where(target < 0, number, target & (SLOTS - 1)))
        select[face] = jnp.where(column == by_slot(first) + field * SLOTS, weights[face // 2], 0.0)


def inner_kernel(state, scale, partial):
    lane = iota((ROWS, HALF), 1)
    start_y, end_y = lane < EDGE, lane >= HALF - EDGE
    start_z, end_z = lane % EDGE == 0, lane % EDGE == EDGE - 1
    weight_x, weight_y, weight_z, weight = (scale[number] for number in range(4))
    tile = 2 * SLOTS
    planes = {0: plane_at(state, 0)}
    for x in range(EDGE):
        if x + 1 < EDGE:
            planes[x + 1] = plane_at(state, x + 1)
        left, right = planes[x]
        up = [turned(half, EDGE) for half in (left, right)]
        down = [turned(half, -EDGE) for half in (left, right)]
        sum_y = (
            jnp.where(start_y, 0.0, up[0]) + jnp.where(end_y, down[1], down[0]),
            jnp.where(start_y, up[0], up[1]) + jnp.where(end_y, 0.0, down[1]),
        )
        for h, half in enumerate((left, right)):
            sum_z = jnp.where(start_z, 0.0, turned(half, 1)) + jnp.where(end_z, 0.0, turned(half, -1))
            if x == 0:
                sum_x = planes[1][h]
            elif x == EDGE - 1:
                sum_x = planes[x - 1][h]
            else:
                sum_x = planes[x - 1][h] + planes[x + 1][h]
            flow = weight * half + weight_x * sum_x + weight_y * sum_y[h] + weight_z * sum_z
            phases, conc = (half[:tile], half[tile : 2 * tile]), half[2 * tile :]
            drive = conc - pltpu.roll(conc, SLOTS, 0)
            total = phases[0] + phases[1]
            total = total + pltpu.roll(total, SLOTS, 0)
            tail = (phase_rate * closure) * (1.0 - total)
            rows = x * ROWS
            for number, value in enumerate(phases):
                gain = value * (1.0 - value) * (coupling[2 * number] * drive + (2.0 * value - 1.0))
                part = flow[number * tile : (number + 1) * tile]
                partial[h, pl.ds(rows + number * tile, tile), :] = part + (phase_rate * gain + tail)
            partial[h, pl.ds(rows + 2 * tile, tile), :] = flow[2 * tile :]


def finish_kernel(last_step, select, partial, *refs):
    own, got_flat, got_deep = refs[0:2], refs[2:4], refs[4:6]
    if last_step:
        result, done, blocks, sent = refs[6:10]
    else:
        done, outs, sends = refs[6], refs[7:9], refs[9:13]
    ghosts = []
    for face in range(6):
        axis, side = face // 2, face % 2
        got = [ref[axis] for ref in got_flat] if axis < 2 else [ref[...] for ref in got_deep]
        tables = jnp.concatenate([own[side][axis], own[1 - side][axis], *got], axis=0)
        chosen = select[face][:, : SOURCES * ROWS]
        ghosts.append(jnp.dot(chosen, tables, precision=lax.Precision.HIGHEST, preferred_element_type=jnp.float32))
    lane = iota((ROWS, HALF), 1)
    start_y, end_y = lane < EDGE, lane >= HALF - EDGE
    ends_z = (lane % EDGE == 0) | (lane % EDGE == EDGE - 1)
    even_group, even_place = (lane // EDGE) % 2 == 0, lane % 2 == 0
    y_pairs, z_pairs = [], []
    for h in range(2):
        lanes = slice(h * HALF, (h + 1) * HALF)
        low, high = ghosts[2][:, lanes], turned(ghosts[3][:, lanes], -EDGE)
        y_pairs.append((jnp.where(even_group, low, high), jnp.where(even_group, high, low)))
        low, high = ghosts[4][:, lanes], turned(ghosts[5][:, lanes], EDGE - 1)
        z_pairs.append((jnp.where(even_place, low, high), jnp.where(even_place, high, low)))
    packer = None if last_step else Packer()
    copies = []
    for x in range(EDGE):
        halves = list(plane_at(partial, x))
        ends = turned(y_pairs[x // GROUPS][x % 2], -EDGE * (x % GROUPS))
        for h in range(2):
            value = halves[h] + jnp.where(start_y if h == 0 else end_y, ends, 0.0)
            value = value + jnp.where(ends_z, turned(z_pairs[h][x % 2], -x), 0.0)
            if x == 0:
                value = value + ghosts[0][:, h * HALF : (h + 1) * HALF]
            if x == EDGE - 1:
                value = value + ghosts[1][:, h * HALF : (h + 1) * HALF]
            done[h, pl.ds(x * ROWS, ROWS), :] = value
            halves[h] = value
        if not last_step:
            packer.add(x, *halves)
        elif x % 8 == 7:
            first = x - 7
            for slot in range(SLOTS):
                for f in range(NFIELD):
                    rows = pl.ds(first * ROWS + f * SLOTS + slot, 8, stride=ROWS)
                    for h in range(2):
                        lanes = pl.ds(h * HALF, HALF)
                        blocks[slot, f, first : first + 8, lanes] = done[h, rows, :]
            part = pl.ds(first, 8)
            copy = pltpu.make_async_copy(blocks.at[:, :, part], result.at[:, :, part], sent.at[x // 8])
            copy.start()
            copies.append(copy)
    for copy in copies:
        copy.wait()
    if not last_step:
        emit_faces(packer, done, outs, sends)


def spec(space):
    return pl.BlockSpec(memory_space=space)


VECTOR, SCALAR = pltpu.VMEM, pltpu.SMEM
SMALL = pltpu.CompilerParams(vmem_limit_bytes=8 << 20)
FLAT = (2, ROWS, PLANE)
TABLES = (STATE, SIDE, SIDE, FLAT, FLAT, FACE, FACE)


def shaped(shape):
    return jax.ShapeDtypeStruct(shape, jnp.float32)


def cost(flops):
    return pl.CostEstimate(flops=flops, bytes_accessed=2 << 20, transcendentals=0)


def body(fields, swap_dev, swap_grp, neighbors, orient):
    first = exchange(fields[:1], "grp", 0)
    last = exchange(fields[SLOTS - 1 :], "dev", 0)
    scale, select = pl.pallas_call(
        plan_kernel,
        name="plan",
        compiler_params=SMALL,
        out_shape=[shaped((4, ROWS, HALF)), shaped((6, ROWS, HALF))],
        in_specs=[spec(SCALAR)] * 2,
        out_specs=[spec(VECTOR)] * 2,
        cost_estimate=cost(1 << 20),
    )(neighbors, orient)
    state, *tables = pl.pallas_call(
        migrate_kernel,
        name="migrate",
        compiler_params=SMALL,
        out_shape=[shaped(shape) for shape in TABLES],
        in_specs=[spec(SCALAR)] * 2 + [spec(VECTOR)] * 4,
        out_specs=[spec(VECTOR)] * 7,
    )(swap_dev, swap_grp, scale, fields, last, first)
    for step in range(STEPS):
        last_step = step == STEPS - 1
        own, sends = tables[:2], tables[2:]
        got = [exchange(sends[number], "dev" if number < 2 else "grp", number % 2) for number in range(4)]
        partial = pl.pallas_call(
            inner_kernel,
            name=f"inner_{step}",
            compiler_params=SMALL,
            out_shape=shaped(STATE),
            in_specs=[spec(VECTOR)] * 2,
            out_specs=spec(VECTOR),
            cost_estimate=cost(4 << 20),
        )(state, scale)
        finish = functools.partial(finish_kernel, last_step)
        in_specs = [spec(VECTOR)] * 8
        if last_step:
            return pl.pallas_call(
                finish,
                name=f"finish_{step}",
                compiler_params=SMALL,
                out_shape=shaped(fields.shape),
                in_specs=in_specs,
                out_specs=spec(pl.ANY),
                scratch_shapes=[
                    pltpu.VMEM(STATE, jnp.float32),
                    pltpu.VMEM(fields.shape, jnp.float32),
                    pltpu.SemaphoreType.DMA((2,)),
                ],
            )(select, partial, *own, *got)
        state, *tables = pl.pallas_call(
            finish,
            name=f"finish_{step}",
            compiler_params=SMALL,
            out_shape=[shaped(shape) for shape in TABLES],
            in_specs=in_specs,
            out_specs=[spec(VECTOR)] * 7,
        )(select, partial, *own, *got)


def solution(mesh):
    in_specs = (
        P(("grp", "dev"), None, None, None),
        P(("grp", "dev")),
        P(("grp", "dev")),
        P(("grp", "dev"), None),
        P(("grp", "dev")),
    )
    out_specs = P(("grp", "dev"), None, None, None)
    return jax.shard_map(body, mesh=mesh, in_specs=in_specs, out_specs=out_specs, check_vma=False)
```

```python
import functools
import math

import jax
import jax.numpy as jnp
from jax import lax
from jax.experimental import pallas as pl
from jax.experimental.pallas import tpu as pltpu
from jax.sharding import PartitionSpec as P

NPHASE = 4
NCONC = 2
NFIELD = NPHASE + NCONC
STEPS = 2
EDGE = 16
PLANE = EDGE * EDGE
HALF = PLANE // 2
GROUPS = HALF // EDGE
SLOTS = 4
ROWS = NFIELD * SLOTS

phase_rate = 0.05
closure = 0.1
coupling = (0.5, -0.5, 1.0, -1.0)
conc_rates = (0.08, 0.04)

STATE = (2, EDGE * ROWS, HALF)
FACE = (ROWS, PLANE)
SIDE = (3, ROWS, PLANE)
SOURCES = 4


def partners(axis, offset):
    sizes = (lax.axis_size("grp"), lax.axis_size("dev"))
    along = ("grp", "dev").index(axis)
    route = []
    for grp in range(sizes[0]):
        for dev in range(sizes[1]):
            own = (grp, dev)
            step = 1 if (own[along] - offset) % 2 == 0 else -1
            partner = list(own)
            partner[along] += step
            if not 0 <= partner[along] < sizes[along]:
                partner = list(own)
                partner[1 - along] ^= 1
                if partner[1 - along] >= sizes[1 - along]:
                    partner = list(own)
            route.append((grp * sizes[1] + dev, partner[0] * sizes[1] + partner[1]))
    return route


def exchange(block, axis, offset):
    return lax.ppermute(block, ("grp", "dev"), partners(axis, offset))


def iota(shape, dim):
    return lax.broadcasted_iota(jnp.int32, shape, dim)


def plane_at(ref, x):
    rows = pl.ds(x * ROWS, ROWS)
    return ref[0, rows, :], ref[1, rows, :]


def turned(value, shift):
    shift %= HALF
    return pltpu.roll(value, shift, 1) if shift else value


class Packer:
    def __init__(self):
        lane = iota((ROWS, HALF), 1)
        self.lane, self.group, self.place = lane, lane // EDGE, lane % EDGE
        self.y = [[None, None], [None, None]]
        self.z = [[None, None], [None, None]]

    def add(self, x, left, right):
        odd, half, at = x % 2, x // GROUPS, x % GROUPS
        ends = turned(jnp.where(self.lane < EDGE, left, right), EDGE * at)
        taken = (self.group == at) | (self.group == (at + GROUPS - 1) % GROUPS)
        before = self.y[half][odd]
        self.y[half][odd] = ends if before is None else jnp.where(taken, ends, before)
        taken = (self.place == x) | (self.place == (x + EDGE - 1) % EDGE)
        for h, value in enumerate((left, right)):
            moved = turned(value, x)
            before = self.z[h][odd]
            self.z[h][odd] = moved if before is None else jnp.where(taken, moved, before)

    def tables(self, h):
        even_group, even_place = self.group % 2 == 0, self.place % 2 == 0
        (y_even, y_odd), (z_even, z_odd) = self.y[h], self.z[h]
        low = (jnp.where(even_group, y_even, y_odd), jnp.where(even_place, z_even, z_odd))
        y_high, z_high = jnp.where(even_group, y_odd, y_even), jnp.where(even_place, z_odd, z_even)
        return low, (turned(y_high, EDGE), turned(z_high, 1 - EDGE))


def emit_faces(packer, state, own, sends):
    low, high = own
    for h in range(2):
        lanes = pl.ds(h * HALF, HALF)
        for ref, x in ((low, 0), (high, EDGE - 1)):
            ref[0, :, lanes] = state[h, pl.ds(x * ROWS, ROWS), :]
        for ref, (y_table, z_table) in zip(own, packer.tables(h)):
            ref[1, :, lanes] = y_table
            ref[2, :, lanes] = z_table
    flat_a, flat_b, deep = sends
    even = lax.rem(lax.axis_index("dev"), 2) == 0
    for face in range(2):
        flat_a[face] = jnp.where(even, high[face], low[face])
        flat_b[face] = jnp.where(even, low[face], high[face])
    grp = lax.axis_index("grp")
    for to in range(deep.shape[0]):
        deep[to] = jnp.where(grp < to, high[2], low[2])


def cut_kernel(fields, first, last, done):
    copies = [
        pltpu.make_async_copy(fields.at[pl.ds(slot, 1)], ref, done.at[number])
        for number, (slot, ref) in enumerate(((0, first), (SLOTS - 1, last)))
    ]
    for copy in copies:
        copy.start()
    for copy in copies:
        copy.wait()


def migrate_kernel(swap_dev, swap_grp, scale, fields, last, first, state, *outs):
    del scale
    own, sends = outs[0:2], outs[2:5]
    for slot in range(SLOTS):
        for f in range(NFIELD):
            value = fields[slot, f]
            if slot == 0:
                value = jnp.where(swap_grp[0] == 1, first[0, f], value)
            if slot == SLOTS - 1:
                value = jnp.where(swap_dev[0] == 1, last[0, f], value)
            for h in range(2):
                state[h, pl.ds(f * SLOTS + slot, EDGE, stride=ROWS), :] = value[:, h * HALF : (h + 1) * HALF]
    packer = Packer()
    for x in range(EDGE):
        packer.add(x, *plane_at(state, x))
    emit_faces(packer, state, own, sends)


def cos_quarter(number):
    turn = number & 7
    size = jnp.where((turn & 3) == 0, 1.0, jnp.where((turn & 3) == 2, 0.0, math.sqrt(0.5)))
    return jnp.where((turn > 2) & (turn < 6), -size, size)


def plan_kernel(neighbors, orient, scale, select):
    shape = (ROWS, HALF)
    slot, field, column = iota(shape, 0) % SLOTS, iota(shape, 0) // SLOTS, iota(shape, 1)
    grp, dev = lax.axis_index("grp"), lax.axis_index("dev")
    rank = grp * lax.axis_size("dev") + dev

    def by_slot(values):
        rows = values[0]
        for number in range(1, SLOTS):
            rows = jnp.where(slot == number, values[number], rows)
        return rows

    spread = []
    for number in range(SLOTS):
        turn = 0.5 * cos_quarter(orient[number])
        lift = 0.5 * cos_quarter(orient[number] + 6)
        spread.append((1.0 + turn, 1.0 - turn, 1.0 + lift))
    conc = jnp.where(field == NPHASE, conc_rates[0], conc_rates[1])
    weights = [jnp.where(field < NPHASE, phase_rate * by_slot([own[axis] for own in spread]), conc) for axis in range(3)]
    for axis in range(3):
        scale[axis] = weights[axis]
    scale[3] = 1.0 - 2.0 * (weights[0] + weights[1] + weights[2])
    for face in range(6):
        first = []
        came = 2 + lax.rem(lax.rem(dev if face < 4 else grp, 2) + face % 2 + 1, 2)
        for number in range(SLOTS):
            target = neighbors[number, face]
            source = jnp.where(target < 0, 0, jnp.where(target // SLOTS == rank, 1, came))
            first.append(source * ROWS + jnp.where(target < 0, number, target & (SLOTS - 1)))
        select[face] = jnp.where(column == by_slot(first) + field * SLOTS, weights[face // 2], 0.0)


def inner_kernel(state, scale, partial):
    lane = iota((ROWS, HALF), 1)
    start_y, end_y = lane < EDGE, lane >= HALF - EDGE
    start_z, end_z = lane % EDGE == 0, lane % EDGE == EDGE - 1
    weight_x, weight_y, weight_z, weight = (scale[number] for number in range(4))
    tile = 2 * SLOTS
    planes = {0: plane_at(state, 0)}
    for x in range(EDGE):
        if x + 1 < EDGE:
            planes[x + 1] = plane_at(state, x + 1)
        left, right = planes[x]
        up = [turned(half, EDGE) for half in (left, right)]
        down = [turned(half, -EDGE) for half in (left, right)]
        sum_y = (
            jnp.where(start_y, 0.0, up[0]) + jnp.where(end_y, down[1], down[0]),
            jnp.where(start_y, up[0], up[1]) + jnp.where(end_y, 0.0, down[1]),
        )
        for h, half in enumerate((left, right)):
            sum_z = jnp.where(start_z, 0.0, turned(half, 1)) + jnp.where(end_z, 0.0, turned(half, -1))
            if x == 0:
                sum_x = planes[1][h]
            elif x == EDGE - 1:
                sum_x = planes[x - 1][h]
            else:
                sum_x = planes[x - 1][h] + planes[x + 1][h]
            flow = weight * half + weight_x * sum_x + weight_y * sum_y[h] + weight_z * sum_z
            phases, conc = (half[:tile], half[tile : 2 * tile]), half[2 * tile :]
            drive = conc - pltpu.roll(conc, SLOTS, 0)
            total = phases[0] + phases[1]
            total = total + pltpu.roll(total, SLOTS, 0)
            tail = (phase_rate * closure) * (1.0 - total)
            rows = x * ROWS
            for number, value in enumerate(phases):
                gain = value * (1.0 - value) * (coupling[2 * number] * drive + (2.0 * value - 1.0))
                part = flow[number * tile : (number + 1) * tile]
                partial[h, pl.ds(rows + number * tile, tile), :] = part + (phase_rate * gain + tail)
            partial[h, pl.ds(rows + 2 * tile, tile), :] = flow[2 * tile :]


def finish_kernel(last_step, select, partial, *refs):
    own, got_flat, deep = refs[0:2], refs[2:4], refs[4]
    if last_step:
        result, done, blocks, sent = refs[5:9]
    else:
        done, outs, sends = refs[5], refs[6:8], refs[8:11]
    grp, even = lax.axis_index("grp"), lax.rem(lax.axis_index("grp"), 2) == 0
    before, after = deep[jnp.maximum(grp - 1, 0)], deep[jnp.minimum(grp + 1, deep.shape[0] - 1)]
    got_deep = jnp.where(even, after, before), jnp.where(even, before, after)
    ghosts = []
    for face in range(6):
        axis, side = face // 2, face % 2
        got = [ref[axis] for ref in got_flat] if axis < 2 else list(got_deep)
        tables = jnp.concatenate([own[side][axis], own[1 - side][axis], *got], axis=0)
        chosen = select[face][:, : SOURCES * ROWS]
        ghosts.append(jnp.dot(chosen, tables, precision=lax.Precision.HIGHEST, preferred_element_type=jnp.float32))
    lane = iota((ROWS, HALF), 1)
    start_y, end_y = lane < EDGE, lane >= HALF - EDGE
    ends_z = (lane % EDGE == 0) | (lane % EDGE == EDGE - 1)
    even_group, even_place = (lane // EDGE) % 2 == 0, lane % 2 == 0
    y_pairs, z_pairs = [], []
    for h in range(2):
        lanes = slice(h * HALF, (h + 1) * HALF)
        low, high = ghosts[2][:, lanes], turned(ghosts[3][:, lanes], -EDGE)
        y_pairs.append((jnp.where(even_group, low, high), jnp.where(even_group, high, low)))
        low, high = ghosts[4][:, lanes], turned(ghosts[5][:, lanes], EDGE - 1)
        z_pairs.append((jnp.where(even_place, low, high), jnp.where(even_place, high, low)))
    packer = None if last_step else Packer()
    copies = []
    for x in range(EDGE):
        halves = list(plane_at(partial, x))
        ends = turned(y_pairs[x // GROUPS][x % 2], -EDGE * (x % GROUPS))
        for h in range(2):
            value = halves[h] + jnp.where(start_y if h == 0 else end_y, ends, 0.0)
            value = value + jnp.where(ends_z, turned(z_pairs[h][x % 2], -x), 0.0)
            if x == 0:
                value = value + ghosts[0][:, h * HALF : (h + 1) * HALF]
            if x == EDGE - 1:
                value = value + ghosts[1][:, h * HALF : (h + 1) * HALF]
            done[h, pl.ds(x * ROWS, ROWS), :] = value
            halves[h] = value
        if not last_step:
            packer.add(x, *halves)
        elif x % 8 == 7:
            first = x - 7
            for slot in range(SLOTS):
                for f in range(NFIELD):
                    rows = pl.ds(first * ROWS + f * SLOTS + slot, 8, stride=ROWS)
                    for h in range(2):
                        lanes = pl.ds(h * HALF, HALF)
                        blocks[slot, f, first : first + 8, lanes] = done[h, rows, :]
            part = pl.ds(first, 8)
            copy = pltpu.make_async_copy(blocks.at[:, :, part], result.at[:, :, part], sent.at[x // 8])
            copy.start()
            copies.append(copy)
    for copy in copies:
        copy.wait()
    if not last_step:
        emit_faces(packer, done, outs, sends)


def spec(space):
    return pl.BlockSpec(memory_space=space)


VECTOR, SCALAR = pltpu.VMEM, pltpu.SMEM
SMALL = pltpu.CompilerParams(vmem_limit_bytes=8 << 20)
FLAT = (2, ROWS, PLANE)
TABLES = (STATE, SIDE, SIDE, FLAT, FLAT)


def shaped(shape):
    return jax.ShapeDtypeStruct(shape, jnp.float32)


def cost(flops):
    return pl.CostEstimate(flops=flops, bytes_accessed=2 << 20, transcendentals=0)


def body(fields, swap_dev, swap_grp, neighbors, orient):
    first, last = pl.pallas_call(
        cut_kernel,
        name="cut",
        compiler_params=SMALL,
        out_shape=[shaped((1, *fields.shape[1:]))] * 2,
        in_specs=[spec(pltpu.HBM)],
        out_specs=[spec(VECTOR)] * 2,
        scratch_shapes=[pltpu.SemaphoreType.DMA((2,))],
    )(pltpu.with_memory_space_constraint(fields, pltpu.HBM))
    first = exchange(first, "grp", 0)
    last = exchange(last, "dev", 0)
    scale, select = pl.pallas_call(
        plan_kernel,
        name="plan",
        compiler_params=SMALL,
        out_shape=[shaped((4, ROWS, HALF)), shaped((6, ROWS, HALF))],
        in_specs=[spec(SCALAR)] * 2,
        out_specs=[spec(VECTOR)] * 2,
        cost_estimate=cost(1 << 20),
    )(neighbors, orient)
    state, *tables = pl.pallas_call(
        migrate_kernel,
        name="migrate",
        compiler_params=SMALL,
        out_shape=[shaped(shape) for shape in (*TABLES, (lax.axis_size("grp"), *FACE))],
        in_specs=[spec(SCALAR)] * 2 + [spec(VECTOR)] * 4,
        out_specs=[spec(VECTOR)] * 6,
    )(swap_dev, swap_grp, scale, fields, last, first)
    for step in range(STEPS):
        last_step = step == STEPS - 1
        own, sends = tables[:2], tables[2:]
        got = [exchange(sends[number], "dev", number) for number in range(2)]
        got.append(lax.all_to_all(sends[2], "grp", 0, 0))
        partial = pl.pallas_call(
            inner_kernel,
            name=f"inner_{step}",
            compiler_params=SMALL,
            out_shape=shaped(STATE),
            in_specs=[spec(VECTOR)] * 2,
            out_specs=spec(VECTOR),
            cost_estimate=cost(4 << 20),
        )(state, scale)
        finish = functools.partial(finish_kernel, last_step)
        in_specs = [spec(VECTOR)] * 7
        if last_step:
            return pl.pallas_call(
                finish,
                name=f"finish_{step}",
                compiler_params=SMALL,
                out_shape=shaped(fields.shape),
                in_specs=in_specs,
                out_specs=spec(pl.ANY),
                scratch_shapes=[
                    pltpu.VMEM(STATE, jnp.float32),
                    pltpu.VMEM(fields.shape, jnp.float32),
                    pltpu.SemaphoreType.DMA((2,)),
                ],
            )(select, partial, *own, *got)
        state, *tables = pl.pallas_call(
            finish,
            name=f"finish_{step}",
            compiler_params=SMALL,
            out_shape=[shaped(shape) for shape in (*TABLES, (lax.axis_size("grp"), *FACE))],
            in_specs=in_specs,
            out_specs=[spec(VECTOR)] * 6,
        )(select, partial, *own, *got)


def solution(mesh):
    in_specs = (
        P(("grp", "dev"), None, None, None),
        P(("grp", "dev")),
        P(("grp", "dev")),
        P(("grp", "dev"), None),
        P(("grp", "dev")),
    )
    out_specs = P(("grp", "dev"), None, None, None)
    return jax.shard_map(body, mesh=mesh, in_specs=in_specs, out_specs=out_specs, check_vma=False)
```

```python
import functools
import math

import jax
import jax.numpy as jnp
from jax import lax
from jax.experimental import pallas as pl
from jax.experimental.pallas import tpu as pltpu
from jax.sharding import PartitionSpec as P

NPHASE = 4
NCONC = 2
NFIELD = NPHASE + NCONC
EDGE = 16
PLANE = EDGE * EDGE
HALF = PLANE // 2
GROUPS = HALF // EDGE
SLOTS = 4
ROWS = NFIELD * SLOTS

phase_rate = 0.05
closure = 0.1
coupling = (0.5, -0.5, 1.0, -1.0)
conc_rates = (0.08, 0.04)

STATE = (2, EDGE * ROWS, HALF)
FACE = (ROWS, PLANE)
SIDE = (3, ROWS, PLANE)
SOURCES = 4


def partners(axis, offset):
    sizes = (lax.axis_size("grp"), lax.axis_size("dev"))
    along = ("grp", "dev").index(axis)
    route = []
    for grp in range(sizes[0]):
        for dev in range(sizes[1]):
            own = (grp, dev)
            step = 1 if (own[along] - offset) % 2 == 0 else -1
            partner = list(own)
            partner[along] += step
            if not 0 <= partner[along] < sizes[along]:
                partner = list(own)
                partner[1 - along] ^= 1
                if partner[1 - along] >= sizes[1 - along]:
                    partner = list(own)
            route.append((grp * sizes[1] + dev, partner[0] * sizes[1] + partner[1]))
    return route


def exchange(block, axis, offset):
    return lax.ppermute(block, ("grp", "dev"), partners(axis, offset))


def iota(shape, dim):
    return lax.broadcasted_iota(jnp.int32, shape, dim)


def plane_at(ref, x):
    rows = pl.ds(x * ROWS, ROWS)
    return ref[0, rows, :], ref[1, rows, :]


def turned(value, shift):
    shift %= HALF
    return pltpu.roll(value, shift, 1) if shift else value


class Packer:
    def __init__(self):
        lane = iota((ROWS, HALF), 1)
        self.lane, self.group, self.place = lane, lane // EDGE, lane % EDGE
        self.y = [[None, None], [None, None]]
        self.z = [[None, None], [None, None]]

    def add(self, x, left, right):
        odd, half, at = x % 2, x // GROUPS, x % GROUPS
        ends = turned(jnp.where(self.lane < EDGE, left, right), EDGE * at)
        taken = (self.group == at) | (self.group == (at + GROUPS - 1) % GROUPS)
        before = self.y[half][odd]
        self.y[half][odd] = ends if before is None else jnp.where(taken, ends, before)
        taken = (self.place == x) | (self.place == (x + EDGE - 1) % EDGE)
        for h, value in enumerate((left, right)):
            moved = turned(value, x)
            before = self.z[h][odd]
            self.z[h][odd] = moved if before is None else jnp.where(taken, moved, before)

    def tables(self, h):
        even_group, even_place = self.group % 2 == 0, self.place % 2 == 0
        (y_even, y_odd), (z_even, z_odd) = self.y[h], self.z[h]
        low = (jnp.where(even_group, y_even, y_odd), jnp.where(even_place, z_even, z_odd))
        y_high, z_high = jnp.where(even_group, y_odd, y_even), jnp.where(even_place, z_odd, z_even)
        return low, (turned(y_high, EDGE), turned(z_high, 1 - EDGE))


def write_tables(packer, state, own):
    low, high = own
    for h in range(2):
        lanes = pl.ds(h * HALF, HALF)
        for ref, x in ((low, 0), (high, EDGE - 1)):
            ref[0, :, lanes] = state[h, pl.ds(x * ROWS, ROWS), :]
        for ref, (y_table, z_table) in zip(own, packer.tables(h)):
            ref[1, :, lanes] = y_table
            ref[2, :, lanes] = z_table


def emit_faces(packer, state, own, sends):
    write_tables(packer, state, own)
    low, high = own
    flat_a, flat_b, deep_a, deep_b = sends
    even = even_place("dev")
    for face in range(2):
        flat_a[face] = jnp.where(even, high[face], low[face])
        flat_b[face] = jnp.where(even, low[face], high[face])
    even = even_place("grp")
    deep_a[...] = jnp.where(even, high[2], low[2])
    deep_b[...] = jnp.where(even, low[2], high[2])


def fill_state(state, blocks):
    for slot, block in enumerate(blocks):
        for f in range(NFIELD):
            value = block(f)
            for h in range(2):
                state[h, pl.ds(f * SLOTS + slot, EDGE, stride=ROWS), :] = value[:, h * HALF : (h + 1) * HALF]


def slot_rows():
    return iota(FACE, 0) % SLOTS


def shifted(value, rows):
    rows %= ROWS
    return pltpu.roll(value, rows, 0) if rows else value


def gathered(tables, slot):
    rows = slot_rows()
    out = shifted(tables[0], -slot)
    for number in range(1, len(tables)):
        out = jnp.where(rows == number, shifted(tables[number], number - slot), out)
    return out


def scattered(table, number, slot):
    return shifted(table, slot - number)


def even_place(axis):
    return lax.rem(lax.axis_index(axis), 2) == 0


def pack_kernel(fields, low, high, faces_grp, faces_dev, state):
    fill_state(state, [lambda f, slot=slot: fields[slot, f] for slot in range(SLOTS)])
    packer = Packer()
    for x in range(EDGE):
        packer.add(x, *plane_at(state, x))
    write_tables(packer, state, (low, high))
    faces_grp[0] = gathered([low[0], high[0], low[1], high[1]], 0)
    faces_grp[1] = jnp.where(even_place("grp"), high[2], low[2])
    faces_dev[0] = gathered([low[0], high[0], low[1], high[1]], SLOTS - 1)
    faces_dev[1] = gathered([low[2], high[2]], SLOTS - 1)


def block_kernel(swap_dev, fields, low, high, to_dev, to_grp):
    last, size = SLOTS - 1, NFIELD * EDGE
    for f in range(NFIELD):
        to_dev[f * EDGE : (f + 1) * EDGE] = fields[last, f]
        to_grp[f * EDGE : (f + 1) * EDGE] = fields[0, f]
    away = jnp.where(even_place("grp"), low[2], high[2])
    to_grp[size : size + ROWS] = jnp.where(slot_rows() == 0, away, jnp.where(swap_dev[0] == 1, 1.0, 0.0))


def faces_kernel(swap_dev, swap_grp, scale, low, high, faces, faces_dev, *outs):
    del scale
    new_low, new_high, flat_a, flat_b, deep_b = outs
    rows, last = slot_rows(), SLOTS - 1
    first_rows = (rows == 0) & (swap_grp[0] == 1)
    last_rows = (rows == last) & (swap_dev[0] == 1)
    even = even_place("grp")
    got_first, got_last, got_last_z = faces[0], faces_dev[0], faces_dev[1]
    for side, (raw, new) in enumerate(((low, new_low), (high, new_high))):
        for axis in range(2):
            number = 2 * axis + side
            table = jnp.where(first_rows, scattered(got_first, number, 0), raw[axis])
            new[axis] = jnp.where(last_rows, scattered(got_last, number, last), table)
        table = jnp.where(first_rows & (even if side == 0 else ~even), faces[1], raw[2])
        new[2] = jnp.where(last_rows, scattered(got_last_z, side, last), table)
    even_dev = even_place("dev")
    for axis in range(2):
        flat_a[axis] = jnp.where(even_dev, new_high[axis], new_low[axis])
        flat_b[axis] = jnp.where(even_dev, new_low[axis], new_high[axis])
    flat_a[2] = faces[1]
    deep_b[...] = jnp.where(even, new_low[2], new_high[2])


def cos_quarter(number):
    turn = number & 7
    size = jnp.where((turn & 3) == 0, 1.0, jnp.where((turn & 3) == 2, 0.0, math.sqrt(0.5)))
    return jnp.where((turn > 2) & (turn < 6), -size, size)


def plan_kernel(neighbors, orient, scale, select):
    shape = (ROWS, HALF)
    slot, field, column = iota(shape, 0) % SLOTS, iota(shape, 0) // SLOTS, iota(shape, 1)
    grp, dev = lax.axis_index("grp"), lax.axis_index("dev")
    rank = grp * lax.axis_size("dev") + dev

    def by_slot(values):
        rows = values[0]
        for number in range(1, SLOTS):
            rows = jnp.where(slot == number, values[number], rows)
        return rows

    spread = []
    for number in range(SLOTS):
        turn = 0.5 * cos_quarter(orient[number])
        lift = 0.5 * cos_quarter(orient[number] + 6)
        spread.append((1.0 + turn, 1.0 - turn, 1.0 + lift))
    conc = jnp.where(field == NPHASE, conc_rates[0], conc_rates[1])
    weights = [jnp.where(field < NPHASE, phase_rate * by_slot([own[axis] for own in spread]), conc) for axis in range(3)]
    for axis in range(3):
        scale[axis] = weights[axis]
    scale[3] = 1.0 - 2.0 * (weights[0] + weights[1] + weights[2])
    for face in range(6):
        first = []
        came = 2 + lax.rem(lax.rem(dev if face < 4 else grp, 2) + face % 2 + 1, 2)
        for number in range(SLOTS):
            target = neighbors[number, face]
            source = jnp.where(target < 0, 0, jnp.where(target // SLOTS == rank, 1, came))
            first.append(source * ROWS + jnp.where(target < 0, number, target & (SLOTS - 1)))
        select[face] = jnp.where(column == by_slot(first) + field * SLOTS, weights[face // 2], 0.0)


def first_inner_kernel(swap_dev, swap_grp, scale, fields, block_dev, block_grp, faces, low, high, new_low, new_high, *refs):
    partial, got_deep, relayed, z_low, z_high, state = refs
    size = NFIELD * EDGE

    def block(slot):
        def of(f):
            value = fields[slot, f]
            if slot == 0:
                value = jnp.where(swap_grp[0] == 1, block_grp[f * EDGE : (f + 1) * EDGE], value)
            if slot == SLOTS - 1:
                value = jnp.where(swap_dev[0] == 1, block_dev[f * EDGE : (f + 1) * EDGE], value)
            return value

        return of

    fill_state(state, [block(slot) for slot in range(SLOTS)])
    rows, even = slot_rows(), even_place("grp")
    first_rows = (rows == 0) & (swap_grp[0] == 1)
    got_deep[...] = jnp.where(first_rows, jnp.where(even, low[2], high[2]), faces[1])
    other = block_grp[size : size + ROWS]
    relayed[...] = jnp.where(rows == SLOTS - 1, jnp.broadcast_to(other[1:2], FACE), 0.0)
    z_low[...] = jnp.where(first_rows & ~even, other, new_low[2])
    z_high[...] = jnp.where(first_rows & even, other, new_high[2])
    inner_kernel(state, scale, partial)


def inner_kernel(state, scale, partial):
    lane = iota((ROWS, HALF), 1)
    start_y, end_y = lane < EDGE, lane >= HALF - EDGE
    start_z, end_z = lane % EDGE == 0, lane % EDGE == EDGE - 1
    weight_x, weight_y, weight_z, weight = (scale[number] for number in range(4))
    tile = 2 * SLOTS
    planes = {0: plane_at(state, 0)}
    for x in range(EDGE):
        if x + 1 < EDGE:
            planes[x + 1] = plane_at(state, x + 1)
        left, right = planes[x]
        up = [turned(half, EDGE) for half in (left, right)]
        down = [turned(half, -EDGE) for half in (left, right)]
        sum_y = (
            jnp.where(start_y, 0.0, up[0]) + jnp.where(end_y, down[1], down[0]),
            jnp.where(start_y, up[0], up[1]) + jnp.where(end_y, 0.0, down[1]),
        )
        for h, half in enumerate((left, right)):
            sum_z = jnp.where(start_z, 0.0, turned(half, 1)) + jnp.where(end_z, 0.0, turned(half, -1))
            if x == 0:
                sum_x = planes[1][h]
            elif x == EDGE - 1:
                sum_x = planes[x - 1][h]
            else:
                sum_x = planes[x - 1][h] + planes[x + 1][h]
            flow = weight * half + weight_x * sum_x + weight_y * sum_y[h] + weight_z * sum_z
            phases, conc = (half[:tile], half[tile : 2 * tile]), half[2 * tile :]
            drive = conc - pltpu.roll(conc, SLOTS, 0)
            total = phases[0] + phases[1]
            total = total + pltpu.roll(total, SLOTS, 0)
            tail = (phase_rate * closure) * (1.0 - total)
            rows = x * ROWS
            for number, value in enumerate(phases):
                gain = value * (1.0 - value) * (coupling[2 * number] * drive + (2.0 * value - 1.0))
                part = flow[number * tile : (number + 1) * tile]
                partial[h, pl.ds(rows + number * tile, tile), :] = part + (phase_rate * gain + tail)
            partial[h, pl.ds(rows + 2 * tile, tile), :] = flow[2 * tile :]


def finish_kernel(last_step, select, partial, *refs):
    own, got_flat = refs[0:2], refs[2:4]
    own_deep = [ref[2] for ref in own]
    if last_step:
        got_deep = [ref[...] for ref in refs[4:6]]
        result, done, blocks, sent = refs[6:10]
    else:
        known, deep_b, relayed, z_low, z_high = refs[4:9]
        got_deep = [jnp.where(relayed[...] > 0.5, got_flat[0][2], known[...]), deep_b[...]]
        own_deep = [z_low[...], z_high[...]]
        done, outs, sends = refs[9], refs[10:12], refs[12:16]
    ghosts = []
    for face in range(6):
        axis, side = face // 2, face % 2
        got = [ref[axis] for ref in got_flat] if axis < 2 else got_deep
        mine = [ref[axis] for ref in own] if axis < 2 else own_deep
        tables = jnp.concatenate([mine[side], mine[1 - side], *got], axis=0)
        chosen = select[face][:, : SOURCES * ROWS]
        ghosts.append(jnp.dot(chosen, tables, precision=lax.Precision.HIGHEST, preferred_element_type=jnp.float32))
    lane = iota((ROWS, HALF), 1)
    start_y, end_y = lane < EDGE, lane >= HALF - EDGE
    ends_z = (lane % EDGE == 0) | (lane % EDGE == EDGE - 1)
    even_group, even_place = (lane // EDGE) % 2 == 0, lane % 2 == 0
    y_pairs, z_pairs = [], []
    for h in range(2):
        lanes = slice(h * HALF, (h + 1) * HALF)
        low, high = ghosts[2][:, lanes], turned(ghosts[3][:, lanes], -EDGE)
        y_pairs.append((jnp.where(even_group, low, high), jnp.where(even_group, high, low)))
        low, high = ghosts[4][:, lanes], turned(ghosts[5][:, lanes], EDGE - 1)
        z_pairs.append((jnp.where(even_place, low, high), jnp.where(even_place, high, low)))
    packer = None if last_step else Packer()
    copies = []
    for x in range(EDGE):
        halves = list(plane_at(partial, x))
        ends = turned(y_pairs[x // GROUPS][x % 2], -EDGE * (x % GROUPS))
        for h in range(2):
            value = halves[h] + jnp.where(start_y if h == 0 else end_y, ends, 0.0)
            value = value + jnp.where(ends_z, turned(z_pairs[h][x % 2], -x), 0.0)
            if x == 0:
                value = value + ghosts[0][:, h * HALF : (h + 1) * HALF]
            if x == EDGE - 1:
                value = value + ghosts[1][:, h * HALF : (h + 1) * HALF]
            done[h, pl.ds(x * ROWS, ROWS), :] = value
            halves[h] = value
        if not last_step:
            packer.add(x, *halves)
        elif x % 8 == 7:
            first = x - 7
            for slot in range(SLOTS):
                for f in range(NFIELD):
                    rows = pl.ds(first * ROWS + f * SLOTS + slot, 8, stride=ROWS)
                    for h in range(2):
                        lanes = pl.ds(h * HALF, HALF)
                        blocks[slot, f, first : first + 8, lanes] = done[h, rows, :]
            part = pl.ds(first, 8)
            copy = pltpu.make_async_copy(blocks.at[:, :, part], result.at[:, :, part], sent.at[x // 8])
            copy.start()
            copies.append(copy)
    for copy in copies:
        copy.wait()
    if not last_step:
        emit_faces(packer, done, outs, sends)


def spec(space):
    return pl.BlockSpec(memory_space=space)


VECTOR, SCALAR = pltpu.VMEM, pltpu.SMEM
SMALL = pltpu.CompilerParams(vmem_limit_bytes=8 << 20)
FLAT = (2, ROWS, PLANE)
TABLES = (STATE, SIDE, SIDE, FLAT, FLAT, FACE, FACE)
TO_DEV = (NFIELD * EDGE, PLANE)
TO_GRP = (NFIELD * EDGE + ROWS, PLANE)


def shaped(shape):
    return jax.ShapeDtypeStruct(shape, jnp.float32)


def cost(flops):
    return pl.CostEstimate(flops=flops, bytes_accessed=min(flops, 2 << 20), transcendentals=0)


def call(kernel, name, shapes, scalars, vectors, flops=1 << 20, scratch=()):
    return pl.pallas_call(
        kernel,
        name=name,
        compiler_params=SMALL,
        out_shape=[shaped(shape) for shape in shapes],
        in_specs=[spec(SCALAR)] * len(scalars) + [spec(VECTOR)] * len(vectors),
        out_specs=[spec(VECTOR)] * len(shapes),
        scratch_shapes=list(scratch),
        cost_estimate=cost(flops),
    )(*scalars, *vectors)


def body(fields, swap_dev, swap_grp, neighbors, orient):
    state = pltpu.VMEM(STATE, jnp.float32)
    low, high, faces, faces_dev = call(pack_kernel, "pack", [SIDE, SIDE, FLAT, FLAT], [], [fields], scratch=[state])
    faces = exchange(faces, "grp", 0)
    faces_dev = exchange(faces_dev, "dev", 0)
    to_dev, to_grp = call(block_kernel, "blocks", [TO_DEV, TO_GRP], [swap_dev], [fields, low, high], 1 << 24)
    block_grp = exchange(to_grp, "grp", 0)
    block_dev = exchange(to_dev, "dev", 0)
    scale, select = call(plan_kernel, "plan", [(4, ROWS, HALF), (6, ROWS, HALF)], [neighbors, orient], [], 0)
    new_low, new_high, *sends = call(
        faces_kernel,
        "faces",
        [SIDE, SIDE, SIDE, FLAT, FACE],
        [swap_dev, swap_grp],
        [scale, low, high, faces, faces_dev],
        1 << 24,
    )
    got_flat = [exchange(sends[number], "dev", number) for number in range(2)]
    got_b = exchange(sends[2], "grp", 1)
    partial, got_a, relayed, z_low, z_high = call(
        first_inner_kernel,
        "inner_0",
        [STATE, FACE, FACE, FACE, FACE],
        [swap_dev, swap_grp],
        [scale, fields, block_dev, block_grp, faces, low, high, new_low, new_high],
        4 << 20,
        [state],
    )
    state, *tables = call(
        functools.partial(finish_kernel, False),
        "finish_0",
        TABLES,
        [],
        [select, partial, new_low, new_high, *got_flat, got_a, got_b, relayed, z_low, z_high],
    )
    own, sends = tables[:2], tables[2:]
    got = [exchange(sends[number], "dev" if number < 2 else "grp", number % 2) for number in range(4)]
    (partial,) = call(inner_kernel, "inner_1", [STATE], [], [state, scale], 4 << 20)
    return pl.pallas_call(
        functools.partial(finish_kernel, True),
        name="finish_1",
        compiler_params=SMALL,
        out_shape=shaped(fields.shape),
        in_specs=[spec(VECTOR)] * 8,
        out_specs=spec(pl.ANY),
        scratch_shapes=[
            pltpu.VMEM(STATE, jnp.float32),
            pltpu.VMEM(fields.shape, jnp.float32),
            pltpu.SemaphoreType.DMA((2,)),
        ],
    )(select, partial, *own, *got)


def solution(mesh):
    in_specs = (
        P(("grp", "dev"), None, None, None),
        P(("grp", "dev")),
        P(("grp", "dev")),
        P(("grp", "dev"), None),
        P(("grp", "dev")),
    )
    out_specs = P(("grp", "dev"), None, None, None)
    return jax.shard_map(body, mesh=mesh, in_specs=in_specs, out_specs=out_specs, check_vma=False)
```

```python
import functools
import math

import jax
import jax.numpy as jnp
from jax import lax
from jax.experimental import pallas as pl
from jax.experimental.pallas import tpu as pltpu
from jax.sharding import PartitionSpec as P

NPHASE = 4
NCONC = 2
NFIELD = NPHASE + NCONC
EDGE = 16
PLANE = EDGE * EDGE
HALF = PLANE // 2
GROUPS = HALF // EDGE
SLOTS = 4
ROWS = NFIELD * SLOTS

phase_rate = 0.05
closure = 0.1
coupling = (0.5, -0.5, 1.0, -1.0)
conc_rates = (0.08, 0.04)

STATE = (2, EDGE * ROWS, HALF)
FACE = (ROWS, PLANE)
SIDE = (3, ROWS, PLANE)
SOURCES = 4


def partners(axis, offset):
    sizes = (lax.axis_size("grp"), lax.axis_size("dev"))
    along = ("grp", "dev").index(axis)
    route = []
    for grp in range(sizes[0]):
        for dev in range(sizes[1]):
            own = (grp, dev)
            step = 1 if (own[along] - offset) % 2 == 0 else -1
            partner = list(own)
            partner[along] += step
            if not 0 <= partner[along] < sizes[along]:
                partner = list(own)
                partner[1 - along] ^= 1
                if partner[1 - along] >= sizes[1 - along]:
                    partner = list(own)
            route.append((grp * sizes[1] + dev, partner[0] * sizes[1] + partner[1]))
    return route


def exchange(block, axis, offset):
    return lax.ppermute(block, ("grp", "dev"), partners(axis, offset))


def iota(shape, dim):
    return lax.broadcasted_iota(jnp.int32, shape, dim)


def plane_at(ref, x):
    rows = pl.ds(x * ROWS, ROWS)
    return ref[0, rows, :], ref[1, rows, :]


def turned(value, shift):
    shift %= HALF
    return pltpu.roll(value, shift, 1) if shift else value


class Packer:
    def __init__(self):
        lane = iota((ROWS, HALF), 1)
        self.lane, self.group, self.place = lane, lane // EDGE, lane % EDGE
        self.y = [[None, None], [None, None]]
        self.z = [[None, None], [None, None]]

    def add(self, x, left, right):
        odd, half, at = x % 2, x // GROUPS, x % GROUPS
        ends = turned(jnp.where(self.lane < EDGE, left, right), EDGE * at)
        taken = (self.group == at) | (self.group == (at + GROUPS - 1) % GROUPS)
        before = self.y[half][odd]
        self.y[half][odd] = ends if before is None else jnp.where(taken, ends, before)
        taken = (self.place == x) | (self.place == (x + EDGE - 1) % EDGE)
        for h, value in enumerate((left, right)):
            moved = turned(value, x)
            before = self.z[h][odd]
            self.z[h][odd] = moved if before is None else jnp.where(taken, moved, before)

    def tables(self, h):
        even_group, even_place = self.group % 2 == 0, self.place % 2 == 0
        (y_even, y_odd), (z_even, z_odd) = self.y[h], self.z[h]
        low = (jnp.where(even_group, y_even, y_odd), jnp.where(even_place, z_even, z_odd))
        y_high, z_high = jnp.where(even_group, y_odd, y_even), jnp.where(even_place, z_odd, z_even)
        return low, (turned(y_high, EDGE), turned(z_high, 1 - EDGE))


def write_tables(packer, state, own):
    low, high = own
    for h in range(2):
        lanes = pl.ds(h * HALF, HALF)
        for ref, x in ((low, 0), (high, EDGE - 1)):
            ref[0, :, lanes] = state[h, pl.ds(x * ROWS, ROWS), :]
        for ref, (y_table, z_table) in zip(own, packer.tables(h)):
            ref[1, :, lanes] = y_table
            ref[2, :, lanes] = z_table


def emit_faces(packer, state, own, sends):
    write_tables(packer, state, own)
    low, high = own
    flat_a, flat_b, deep_a, deep_b = sends
    even = even_place("dev")
    for face in range(2):
        flat_a[face] = jnp.where(even, high[face], low[face])
        flat_b[face] = jnp.where(even, low[face], high[face])
    even = even_place("grp")
    deep_a[...] = jnp.where(even, high[2], low[2])
    deep_b[...] = jnp.where(even, low[2], high[2])


def fill_slot(state, slot, block):
    for f in range(NFIELD):
        value = block(f)
        for h in range(2):
            state[h, pl.ds(f * SLOTS + slot, EDGE, stride=ROWS), :] = value[:, h * HALF : (h + 1) * HALF]


def slot_rows():
    return iota(FACE, 0) % SLOTS


def shifted(value, rows):
    rows %= ROWS
    return pltpu.roll(value, rows, 0) if rows else value


def gathered(tables, slot):
    rows = slot_rows()
    out = shifted(tables[0], -slot)
    for number in range(1, len(tables)):
        out = jnp.where(rows == number, shifted(tables[number], number - slot), out)
    return out


def scattered(table, number, slot):
    return shifted(table, slot - number)


def even_place(axis):
    return lax.rem(lax.axis_index(axis), 2) == 0


def block_kernel(masks, fields, low, high, to_dev, to_grp):
    last, size = SLOTS - 1, NFIELD * EDGE
    for f in range(NFIELD):
        to_dev[f * EDGE : (f + 1) * EDGE] = fields[last, f]
        to_grp[f * EDGE : (f + 1) * EDGE] = fields[0, f]
    away = jnp.where(even_place("grp"), low[2], high[2])
    to_grp[size : size + ROWS] = jnp.where(slot_rows() == 0, away, masks[0])


def faces_kernel(masks, low, high, faces, faces_dev, *outs):
    new_low, new_high, flat_a, flat_b, deep_b, relay = outs
    rows, last = slot_rows(), SLOTS - 1
    first_rows = (rows == 0) & (masks[1] > 0.5)
    last_rows = (rows == last) & (masks[0] > 0.5)
    even = even_place("grp")
    got_first, got_last, got_last_z = faces[0], faces_dev[0], faces_dev[1]
    for side, (raw, new) in enumerate(((low, new_low), (high, new_high))):
        for axis in range(2):
            number = 2 * axis + side
            table = jnp.where(first_rows, scattered(got_first, number, 0), raw[axis])
            new[axis] = jnp.where(last_rows, scattered(got_last, number, last), table)
        table = jnp.where(first_rows & (even if side == 0 else ~even), faces[1], raw[2])
        new[2] = jnp.where(last_rows, scattered(got_last_z, side, last), table)
    even_dev = even_place("dev")
    for axis in range(2):
        flat_a[axis] = jnp.where(even_dev, new_high[axis], new_low[axis])
        flat_b[axis] = jnp.where(even_dev, new_low[axis], new_high[axis])
    relay[...] = faces[1]
    deep_b[...] = jnp.where(even, new_low[2], new_high[2])


def cos_quarter(number):
    turn = number & 7
    size = jnp.where((turn & 3) == 0, 1.0, jnp.where((turn & 3) == 2, 0.0, math.sqrt(0.5)))
    return jnp.where((turn > 2) & (turn < 6), -size, size)


def plan_kernel(neighbors, orient, scale, select):
    shape = (ROWS, HALF)
    slot, field, column = iota(shape, 0) % SLOTS, iota(shape, 0) // SLOTS, iota(shape, 1)
    grp, dev = lax.axis_index("grp"), lax.axis_index("dev")
    rank = grp * lax.axis_size("dev") + dev

    def by_slot(values):
        rows = values[0]
        for number in range(1, SLOTS):
            rows = jnp.where(slot == number, values[number], rows)
        return rows

    spread = []
    for number in range(SLOTS):
        turn = 0.5 * cos_quarter(orient[number])
        lift = 0.5 * cos_quarter(orient[number] + 6)
        spread.append((1.0 + turn, 1.0 - turn, 1.0 + lift))
    conc = jnp.where(field == NPHASE, conc_rates[0], conc_rates[1])
    weights = [jnp.where(field < NPHASE, phase_rate * by_slot([own[axis] for own in spread]), conc) for axis in range(3)]
    for axis in range(3):
        scale[axis] = weights[axis]
    scale[3] = 1.0 - 2.0 * (weights[0] + weights[1] + weights[2])
    for face in range(6):
        first = []
        came = 2 + lax.rem(lax.rem(dev if face < 4 else grp, 2) + face % 2 + 1, 2)
        for number in range(SLOTS):
            target = neighbors[number, face]
            source = jnp.where(target < 0, 0, jnp.where(target // SLOTS == rank, 1, came))
            first.append(source * ROWS + jnp.where(target < 0, number, target & (SLOTS - 1)))
        select[face] = jnp.where(column == by_slot(first) + field * SLOTS, weights[face // 2], 0.0)


def start_kernel(fields, neighbors, orient, *refs):
    fetched, low, high, faces_grp, faces_dev, scale, select = refs[:7]
    state, near, turn, arrived = refs[7:]
    scalars = ((neighbors, near), (orient, turn))
    blocks = tuple((fields.at[slot], fetched.at[slot]) for slot in range(SLOTS))
    copies = [pltpu.make_async_copy(*pair, arrived.at[number]) for number, pair in enumerate((*scalars, *blocks))]
    for copy in copies:
        copy.start()
    for copy in copies[: len(scalars)]:
        copy.wait()
    plan_kernel(near, turn, scale, select)
    for slot in range(SLOTS):
        copies[len(scalars) + slot].wait()
        fill_slot(state, slot, lambda f: fetched[slot, f])
    packer = Packer()
    for x in range(EDGE):
        packer.add(x, *plane_at(state, x))
    write_tables(packer, state, (low, high))
    faces_grp[0] = gathered([low[0], high[0], low[1], high[1]], 0)
    faces_grp[1] = jnp.where(even_place("grp"), high[2], low[2])
    faces_dev[0] = gathered([low[0], high[0], low[1], high[1]], SLOTS - 1)
    faces_dev[1] = gathered([low[2], high[2]], SLOTS - 1)


def first_inner_kernel(masks, scale, fields, block_dev, block_grp, faces, low, high, new_low, new_high, *refs):
    partial, got_deep, relayed, z_low, z_high, state = refs
    size = NFIELD * EDGE
    swap_dev, swap_grp = masks[0] > 0.5, masks[1] > 0.5

    def block(slot):
        def of(f):
            value = fields[slot, f]
            if slot == 0:
                value = jnp.where(swap_grp[:EDGE], block_grp[f * EDGE : (f + 1) * EDGE], value)
            if slot == SLOTS - 1:
                value = jnp.where(swap_dev[:EDGE], block_dev[f * EDGE : (f + 1) * EDGE], value)
            return value

        return of

    for slot in range(SLOTS):
        fill_slot(state, slot, block(slot))
    rows, even = slot_rows(), even_place("grp")
    first_rows = (rows == 0) & swap_grp
    got_deep[...] = jnp.where(first_rows, jnp.where(even, low[2], high[2]), faces[1])
    other = block_grp[size : size + ROWS]
    relayed[...] = jnp.where(rows == SLOTS - 1, jnp.broadcast_to(other[1:2], FACE), 0.0)
    z_low[...] = jnp.where(first_rows & ~even, other, new_low[2])
    z_high[...] = jnp.where(first_rows & even, other, new_high[2])
    inner_kernel(state, scale, partial)


def inner_kernel(state, scale, partial):
    lane = iota((ROWS, HALF), 1)
    start_y, end_y = lane < EDGE, lane >= HALF - EDGE
    start_z, end_z = lane % EDGE == 0, lane % EDGE == EDGE - 1
    weight_x, weight_y, weight_z, weight = (scale[number] for number in range(4))
    tile = 2 * SLOTS
    planes = {0: plane_at(state, 0)}
    for x in range(EDGE):
        if x + 1 < EDGE:
            planes[x + 1] = plane_at(state, x + 1)
        left, right = planes[x]
        up = [turned(half, EDGE) for half in (left, right)]
        down = [turned(half, -EDGE) for half in (left, right)]
        sum_y = (
            jnp.where(start_y, 0.0, up[0]) + jnp.where(end_y, down[1], down[0]),
            jnp.where(start_y, up[0], up[1]) + jnp.where(end_y, 0.0, down[1]),
        )
        for h, half in enumerate((left, right)):
            sum_z = jnp.where(start_z, 0.0, turned(half, 1)) + jnp.where(end_z, 0.0, turned(half, -1))
            if x == 0:
                sum_x = planes[1][h]
            elif x == EDGE - 1:
                sum_x = planes[x - 1][h]
            else:
                sum_x = planes[x - 1][h] + planes[x + 1][h]
            flow = weight * half + weight_x * sum_x + weight_y * sum_y[h] + weight_z * sum_z
            phases, conc = (half[:tile], half[tile : 2 * tile]), half[2 * tile :]
            drive = conc - pltpu.roll(conc, SLOTS, 0)
            total = phases[0] + phases[1]
            total = total + pltpu.roll(total, SLOTS, 0)
            tail = (phase_rate * closure) * (1.0 - total)
            rows = x * ROWS
            for number, value in enumerate(phases):
                gain = value * (1.0 - value) * (coupling[2 * number] * drive + (2.0 * value - 1.0))
                part = flow[number * tile : (number + 1) * tile]
                partial[h, pl.ds(rows + number * tile, tile), :] = part + (phase_rate * gain + tail)
            partial[h, pl.ds(rows + 2 * tile, tile), :] = flow[2 * tile :]


def finish_kernel(last_step, select, partial, *refs):
    own, got_flat = refs[0:2], (refs[3], refs[2])
    own_deep = [ref[2] for ref in own]
    if last_step:
        got_deep = [ref[...] for ref in refs[4:6]]
        result, done, blocks, sent = refs[6:10]
    else:
        known, deep_b, relay, relayed, z_low, z_high = refs[4:10]
        got_deep = [jnp.where(relayed[...] > 0.5, relay[...], known[...]), deep_b[...]]
        own_deep = [z_low[...], z_high[...]]
        done, outs, sends = refs[10], refs[11:13], refs[13:17]
    ghosts = []
    for face in range(6):
        axis, side = face // 2, face % 2
        got = [ref[axis] for ref in got_flat] if axis < 2 else got_deep
        mine = [ref[axis] for ref in own] if axis < 2 else own_deep
        tables = jnp.concatenate([mine[side], mine[1 - side], *got], axis=0)
        chosen = select[face][:, : SOURCES * ROWS]
        ghosts.append(jnp.dot(chosen, tables, precision=lax.Precision.HIGHEST, preferred_element_type=jnp.float32))
    lane = iota((ROWS, HALF), 1)
    start_y, end_y = lane < EDGE, lane >= HALF - EDGE
    ends_z = (lane % EDGE == 0) | (lane % EDGE == EDGE - 1)
    even_group, even_place = (lane // EDGE) % 2 == 0, lane % 2 == 0
    y_pairs, z_pairs = [], []
    for h in range(2):
        lanes = slice(h * HALF, (h + 1) * HALF)
        low, high = ghosts[2][:, lanes], turned(ghosts[3][:, lanes], -EDGE)
        y_pairs.append((jnp.where(even_group, low, high), jnp.where(even_group, high, low)))
        low, high = ghosts[4][:, lanes], turned(ghosts[5][:, lanes], EDGE - 1)
        z_pairs.append((jnp.where(even_place, low, high), jnp.where(even_place, high, low)))
    packer = None if last_step else Packer()
    copies = []
    for x in range(EDGE):
        halves = list(plane_at(partial, x))
        ends = turned(y_pairs[x // GROUPS][x % 2], -EDGE * (x % GROUPS))
        for h in range(2):
            value = halves[h] + jnp.where(start_y if h == 0 else end_y, ends, 0.0)
            value = value + jnp.where(ends_z, turned(z_pairs[h][x % 2], -x), 0.0)
            if x == 0:
                value = value + ghosts[0][:, h * HALF : (h + 1) * HALF]
            if x == EDGE - 1:
                value = value + ghosts[1][:, h * HALF : (h + 1) * HALF]
            done[h, pl.ds(x * ROWS, ROWS), :] = value
            halves[h] = value
        if not last_step:
            packer.add(x, *halves)
        elif x % 8 == 7:
            first = x - 7
            for slot in range(SLOTS):
                for f in range(NFIELD):
                    rows = pl.ds(first * ROWS + f * SLOTS + slot, 8, stride=ROWS)
                    for h in range(2):
                        lanes = pl.ds(h * HALF, HALF)
                        blocks[slot, f, first : first + 8, lanes] = done[h, rows, :]
            part = pl.ds(first, 8)
            copy = pltpu.make_async_copy(blocks.at[:, :, part], result.at[:, :, part], sent.at[x // 8])
            copy.start()
            copies.append(copy)
    for copy in copies:
        copy.wait()
    if not last_step:
        emit_faces(packer, done, outs, sends)


def spec(space):
    return pl.BlockSpec(memory_space=space)


VECTOR = pltpu.VMEM
SMALL = pltpu.CompilerParams(vmem_limit_bytes=8 << 20)
FLAT = (2, ROWS, PLANE)
TABLES = (STATE, SIDE, SIDE, FLAT, FLAT, FACE, FACE)
TO_DEV = (NFIELD * EDGE, PLANE)
TO_GRP = (NFIELD * EDGE + ROWS, PLANE)


def shaped(shape):
    return jax.ShapeDtypeStruct(shape, jnp.float32)


def cost(flops):
    return pl.CostEstimate(flops=flops, bytes_accessed=min(flops, 2 << 20), transcendentals=0)


def call(kernel, name, shapes, vectors, flops=1 << 20, scratch=()):
    return pl.pallas_call(
        kernel,
        name=name,
        compiler_params=SMALL,
        out_shape=[shaped(shape) for shape in shapes],
        in_specs=[spec(VECTOR)] * len(vectors),
        out_specs=[spec(VECTOR)] * len(shapes),
        scratch_shapes=list(scratch),
        cost_estimate=cost(flops),
    )(*vectors)


def start(arguments):
    shapes = (arguments[0].shape, SIDE, SIDE, FLAT, FLAT, (4, ROWS, HALF), (6, ROWS, HALF))
    return pl.pallas_call(
        start_kernel,
        name="start",
        compiler_params=SMALL,
        out_shape=[shaped(shape) for shape in shapes],
        in_specs=[spec(pl.ANY)] * len(arguments),
        out_specs=[spec(VECTOR)] * len(shapes),
        scratch_shapes=[
            pltpu.VMEM(STATE, jnp.float32),
            *(pltpu.SMEM(array.shape, jnp.int32) for array in arguments[1:]),
            pltpu.SemaphoreType.DMA((len(arguments) - 1 + SLOTS,)),
        ],
    )(*(pltpu.with_memory_space_constraint(array, pltpu.HBM) for array in arguments))


def body(fields, swap_dev, swap_grp, neighbors, orient):
    fields, low, high, faces, faces_dev, scale, select = start((fields, neighbors, orient))
    swap_dev, swap_grp, faces = lax.optimization_barrier((swap_dev, swap_grp, faces))
    flags = jnp.concatenate([swap_dev, swap_grp])
    masks = jnp.broadcast_to(jnp.where(flags == 1, 1.0, 0.0).reshape(2, 1, 1), (2, *FACE))
    faces = exchange(faces, "grp", 0)
    faces_dev = exchange(faces_dev, "dev", 0)
    to_dev, to_grp = call(block_kernel, "blocks", [TO_DEV, TO_GRP], [masks, fields, low, high], 1 << 30)
    block_grp = exchange(to_grp, "grp", 0)
    block_dev = exchange(to_dev, "dev", 0)
    new_low, new_high, *sends = call(
        faces_kernel,
        "faces",
        [SIDE, SIDE, FLAT, FLAT, FACE, FACE],
        [masks, low, high, faces, faces_dev],
        1 << 30,
    )
    flat_b = exchange(sends[1], "dev", 1)
    deep_b = exchange(sends[2], "grp", 1)
    flat_a = exchange(sends[0], "dev", 0)
    relay = exchange(sends[3], "dev", 0)
    partial, deep_a, relayed, z_low, z_high = call(
        first_inner_kernel,
        "inner_0",
        [STATE, FACE, FACE, FACE, FACE],
        [masks, scale, fields, block_dev, block_grp, faces, low, high, new_low, new_high],
        4 << 20,
        [pltpu.VMEM(STATE, jnp.float32)],
    )
    state, *tables = call(
        functools.partial(finish_kernel, False),
        "finish_0",
        TABLES,
        [select, partial, new_low, new_high, flat_b, flat_a, deep_a, deep_b, relay, relayed, z_low, z_high],
    )
    own, sends = tables[:2], tables[2:]
    flat_b = exchange(sends[1], "dev", 1)
    deep_a = exchange(sends[2], "grp", 0)
    deep_b = exchange(sends[3], "grp", 1)
    flat_a = exchange(sends[0], "dev", 0)
    (partial,) = call(inner_kernel, "inner_1", [STATE], [state, scale], 4 << 20)
    return pl.pallas_call(
        functools.partial(finish_kernel, True),
        name="finish_1",
        compiler_params=SMALL,
        out_shape=shaped(fields.shape),
        in_specs=[spec(VECTOR)] * 8,
        out_specs=spec(pl.ANY),
        scratch_shapes=[
            pltpu.VMEM(STATE, jnp.float32),
            pltpu.VMEM(fields.shape, jnp.float32),
            pltpu.SemaphoreType.DMA((2,)),
        ],
    )(select, partial, *own, flat_b, flat_a, deep_a, deep_b)


def solution(mesh):
    in_specs = (
        P(("grp", "dev"), None, None, None),
        P(("grp", "dev")),
        P(("grp", "dev")),
        P(("grp", "dev"), None),
        P(("grp", "dev")),
    )
    out_specs = P(("grp", "dev"), None, None, None)
    return jax.shard_map(body, mesh=mesh, in_specs=in_specs, out_specs=out_specs, check_vma=False)
```

```python
import functools
import math

import jax
import jax.numpy as jnp
from jax import lax
from jax.experimental import pallas as pl
from jax.experimental.pallas import tpu as pltpu
from jax.sharding import PartitionSpec as P

NPHASE = 4
NCONC = 2
NFIELD = NPHASE + NCONC
EDGE = 16
PLANE = EDGE * EDGE
HALF = PLANE // 2
GROUPS = HALF // EDGE
SLOTS = 4
ROWS = NFIELD * SLOTS

phase_rate = 0.05
closure = 0.1
coupling = (0.5, -0.5, 1.0, -1.0)
conc_rates = (0.08, 0.04)

STATE = (2, EDGE * ROWS, HALF)
FACE = (ROWS, PLANE)
SIDE = (3, ROWS, PLANE)
SOURCES = 4


def partners(axis, offset):
    sizes = (lax.axis_size("grp"), lax.axis_size("dev"))
    along = ("grp", "dev").index(axis)
    route = []
    for grp in range(sizes[0]):
        for dev in range(sizes[1]):
            own = (grp, dev)
            step = 1 if (own[along] - offset) % 2 == 0 else -1
            partner = list(own)
            partner[along] += step
            if not 0 <= partner[along] < sizes[along]:
                partner = list(own)
                partner[1 - along] ^= 1
                if partner[1 - along] >= sizes[1 - along]:
                    partner = list(own)
            route.append((grp * sizes[1] + dev, partner[0] * sizes[1] + partner[1]))
    return route


def exchange(block, axis, offset):
    return lax.ppermute(block, ("grp", "dev"), partners(axis, offset))


def iota(shape, dim):
    return lax.broadcasted_iota(jnp.int32, shape, dim)


def plane_at(ref, x):
    rows = pl.ds(x * ROWS, ROWS)
    return ref[0, rows, :], ref[1, rows, :]


def turned(value, shift):
    shift %= HALF
    return pltpu.roll(value, shift, 1) if shift else value


class Packer:
    def __init__(self):
        lane = iota((ROWS, HALF), 1)
        self.lane, self.group, self.place = lane, lane // EDGE, lane % EDGE
        self.y = [[None, None], [None, None]]
        self.z = [[None, None], [None, None]]

    def add(self, x, left, right):
        odd, half, at = x % 2, x // GROUPS, x % GROUPS
        ends = turned(jnp.where(self.lane < EDGE, left, right), EDGE * at)
        taken = (self.group == at) | (self.group == (at + GROUPS - 1) % GROUPS)
        before = self.y[half][odd]
        self.y[half][odd] = ends if before is None else jnp.where(taken, ends, before)
        taken = (self.place == x) | (self.place == (x + EDGE - 1) % EDGE)
        for h, value in enumerate((left, right)):
            moved = turned(value, x)
            before = self.z[h][odd]
            self.z[h][odd] = moved if before is None else jnp.where(taken, moved, before)

    def tables(self, h):
        even_group, even_place = self.group % 2 == 0, self.place % 2 == 0
        (y_even, y_odd), (z_even, z_odd) = self.y[h], self.z[h]
        low = (jnp.where(even_group, y_even, y_odd), jnp.where(even_place, z_even, z_odd))
        y_high, z_high = jnp.where(even_group, y_odd, y_even), jnp.where(even_place, z_odd, z_even)
        return low, (turned(y_high, EDGE), turned(z_high, 1 - EDGE))


def write_tables(packer, state, own):
    low, high = own
    for h in range(2):
        lanes = pl.ds(h * HALF, HALF)
        for ref, x in ((low, 0), (high, EDGE - 1)):
            ref[0, :, lanes] = state[h, pl.ds(x * ROWS, ROWS), :]
        for ref, (y_table, z_table) in zip(own, packer.tables(h)):
            ref[1, :, lanes] = y_table
            ref[2, :, lanes] = z_table


def emit_faces(packer, state, own, sends):
    write_tables(packer, state, own)
    low, high = own
    flat_a, flat_b, deep_a, deep_b = sends
    even = even_place("dev")
    for face in range(2):
        flat_a[face] = jnp.where(even, high[face], low[face])
        flat_b[face] = jnp.where(even, low[face], high[face])
    even = even_place("grp")
    deep_a[...] = jnp.where(even, high[2], low[2])
    deep_b[...] = jnp.where(even, low[2], high[2])


def fill_slot(state, slot, block):
    for f in range(NFIELD):
        value = block(f)
        for h in range(2):
            state[h, pl.ds(f * SLOTS + slot, EDGE, stride=ROWS), :] = value[:, h * HALF : (h + 1) * HALF]


def slot_rows():
    return iota(FACE, 0) % SLOTS


def shifted(value, rows):
    rows %= ROWS
    return pltpu.roll(value, rows, 0) if rows else value


def gathered(tables, slot):
    rows = slot_rows()
    out = shifted(tables[0], -slot)
    for number in range(1, len(tables)):
        out = jnp.where(rows == number, shifted(tables[number], number - slot), out)
    return out


def scattered(table, number, slot):
    return shifted(table, slot - number)


def even_place(axis):
    return lax.rem(lax.axis_index(axis), 2) == 0


def block_kernel(masks, fields, low, high, to_dev, to_grp):
    last, size = SLOTS - 1, NFIELD * EDGE
    for f in range(NFIELD):
        to_dev[f * EDGE : (f + 1) * EDGE] = fields[last, f]
        to_grp[f * EDGE : (f + 1) * EDGE] = fields[0, f]
    away = jnp.where(even_place("grp"), low[2], high[2])
    to_grp[size : size + ROWS] = jnp.where(slot_rows() == 0, away, masks[0])


def faces_kernel(masks, low, high, faces, faces_dev, *outs):
    new_low, new_high, flat_a, flat_b, deep_b = outs
    rows, last = slot_rows(), SLOTS - 1
    first_rows = (rows == 0) & (masks[1] > 0.5)
    last_rows = (rows == last) & (masks[0] > 0.5)
    even = even_place("grp")
    got_first, got_last, got_last_z = faces[0], faces_dev[0], faces_dev[1]
    for side, (raw, new) in enumerate(((low, new_low), (high, new_high))):
        for axis in range(2):
            number = 2 * axis + side
            table = jnp.where(first_rows, scattered(got_first, number, 0), raw[axis])
            new[axis] = jnp.where(last_rows, scattered(got_last, number, last), table)
        table = jnp.where(first_rows & (even if side == 0 else ~even), faces[1], raw[2])
        new[2] = jnp.where(last_rows, scattered(got_last_z, side, last), table)
    even_dev = even_place("dev")
    for axis in range(2):
        flat_a[axis] = jnp.where(even_dev, new_high[axis], new_low[axis])
        flat_b[axis] = jnp.where(even_dev, new_low[axis], new_high[axis])
    flat_a[2] = faces[1]
    deep_b[...] = jnp.where(even, new_low[2], new_high[2])


def cos_quarter(number):
    turn = number & 7
    size = jnp.where((turn & 3) == 0, 1.0, jnp.where((turn & 3) == 2, 0.0, math.sqrt(0.5)))
    return jnp.where((turn > 2) & (turn < 6), -size, size)


def plan_kernel(neighbors, orient, scale, select):
    shape = (ROWS, HALF)
    slot, field, column = iota(shape, 0) % SLOTS, iota(shape, 0) // SLOTS, iota(shape, 1)
    grp, dev = lax.axis_index("grp"), lax.axis_index("dev")
    rank = grp * lax.axis_size("dev") + dev

    def by_slot(values):
        rows = values[0]
        for number in range(1, SLOTS):
            rows = jnp.where(slot == number, values[number], rows)
        return rows

    spread = []
    for number in range(SLOTS):
        turn = 0.5 * cos_quarter(orient[number])
        lift = 0.5 * cos_quarter(orient[number] + 6)
        spread.append((1.0 + turn, 1.0 - turn, 1.0 + lift))
    conc = jnp.where(field == NPHASE, conc_rates[0], conc_rates[1])
    weights = [jnp.where(field < NPHASE, phase_rate * by_slot([own[axis] for own in spread]), conc) for axis in range(3)]
    for axis in range(3):
        scale[axis] = weights[axis]
    scale[3] = 1.0 - 2.0 * (weights[0] + weights[1] + weights[2])
    for face in range(6):
        first = []
        came = 2 + lax.rem(lax.rem(dev if face < 4 else grp, 2) + face % 2 + 1, 2)
        for number in range(SLOTS):
            target = neighbors[number, face]
            source = jnp.where(target < 0, 0, jnp.where(target // SLOTS == rank, 1, came))
            first.append(source * ROWS + jnp.where(target < 0, number, target & (SLOTS - 1)))
        select[face] = jnp.where(column == by_slot(first) + field * SLOTS, weights[face // 2], 0.0)


def start_kernel(fields, neighbors, orient, *refs):
    fetched, low, high, faces_grp, faces_dev, scale, select = refs[:7]
    state, near, turn, arrived = refs[7:]
    scalars = ((neighbors, near), (orient, turn))
    blocks = tuple((fields.at[slot], fetched.at[slot]) for slot in range(SLOTS))
    copies = [pltpu.make_async_copy(*pair, arrived.at[number]) for number, pair in enumerate((*scalars, *blocks))]
    for copy in copies:
        copy.start()
    for copy in copies[: len(scalars)]:
        copy.wait()
    plan_kernel(near, turn, scale, select)
    for slot in range(SLOTS):
        copies[len(scalars) + slot].wait()
        fill_slot(state, slot, lambda f: fetched[slot, f])
    packer = Packer()
    for x in range(EDGE):
        packer.add(x, *plane_at(state, x))
    write_tables(packer, state, (low, high))
    faces_grp[0] = gathered([low[0], high[0], low[1], high[1]], 0)
    faces_grp[1] = jnp.where(even_place("grp"), high[2], low[2])
    faces_dev[0] = gathered([low[0], high[0], low[1], high[1]], SLOTS - 1)
    faces_dev[1] = gathered([low[2], high[2]], SLOTS - 1)


def first_inner_kernel(masks, scale, fields, block_dev, block_grp, faces, low, high, new_low, new_high, *refs):
    partial, got_deep, relayed, z_low, z_high, state = refs
    size = NFIELD * EDGE
    swap_dev, swap_grp = masks[0] > 0.5, masks[1] > 0.5

    def block(slot):
        def of(f):
            value = fields[slot, f]
            if slot == 0:
                value = jnp.where(swap_grp[:EDGE], block_grp[f * EDGE : (f + 1) * EDGE], value)
            if slot == SLOTS - 1:
                value = jnp.where(swap_dev[:EDGE], block_dev[f * EDGE : (f + 1) * EDGE], value)
            return value

        return of

    for slot in range(SLOTS):
        fill_slot(state, slot, block(slot))
    rows, even = slot_rows(), even_place("grp")
    first_rows = (rows == 0) & swap_grp
    got_deep[...] = jnp.where(first_rows, jnp.where(even, low[2], high[2]), faces[1])
    other = block_grp[size : size + ROWS]
    relayed[...] = jnp.where(rows == SLOTS - 1, jnp.broadcast_to(other[1:2], FACE), 0.0)
    z_low[...] = jnp.where(first_rows & ~even, other, new_low[2])
    z_high[...] = jnp.where(first_rows & even, other, new_high[2])
    inner_kernel(state, scale, partial)


def inner_kernel(state, scale, partial):
    lane = iota((ROWS, HALF), 1)
    start_y, end_y = lane < EDGE, lane >= HALF - EDGE
    start_z, end_z = lane % EDGE == 0, lane % EDGE == EDGE - 1
    weight_x, weight_y, weight_z, weight = (scale[number] for number in range(4))
    tile = 2 * SLOTS
    planes = {0: plane_at(state, 0)}
    for x in range(EDGE):
        if x + 1 < EDGE:
            planes[x + 1] = plane_at(state, x + 1)
        left, right = planes[x]
        up = [turned(half, EDGE) for half in (left, right)]
        down = [turned(half, -EDGE) for half in (left, right)]
        sum_y = (
            jnp.where(start_y, 0.0, up[0]) + jnp.where(end_y, down[1], down[0]),
            jnp.where(start_y, up[0], up[1]) + jnp.where(end_y, 0.0, down[1]),
        )
        for h, half in enumerate((left, right)):
            sum_z = jnp.where(start_z, 0.0, turned(half, 1)) + jnp.where(end_z, 0.0, turned(half, -1))
            if x == 0:
                sum_x = planes[1][h]
            elif x == EDGE - 1:
                sum_x = planes[x - 1][h]
            else:
                sum_x = planes[x - 1][h] + planes[x + 1][h]
            flow = weight * half + weight_x * sum_x + weight_y * sum_y[h] + weight_z * sum_z
            phases, conc = (half[:tile], half[tile : 2 * tile]), half[2 * tile :]
            drive = conc - pltpu.roll(conc, SLOTS, 0)
            total = phases[0] + phases[1]
            total = total + pltpu.roll(total, SLOTS, 0)
            tail = (phase_rate * closure) * (1.0 - total)
            rows = x * ROWS
            for number, value in enumerate(phases):
                gain = value * (1.0 - value) * (coupling[2 * number] * drive + (2.0 * value - 1.0))
                part = flow[number * tile : (number + 1) * tile]
                partial[h, pl.ds(rows + number * tile, tile), :] = part + (phase_rate * gain + tail)
            partial[h, pl.ds(rows + 2 * tile, tile), :] = flow[2 * tile :]


def finish_kernel(last_step, select, partial, *refs):
    own, got_flat = refs[0:2], refs[2:4]
    own_deep = [ref[2] for ref in own]
    if last_step:
        got_deep = [ref[...] for ref in refs[4:6]]
        result, done, blocks, sent = refs[6:10]
    else:
        known, deep_b, relayed, z_low, z_high = refs[4:9]
        got_deep = [jnp.where(relayed[...] > 0.5, got_flat[0][2], known[...]), deep_b[...]]
        own_deep = [z_low[...], z_high[...]]
        done, outs, sends = refs[9], refs[10:12], refs[12:16]
    ghosts = []
    for face in range(6):
        axis, side = face // 2, face % 2
        got = [ref[axis] for ref in got_flat] if axis < 2 else got_deep
        mine = [ref[axis] for ref in own] if axis < 2 else own_deep
        tables = jnp.concatenate([mine[side], mine[1 - side], *got], axis=0)
        chosen = select[face][:, : SOURCES * ROWS]
        ghosts.append(jnp.dot(chosen, tables, precision=lax.Precision.HIGHEST, preferred_element_type=jnp.float32))
    lane = iota((ROWS, HALF), 1)
    start_y, end_y = lane < EDGE, lane >= HALF - EDGE
    ends_z = (lane % EDGE == 0) | (lane % EDGE == EDGE - 1)
    even_group, even_place = (lane // EDGE) % 2 == 0, lane % 2 == 0
    y_pairs, z_pairs = [], []
    for h in range(2):
        lanes = slice(h * HALF, (h + 1) * HALF)
        low, high = ghosts[2][:, lanes], turned(ghosts[3][:, lanes], -EDGE)
        y_pairs.append((jnp.where(even_group, low, high), jnp.where(even_group, high, low)))
        low, high = ghosts[4][:, lanes], turned(ghosts[5][:, lanes], EDGE - 1)
        z_pairs.append((jnp.where(even_place, low, high), jnp.where(even_place, high, low)))
    packer = None if last_step else Packer()
    copies = []
    for x in range(EDGE):
        halves = list(plane_at(partial, x))
        ends = turned(y_pairs[x // GROUPS][x % 2], -EDGE * (x % GROUPS))
        for h in range(2):
            value = halves[h] + jnp.where(start_y if h == 0 else end_y, ends, 0.0)
            value = value + jnp.where(ends_z, turned(z_pairs[h][x % 2], -x), 0.0)
            if x == 0:
                value = value + ghosts[0][:, h * HALF : (h + 1) * HALF]
            if x == EDGE - 1:
                value = value + ghosts[1][:, h * HALF : (h + 1) * HALF]
            done[h, pl.ds(x * ROWS, ROWS), :] = value
            halves[h] = value
        if not last_step:
            packer.add(x, *halves)
        elif x % 8 == 7:
            first = x - 7
            for slot in range(SLOTS):
                for f in range(NFIELD):
                    rows = pl.ds(first * ROWS + f * SLOTS + slot, 8, stride=ROWS)
                    for h in range(2):
                        lanes = pl.ds(h * HALF, HALF)
                        blocks[slot, f, first : first + 8, lanes] = done[h, rows, :]
            part = pl.ds(first, 8)
            copy = pltpu.make_async_copy(blocks.at[:, :, part], result.at[:, :, part], sent.at[x // 8])
            copy.start()
            copies.append(copy)
    for copy in copies:
        copy.wait()
    if not last_step:
        emit_faces(packer, done, outs, sends)


def spec(space):
    return pl.BlockSpec(memory_space=space)


VECTOR = pltpu.VMEM
SMALL = pltpu.CompilerParams(vmem_limit_bytes=8 << 20)
FLAT = (2, ROWS, PLANE)
TABLES = (STATE, SIDE, SIDE, FLAT, FLAT, FACE, FACE)
TO_DEV = (NFIELD * EDGE, PLANE)
TO_GRP = (NFIELD * EDGE + ROWS, PLANE)


def shaped(shape):
    return jax.ShapeDtypeStruct(shape, jnp.float32)


def cost(flops):
    return pl.CostEstimate(flops=flops, bytes_accessed=min(flops, 2 << 20), transcendentals=0)


def call(kernel, name, shapes, vectors, flops=1 << 20, scratch=()):
    return pl.pallas_call(
        kernel,
        name=name,
        compiler_params=SMALL,
        out_shape=[shaped(shape) for shape in shapes],
        in_specs=[spec(VECTOR)] * len(vectors),
        out_specs=[spec(VECTOR)] * len(shapes),
        scratch_shapes=list(scratch),
        cost_estimate=cost(flops),
    )(*vectors)


def start(arguments):
    shapes = (arguments[0].shape, SIDE, SIDE, FLAT, FLAT, (4, ROWS, HALF), (6, ROWS, HALF))
    return pl.pallas_call(
        start_kernel,
        name="start",
        compiler_params=SMALL,
        out_shape=[shaped(shape) for shape in shapes],
        in_specs=[spec(pl.ANY)] * len(arguments),
        out_specs=[spec(VECTOR)] * len(shapes),
        scratch_shapes=[
            pltpu.VMEM(STATE, jnp.float32),
            *(pltpu.SMEM(array.shape, jnp.int32) for array in arguments[1:]),
            pltpu.SemaphoreType.DMA((len(arguments) - 1 + SLOTS,)),
        ],
    )(*(pltpu.with_memory_space_constraint(array, pltpu.HBM) for array in arguments))


def body(fields, swap_dev, swap_grp, neighbors, orient):
    fields, low, high, faces, faces_dev, scale, select = start((fields, neighbors, orient))
    swap_dev, swap_grp, faces = lax.optimization_barrier((swap_dev, swap_grp, faces))
    flags = jnp.concatenate([swap_dev, swap_grp])
    masks = jnp.broadcast_to(jnp.where(flags == 1, 1.0, 0.0).reshape(2, 1, 1), (2, *FACE))
    faces = exchange(faces, "grp", 0)
    faces_dev = exchange(faces_dev, "dev", 0)
    to_dev, to_grp = call(block_kernel, "blocks", [TO_DEV, TO_GRP], [masks, fields, low, high], 1 << 24)
    block_grp = exchange(to_grp, "grp", 0)
    block_dev = exchange(to_dev, "dev", 0)
    new_low, new_high, *sends = call(
        faces_kernel,
        "faces",
        [SIDE, SIDE, SIDE, FLAT, FACE],
        [masks, low, high, faces, faces_dev],
        1 << 24,
    )
    flat_a = exchange(sends[0], "dev", 0)
    flat_b = exchange(sends[1], "dev", 1)
    deep_b = exchange(sends[2], "grp", 1)
    partial, deep_a, relayed, z_low, z_high = call(
        first_inner_kernel,
        "inner_0",
        [STATE, FACE, FACE, FACE, FACE],
        [masks, scale, fields, block_dev, block_grp, faces, low, high, new_low, new_high],
        4 << 20,
        [pltpu.VMEM(STATE, jnp.float32)],
    )
    state, *tables = call(
        functools.partial(finish_kernel, False),
        "finish_0",
        TABLES,
        [select, partial, new_low, new_high, flat_a, flat_b, deep_a, deep_b, relayed, z_low, z_high],
    )
    own, sends = tables[:2], tables[2:]
    flat_a = exchange(sends[0], "dev", 0)
    flat_b = exchange(sends[1], "dev", 1)
    deep_a = exchange(sends[2], "grp", 0)
    deep_b = exchange(sends[3], "grp", 1)
    (partial,) = call(inner_kernel, "inner_1", [STATE], [state, scale], 4 << 20)
    return pl.pallas_call(
        functools.partial(finish_kernel, True),
        name="finish_1",
        compiler_params=SMALL,
        out_shape=shaped(fields.shape),
        in_specs=[spec(VECTOR)] * 8,
        out_specs=spec(pl.ANY),
        scratch_shapes=[
            pltpu.VMEM(STATE, jnp.float32),
            pltpu.VMEM(fields.shape, jnp.float32),
            pltpu.SemaphoreType.DMA((2,)),
        ],
    )(select, partial, *own, flat_a, flat_b, deep_a, deep_b)


def solution(mesh):
    in_specs = (
        P(("grp", "dev"), None, None, None),
        P(("grp", "dev")),
        P(("grp", "dev")),
        P(("grp", "dev"), None),
        P(("grp", "dev")),
    )
    out_specs = P(("grp", "dev"), None, None, None)
    return jax.shard_map(body, mesh=mesh, in_specs=in_specs, out_specs=out_specs, check_vma=False)
```

```python
import functools
import math

import jax
import jax.numpy as jnp
from jax import lax
from jax.experimental import pallas as pl
from jax.experimental.pallas import tpu as pltpu
from jax.sharding import PartitionSpec as P

NPHASE = 4
NCONC = 2
NFIELD = NPHASE + NCONC
EDGE = 16
PLANE = EDGE * EDGE
HALF = PLANE // 2
GROUPS = HALF // EDGE
SLOTS = 4
ROWS = NFIELD * SLOTS

phase_rate = 0.05
closure = 0.1
coupling = (0.5, -0.5, 1.0, -1.0)
conc_rates = (0.08, 0.04)

STATE = (2, EDGE * ROWS, HALF)
FACE = (ROWS, PLANE)
SIDE = (3, ROWS, PLANE)
SOURCES = 4
PARTS = 2
SELECT = (3, 2 * ROWS, PARTS * SOURCES * ROWS)


def partners(axis, offset):
    sizes = (lax.axis_size("grp"), lax.axis_size("dev"))
    along = ("grp", "dev").index(axis)
    route = []
    for grp in range(sizes[0]):
        for dev in range(sizes[1]):
            own = (grp, dev)
            step = 1 if (own[along] - offset) % 2 == 0 else -1
            partner = list(own)
            partner[along] += step
            if not 0 <= partner[along] < sizes[along]:
                partner = list(own)
                partner[1 - along] ^= 1
                if partner[1 - along] >= sizes[1 - along]:
                    partner = list(own)
            route.append((grp * sizes[1] + dev, partner[0] * sizes[1] + partner[1]))
    return route


def exchange(block, axis, offset):
    return lax.ppermute(block, ("grp", "dev"), partners(axis, offset))


def iota(shape, dim):
    return lax.broadcasted_iota(jnp.int32, shape, dim)


def plane_at(ref, x):
    rows = pl.ds(x * ROWS, ROWS)
    return ref[0, rows, :], ref[1, rows, :]


def turned(value, shift):
    shift %= HALF
    return pltpu.roll(value, shift, 1) if shift else value


class Packer:
    def __init__(self):
        lane = iota((ROWS, HALF), 1)
        self.lane, self.group, self.place = lane, lane // EDGE, lane % EDGE
        self.y = [[None, None], [None, None]]
        self.z = [[None, None], [None, None]]

    def add(self, x, left, right):
        odd, half, at = x % 2, x // GROUPS, x % GROUPS
        ends = turned(jnp.where(self.lane < EDGE, left, right), EDGE * at)
        taken = (self.group == at) | (self.group == (at + GROUPS - 1) % GROUPS)
        before = self.y[half][odd]
        self.y[half][odd] = ends if before is None else jnp.where(taken, ends, before)
        taken = (self.place == x) | (self.place == (x + EDGE - 1) % EDGE)
        for h, value in enumerate((left, right)):
            moved = turned(value, x)
            before = self.z[h][odd]
            self.z[h][odd] = moved if before is None else jnp.where(taken, moved, before)

    def tables(self, h):
        even_group, even_place = self.group % 2 == 0, self.place % 2 == 0
        (y_even, y_odd), (z_even, z_odd) = self.y[h], self.z[h]
        low = (jnp.where(even_group, y_even, y_odd), jnp.where(even_place, z_even, z_odd))
        y_high, z_high = jnp.where(even_group, y_odd, y_even), jnp.where(even_place, z_odd, z_even)
        return low, (turned(y_high, EDGE), turned(z_high, 1 - EDGE))


def write_tables(packer, state, own):
    low, high = own
    for h in range(2):
        lanes = pl.ds(h * HALF, HALF)
        for ref, x in ((low, 0), (high, EDGE - 1)):
            ref[0, :, lanes] = state[h, pl.ds(x * ROWS, ROWS), :]
        for ref, (y_table, z_table) in zip(own, packer.tables(h)):
            ref[1, :, lanes] = y_table
            ref[2, :, lanes] = z_table


def emit_faces(packer, state, own, sends):
    write_tables(packer, state, own)
    low, high = own
    flat_a, flat_b, deep_a, deep_b = sends
    even = even_place("dev")
    for face in range(2):
        flat_a[face] = jnp.where(even, high[face], low[face])
        flat_b[face] = jnp.where(even, low[face], high[face])
    even = even_place("grp")
    deep_a[...] = jnp.where(even, high[2], low[2])
    deep_b[...] = jnp.where(even, low[2], high[2])


def fill_slot(state, slot, block, first=0, count=EDGE):
    for f in range(NFIELD):
        value = block(f)
        for h in range(2):
            rows = pl.ds(first * ROWS + f * SLOTS + slot, count, stride=ROWS)
            state[h, rows, :] = value[:, h * HALF : (h + 1) * HALF]


def slot_rows():
    return iota(FACE, 0) % SLOTS


def shifted(value, rows):
    rows %= ROWS
    return pltpu.roll(value, rows, 0) if rows else value


def gathered(tables, slot):
    rows = slot_rows()
    out = shifted(tables[0], -slot)
    for number in range(1, len(tables)):
        out = jnp.where(rows == number, shifted(tables[number], number - slot), out)
    return out


def scattered(table, number, slot):
    return shifted(table, slot - number)


def even_place(axis):
    return lax.rem(lax.axis_index(axis), 2) == 0


def block_kernel(mask_dev, fields, low, high, to_dev, to_grp):
    last, size = SLOTS - 1, NFIELD * EDGE
    for f in range(NFIELD):
        to_dev[f * EDGE : (f + 1) * EDGE] = fields[last, f]
        to_grp[f * EDGE : (f + 1) * EDGE] = fields[0, f]
    away = jnp.where(even_place("grp"), low[2], high[2])
    to_grp[size : size + ROWS] = jnp.where(slot_rows() == 0, away, mask_dev[...])


def faces_kernel(mask_dev, mask_grp, low, high, faces, faces_dev, *outs):
    new_low, new_high, flat_a, flat_b, deep_b = outs
    rows, last = slot_rows(), SLOTS - 1
    first_rows = (rows == 0) & (mask_grp[...] > 0.5)
    last_rows = (rows == last) & (mask_dev[...] > 0.5)
    even = even_place("grp")
    got_first, got_last, got_last_z = faces[0], faces_dev[0], faces_dev[1]
    for side, (raw, new) in enumerate(((low, new_low), (high, new_high))):
        for axis in range(2):
            number = 2 * axis + side
            table = jnp.where(first_rows, scattered(got_first, number, 0), raw[axis])
            new[axis] = jnp.where(last_rows, scattered(got_last, number, last), table)
        table = jnp.where(first_rows & (even if side == 0 else ~even), faces[1], raw[2])
        new[2] = jnp.where(last_rows, scattered(got_last_z, side, last), table)
    even_dev = even_place("dev")
    for axis in range(2):
        flat_a[axis] = jnp.where(even_dev, new_high[axis], new_low[axis])
        flat_b[axis] = jnp.where(even_dev, new_low[axis], new_high[axis])
    flat_a[2] = faces[1]
    deep_b[...] = jnp.where(even, new_low[2], new_high[2])


def cos_quarter(number):
    turn = number & 7
    size = jnp.where((turn & 3) == 0, 1.0, jnp.where((turn & 3) == 2, 0.0, math.sqrt(0.5)))
    return jnp.where((turn > 2) & (turn < 6), -size, size)


def plan_kernel(neighbors, orient, scale, select):
    shape = (ROWS, HALF)
    slot, field, column = iota(shape, 0) % SLOTS, iota(shape, 0) // SLOTS, iota(shape, 1)
    grp, dev = lax.axis_index("grp"), lax.axis_index("dev")
    rank = grp * lax.axis_size("dev") + dev

    def by_slot(values):
        rows = values[0]
        for number in range(1, SLOTS):
            rows = jnp.where(slot == number, values[number], rows)
        return rows

    spread = []
    for number in range(SLOTS):
        turn = 0.5 * cos_quarter(orient[number])
        lift = 0.5 * cos_quarter(orient[number] + 6)
        spread.append((1.0 + turn, 1.0 - turn, 1.0 + lift))
    conc = jnp.where(field == NPHASE, conc_rates[0], conc_rates[1])
    weights = [jnp.where(field < NPHASE, phase_rate * by_slot([own[axis] for own in spread]), conc) for axis in range(3)]
    for axis in range(3):
        scale[axis] = weights[axis]
    scale[3] = 1.0 - 2.0 * (weights[0] + weights[1] + weights[2])
    for face in range(6):
        first = []
        came = 2 + lax.rem(lax.rem(dev if face < 4 else grp, 2) + face % 2 + 1, 2)
        for number in range(SLOTS):
            target = neighbors[number, face]
            source = jnp.where(target < 0, face % 2, jnp.where(target // SLOTS == rank, 1 - face % 2, came))
            first.append(source * ROWS + jnp.where(target < 0, number, target & (SLOTS - 1)))
        chosen = jnp.where(column == by_slot(first) + field * SLOTS, 1.0, 0.0)[:, : SOURCES * ROWS]
        rows = pl.ds(face % 2 * ROWS, ROWS)
        for part in range(PARTS):
            select[face // 2, rows, pl.ds(part * SOURCES * ROWS, SOURCES * ROWS)] = chosen


def start_kernel(fields, neighbors, orient, *refs):
    fetched, low, high, faces_grp, faces_dev, scale, select = refs[:7]
    state, near, turn, arrived = refs[7:]
    scalars = ((neighbors, near), (orient, turn))
    parts = [pl.ds(first, EDGE // 2) for first in (0, EDGE // 2)]
    blocks = tuple((fields.at[:, :, part], fetched.at[:, :, part]) for part in parts)
    copies = [pltpu.make_async_copy(*pair, arrived.at[number]) for number, pair in enumerate((*scalars, *blocks))]
    for copy in copies:
        copy.start()
    for copy in copies[: len(scalars)]:
        copy.wait()
    plan_kernel(near, turn, scale, select)
    packer = Packer()
    for number, part in enumerate(parts):
        copies[len(scalars) + number].wait()
        first = number * (EDGE // 2)
        for slot in range(SLOTS):
            fill_slot(state, slot, lambda f: fetched[slot, f, part], first, EDGE // 2)
        for x in range(first, first + EDGE // 2):
            packer.add(x, *plane_at(state, x))
    write_tables(packer, state, (low, high))
    faces_grp[0] = gathered([low[0], high[0], low[1], high[1]], 0)
    faces_grp[1] = jnp.where(even_place("grp"), high[2], low[2])
    faces_dev[0] = gathered([low[0], high[0], low[1], high[1]], SLOTS - 1)
    faces_dev[1] = gathered([low[2], high[2]], SLOTS - 1)


def first_inner_kernel(mask_dev, mask_grp, scale, fields, block_dev, block_grp, faces, low, high, new_low, new_high, *refs):
    partial, got_deep, relayed, z_low, z_high, state = refs
    size = NFIELD * EDGE
    swap_dev, swap_grp = mask_dev[...] > 0.5, mask_grp[...] > 0.5

    def block(slot):
        def of(f):
            value = fields[slot, f]
            if slot == 0:
                value = jnp.where(swap_grp[:EDGE], block_grp[f * EDGE : (f + 1) * EDGE], value)
            if slot == SLOTS - 1:
                value = jnp.where(swap_dev[:EDGE], block_dev[f * EDGE : (f + 1) * EDGE], value)
            return value

        return of

    for slot in range(SLOTS):
        fill_slot(state, slot, block(slot))
    rows, even = slot_rows(), even_place("grp")
    first_rows = (rows == 0) & swap_grp
    got_deep[...] = jnp.where(first_rows, jnp.where(even, low[2], high[2]), faces[1])
    other = block_grp[size : size + ROWS]
    relayed[...] = jnp.where(rows == SLOTS - 1, jnp.broadcast_to(other[1:2], FACE), 0.0)
    z_low[...] = jnp.where(first_rows & ~even, other, new_low[2])
    z_high[...] = jnp.where(first_rows & even, other, new_high[2])
    inner_kernel(state, scale, partial)


def inner_kernel(state, scale, partial):
    lane = iota((ROWS, HALF), 1)
    start_y, end_y = lane < EDGE, lane >= HALF - EDGE
    start_z, end_z = lane % EDGE == 0, lane % EDGE == EDGE - 1
    weight_x, weight_y, weight_z, weight = (scale[number] for number in range(4))
    tile = 2 * SLOTS
    planes = {0: plane_at(state, 0)}
    for x in range(EDGE):
        if x + 1 < EDGE:
            planes[x + 1] = plane_at(state, x + 1)
        left, right = planes[x]
        up = [turned(half, EDGE) for half in (left, right)]
        down = [turned(half, -EDGE) for half in (left, right)]
        sum_y = (
            jnp.where(start_y, 0.0, up[0]) + jnp.where(end_y, down[1], down[0]),
            jnp.where(start_y, up[0], up[1]) + jnp.where(end_y, 0.0, down[1]),
        )
        for h, half in enumerate((left, right)):
            sum_z = jnp.where(start_z, 0.0, turned(half, 1)) + jnp.where(end_z, 0.0, turned(half, -1))
            if x == 0:
                sum_x = planes[1][h]
            elif x == EDGE - 1:
                sum_x = planes[x - 1][h]
            else:
                sum_x = planes[x - 1][h] + planes[x + 1][h]
            flow = weight * half + weight_x * sum_x + weight_y * sum_y[h] + weight_z * sum_z
            phases, conc = (half[:tile], half[tile : 2 * tile]), half[2 * tile :]
            drive = conc - pltpu.roll(conc, SLOTS, 0)
            total = phases[0] + phases[1]
            total = total + pltpu.roll(total, SLOTS, 0)
            tail = (phase_rate * closure) * (1.0 - total)
            rows = x * ROWS
            for number, value in enumerate(phases):
                gain = value * (1.0 - value) * (coupling[2 * number] * drive + (2.0 * value - 1.0))
                part = flow[number * tile : (number + 1) * tile]
                partial[h, pl.ds(rows + number * tile, tile), :] = part + (phase_rate * gain + tail)
            partial[h, pl.ds(rows + 2 * tile, tile), :] = flow[2 * tile :]


def finish_kernel(last_step, scale, select, partial, *refs):
    own, got_flat = refs[0:2], refs[2:4]
    own_deep = [ref[2] for ref in own]
    if last_step:
        got_deep = [ref[...] for ref in refs[4:6]]
        result, done, blocks, sent = refs[6:10]
    else:
        known, deep_b, relayed, z_low, z_high = refs[4:9]
        got_deep = [jnp.where(relayed[...] > 0.5, got_flat[0][2], known[...]), deep_b[...]]
        own_deep = [z_low[...], z_high[...]]
        done, outs, sends = refs[9], refs[10:12], refs[12:16]
    ghosts = []
    for axis in range(3):
        got = [ref[axis] for ref in got_flat] if axis < 2 else got_deep
        mine = [ref[axis] for ref in own] if axis < 2 else own_deep
        tables = jnp.concatenate([*mine, *got], axis=0)
        near = tables.astype(jnp.bfloat16)
        rest = (tables - near.astype(jnp.float32)).astype(jnp.bfloat16)
        both = jnp.concatenate([near, rest], axis=0)
        pair = jnp.dot(select[axis].astype(jnp.bfloat16), both, preferred_element_type=jnp.float32)
        weight = jnp.concatenate([scale[axis]] * 2, axis=1)
        ghosts += [weight * pair[:ROWS], weight * pair[ROWS:]]
    lane = iota((ROWS, HALF), 1)
    start_y, end_y = lane < EDGE, lane >= HALF - EDGE
    ends_z = (lane % EDGE == 0) | (lane % EDGE == EDGE - 1)
    even_group, even_place = (lane // EDGE) % 2 == 0, lane % 2 == 0
    y_pairs, z_pairs = [], []
    for h in range(2):
        lanes = slice(h * HALF, (h + 1) * HALF)
        low, high = ghosts[2][:, lanes], turned(ghosts[3][:, lanes], -EDGE)
        y_pairs.append((jnp.where(even_group, low, high), jnp.where(even_group, high, low)))
        low, high = ghosts[4][:, lanes], turned(ghosts[5][:, lanes], EDGE - 1)
        z_pairs.append((jnp.where(even_place, low, high), jnp.where(even_place, high, low)))
    packer = None if last_step else Packer()
    copies = []
    for x in range(EDGE):
        halves = list(plane_at(partial, x))
        ends = turned(y_pairs[x // GROUPS][x % 2], -EDGE * (x % GROUPS))
        for h in range(2):
            value = halves[h] + jnp.where(start_y if h == 0 else end_y, ends, 0.0)
            value = value + jnp.where(ends_z, turned(z_pairs[h][x % 2], -x), 0.0)
            if x == 0:
                value = value + ghosts[0][:, h * HALF : (h + 1) * HALF]
            if x == EDGE - 1:
                value = value + ghosts[1][:, h * HALF : (h + 1) * HALF]
            done[h, pl.ds(x * ROWS, ROWS), :] = value
            halves[h] = value
        if not last_step:
            packer.add(x, *halves)
        elif x % 8 == 7:
            first = x - 7
            for slot in range(SLOTS):
                for f in range(NFIELD):
                    rows = pl.ds(first * ROWS + f * SLOTS + slot, 8, stride=ROWS)
                    for h in range(2):
                        lanes = pl.ds(h * HALF, HALF)
                        blocks[slot, f, first : first + 8, lanes] = done[h, rows, :]
            part = pl.ds(first, 8)
            copy = pltpu.make_async_copy(blocks.at[:, :, part], result.at[:, :, part], sent.at[x // 8])
            copy.start()
            copies.append(copy)
    for copy in copies:
        copy.wait()
    if not last_step:
        emit_faces(packer, done, outs, sends)


def spec(space):
    return pl.BlockSpec(memory_space=space)


VECTOR = pltpu.VMEM
SMALL = pltpu.CompilerParams(vmem_limit_bytes=8 << 20)
FLAT = (2, ROWS, PLANE)
TABLES = (STATE, SIDE, SIDE, FLAT, FLAT, FACE, FACE)
TO_DEV = (NFIELD * EDGE, PLANE)
TO_GRP = (NFIELD * EDGE + ROWS, PLANE)


def shaped(shape):
    return jax.ShapeDtypeStruct(shape, jnp.float32)


def cost(flops):
    return pl.CostEstimate(flops=flops, bytes_accessed=min(flops, 2 << 20), transcendentals=0)


def call(kernel, name, shapes, vectors, flops=1 << 20, scratch=()):
    return pl.pallas_call(
        kernel,
        name=name,
        compiler_params=SMALL,
        out_shape=[shaped(shape) for shape in shapes],
        in_specs=[spec(VECTOR)] * len(vectors),
        out_specs=[spec(VECTOR)] * len(shapes),
        scratch_shapes=list(scratch),
        cost_estimate=cost(flops),
    )(*vectors)


def start(arguments):
    shapes = (arguments[0].shape, SIDE, SIDE, FLAT, FLAT, (4, ROWS, HALF), SELECT)
    return pl.pallas_call(
        start_kernel,
        name="start",
        compiler_params=SMALL,
        out_shape=[shaped(shape) for shape in shapes],
        in_specs=[spec(pl.ANY)] * len(arguments),
        out_specs=[spec(VECTOR)] * len(shapes),
        scratch_shapes=[
            pltpu.VMEM(STATE, jnp.float32),
            *(pltpu.SMEM(array.shape, jnp.int32) for array in arguments[1:]),
            pltpu.SemaphoreType.DMA((len(arguments) + 1,)),
        ],
    )(*(pltpu.with_memory_space_constraint(array, pltpu.HBM) for array in arguments))


def mask(flag):
    return jnp.broadcast_to(jnp.where(flag == 1, 1.0, 0.0).reshape(1, 1), FACE)


def body(fields, swap_dev, swap_grp, neighbors, orient):
    fields, low, high, faces, faces_dev, scale, select = start((fields, neighbors, orient))
    swap_dev, faces = lax.optimization_barrier((swap_dev, faces))
    faces = exchange(faces, "grp", 0)
    faces_dev = exchange(faces_dev, "dev", 0)
    mask_dev = mask(swap_dev)
    to_dev, to_grp = call(block_kernel, "blocks", [TO_DEV, TO_GRP], [mask_dev, fields, low, high], 1 << 24)
    swap_grp, to_grp = lax.optimization_barrier((swap_grp, to_grp))
    mask_grp = mask(swap_grp)
    block_grp = exchange(to_grp, "grp", 0)
    block_dev = exchange(to_dev, "dev", 0)
    new_low, new_high, *sends = call(
        faces_kernel,
        "faces",
        [SIDE, SIDE, SIDE, FLAT, FACE],
        [mask_dev, mask_grp, low, high, faces, faces_dev],
        1 << 24,
    )
    flat_a = exchange(sends[0], "dev", 0)
    flat_b = exchange(sends[1], "dev", 1)
    deep_b = exchange(sends[2], "grp", 1)
    partial, deep_a, relayed, z_low, z_high = call(
        first_inner_kernel,
        "inner_0",
        [STATE, FACE, FACE, FACE, FACE],
        [mask_dev, mask_grp, scale, fields, block_dev, block_grp, faces, low, high, new_low, new_high],
        4 << 20,
        [pltpu.VMEM(STATE, jnp.float32)],
    )
    state, *tables = call(
        functools.partial(finish_kernel, False),
        "finish_0",
        TABLES,
        [scale, select, partial, new_low, new_high, flat_a, flat_b, deep_a, deep_b, relayed, z_low, z_high],
    )
    own, sends = tables[:2], tables[2:]
    flat_a = exchange(sends[0], "dev", 0)
    flat_b = exchange(sends[1], "dev", 1)
    deep_a = exchange(sends[2], "grp", 0)
    deep_b = exchange(sends[3], "grp", 1)
    (partial,) = call(inner_kernel, "inner_1", [STATE], [state, scale], 4 << 20)
    return pl.pallas_call(
        functools.partial(finish_kernel, True),
        name="finish_1",
        compiler_params=SMALL,
        out_shape=shaped(fields.shape),
        in_specs=[spec(VECTOR)] * 9,
        out_specs=spec(pl.ANY),
        scratch_shapes=[
            pltpu.VMEM(STATE, jnp.float32),
            pltpu.VMEM(fields.shape, jnp.float32),
            pltpu.SemaphoreType.DMA((2,)),
        ],
    )(scale, select, partial, *own, flat_a, flat_b, deep_a, deep_b)


def solution(mesh):
    in_specs = (
        P(("grp", "dev"), None, None, None),
        P(("grp", "dev")),
        P(("grp", "dev")),
        P(("grp", "dev"), None),
        P(("grp", "dev")),
    )
    out_specs = P(("grp", "dev"), None, None, None)
    return jax.shard_map(body, mesh=mesh, in_specs=in_specs, out_specs=out_specs, check_vma=False)
```

```python
import functools
import math

import jax
import jax.numpy as jnp
from jax import lax
from jax.experimental import pallas as pl
from jax.experimental.pallas import tpu as pltpu
from jax.sharding import PartitionSpec as P

NPHASE = 4
NCONC = 2
NFIELD = NPHASE + NCONC
EDGE = 16
PLANE = EDGE * EDGE
HALF = PLANE // 2
GROUPS = HALF // EDGE
SLOTS = 4
ROWS = NFIELD * SLOTS

phase_rate = 0.05
closure = 0.1
coupling = (0.5, -0.5, 1.0, -1.0)
conc_rates = (0.08, 0.04)

STATE = (2, EDGE * ROWS, HALF)
FACE = (ROWS, PLANE)
SIDE = (3, ROWS, PLANE)
SOURCES = 4
PARTS = 2
SELECT = (3, 2 * ROWS, PARTS * SOURCES * ROWS)


def partners(axis, offset):
    sizes = (lax.axis_size("grp"), lax.axis_size("dev"))
    route = []
    for grp in range(sizes[0]):
        for dev in range(sizes[1]):
            place = dev if axis == "dev" else grp
            beside = place + (1 if (place - offset) % 2 == 0 else -1)
            if axis == "dev":
                partner = (grp, beside % sizes[1])
            elif 0 <= beside < sizes[0]:
                partner = (beside, dev)
            else:
                partner = (grp, dev ^ 1)
            route.append((grp * sizes[1] + dev, partner[0] * sizes[1] + partner[1]))
    return route


def exchange(block, axis, offset):
    return lax.ppermute(block, ("grp", "dev"), partners(axis, offset))


def iota(shape, dim):
    return lax.broadcasted_iota(jnp.int32, shape, dim)


def plane_at(ref, x):
    rows = pl.ds(x * ROWS, ROWS)
    return ref[0, rows, :], ref[1, rows, :]


def turned(value, shift):
    shift %= HALF
    return pltpu.roll(value, shift, 1) if shift else value


class Packer:
    def __init__(self):
        lane = iota((ROWS, HALF), 1)
        self.lane, self.group, self.place = lane, lane // EDGE, lane % EDGE
        self.y = [[None, None], [None, None]]
        self.z = [[None, None], [None, None]]

    def add(self, x, left, right):
        odd, half, at = x % 2, x // GROUPS, x % GROUPS
        ends = turned(jnp.where(self.lane < EDGE, left, right), EDGE * at)
        taken = (self.group == at) | (self.group == (at + GROUPS - 1) % GROUPS)
        before = self.y[half][odd]
        self.y[half][odd] = ends if before is None else jnp.where(taken, ends, before)
        taken = (self.place == x) | (self.place == (x + EDGE - 1) % EDGE)
        for h, value in enumerate((left, right)):
            moved = turned(value, x)
            before = self.z[h][odd]
            self.z[h][odd] = moved if before is None else jnp.where(taken, moved, before)

    def tables(self, h):
        even_group, even_place = self.group % 2 == 0, self.place % 2 == 0
        (y_even, y_odd), (z_even, z_odd) = self.y[h], self.z[h]
        low = (jnp.where(even_group, y_even, y_odd), jnp.where(even_place, z_even, z_odd))
        y_high, z_high = jnp.where(even_group, y_odd, y_even), jnp.where(even_place, z_odd, z_even)
        return low, (turned(y_high, EDGE), turned(z_high, 1 - EDGE))


def write_tables(packer, state, own):
    low, high = own
    for h in range(2):
        lanes = pl.ds(h * HALF, HALF)
        for ref, x in ((low, 0), (high, EDGE - 1)):
            ref[0, :, lanes] = state[h, pl.ds(x * ROWS, ROWS), :]
        for ref, (y_table, z_table) in zip(own, packer.tables(h)):
            ref[1, :, lanes] = y_table
            ref[2, :, lanes] = z_table


def emit_faces(packer, state, own, sends):
    write_tables(packer, state, own)
    low, high = own
    flat_a, flat_b, deep_a, deep_b = sends
    even = even_place("dev")
    for face in range(2):
        flat_a[face] = jnp.where(even, high[face], low[face])
        flat_b[face] = jnp.where(even, low[face], high[face])
    even = even_place("grp")
    deep_a[...] = jnp.where(even, high[2], low[2])
    deep_b[...] = jnp.where(even, low[2], high[2])


def fill_slot(state, slot, block, first=0, count=EDGE):
    for f in range(NFIELD):
        value = block(f)
        for h in range(2):
            rows = pl.ds(first * ROWS + f * SLOTS + slot, count, stride=ROWS)
            state[h, rows, :] = value[:, h * HALF : (h + 1) * HALF]


def slot_rows():
    return iota(FACE, 0) % SLOTS


def shifted(value, rows):
    rows %= ROWS
    return pltpu.roll(value, rows, 0) if rows else value


def gathered(tables, slot):
    rows = slot_rows()
    out = shifted(tables[0], -slot)
    for number in range(1, len(tables)):
        out = jnp.where(rows == number, shifted(tables[number], number - slot), out)
    return out


def scattered(table, number, slot):
    return shifted(table, slot - number)


def even_place(axis):
    return lax.rem(lax.axis_index(axis), 2) == 0


def block_kernel(mask_dev, fields, low, high, to_dev, to_grp):
    last, size = SLOTS - 1, NFIELD * EDGE
    for f in range(NFIELD):
        to_dev[f * EDGE : (f + 1) * EDGE] = fields[last, f]
        to_grp[f * EDGE : (f + 1) * EDGE] = fields[0, f]
    away = jnp.where(even_place("grp"), low[2], high[2])
    to_grp[size : size + ROWS] = jnp.where(slot_rows() == 0, away, mask_dev[...])


def faces_kernel(mask_dev, mask_grp, low, high, faces, faces_dev, *outs):
    new_low, new_high, flat_a, flat_b, deep_b = outs
    rows, last = slot_rows(), SLOTS - 1
    first_rows = (rows == 0) & (mask_grp[...] > 0.5)
    last_rows = (rows == last) & (mask_dev[...] > 0.5)
    even = even_place("grp")
    got_first, got_last, got_last_z = faces[0], faces_dev[0], faces_dev[1]
    for side, (raw, new) in enumerate(((low, new_low), (high, new_high))):
        for axis in range(2):
            number = 2 * axis + side
            table = jnp.where(first_rows, scattered(got_first, number, 0), raw[axis])
            new[axis] = jnp.where(last_rows, scattered(got_last, number, last), table)
        table = jnp.where(first_rows & (even if side == 0 else ~even), faces[1], raw[2])
        new[2] = jnp.where(last_rows, scattered(got_last_z, side, last), table)
    even_dev = even_place("dev")
    for axis in range(2):
        flat_a[axis] = jnp.where(even_dev, new_high[axis], new_low[axis])
        flat_b[axis] = jnp.where(even_dev, new_low[axis], new_high[axis])
    flat_a[2] = faces[1]
    deep_b[...] = jnp.where(even, new_low[2], new_high[2])


def cos_quarter(number):
    turn = number & 7
    size = jnp.where((turn & 3) == 0, 1.0, jnp.where((turn & 3) == 2, 0.0, math.sqrt(0.5)))
    return jnp.where((turn > 2) & (turn < 6), -size, size)


def plan_kernel(neighbors, orient, sent, scale, select):
    del sent
    shape = (ROWS, HALF)
    slot, field, column = iota(shape, 0) % SLOTS, iota(shape, 0) // SLOTS, iota(shape, 1)
    grp, dev = lax.axis_index("grp"), lax.axis_index("dev")
    rank = grp * lax.axis_size("dev") + dev

    def by_slot(values):
        rows = values[0]
        for number in range(1, SLOTS):
            rows = jnp.where(slot == number, values[number], rows)
        return rows

    spread = []
    for number in range(SLOTS):
        turn = 0.5 * cos_quarter(orient[number])
        lift = 0.5 * cos_quarter(orient[number] + 6)
        spread.append((1.0 + turn, 1.0 - turn, 1.0 + lift))
    conc = jnp.where(field == NPHASE, conc_rates[0], conc_rates[1])
    weights = [jnp.where(field < NPHASE, phase_rate * by_slot([own[axis] for own in spread]), conc) for axis in range(3)]
    for axis in range(3):
        scale[axis] = weights[axis]
    scale[3] = 1.0 - 2.0 * (weights[0] + weights[1] + weights[2])
    for face in range(6):
        first = []
        came = 2 + lax.rem(lax.rem(dev if face < 4 else grp, 2) + face % 2 + 1, 2)
        for number in range(SLOTS):
            target = neighbors[number, face]
            source = jnp.where(target < 0, face % 2, jnp.where(target // SLOTS == rank, 1 - face % 2, came))
            first.append(source * ROWS + jnp.where(target < 0, number, target & (SLOTS - 1)))
        chosen = jnp.where(column == by_slot(first) + field * SLOTS, 1.0, 0.0)[:, : SOURCES * ROWS]
        rows = pl.ds(face % 2 * ROWS, ROWS)
        for part in range(PARTS):
            select[face // 2, rows, pl.ds(part * SOURCES * ROWS, SOURCES * ROWS)] = chosen


def start_kernel(fields, fetched, low, high, faces_grp, faces_dev, state, arrived):
    parts = [pl.ds(first, EDGE // 2) for first in (0, EDGE // 2)]
    copies = [
        pltpu.make_async_copy(fields.at[:, :, part], fetched.at[:, :, part], arrived.at[number])
        for number, part in enumerate(parts)
    ]
    for copy in copies:
        copy.start()
    packer = Packer()
    for number, part in enumerate(parts):
        copies[number].wait()
        first = number * (EDGE // 2)
        for slot in range(SLOTS):
            fill_slot(state, slot, lambda f: fetched[slot, f, part], first, EDGE // 2)
        for x in range(first, first + EDGE // 2):
            packer.add(x, *plane_at(state, x))
    write_tables(packer, state, (low, high))
    faces_grp[0] = gathered([low[0], high[0], low[1], high[1]], 0)
    faces_grp[1] = jnp.where(even_place("grp"), high[2], low[2])
    faces_dev[0] = gathered([low[0], high[0], low[1], high[1]], SLOTS - 1)
    faces_dev[1] = gathered([low[2], high[2]], SLOTS - 1)


def first_inner_kernel(mask_dev, mask_grp, scale, fields, block_dev, block_grp, faces, low, high, new_low, new_high, *refs):
    partial, got_deep, relayed, z_low, z_high, state = refs
    size = NFIELD * EDGE
    swap_dev, swap_grp = mask_dev[...] > 0.5, mask_grp[...] > 0.5

    def block(slot):
        def of(f):
            value = fields[slot, f]
            if slot == 0:
                value = jnp.where(swap_grp[:EDGE], block_grp[f * EDGE : (f + 1) * EDGE], value)
            if slot == SLOTS - 1:
                value = jnp.where(swap_dev[:EDGE], block_dev[f * EDGE : (f + 1) * EDGE], value)
            return value

        return of

    for slot in range(SLOTS):
        fill_slot(state, slot, block(slot))
    rows, even = slot_rows(), even_place("grp")
    first_rows = (rows == 0) & swap_grp
    got_deep[...] = jnp.where(first_rows, jnp.where(even, low[2], high[2]), faces[1])
    other = block_grp[size : size + ROWS]
    relayed[...] = jnp.where(rows == SLOTS - 1, jnp.broadcast_to(other[1:2], FACE), 0.0)
    z_low[...] = jnp.where(first_rows & ~even, other, new_low[2])
    z_high[...] = jnp.where(first_rows & even, other, new_high[2])
    inner_kernel(state, scale, partial)


def inner_kernel(state, scale, partial):
    lane = iota((ROWS, HALF), 1)
    start_y, end_y = lane < EDGE, lane >= HALF - EDGE
    start_z, end_z = lane % EDGE == 0, lane % EDGE == EDGE - 1
    weight_x, weight_y, weight_z, weight = (scale[number] for number in range(4))
    tile = 2 * SLOTS
    planes = {0: plane_at(state, 0)}
    for x in range(EDGE):
        if x + 1 < EDGE:
            planes[x + 1] = plane_at(state, x + 1)
        left, right = planes[x]
        up = [turned(half, EDGE) for half in (left, right)]
        down = [turned(half, -EDGE) for half in (left, right)]
        sum_y = (
            jnp.where(start_y, 0.0, up[0]) + jnp.where(end_y, down[1], down[0]),
            jnp.where(start_y, up[0], up[1]) + jnp.where(end_y, 0.0, down[1]),
        )
        for h, half in enumerate((left, right)):
            sum_z = jnp.where(start_z, 0.0, turned(half, 1)) + jnp.where(end_z, 0.0, turned(half, -1))
            if x == 0:
                sum_x = planes[1][h]
            elif x == EDGE - 1:
                sum_x = planes[x - 1][h]
            else:
                sum_x = planes[x - 1][h] + planes[x + 1][h]
            flow = weight * half + weight_x * sum_x + weight_y * sum_y[h] + weight_z * sum_z
            phases, conc = (half[:tile], half[tile : 2 * tile]), half[2 * tile :]
            drive = conc - pltpu.roll(conc, SLOTS, 0)
            total = phases[0] + phases[1]
            total = total + pltpu.roll(total, SLOTS, 0)
            tail = (phase_rate * closure) * (1.0 - total)
            rows = x * ROWS
            for number, value in enumerate(phases):
                gain = value * (1.0 - value) * (coupling[2 * number] * drive + (2.0 * value - 1.0))
                part = flow[number * tile : (number + 1) * tile]
                partial[h, pl.ds(rows + number * tile, tile), :] = part + (phase_rate * gain + tail)
            partial[h, pl.ds(rows + 2 * tile, tile), :] = flow[2 * tile :]


def finish_kernel(last_step, scale, select, partial, *refs):
    own, got_flat = refs[0:2], refs[2:4]
    own_deep = [ref[2] for ref in own]
    if last_step:
        got_deep = [ref[...] for ref in refs[4:6]]
        result, done, blocks, sent = refs[6:10]
    else:
        known, deep_b, relayed, z_low, z_high = refs[4:9]
        got_deep = [jnp.where(relayed[...] > 0.5, got_flat[0][2], known[...]), deep_b[...]]
        own_deep = [z_low[...], z_high[...]]
        done, outs, sends = refs[9], refs[10:12], refs[12:16]
    ghosts = []
    for axis in range(3):
        got = [ref[axis] for ref in got_flat] if axis < 2 else got_deep
        mine = [ref[axis] for ref in own] if axis < 2 else own_deep
        tables = jnp.concatenate([*mine, *got], axis=0)
        near = tables.astype(jnp.bfloat16)
        rest = (tables - near.astype(jnp.float32)).astype(jnp.bfloat16)
        both = jnp.concatenate([near, rest], axis=0)
        pair = jnp.dot(select[axis].astype(jnp.bfloat16), both, preferred_element_type=jnp.float32)
        weight = jnp.concatenate([scale[axis]] * 2, axis=1)
        ghosts += [weight * pair[:ROWS], weight * pair[ROWS:]]
    lane = iota((ROWS, HALF), 1)
    start_y, end_y = lane < EDGE, lane >= HALF - EDGE
    ends_z = (lane % EDGE == 0) | (lane % EDGE == EDGE - 1)
    even_group, even_place = (lane // EDGE) % 2 == 0, lane % 2 == 0
    y_pairs, z_pairs = [], []
    for h in range(2):
        lanes = slice(h * HALF, (h + 1) * HALF)
        low, high = ghosts[2][:, lanes], turned(ghosts[3][:, lanes], -EDGE)
        y_pairs.append((jnp.where(even_group, low, high), jnp.where(even_group, high, low)))
        low, high = ghosts[4][:, lanes], turned(ghosts[5][:, lanes], EDGE - 1)
        z_pairs.append((jnp.where(even_place, low, high), jnp.where(even_place, high, low)))
    packer = None if last_step else Packer()
    copies = []

    def finished(x, h):
        value = plane_at(partial, x)[h]
        ends = turned(y_pairs[x // GROUPS][x % 2], -EDGE * (x % GROUPS))
        value = value + jnp.where(start_y if h == 0 else end_y, ends, 0.0)
        value = value + jnp.where(ends_z, turned(z_pairs[h][x % 2], -x), 0.0)
        if x == 0:
            value = value + ghosts[0][:, h * HALF : (h + 1) * HALF]
        if x == EDGE - 1:
            value = value + ghosts[1][:, h * HALF : (h + 1) * HALF]
        done[h, pl.ds(x * ROWS, ROWS), :] = value
        return value

    def write(first, halves, number):
        for slot in range(SLOTS):
            for f in range(NFIELD):
                rows = pl.ds(first * ROWS + f * SLOTS + slot, 8, stride=ROWS)
                for h in halves:
                    blocks[slot, f, first : first + 8, h * HALF : (h + 1) * HALF] = done[h, rows, :]
        part = (slice(None), slice(None), pl.ds(first, 8), pl.ds(halves[0] * HALF, len(halves) * HALF))
        copy = pltpu.make_async_copy(blocks.at[part], result.at[part], sent.at[number])
        copy.start()
        copies.append(copy)

    if last_step:
        for number, (first, halves) in enumerate(((0, (0, 1)), (8, (0,)), (8, (1,)))):
            for x in range(first, first + 8):
                for h in halves:
                    finished(x, h)
            write(first, halves, number)
    else:
        for x in range(EDGE):
            packer.add(x, finished(x, 0), finished(x, 1))
    for copy in copies:
        copy.wait()
    if not last_step:
        emit_faces(packer, done, outs, sends)


def spec(space):
    return pl.BlockSpec(memory_space=space)


VECTOR = pltpu.VMEM
SMALL = pltpu.CompilerParams(vmem_limit_bytes=8 << 20)
FLAT = (2, ROWS, PLANE)
TABLES = (STATE, SIDE, SIDE, FLAT, FLAT, FACE, FACE)
TO_DEV = (NFIELD * EDGE, PLANE)
TO_GRP = (NFIELD * EDGE + ROWS, PLANE)


def shaped(shape):
    return jax.ShapeDtypeStruct(shape, jnp.float32)


def cost(flops):
    return pl.CostEstimate(flops=flops, bytes_accessed=min(flops, 2 << 20), transcendentals=0)


def call(kernel, name, shapes, vectors, flops=1 << 20, scratch=()):
    return pl.pallas_call(
        kernel,
        name=name,
        compiler_params=SMALL,
        out_shape=[shaped(shape) for shape in shapes],
        in_specs=[spec(VECTOR)] * len(vectors),
        out_specs=[spec(VECTOR)] * len(shapes),
        scratch_shapes=list(scratch),
        cost_estimate=cost(flops),
    )(*vectors)


def start(fields):
    shapes = (fields.shape, SIDE, SIDE, FLAT, FLAT)
    return pl.pallas_call(
        start_kernel,
        name="start",
        compiler_params=SMALL,
        out_shape=[shaped(shape) for shape in shapes],
        in_specs=[spec(pl.ANY)],
        out_specs=[spec(VECTOR)] * len(shapes),
        scratch_shapes=[pltpu.VMEM(STATE, jnp.float32), pltpu.SemaphoreType.DMA((2,))],
    )(pltpu.with_memory_space_constraint(fields, pltpu.HBM))


def plan(neighbors, orient, sent):
    return pl.pallas_call(
        plan_kernel,
        name="plan",
        compiler_params=SMALL,
        out_shape=[shaped((4, ROWS, HALF)), shaped(SELECT)],
        in_specs=[spec(pltpu.SMEM)] * 2 + [spec(VECTOR)],
        out_specs=[spec(VECTOR)] * 2,
        cost_estimate=cost(1 << 20),
    )(neighbors, orient, sent)


def mask(flag):
    return jnp.broadcast_to(jnp.where(flag == 1, 1.0, 0.0).reshape(1, 1), FACE)


def body(fields, swap_dev, swap_grp, neighbors, orient):
    fields, low, high, faces, faces_dev = start(fields)
    swap_dev, faces = lax.optimization_barrier((swap_dev, faces))
    faces = exchange(faces, "grp", 0)
    faces_dev = exchange(faces_dev, "dev", 0)
    mask_dev = mask(swap_dev)
    to_dev, to_grp = call(block_kernel, "blocks", [TO_DEV, TO_GRP], [mask_dev, fields, low, high], 1 << 24)
    swap_grp, to_grp = lax.optimization_barrier((swap_grp, to_grp))
    mask_grp = mask(swap_grp)
    block_grp = exchange(to_grp, "grp", 0)
    block_dev = exchange(to_dev, "dev", 0)
    new_low, new_high, *sends = call(
        faces_kernel,
        "faces",
        [SIDE, SIDE, SIDE, FLAT, FACE],
        [mask_dev, mask_grp, low, high, faces, faces_dev],
        1 << 24,
    )
    flat_a = exchange(sends[0], "dev", 0)
    flat_b = exchange(sends[1], "dev", 1)
    deep_b = exchange(sends[2], "grp", 1)
    scale, select = plan(neighbors, orient, sends[2])
    partial, deep_a, relayed, z_low, z_high = call(
        first_inner_kernel,
        "inner_0",
        [STATE, FACE, FACE, FACE, FACE],
        [mask_dev, mask_grp, scale, fields, block_dev, block_grp, faces, low, high, new_low, new_high],
        4 << 20,
        [pltpu.VMEM(STATE, jnp.float32)],
    )
    state, *tables = call(
        functools.partial(finish_kernel, False),
        "finish_0",
        TABLES,
        [scale, select, partial, new_low, new_high, flat_a, flat_b, deep_a, deep_b, relayed, z_low, z_high],
    )
    own, sends = tables[:2], tables[2:]
    flat_a = exchange(sends[0], "dev", 0)
    flat_b = exchange(sends[1], "dev", 1)
    deep_a = exchange(sends[2], "grp", 0)
    deep_b = exchange(sends[3], "grp", 1)
    (partial,) = call(inner_kernel, "inner_1", [STATE], [state, scale], 4 << 20)
    return pl.pallas_call(
        functools.partial(finish_kernel, True),
        name="finish_1",
        compiler_params=SMALL,
        out_shape=shaped(fields.shape),
        in_specs=[spec(VECTOR)] * 9,
        out_specs=spec(pl.ANY),
        scratch_shapes=[
            pltpu.VMEM(STATE, jnp.float32),
            pltpu.VMEM(fields.shape, jnp.float32),
            pltpu.SemaphoreType.DMA((3,)),
        ],
    )(scale, select, partial, *own, flat_a, flat_b, deep_a, deep_b)


def solution(mesh):
    in_specs = (
        P(("grp", "dev"), None, None, None),
        P(("grp", "dev")),
        P(("grp", "dev")),
        P(("grp", "dev"), None),
        P(("grp", "dev")),
    )
    out_specs = P(("grp", "dev"), None, None, None)
    return jax.shard_map(body, mesh=mesh, in_specs=in_specs, out_specs=out_specs, check_vma=False)
```

```python
import functools
import math

import jax
import jax.numpy as jnp
from jax import lax
from jax.experimental import pallas as pl
from jax.experimental.pallas import tpu as pltpu
from jax.sharding import PartitionSpec as P

NPHASE = 4
NCONC = 2
NFIELD = NPHASE + NCONC
EDGE = 16
PLANE = EDGE * EDGE
HALF = PLANE // 2
GROUPS = HALF // EDGE
SLOTS = 4
ROWS = NFIELD * SLOTS

phase_rate = 0.05
closure = 0.1
coupling = (0.5, -0.5, 1.0, -1.0)
conc_rates = (0.08, 0.04)

STATE = (2, EDGE * ROWS, HALF)
FACE = (ROWS, PLANE)
SIDE = (3, ROWS, PLANE)
SOURCES = 4
PARTS = 2
SELECT = (3, 2 * ROWS, PARTS * SOURCES * ROWS)


def partners(axis, offset):
    sizes = (lax.axis_size("grp"), lax.axis_size("dev"))
    along = ("grp", "dev").index(axis)
    route = []
    for grp in range(sizes[0]):
        for dev in range(sizes[1]):
            own = (grp, dev)
            partner = list(own)
            partner[along] += 1 if (own[along] - offset) % 2 == 0 else -1
            if not 0 <= partner[along] < sizes[along]:
                if axis == "dev":
                    continue
                partner = [grp, dev ^ 1]
            route.append((grp * sizes[1] + dev, partner[0] * sizes[1] + partner[1]))
    return route


def exchange(block, axis, offset):
    return lax.ppermute(block, ("grp", "dev"), partners(axis, offset))


def iota(shape, dim):
    return lax.broadcasted_iota(jnp.int32, shape, dim)


def plane_at(ref, x):
    rows = pl.ds(x * ROWS, ROWS)
    return ref[0, rows, :], ref[1, rows, :]


def turned(value, shift):
    shift %= HALF
    return pltpu.roll(value, shift, 1) if shift else value


class Packer:
    def __init__(self):
        lane = iota((ROWS, HALF), 1)
        self.lane, self.group, self.place = lane, lane // EDGE, lane % EDGE
        self.y = [[None, None], [None, None]]
        self.z = [[None, None], [None, None]]

    def add(self, x, left, right):
        odd, half, at = x % 2, x // GROUPS, x % GROUPS
        ends = turned(jnp.where(self.lane < EDGE, left, right), EDGE * at)
        taken = (self.group == at) | (self.group == (at + GROUPS - 1) % GROUPS)
        before = self.y[half][odd]
        self.y[half][odd] = ends if before is None else jnp.where(taken, ends, before)
        taken = (self.place == x) | (self.place == (x + EDGE - 1) % EDGE)
        for h, value in enumerate((left, right)):
            moved = turned(value, x)
            before = self.z[h][odd]
            self.z[h][odd] = moved if before is None else jnp.where(taken, moved, before)

    def tables(self, h):
        even_group, even_place = self.group % 2 == 0, self.place % 2 == 0
        (y_even, y_odd), (z_even, z_odd) = self.y[h], self.z[h]
        low = (jnp.where(even_group, y_even, y_odd), jnp.where(even_place, z_even, z_odd))
        y_high, z_high = jnp.where(even_group, y_odd, y_even), jnp.where(even_place, z_odd, z_even)
        return low, (turned(y_high, EDGE), turned(z_high, 1 - EDGE))


def write_tables(packer, state, own):
    low, high = own
    for h in range(2):
        lanes = pl.ds(h * HALF, HALF)
        for ref, x in ((low, 0), (high, EDGE - 1)):
            ref[0, :, lanes] = state[h, pl.ds(x * ROWS, ROWS), :]
        for ref, (y_table, z_table) in zip(own, packer.tables(h)):
            ref[1, :, lanes] = y_table
            ref[2, :, lanes] = z_table


def emit_faces(packer, state, own, sends):
    write_tables(packer, state, own)
    low, high = own
    flat_a, flat_b, deep_a, deep_b = sends
    even = even_place("dev")
    for face in range(2):
        flat_a[face] = jnp.where(even, high[face], low[face])
        flat_b[face] = jnp.where(even, low[face], high[face])
    even = even_place("grp")
    deep_a[...] = jnp.where(even, high[2], low[2])
    deep_b[...] = jnp.where(even, low[2], high[2])


def fill_slot(state, slot, block, first=0, count=EDGE):
    for f in range(NFIELD):
        value = block(f)
        for h in range(2):
            rows = pl.ds(first * ROWS + f * SLOTS + slot, count, stride=ROWS)
            state[h, rows, :] = value[:, h * HALF : (h + 1) * HALF]


def slot_rows():
    return iota(FACE, 0) % SLOTS


def shifted(value, rows):
    rows %= ROWS
    return pltpu.roll(value, rows, 0) if rows else value


def gathered(tables, slot):
    rows = slot_rows()
    out = shifted(tables[0], -slot)
    for number in range(1, len(tables)):
        out = jnp.where(rows == number, shifted(tables[number], number - slot), out)
    return out


def scattered(table, number, slot):
    return shifted(table, slot - number)


def even_place(axis):
    return lax.rem(lax.axis_index(axis), 2) == 0


def block_kernel(mask_dev, fields, low, high, to_dev, to_grp):
    last, size = SLOTS - 1, NFIELD * EDGE
    for f in range(NFIELD):
        to_dev[f * EDGE : (f + 1) * EDGE] = fields[last, f]
        to_grp[f * EDGE : (f + 1) * EDGE] = fields[0, f]
    away = jnp.where(even_place("grp"), low[2], high[2])
    to_grp[size : size + ROWS] = jnp.where(slot_rows() == 0, away, mask_dev[...])


def faces_kernel(mask_dev, mask_grp, low, high, faces, faces_dev, *outs):
    new_low, new_high, flat_a, flat_b, deep_b = outs
    rows, last = slot_rows(), SLOTS - 1
    first_rows = (rows == 0) & (mask_grp[...] > 0.5)
    last_rows = (rows == last) & (mask_dev[...] > 0.5)
    even = even_place("grp")
    got_first, got_last, got_last_z = faces[0], faces_dev[0], faces_dev[1]
    for side, (raw, new) in enumerate(((low, new_low), (high, new_high))):
        for axis in range(2):
            number = 2 * axis + side
            table = jnp.where(first_rows, scattered(got_first, number, 0), raw[axis])
            new[axis] = jnp.where(last_rows, scattered(got_last, number, last), table)
        table = jnp.where(first_rows & (even if side == 0 else ~even), faces[1], raw[2])
        new[2] = jnp.where(last_rows, scattered(got_last_z, side, last), table)
    even_dev = even_place("dev")
    for axis in range(2):
        flat_a[axis] = jnp.where(even_dev, new_high[axis], new_low[axis])
        flat_b[axis] = jnp.where(even_dev, new_low[axis], new_high[axis])
    flat_a[2] = faces[1]
    deep_b[...] = jnp.where(even, new_low[2], new_high[2])


def cos_quarter(number):
    turn = number & 7
    size = jnp.where((turn & 3) == 0, 1.0, jnp.where((turn & 3) == 2, 0.0, math.sqrt(0.5)))
    return jnp.where((turn > 2) & (turn < 6), -size, size)


def plan_kernel(neighbors, orient, scale, select):
    shape = (ROWS, HALF)
    slot, field, column = iota(shape, 0) % SLOTS, iota(shape, 0) // SLOTS, iota(shape, 1)
    grp, dev = lax.axis_index("grp"), lax.axis_index("dev")
    rank = grp * lax.axis_size("dev") + dev

    def by_slot(values):
        rows = values[0]
        for number in range(1, SLOTS):
            rows = jnp.where(slot == number, values[number], rows)
        return rows

    spread = []
    for number in range(SLOTS):
        turn = 0.5 * cos_quarter(orient[number])
        lift = 0.5 * cos_quarter(orient[number] + 6)
        spread.append((1.0 + turn, 1.0 - turn, 1.0 + lift))
    conc = jnp.where(field == NPHASE, conc_rates[0], conc_rates[1])
    weights = [jnp.where(field < NPHASE, phase_rate * by_slot([own[axis] for own in spread]), conc) for axis in range(3)]
    for axis in range(3):
        scale[axis] = weights[axis]
    scale[3] = 1.0 - 2.0 * (weights[0] + weights[1] + weights[2])
    for face in range(6):
        first = []
        came = 2 + lax.rem(lax.rem(dev if face < 4 else grp, 2) + face % 2 + 1, 2)
        for number in range(SLOTS):
            target = neighbors[number, face]
            source = jnp.where(target < 0, face % 2, jnp.where(target // SLOTS == rank, 1 - face % 2, came))
            first.append(source * ROWS + jnp.where(target < 0, number, target & (SLOTS - 1)))
        chosen = jnp.where(column == by_slot(first) + field * SLOTS, 1.0, 0.0)[:, : SOURCES * ROWS]
        rows = pl.ds(face % 2 * ROWS, ROWS)
        for part in range(PARTS):
            select[face // 2, rows, pl.ds(part * SOURCES * ROWS, SOURCES * ROWS)] = chosen


def start_kernel(fields, neighbors, orient, *refs):
    fetched, low, high, faces_grp, faces_dev, scale, select = refs[:7]
    state, near, turn, arrived = refs[7:]
    scalars = ((neighbors, near), (orient, turn))
    parts = [pl.ds(first, EDGE // 2) for first in (0, EDGE // 2)]
    blocks = tuple((fields.at[:, :, part], fetched.at[:, :, part]) for part in parts)
    copies = [pltpu.make_async_copy(*pair, arrived.at[number]) for number, pair in enumerate((*scalars, *blocks))]
    for copy in copies:
        copy.start()
    for copy in copies[: len(scalars)]:
        copy.wait()
    plan_kernel(near, turn, scale, select)
    packer = Packer()
    for number, part in enumerate(parts):
        copies[len(scalars) + number].wait()
        first = number * (EDGE // 2)
        for slot in range(SLOTS):
            fill_slot(state, slot, lambda f: fetched[slot, f, part], first, EDGE // 2)
        for x in range(first, first + EDGE // 2):
            packer.add(x, *plane_at(state, x))
    write_tables(packer, state, (low, high))
    faces_grp[0] = gathered([low[0], high[0], low[1], high[1]], 0)
    faces_grp[1] = jnp.where(even_place("grp"), high[2], low[2])
    faces_dev[0] = gathered([low[0], high[0], low[1], high[1]], SLOTS - 1)
    faces_dev[1] = gathered([low[2], high[2]], SLOTS - 1)


def first_inner_kernel(mask_dev, mask_grp, scale, fields, block_dev, block_grp, faces, low, high, new_low, new_high, *refs):
    partial, got_deep, relayed, z_low, z_high, state = refs
    size = NFIELD * EDGE
    swap_dev, swap_grp = mask_dev[...] > 0.5, mask_grp[...] > 0.5

    def block(slot):
        def of(f):
            value = fields[slot, f]
            if slot == 0:
                value = jnp.where(swap_grp[:EDGE], block_grp[f * EDGE : (f + 1) * EDGE], value)
            if slot == SLOTS - 1:
                value = jnp.where(swap_dev[:EDGE], block_dev[f * EDGE : (f + 1) * EDGE], value)
            return value

        return of

    for slot in range(SLOTS):
        fill_slot(state, slot, block(slot))
    rows, even = slot_rows(), even_place("grp")
    first_rows = (rows == 0) & swap_grp
    got_deep[...] = jnp.where(first_rows, jnp.where(even, low[2], high[2]), faces[1])
    other = block_grp[size : size + ROWS]
    relayed[...] = jnp.where(rows == SLOTS - 1, jnp.broadcast_to(other[1:2], FACE), 0.0)
    z_low[...] = jnp.where(first_rows & ~even, other, new_low[2])
    z_high[...] = jnp.where(first_rows & even, other, new_high[2])
    inner_kernel(state, scale, partial)


def inner_kernel(state, scale, partial):
    lane = iota((ROWS, HALF), 1)
    start_y, end_y = lane < EDGE, lane >= HALF - EDGE
    start_z, end_z = lane % EDGE == 0, lane % EDGE == EDGE - 1
    weight_x, weight_y, weight_z, weight = (scale[number] for number in range(4))
    tile = 2 * SLOTS
    planes = {0: plane_at(state, 0)}
    for x in range(EDGE):
        if x + 1 < EDGE:
            planes[x + 1] = plane_at(state, x + 1)
        left, right = planes[x]
        up = [turned(half, EDGE) for half in (left, right)]
        down = [turned(half, -EDGE) for half in (left, right)]
        sum_y = (
            jnp.where(start_y, 0.0, up[0]) + jnp.where(end_y, down[1], down[0]),
            jnp.where(start_y, up[0], up[1]) + jnp.where(end_y, 0.0, down[1]),
        )
        for h, half in enumerate((left, right)):
            sum_z = jnp.where(start_z, 0.0, turned(half, 1)) + jnp.where(end_z, 0.0, turned(half, -1))
            if x == 0:
                sum_x = planes[1][h]
            elif x == EDGE - 1:
                sum_x = planes[x - 1][h]
            else:
                sum_x = planes[x - 1][h] + planes[x + 1][h]
            flow = weight * half + weight_x * sum_x + weight_y * sum_y[h] + weight_z * sum_z
            phases, conc = (half[:tile], half[tile : 2 * tile]), half[2 * tile :]
            drive = conc - pltpu.roll(conc, SLOTS, 0)
            total = phases[0] + phases[1]
            total = total + pltpu.roll(total, SLOTS, 0)
            tail = (phase_rate * closure) * (1.0 - total)
            rows = x * ROWS
            for number, value in enumerate(phases):
                gain = value * (1.0 - value) * (coupling[2 * number] * drive + (2.0 * value - 1.0))
                part = flow[number * tile : (number + 1) * tile]
                partial[h, pl.ds(rows + number * tile, tile), :] = part + (phase_rate * gain + tail)
            partial[h, pl.ds(rows + 2 * tile, tile), :] = flow[2 * tile :]


def finish_kernel(last_step, scale, select, partial, *refs):
    own, got_flat = refs[0:2], refs[2:4]
    own_deep = [ref[2] for ref in own]
    if last_step:
        got_deep = [ref[...] for ref in refs[4:6]]
        result, done, blocks, sent = refs[6:10]
    else:
        known, deep_b, relayed, z_low, z_high = refs[4:9]
        got_deep = [jnp.where(relayed[...] > 0.5, got_flat[0][2], known[...]), deep_b[...]]
        own_deep = [z_low[...], z_high[...]]
        done, outs, sends = refs[9], refs[10:12], refs[12:16]
    ghosts = []
    for axis in range(3):
        got = [ref[axis] for ref in got_flat] if axis < 2 else got_deep
        mine = [ref[axis] for ref in own] if axis < 2 else own_deep
        tables = jnp.concatenate([*mine, *got], axis=0)
        near = tables.astype(jnp.bfloat16)
        rest = (tables - near.astype(jnp.float32)).astype(jnp.bfloat16)
        both = jnp.concatenate([near, rest], axis=0)
        pair = jnp.dot(select[axis].astype(jnp.bfloat16), both, preferred_element_type=jnp.float32)
        weight = jnp.concatenate([scale[axis]] * 2, axis=1)
        ghosts += [weight * pair[:ROWS], weight * pair[ROWS:]]
    lane = iota((ROWS, HALF), 1)
    start_y, end_y = lane < EDGE, lane >= HALF - EDGE
    ends_z = (lane % EDGE == 0) | (lane % EDGE == EDGE - 1)
    even_group, even_place = (lane // EDGE) % 2 == 0, lane % 2 == 0
    y_pairs, z_pairs = [], []
    for h in range(2):
        lanes = slice(h * HALF, (h + 1) * HALF)
        low, high = ghosts[2][:, lanes], turned(ghosts[3][:, lanes], -EDGE)
        y_pairs.append((jnp.where(even_group, low, high), jnp.where(even_group, high, low)))
        low, high = ghosts[4][:, lanes], turned(ghosts[5][:, lanes], EDGE - 1)
        z_pairs.append((jnp.where(even_place, low, high), jnp.where(even_place, high, low)))
    packer = None if last_step else Packer()
    copies = []
    for x in range(EDGE):
        halves = list(plane_at(partial, x))
        ends = turned(y_pairs[x // GROUPS][x % 2], -EDGE * (x % GROUPS))
        for h in range(2):
            value = halves[h] + jnp.where(start_y if h == 0 else end_y, ends, 0.0)
            value = value + jnp.where(ends_z, turned(z_pairs[h][x % 2], -x), 0.0)
            if x == 0:
                value = value + ghosts[0][:, h * HALF : (h + 1) * HALF]
            if x == EDGE - 1:
                value = value + ghosts[1][:, h * HALF : (h + 1) * HALF]
            done[h, pl.ds(x * ROWS, ROWS), :] = value
            halves[h] = value
        if not last_step:
            packer.add(x, *halves)
        elif x % 8 == 7:
            first = x - 7
            for slot in range(SLOTS):
                for f in range(NFIELD):
                    rows = pl.ds(first * ROWS + f * SLOTS + slot, 8, stride=ROWS)
                    for h in range(2):
                        lanes = pl.ds(h * HALF, HALF)
                        blocks[slot, f, first : first + 8, lanes] = done[h, rows, :]
            part = pl.ds(first, 8)
            copy = pltpu.make_async_copy(blocks.at[:, :, part], result.at[:, :, part], sent.at[x // 8])
            copy.start()
            copies.append(copy)
    for copy in copies:
        copy.wait()
    if not last_step:
        emit_faces(packer, done, outs, sends)


def spec(space):
    return pl.BlockSpec(memory_space=space)


VECTOR = pltpu.VMEM
SMALL = pltpu.CompilerParams(vmem_limit_bytes=8 << 20)
FLAT = (2, ROWS, PLANE)
TABLES = (STATE, SIDE, SIDE, FLAT, FLAT, FACE, FACE)
TO_DEV = (NFIELD * EDGE, PLANE)
TO_GRP = (NFIELD * EDGE + ROWS, PLANE)


def shaped(shape):
    return jax.ShapeDtypeStruct(shape, jnp.float32)


def cost(flops):
    return pl.CostEstimate(flops=flops, bytes_accessed=min(flops, 2 << 20), transcendentals=0)


def call(kernel, name, shapes, vectors, flops=1 << 20, scratch=()):
    return pl.pallas_call(
        kernel,
        name=name,
        compiler_params=SMALL,
        out_shape=[shaped(shape) for shape in shapes],
        in_specs=[spec(VECTOR)] * len(vectors),
        out_specs=[spec(VECTOR)] * len(shapes),
        scratch_shapes=list(scratch),
        cost_estimate=cost(flops),
    )(*vectors)


def start(arguments):
    shapes = (arguments[0].shape, SIDE, SIDE, FLAT, FLAT, (4, ROWS, HALF), SELECT)
    return pl.pallas_call(
        start_kernel,
        name="start",
        compiler_params=SMALL,
        out_shape=[shaped(shape) for shape in shapes],
        in_specs=[spec(pl.ANY)] * len(arguments),
        out_specs=[spec(VECTOR)] * len(shapes),
        scratch_shapes=[
            pltpu.VMEM(STATE, jnp.float32),
            *(pltpu.SMEM(array.shape, jnp.int32) for array in arguments[1:]),
            pltpu.SemaphoreType.DMA((len(arguments) + 1,)),
        ],
    )(*(pltpu.with_memory_space_constraint(array, pltpu.HBM) for array in arguments))


def mask(flag):
    return jnp.broadcast_to(jnp.where(flag == 1, 1.0, 0.0).reshape(1, 1), FACE)


def body(fields, swap_dev, swap_grp, neighbors, orient):
    fields, low, high, faces, faces_dev, scale, select = start((fields, neighbors, orient))
    swap_dev, faces = lax.optimization_barrier((swap_dev, faces))
    faces = exchange(faces, "grp", 0)
    faces_dev = exchange(faces_dev, "dev", 0)
    mask_dev = mask(swap_dev)
    to_dev, to_grp = call(block_kernel, "blocks", [TO_DEV, TO_GRP], [mask_dev, fields, low, high], 1 << 24)
    swap_grp, to_grp = lax.optimization_barrier((swap_grp, to_grp))
    mask_grp = mask(swap_grp)
    block_grp = exchange(to_grp, "grp", 0)
    block_dev = exchange(to_dev, "dev", 0)
    new_low, new_high, *sends = call(
        faces_kernel,
        "faces",
        [SIDE, SIDE, SIDE, FLAT, FACE],
        [mask_dev, mask_grp, low, high, faces, faces_dev],
        1 << 24,
    )
    flat_a = exchange(sends[0], "dev", 0)
    flat_b = exchange(sends[1], "dev", 1)
    deep_b = exchange(sends[2], "grp", 1)
    partial, deep_a, relayed, z_low, z_high = call(
        first_inner_kernel,
        "inner_0",
        [STATE, FACE, FACE, FACE, FACE],
        [mask_dev, mask_grp, scale, fields, block_dev, block_grp, faces, low, high, new_low, new_high],
        4 << 20,
        [pltpu.VMEM(STATE, jnp.float32)],
    )
    state, *tables = call(
        functools.partial(finish_kernel, False),
        "finish_0",
        TABLES,
        [scale, select, partial, new_low, new_high, flat_a, flat_b, deep_a, deep_b, relayed, z_low, z_high],
    )
    own, sends = tables[:2], tables[2:]
    flat_a = exchange(sends[0], "dev", 0)
    flat_b = exchange(sends[1], "dev", 1)
    deep_a = exchange(sends[2], "grp", 0)
    deep_b = exchange(sends[3], "grp", 1)
    (partial,) = call(inner_kernel, "inner_1", [STATE], [state, scale], 4 << 20)
    return pl.pallas_call(
        functools.partial(finish_kernel, True),
        name="finish_1",
        compiler_params=SMALL,
        out_shape=shaped(fields.shape),
        in_specs=[spec(VECTOR)] * 9,
        out_specs=spec(pl.ANY),
        scratch_shapes=[
            pltpu.VMEM(STATE, jnp.float32),
            pltpu.VMEM(fields.shape, jnp.float32),
            pltpu.SemaphoreType.DMA((2,)),
        ],
    )(scale, select, partial, *own, flat_a, flat_b, deep_a, deep_b)


def solution(mesh):
    in_specs = (
        P(("grp", "dev"), None, None, None),
        P(("grp", "dev")),
        P(("grp", "dev")),
        P(("grp", "dev"), None),
        P(("grp", "dev")),
    )
    out_specs = P(("grp", "dev"), None, None, None)
    return jax.shard_map(body, mesh=mesh, in_specs=in_specs, out_specs=out_specs, check_vma=False)
```

```python
import functools
import math

import jax
import jax.numpy as jnp
from jax import lax
from jax.experimental import pallas as pl
from jax.experimental.pallas import tpu as pltpu
from jax.sharding import PartitionSpec as P

NPHASE = 4
NCONC = 2
NFIELD = NPHASE + NCONC
EDGE = 16
PLANE = EDGE * EDGE
HALF = PLANE // 2
GROUPS = HALF // EDGE
SLOTS = 4
ROWS = NFIELD * SLOTS

phase_rate = 0.05
closure = 0.1
coupling = (0.5, -0.5, 1.0, -1.0)
conc_rates = (0.08, 0.04)

STATE = (2, EDGE * ROWS, HALF)
FACE = (ROWS, PLANE)
SIDE = (3, ROWS, PLANE)
SOURCES = 4
PARTS = 2
SELECT = (3, 2 * ROWS, PARTS * SOURCES * ROWS)


def partners(axis, offset):
    sizes = (lax.axis_size("grp"), lax.axis_size("dev"))
    along = ("grp", "dev").index(axis)
    route = []
    for grp in range(sizes[0]):
        for dev in range(sizes[1]):
            own = (grp, dev)
            step = 1 if (own[along] - offset) % 2 == 0 else -1
            partner = list(own)
            partner[along] += step
            if not 0 <= partner[along] < sizes[along]:
                partner = list(own)
                partner[1 - along] ^= 1
                if partner[1 - along] >= sizes[1 - along]:
                    partner = list(own)
            route.append((grp * sizes[1] + dev, partner[0] * sizes[1] + partner[1]))
    return route


def exchange(block, axis, offset):
    return lax.ppermute(block, ("grp", "dev"), partners(axis, offset))


def iota(shape, dim):
    return lax.broadcasted_iota(jnp.int32, shape, dim)


def plane_at(ref, x):
    rows = pl.ds(x * ROWS, ROWS)
    return ref[0, rows, :], ref[1, rows, :]


def turned(value, shift):
    shift %= HALF
    return pltpu.roll(value, shift, 1) if shift else value


class Packer:
    def __init__(self):
        lane = iota((ROWS, HALF), 1)
        self.lane, self.group, self.place = lane, lane // EDGE, lane % EDGE
        self.y = [[None, None], [None, None]]
        self.z = [[None, None], [None, None]]

    def add(self, x, left, right):
        odd, half, at = x % 2, x // GROUPS, x % GROUPS
        ends = turned(jnp.where(self.lane < EDGE, left, right), EDGE * at)
        taken = (self.group == at) | (self.group == (at + GROUPS - 1) % GROUPS)
        before = self.y[half][odd]
        self.y[half][odd] = ends if before is None else jnp.where(taken, ends, before)
        taken = (self.place == x) | (self.place == (x + EDGE - 1) % EDGE)
        for h, value in enumerate((left, right)):
            moved = turned(value, x)
            before = self.z[h][odd]
            self.z[h][odd] = moved if before is None else jnp.where(taken, moved, before)

    def tables(self, h):
        even_group, even_place = self.group % 2 == 0, self.place % 2 == 0
        (y_even, y_odd), (z_even, z_odd) = self.y[h], self.z[h]
        low = (jnp.where(even_group, y_even, y_odd), jnp.where(even_place, z_even, z_odd))
        y_high, z_high = jnp.where(even_group, y_odd, y_even), jnp.where(even_place, z_odd, z_even)
        return low, (turned(y_high, EDGE), turned(z_high, 1 - EDGE))


def write_tables(packer, state, own):
    low, high = own
    for h in range(2):
        lanes = pl.ds(h * HALF, HALF)
        for ref, x in ((low, 0), (high, EDGE - 1)):
            ref[0, :, lanes] = state[h, pl.ds(x * ROWS, ROWS), :]
        for ref, (y_table, z_table) in zip(own, packer.tables(h)):
            ref[1, :, lanes] = y_table
            ref[2, :, lanes] = z_table


def emit_faces(packer, state, own, sends):
    write_tables(packer, state, own)
    low, high = own
    flat_a, flat_b, deep_a, deep_b = sends
    even = even_place("dev")
    for face in range(2):
        flat_a[face] = jnp.where(even, high[face], low[face])
        flat_b[face] = jnp.where(even, low[face], high[face])
    even = even_place("grp")
    deep_a[...] = jnp.where(even, high[2], low[2])
    deep_b[...] = jnp.where(even, low[2], high[2])


def fill_slot(state, slot, block, first=0, count=EDGE):
    for f in range(NFIELD):
        value = block(f)
        for h in range(2):
            rows = pl.ds(first * ROWS + f * SLOTS + slot, count, stride=ROWS)
            state[h, rows, :] = value[:, h * HALF : (h + 1) * HALF]


def slot_rows():
    return iota(FACE, 0) % SLOTS


def shifted(value, rows):
    rows %= ROWS
    return pltpu.roll(value, rows, 0) if rows else value


def gathered(tables, slot):
    rows = slot_rows()
    out = shifted(tables[0], -slot)
    for number in range(1, len(tables)):
        out = jnp.where(rows == number, shifted(tables[number], number - slot), out)
    return out


def scattered(table, number, slot):
    return shifted(table, slot - number)


def even_place(axis):
    return lax.rem(lax.axis_index(axis), 2) == 0


def block_kernel(mask_dev, fields, low, high, to_dev, to_grp):
    last, size = SLOTS - 1, NFIELD * EDGE
    for f in range(NFIELD):
        to_dev[f * EDGE : (f + 1) * EDGE] = fields[last, f]
        to_grp[f * EDGE : (f + 1) * EDGE] = fields[0, f]
    away = jnp.where(even_place("grp"), low[2], high[2])
    to_grp[size : size + ROWS] = jnp.where(slot_rows() == 0, away, mask_dev[...])


def faces_kernel(mask_dev, mask_grp, low, high, faces, faces_dev, *outs):
    new_low, new_high, flat_a, flat_b, deep_b = outs
    rows, last = slot_rows(), SLOTS - 1
    first_rows = (rows == 0) & (mask_grp[...] > 0.5)
    last_rows = (rows == last) & (mask_dev[...] > 0.5)
    even = even_place("grp")
    got_first, got_last, got_last_z = faces[0], faces_dev[0], faces_dev[1]
    for side, (raw, new) in enumerate(((low, new_low), (high, new_high))):
        for axis in range(2):
            number = 2 * axis + side
            table = jnp.where(first_rows, scattered(got_first, number, 0), raw[axis])
            new[axis] = jnp.where(last_rows, scattered(got_last, number, last), table)
        table = jnp.where(first_rows & (even if side == 0 else ~even), faces[1], raw[2])
        new[2] = jnp.where(last_rows, scattered(got_last_z, side, last), table)
    even_dev = even_place("dev")
    for axis in range(2):
        flat_a[axis] = jnp.where(even_dev, new_high[axis], new_low[axis])
        flat_b[axis] = jnp.where(even_dev, new_low[axis], new_high[axis])
    flat_a[2] = faces[1]
    deep_b[...] = jnp.where(even, new_low[2], new_high[2])


def cos_quarter(number):
    turn = number & 7
    size = jnp.where((turn & 3) == 0, 1.0, jnp.where((turn & 3) == 2, 0.0, math.sqrt(0.5)))
    return jnp.where((turn > 2) & (turn < 6), -size, size)


def plan_kernel(neighbors, orient, scale, select):
    shape = (ROWS, HALF)
    slot, field, column = iota(shape, 0) % SLOTS, iota(shape, 0) // SLOTS, iota(shape, 1)
    grp, dev = lax.axis_index("grp"), lax.axis_index("dev")
    rank = grp * lax.axis_size("dev") + dev

    def by_slot(values):
        rows = values[0]
        for number in range(1, SLOTS):
            rows = jnp.where(slot == number, values[number], rows)
        return rows

    spread = []
    for number in range(SLOTS):
        turn = 0.5 * cos_quarter(orient[number])
        lift = 0.5 * cos_quarter(orient[number] + 6)
        spread.append((1.0 + turn, 1.0 - turn, 1.0 + lift))
    conc = jnp.where(field == NPHASE, conc_rates[0], conc_rates[1])
    weights = [jnp.where(field < NPHASE, phase_rate * by_slot([own[axis] for own in spread]), conc) for axis in range(3)]
    for axis in range(3):
        scale[axis] = weights[axis]
    scale[3] = 1.0 - 2.0 * (weights[0] + weights[1] + weights[2])
    for face in range(6):
        first = []
        came = 2 + lax.rem(lax.rem(dev if face < 4 else grp, 2) + face % 2 + 1, 2)
        for number in range(SLOTS):
            target = neighbors[number, face]
            source = jnp.where(target < 0, face % 2, jnp.where(target // SLOTS == rank, 1 - face % 2, came))
            first.append(source * ROWS + jnp.where(target < 0, number, target & (SLOTS - 1)))
        chosen = jnp.where(column == by_slot(first) + field * SLOTS, 1.0, 0.0)[:, : SOURCES * ROWS]
        rows = pl.ds(face % 2 * ROWS, ROWS)
        for part in range(PARTS):
            select[face // 2, rows, pl.ds(part * SOURCES * ROWS, SOURCES * ROWS)] = chosen


def start_kernel(fields, neighbors, orient, *refs):
    fetched, low, high, faces_grp, faces_dev, scale, select = refs[:7]
    state, near, turn, arrived = refs[7:]
    scalars = ((neighbors, near), (orient, turn))
    parts = [pl.ds(first, EDGE // 2) for first in (0, EDGE // 2)]
    blocks = tuple((fields.at[:, :, part], fetched.at[:, :, part]) for part in parts)
    copies = [pltpu.make_async_copy(*pair, arrived.at[number]) for number, pair in enumerate((*scalars, *blocks))]
    for copy in copies:
        copy.start()
    for copy in copies[: len(scalars)]:
        copy.wait()
    plan_kernel(near, turn, scale, select)
    packer = Packer()
    for number, part in enumerate(parts):
        copies[len(scalars) + number].wait()
        first = number * (EDGE // 2)
        for slot in range(SLOTS):
            fill_slot(state, slot, lambda f: fetched[slot, f, part], first, EDGE // 2)
        for x in range(first, first + EDGE // 2):
            packer.add(x, *plane_at(state, x))
    write_tables(packer, state, (low, high))
    faces_grp[0] = gathered([low[0], high[0], low[1], high[1]], 0)
    faces_grp[1] = jnp.where(even_place("grp"), high[2], low[2])
    faces_dev[0] = gathered([low[0], high[0], low[1], high[1]], SLOTS - 1)
    faces_dev[1] = gathered([low[2], high[2]], SLOTS - 1)


def first_inner_kernel(mask_dev, mask_grp, scale, fields, block_dev, block_grp, faces, low, high, new_low, new_high, *refs):
    partial, got_deep, relayed, z_low, z_high, state = refs
    size = NFIELD * EDGE
    swap_dev, swap_grp = mask_dev[...] > 0.5, mask_grp[...] > 0.5

    def block(slot):
        def of(f):
            value = fields[slot, f]
            if slot == 0:
                value = jnp.where(swap_grp[:EDGE], block_grp[f * EDGE : (f + 1) * EDGE], value)
            if slot == SLOTS - 1:
                value = jnp.where(swap_dev[:EDGE], block_dev[f * EDGE : (f + 1) * EDGE], value)
            return value

        return of

    for slot in range(SLOTS):
        fill_slot(state, slot, block(slot))
    rows, even = slot_rows(), even_place("grp")
    first_rows = (rows == 0) & swap_grp
    got_deep[...] = jnp.where(first_rows, jnp.where(even, low[2], high[2]), faces[1])
    other = block_grp[size : size + ROWS]
    relayed[...] = jnp.where(rows == SLOTS - 1, jnp.broadcast_to(other[1:2], FACE), 0.0)
    z_low[...] = jnp.where(first_rows & ~even, other, new_low[2])
    z_high[...] = jnp.where(first_rows & even, other, new_high[2])
    inner_kernel(state, scale, partial)


def inner_kernel(state, scale, partial):
    lane = iota((ROWS, HALF), 1)
    start_y, end_y = lane < EDGE, lane >= HALF - EDGE
    start_z, end_z = lane % EDGE == 0, lane % EDGE == EDGE - 1
    weight_x, weight_y, weight_z, weight = (scale[number] for number in range(4))
    tile = 2 * SLOTS
    planes = {0: plane_at(state, 0)}
    for x in range(EDGE):
        if x + 1 < EDGE:
            planes[x + 1] = plane_at(state, x + 1)
        left, right = planes[x]
        up = [turned(half, EDGE) for half in (left, right)]
        down = [turned(half, -EDGE) for half in (left, right)]
        sum_y = (
            jnp.where(start_y, 0.0, up[0]) + jnp.where(end_y, down[1], down[0]),
            jnp.where(start_y, up[0], up[1]) + jnp.where(end_y, 0.0, down[1]),
        )
        for h, half in enumerate((left, right)):
            sum_z = jnp.where(start_z, 0.0, turned(half, 1)) + jnp.where(end_z, 0.0, turned(half, -1))
            if x == 0:
                sum_x = planes[1][h]
            elif x == EDGE - 1:
                sum_x = planes[x - 1][h]
            else:
                sum_x = planes[x - 1][h] + planes[x + 1][h]
            flow = weight * half + weight_x * sum_x + weight_y * sum_y[h] + weight_z * sum_z
            phases, conc = (half[:tile], half[tile : 2 * tile]), half[2 * tile :]
            drive = conc - pltpu.roll(conc, SLOTS, 0)
            total = phases[0] + phases[1]
            total = total + pltpu.roll(total, SLOTS, 0)
            tail = (phase_rate * closure) * (1.0 - total)
            rows = x * ROWS
            for number, value in enumerate(phases):
                gain = value * (1.0 - value) * (coupling[2 * number] * drive + (2.0 * value - 1.0))
                part = flow[number * tile : (number + 1) * tile]
                partial[h, pl.ds(rows + number * tile, tile), :] = part + (phase_rate * gain + tail)
            partial[h, pl.ds(rows + 2 * tile, tile), :] = flow[2 * tile :]


def ghosts_of(axis, scale, select, tables):
    tables = jnp.concatenate(tables, axis=0)
    near = tables.astype(jnp.bfloat16)
    rest = (tables - near.astype(jnp.float32)).astype(jnp.bfloat16)
    both = jnp.concatenate([near, rest], axis=0)
    pair = jnp.dot(select[axis].astype(jnp.bfloat16), both, preferred_element_type=jnp.float32)
    weight = jnp.concatenate([scale[axis]] * 2, axis=1)
    return weight * pair[:ROWS], weight * pair[ROWS:]


def side_by_side(low, high, even):
    return jnp.where(even, low, high), jnp.where(even, high, low)


def sides_kernel(scale, select, partial, low, high, flat_a, flat_b, done):
    sources = (low, high, flat_a, flat_b)
    x_low, x_high = ghosts_of(0, scale, select, [ref[0] for ref in sources])
    y_low, y_high = ghosts_of(1, scale, select, [ref[1] for ref in sources])
    lane = iota((ROWS, HALF), 1)
    inside = (lane < EDGE, lane >= HALF - EDGE)
    even = (lane // EDGE) % 2 == 0
    pairs = []
    for h in range(2):
        lanes = slice(h * HALF, (h + 1) * HALF)
        pairs.append(side_by_side(y_low[:, lanes], turned(y_high[:, lanes], -EDGE), even))
    for x in range(EDGE):
        ends = turned(pairs[x // GROUPS][x % 2], -EDGE * (x % GROUPS))
        for h, value in enumerate(plane_at(partial, x)):
            value = value + jnp.where(inside[h], ends, 0.0)
            if x == 0:
                value = value + x_low[:, h * HALF : (h + 1) * HALF]
            if x == EDGE - 1:
                value = value + x_high[:, h * HALF : (h + 1) * HALF]
            done[h, pl.ds(x * ROWS, ROWS), :] = value


def finish_kernel(last_step, scale, select, partial, *refs):
    if last_step:
        low, high, deep_a, deep_b = refs[:4]
        tables = [low[2], high[2], deep_a[...], deep_b[...]]
        result, done, blocks, sent = refs[4:8]
    else:
        known, deep_b, flat_a, relayed, z_low, z_high = refs[:6]
        tables = [z_low[...], z_high[...], jnp.where(relayed[...] > 0.5, flat_a[2], known[...]), deep_b[...]]
        done, outs, sends = refs[6], refs[7:9], refs[9:13]
    z_low, z_high = ghosts_of(2, scale, select, tables)
    lane = iota((ROWS, HALF), 1)
    ends_z = (lane % EDGE == 0) | (lane % EDGE == EDGE - 1)
    pairs = []
    for h in range(2):
        lanes = slice(h * HALF, (h + 1) * HALF)
        pairs.append(side_by_side(z_low[:, lanes], turned(z_high[:, lanes], EDGE - 1), lane % 2 == 0))
    packer = None if last_step else Packer()
    copies = []
    for x in range(EDGE):
        halves = []
        for h, value in enumerate(plane_at(partial, x)):
            value = value + jnp.where(ends_z, turned(pairs[h][x % 2], -x), 0.0)
            done[h, pl.ds(x * ROWS, ROWS), :] = value
            halves.append(value)
        if not last_step:
            packer.add(x, *halves)
        elif x % 8 == 7:
            first = x - 7
            for slot in range(SLOTS):
                for f in range(NFIELD):
                    rows = pl.ds(first * ROWS + f * SLOTS + slot, 8, stride=ROWS)
                    for h in range(2):
                        lanes = pl.ds(h * HALF, HALF)
                        blocks[slot, f, first : first + 8, lanes] = done[h, rows, :]
            part = pl.ds(first, 8)
            copy = pltpu.make_async_copy(blocks.at[:, :, part], result.at[:, :, part], sent.at[x // 8])
            copy.start()
            copies.append(copy)
    for copy in copies:
        copy.wait()
    if not last_step:
        emit_faces(packer, done, outs, sends)


def spec(space):
    return pl.BlockSpec(memory_space=space)


VECTOR = pltpu.VMEM
SMALL = pltpu.CompilerParams(vmem_limit_bytes=8 << 20)
FLAT = (2, ROWS, PLANE)
TABLES = (STATE, SIDE, SIDE, FLAT, FLAT, FACE, FACE)
TO_DEV = (NFIELD * EDGE, PLANE)
TO_GRP = (NFIELD * EDGE + ROWS, PLANE)


def shaped(shape):
    return jax.ShapeDtypeStruct(shape, jnp.float32)


def cost(flops):
    return pl.CostEstimate(flops=flops, bytes_accessed=min(flops, 2 << 20), transcendentals=0)


def call(kernel, name, shapes, vectors, flops=1 << 20, scratch=()):
    return pl.pallas_call(
        kernel,
        name=name,
        compiler_params=SMALL,
        out_shape=[shaped(shape) for shape in shapes],
        in_specs=[spec(VECTOR)] * len(vectors),
        out_specs=[spec(VECTOR)] * len(shapes),
        scratch_shapes=list(scratch),
        cost_estimate=cost(flops),
    )(*vectors)


def start(arguments):
    shapes = (arguments[0].shape, SIDE, SIDE, FLAT, FLAT, (4, ROWS, HALF), SELECT)
    return pl.pallas_call(
        start_kernel,
        name="start",
        compiler_params=SMALL,
        out_shape=[shaped(shape) for shape in shapes],
        in_specs=[spec(pl.ANY)] * len(arguments),
        out_specs=[spec(VECTOR)] * len(shapes),
        scratch_shapes=[
            pltpu.VMEM(STATE, jnp.float32),
            *(pltpu.SMEM(array.shape, jnp.int32) for array in arguments[1:]),
            pltpu.SemaphoreType.DMA((len(arguments) + 1,)),
        ],
    )(*(pltpu.with_memory_space_constraint(array, pltpu.HBM) for array in arguments))


def mask(flag):
    return jnp.broadcast_to(jnp.where(flag == 1, 1.0, 0.0).reshape(1, 1), FACE)


def body(fields, swap_dev, swap_grp, neighbors, orient):
    fields, low, high, faces, faces_dev, scale, select = start((fields, neighbors, orient))
    swap_dev, faces = lax.optimization_barrier((swap_dev, faces))
    faces = exchange(faces, "grp", 0)
    faces_dev = exchange(faces_dev, "dev", 0)
    mask_dev = mask(swap_dev)
    to_dev, to_grp = call(block_kernel, "blocks", [TO_DEV, TO_GRP], [mask_dev, fields, low, high], 1 << 24)
    swap_grp, to_grp = lax.optimization_barrier((swap_grp, to_grp))
    mask_grp = mask(swap_grp)
    block_grp = exchange(to_grp, "grp", 0)
    block_dev = exchange(to_dev, "dev", 0)
    new_low, new_high, *sends = call(
        faces_kernel,
        "faces",
        [SIDE, SIDE, SIDE, FLAT, FACE],
        [mask_dev, mask_grp, low, high, faces, faces_dev],
        1 << 24,
    )
    flat_a = exchange(sends[0], "dev", 0)
    flat_b = exchange(sends[1], "dev", 1)
    deep_b = exchange(sends[2], "grp", 1)
    partial, deep_a, relayed, z_low, z_high = call(
        first_inner_kernel,
        "inner_0",
        [STATE, FACE, FACE, FACE, FACE],
        [mask_dev, mask_grp, scale, fields, block_dev, block_grp, faces, low, high, new_low, new_high],
        4 << 20,
        [pltpu.VMEM(STATE, jnp.float32)],
    )
    (partial,) = call(sides_kernel, "sides_0", [STATE], [scale, select, partial, new_low, new_high, flat_a, flat_b])
    state, *tables = call(
        functools.partial(finish_kernel, False),
        "finish_0",
        TABLES,
        [scale, select, partial, deep_a, deep_b, flat_a, relayed, z_low, z_high],
    )
    own, sends = tables[:2], tables[2:]
    flat_a = exchange(sends[0], "dev", 0)
    flat_b = exchange(sends[1], "dev", 1)
    deep_a = exchange(sends[2], "grp", 0)
    deep_b = exchange(sends[3], "grp", 1)
    (partial,) = call(inner_kernel, "inner_1", [STATE], [state, scale], 4 << 20)
    (partial,) = call(sides_kernel, "sides_1", [STATE], [scale, select, partial, *own, flat_a, flat_b])
    return pl.pallas_call(
        functools.partial(finish_kernel, True),
        name="finish_1",
        compiler_params=SMALL,
        out_shape=shaped(fields.shape),
        in_specs=[spec(VECTOR)] * 7,
        out_specs=spec(pl.ANY),
        scratch_shapes=[
            pltpu.VMEM(STATE, jnp.float32),
            pltpu.VMEM(fields.shape, jnp.float32),
            pltpu.SemaphoreType.DMA((2,)),
        ],
    )(scale, select, partial, *own, deep_a, deep_b)


def solution(mesh):
    in_specs = (
        P(("grp", "dev"), None, None, None),
        P(("grp", "dev")),
        P(("grp", "dev")),
        P(("grp", "dev"), None),
        P(("grp", "dev")),
    )
    out_specs = P(("grp", "dev"), None, None, None)
    return jax.shard_map(body, mesh=mesh, in_specs=in_specs, out_specs=out_specs, check_vma=False)
```

```python
import math

import jax
import jax.numpy as jnp
from jax import lax
from jax.experimental import pallas as pl
from jax.experimental.pallas import tpu as pltpu
from jax.sharding import PartitionSpec as P

NPHASE = 4
NCONC = 2
NFIELD = NPHASE + NCONC
EDGE = 16
PLANE = EDGE * EDGE
HALF = PLANE // 2
GROUPS = HALF // EDGE
SLOTS = 4
ROWS = NFIELD * SLOTS

phase_rate = 0.05
closure = 0.1
coupling = (0.5, -0.5, 1.0, -1.0)
conc_rates = (0.08, 0.04)

STATE = (2, EDGE * ROWS, HALF)
SPARE = (2, (EDGE + 1) * ROWS, HALF)
FACE = (ROWS, PLANE)
SIDE = (3, ROWS, PLANE)
SOURCES = 4
PARTS = 2
SELECT = (3, 2 * ROWS, PARTS * SOURCES * ROWS)


def partners(axis, offset):
    sizes = (lax.axis_size("grp"), lax.axis_size("dev"))
    along = ("grp", "dev").index(axis)
    route = []
    for grp in range(sizes[0]):
        for dev in range(sizes[1]):
            own = (grp, dev)
            step = 1 if (own[along] - offset) % 2 == 0 else -1
            partner = list(own)
            partner[along] += step
            if not 0 <= partner[along] < sizes[along]:
                partner = list(own)
                partner[1 - along] ^= 1
                if partner[1 - along] >= sizes[1 - along]:
                    partner = list(own)
            route.append((grp * sizes[1] + dev, partner[0] * sizes[1] + partner[1]))
    return route


def exchange(block, axis, offset):
    return lax.ppermute(block, ("grp", "dev"), partners(axis, offset))


def iota(shape, dim):
    return lax.broadcasted_iota(jnp.int32, shape, dim)


def plane_at(ref, x):
    rows = pl.ds(x * ROWS, ROWS)
    return ref[0, rows, :], ref[1, rows, :]


def turned(value, shift):
    shift %= HALF
    return pltpu.roll(value, shift, 1) if shift else value


class Packer:
    def __init__(self):
        lane = iota((ROWS, HALF), 1)
        self.lane, self.group, self.place = lane, lane // EDGE, lane % EDGE
        self.y = [[None, None], [None, None]]
        self.z = [[None, None], [None, None]]

    def add(self, x, left, right):
        odd, half, at = x % 2, x // GROUPS, x % GROUPS
        ends = turned(jnp.where(self.lane < EDGE, left, right), EDGE * at)
        taken = (self.group == at) | (self.group == (at + GROUPS - 1) % GROUPS)
        before = self.y[half][odd]
        self.y[half][odd] = ends if before is None else jnp.where(taken, ends, before)
        at = EDGE - 1 - x
        odd = at % 2
        taken = (self.place == at) | (self.place == (at + EDGE - 1) % EDGE)
        for h, value in enumerate((left, right)):
            moved = turned(value, at)
            before = self.z[h][odd]
            self.z[h][odd] = moved if before is None else jnp.where(taken, moved, before)

    def tables(self, h):
        even_group, even_place = self.group % 2 == 0, self.place % 2 == 0
        (y_even, y_odd), (z_even, z_odd) = self.y[h], self.z[h]
        low = (jnp.where(even_group, y_even, y_odd), jnp.where(even_place, z_even, z_odd))
        y_high, z_high = jnp.where(even_group, y_odd, y_even), jnp.where(even_place, z_odd, z_even)
        return low, (turned(y_high, EDGE), turned(z_high, 1 - EDGE))


def write_tables(packer, state, own):
    low, high = own
    for h in range(2):
        lanes = pl.ds(h * HALF, HALF)
        for ref, x in ((low, 0), (high, EDGE - 1)):
            ref[0, :, lanes] = state[h, pl.ds(x * ROWS, ROWS), :]
        for ref, (y_table, z_table) in zip(own, packer.tables(h)):
            ref[1, :, lanes] = y_table
            ref[2, :, lanes] = z_table


def emit_faces(packer, state, own, sends):
    write_tables(packer, state, own)
    low, high = own
    flat_a, flat_b, deep_a, deep_b = sends
    even = even_place("dev")
    for face in range(2):
        flat_a[face] = jnp.where(even, high[face], low[face])
        flat_b[face] = jnp.where(even, low[face], high[face])
    even = even_place("grp")
    deep_a[...] = jnp.where(even, high[2], low[2])
    deep_b[...] = jnp.where(even, low[2], high[2])


def fill_slot(state, slot, block, first=0, count=EDGE):
    for f in range(NFIELD):
        value = block(f)
        for h in range(2):
            rows = pl.ds(first * ROWS + f * SLOTS + slot, count, stride=ROWS)
            state[h, rows, :] = value[:, h * HALF : (h + 1) * HALF]


def slot_rows():
    return iota(FACE, 0) % SLOTS


def shifted(value, rows):
    rows %= ROWS
    return pltpu.roll(value, rows, 0) if rows else value


def gathered(tables, slot):
    rows = slot_rows()
    out = shifted(tables[0], -slot)
    for number in range(1, len(tables)):
        out = jnp.where(rows == number, shifted(tables[number], number - slot), out)
    return out


def scattered(table, number, slot):
    return shifted(table, slot - number)


def even_place(axis):
    return lax.rem(lax.axis_index(axis), 2) == 0


def block_kernel(mask_dev, fields, low, high, to_dev, to_grp):
    last, size = SLOTS - 1, NFIELD * EDGE
    for f in range(NFIELD):
        to_dev[f * EDGE : (f + 1) * EDGE] = fields[last, f]
        to_grp[f * EDGE : (f + 1) * EDGE] = fields[0, f]
    away = jnp.where(even_place("grp"), low[2], high[2])
    to_grp[size : size + ROWS] = jnp.where(slot_rows() == 0, away, mask_dev[...])


def faces_kernel(mask_dev, mask_grp, low, high, faces, faces_dev, *outs):
    new_low, new_high, flat_a, flat_b, deep_b = outs
    rows, last = slot_rows(), SLOTS - 1
    first_rows = (rows == 0) & (mask_grp[...] > 0.5)
    last_rows = (rows == last) & (mask_dev[...] > 0.5)
    even = even_place("grp")
    got_first, got_last, got_last_z = faces[0], faces_dev[0], faces_dev[1]
    for side, (raw, new) in enumerate(((low, new_low), (high, new_high))):
        for axis in range(2):
            number = 2 * axis + side
            table = jnp.where(first_rows, scattered(got_first, number, 0), raw[axis])
            new[axis] = jnp.where(last_rows, scattered(got_last, number, last), table)
        table = jnp.where(first_rows & (even if side == 0 else ~even), faces[1], raw[2])
        new[2] = jnp.where(last_rows, scattered(got_last_z, side, last), table)
    even_dev = even_place("dev")
    for axis in range(2):
        flat_a[axis] = jnp.where(even_dev, new_high[axis], new_low[axis])
        flat_b[axis] = jnp.where(even_dev, new_low[axis], new_high[axis])
    flat_a[2] = faces[1]
    deep_b[...] = jnp.where(even, new_low[2], new_high[2])


def cos_quarter(number):
    turn = number & 7
    size = jnp.where((turn & 3) == 0, 1.0, jnp.where((turn & 3) == 2, 0.0, math.sqrt(0.5)))
    return jnp.where((turn > 2) & (turn < 6), -size, size)


def plan_kernel(neighbors, orient, scale, select):
    shape = (ROWS, HALF)
    slot, field, column = iota(shape, 0) % SLOTS, iota(shape, 0) // SLOTS, iota(shape, 1)
    grp, dev = lax.axis_index("grp"), lax.axis_index("dev")
    rank = grp * lax.axis_size("dev") + dev

    def by_slot(values):
        rows = values[0]
        for number in range(1, SLOTS):
            rows = jnp.where(slot == number, values[number], rows)
        return rows

    spread = []
    for number in range(SLOTS):
        turn = 0.5 * cos_quarter(orient[number])
        lift = 0.5 * cos_quarter(orient[number] + 6)
        spread.append((1.0 + turn, 1.0 - turn, 1.0 + lift))
    conc = jnp.where(field == NPHASE, conc_rates[0], conc_rates[1])
    weights = [jnp.where(field < NPHASE, phase_rate * by_slot([own[axis] for own in spread]), conc) for axis in range(3)]
    for axis in range(3):
        scale[axis] = weights[axis]
    scale[3] = 1.0 - 2.0 * (weights[0] + weights[1] + weights[2])
    for face in range(6):
        first = []
        came = 2 + lax.rem(lax.rem(dev if face < 4 else grp, 2) + face % 2 + 1, 2)
        for number in range(SLOTS):
            target = neighbors[number, face]
            source = jnp.where(target < 0, face % 2, jnp.where(target // SLOTS == rank, 1 - face % 2, came))
            first.append(source * ROWS + jnp.where(target < 0, number, target & (SLOTS - 1)))
        chosen = jnp.where(column == by_slot(first) + field * SLOTS, 1.0, 0.0)[:, : SOURCES * ROWS]
        rows = pl.ds(face % 2 * ROWS, ROWS)
        for part in range(PARTS):
            select[face // 2, rows, pl.ds(part * SOURCES * ROWS, SOURCES * ROWS)] = chosen


def start_kernel(fields, neighbors, orient, *refs):
    fetched, low, high, faces_grp, faces_dev, scale, select = refs[:7]
    state, near, turn, arrived = refs[7:]
    scalars = ((neighbors, near), (orient, turn))
    parts = [pl.ds(first, EDGE // 2) for first in (0, EDGE // 2)]
    blocks = tuple((fields.at[:, :, part], fetched.at[:, :, part]) for part in parts)
    copies = [pltpu.make_async_copy(*pair, arrived.at[number]) for number, pair in enumerate((*scalars, *blocks))]
    for copy in copies:
        copy.start()
    for copy in copies[: len(scalars)]:
        copy.wait()
    plan_kernel(near, turn, scale, select)
    packer = Packer()
    for number, part in enumerate(parts):
        copies[len(scalars) + number].wait()
        first = number * (EDGE // 2)
        for slot in range(SLOTS):
            fill_slot(state, slot, lambda f: fetched[slot, f, part], first, EDGE // 2)
        for x in range(first, first + EDGE // 2):
            packer.add(x, *plane_at(state, x))
    write_tables(packer, state, (low, high))
    faces_grp[0] = gathered([low[0], high[0], low[1], high[1]], 0)
    faces_grp[1] = jnp.where(even_place("grp"), high[2], low[2])
    faces_dev[0] = gathered([low[0], high[0], low[1], high[1]], SLOTS - 1)
    faces_dev[1] = gathered([low[2], high[2]], SLOTS - 1)


def first_inner_kernel(mask_dev, mask_grp, scale, fields, block_dev, block_grp, faces, low, high, new_low, new_high, *refs):
    partial, got_deep, relayed, z_low, z_high, state = refs
    size = NFIELD * EDGE
    swap_dev, swap_grp = mask_dev[...] > 0.5, mask_grp[...] > 0.5

    def block(slot):
        def of(f):
            value = fields[slot, f]
            if slot == 0:
                value = jnp.where(swap_grp[:EDGE], block_grp[f * EDGE : (f + 1) * EDGE], value)
            if slot == SLOTS - 1:
                value = jnp.where(swap_dev[:EDGE], block_dev[f * EDGE : (f + 1) * EDGE], value)
            return value

        return of

    for slot in range(SLOTS):
        fill_slot(state, slot, block(slot))
    rows, even = slot_rows(), even_place("grp")
    first_rows = (rows == 0) & swap_grp
    got_deep[...] = jnp.where(first_rows, jnp.where(even, low[2], high[2]), faces[1])
    other = block_grp[size : size + ROWS]
    relayed[...] = jnp.where(rows == SLOTS - 1, jnp.broadcast_to(other[1:2], FACE), 0.0)
    z_low[...] = jnp.where(first_rows & ~even, other, new_low[2])
    z_high[...] = jnp.where(first_rows & even, other, new_high[2])
    inner_kernel(state, scale, partial)


def inner_kernel(state, scale, partial):
    lane = iota((ROWS, HALF), 1)
    start_y, end_y = lane < EDGE, lane >= HALF - EDGE
    start_z, end_z = lane % EDGE == 0, lane % EDGE == EDGE - 1
    weight_x, weight_y, weight_z, weight = (scale[number] for number in range(4))
    tile = 2 * SLOTS
    planes = {0: plane_at(state, 0)}
    for x in range(EDGE):
        if x + 1 < EDGE:
            planes[x + 1] = plane_at(state, x + 1)
        left, right = planes[x]
        up = [turned(half, EDGE) for half in (left, right)]
        down = [turned(half, -EDGE) for half in (left, right)]
        sum_y = (
            jnp.where(start_y, 0.0, up[0]) + jnp.where(end_y, down[1], down[0]),
            jnp.where(start_y, up[0], up[1]) + jnp.where(end_y, 0.0, down[1]),
        )
        for h, half in enumerate((left, right)):
            sum_z = jnp.where(start_z, 0.0, turned(half, 1)) + jnp.where(end_z, 0.0, turned(half, -1))
            if x == 0:
                sum_x = planes[1][h]
            elif x == EDGE - 1:
                sum_x = planes[x - 1][h]
            else:
                sum_x = planes[x - 1][h] + planes[x + 1][h]
            flow = weight * half + weight_x * sum_x + weight_y * sum_y[h] + weight_z * sum_z
            phases, conc = (half[:tile], half[tile : 2 * tile]), half[2 * tile :]
            drive = conc - pltpu.roll(conc, SLOTS, 0)
            total = phases[0] + phases[1]
            total = total + pltpu.roll(total, SLOTS, 0)
            tail = (phase_rate * closure) * (1.0 - total)
            rows = x * ROWS
            for number, value in enumerate(phases):
                gain = value * (1.0 - value) * (coupling[2 * number] * drive + (2.0 * value - 1.0))
                part = flow[number * tile : (number + 1) * tile]
                partial[h, pl.ds(rows + number * tile, tile), :] = part + (phase_rate * gain + tail)
            partial[h, pl.ds(rows + 2 * tile, tile), :] = flow[2 * tile :]


def ghosts_of(axis, scale, select, tables):
    tables = jnp.concatenate(tables, axis=0)
    near = tables.astype(jnp.bfloat16)
    rest = (tables - near.astype(jnp.float32)).astype(jnp.bfloat16)
    both = jnp.concatenate([near, rest], axis=0)
    pair = jnp.dot(select[axis].astype(jnp.bfloat16), both, preferred_element_type=jnp.float32)
    weight = jnp.concatenate([scale[axis]] * 2, axis=1)
    return weight * pair[:ROWS], weight * pair[ROWS:]


def side_by_side(low, high, even):
    return jnp.where(even, low, high), jnp.where(even, high, low)


def sides_kernel(scale, select, partial, low, high, flat_a, flat_b, done, blocks=None):
    if blocks is not None:
        blocks, done = done, blocks
    sources = (low, high, flat_a, flat_b)
    x_low, x_high = ghosts_of(0, scale, select, [ref[0] for ref in sources])
    y_low, y_high = ghosts_of(1, scale, select, [ref[1] for ref in sources])
    lane = iota((ROWS, HALF), 1)
    inside = (lane < EDGE, lane >= HALF - EDGE)
    even = (lane // EDGE) % 2 == 0
    pairs = []
    for h in range(2):
        lanes = slice(h * HALF, (h + 1) * HALF)
        pairs.append(side_by_side(y_low[:, lanes], turned(y_high[:, lanes], -EDGE), even))
    for x in range(EDGE):
        ends = turned(pairs[x // GROUPS][x % 2], -EDGE * (x % GROUPS))
        for h, value in enumerate(plane_at(partial, x)):
            value = value + jnp.where(inside[h], ends, 0.0)
            if x == 0:
                value = value + x_low[:, h * HALF : (h + 1) * HALF]
            if x == EDGE - 1:
                value = value + x_high[:, h * HALF : (h + 1) * HALF]
            done[h, pl.ds(x * ROWS, ROWS), :] = value
    if blocks is not None:
        for slot in range(SLOTS):
            for f in range(NFIELD):
                for h in range(2):
                    rows = pl.ds(f * SLOTS + slot, EDGE, stride=ROWS)
                    blocks[slot, f, :, h * HALF : (h + 1) * HALF] = done[h, rows, :]


def z_pairs(scale, select, tables):
    z_low, z_high = ghosts_of(2, scale, select, tables)
    even = iota((ROWS, HALF), 1) % 2 == 0
    halves = [slice(h * HALF, (h + 1) * HALF) for h in range(2)]
    return [side_by_side(z_low[:, lanes], turned(z_high[:, lanes], EDGE - 1), even) for lanes in halves]


def ends_of(shape):
    place = iota(shape, 1) % EDGE
    return (place == 0) | (place == EDGE - 1)


def finish_kernel(scale, select, partial, known, deep_b, flat_a, relayed, z_low, z_high, done, *outs):
    deep_a = jnp.where(relayed[...] > 0.5, flat_a[2], known[...])
    pairs = z_pairs(scale, select, [z_low[...], z_high[...], deep_a, deep_b[...]])
    ends = ends_of((ROWS, HALF))
    packer = Packer()
    for x in range(EDGE):
        halves, at = [], EDGE - 1 - x
        for h, value in enumerate(plane_at(partial, x)):
            value = value + jnp.where(ends, turned(pairs[h][at % 2], -at), 0.0)
            done[h, pl.ds(x * ROWS, ROWS), :] = value
            halves.append(value)
        packer.add(x, *halves)
    emit_faces(packer, done, outs[0:2], outs[2:6])


def last_kernel(scale, select, partial, low, high, deep_a, deep_b, result, rows_of, blocks, sent):
    for h, pair in enumerate(z_pairs(scale, select, [low[2], high[2], deep_a[...], deep_b[...]])):
        for odd in range(2):
            rows_of[h, odd] = pair[odd]
    shape = (EDGE, HALF)
    ends, even = ends_of(shape), iota(shape, 0) % 2 == 0
    copies = []
    for slot in range(SLOTS):
        for f in range(NFIELD):
            row = pl.ds(f * SLOTS + slot, 1)
            for h in range(2):
                both = [jnp.broadcast_to(rows_of[h, odd, row, :], shape) for odd in (1, 0)]
                ghost = pltpu.roll(jnp.where(even, *both), HALF - EDGE + 1, 1, stride=1, stride_axis=0)
                lanes = pl.ds(h * HALF, HALF)
                blocks[slot, f, :, lanes] = partial[slot, f, :, lanes] + jnp.where(ends, ghost, 0.0)
        copy = pltpu.make_async_copy(blocks.at[slot], result.at[slot], sent.at[slot])
        copy.start()
        copies.append(copy)
    for copy in copies:
        copy.wait()


def spec(space):
    return pl.BlockSpec(memory_space=space)


VECTOR = pltpu.VMEM
SMALL = pltpu.CompilerParams(vmem_limit_bytes=8 << 20)
FLAT = (2, ROWS, PLANE)
TABLES = (STATE, SIDE, SIDE, FLAT, FLAT, FACE, FACE)
TO_DEV = (NFIELD * EDGE, PLANE)
TO_GRP = (NFIELD * EDGE + ROWS, PLANE)


def shaped(shape):
    return jax.ShapeDtypeStruct(shape, jnp.float32)


def cost(flops):
    return pl.CostEstimate(flops=flops, bytes_accessed=min(flops, 2 << 20), transcendentals=0)


def call(kernel, name, shapes, vectors, flops=1 << 20, scratch=()):
    return pl.pallas_call(
        kernel,
        name=name,
        compiler_params=SMALL,
        out_shape=[shaped(shape) for shape in shapes],
        in_specs=[spec(VECTOR)] * len(vectors),
        out_specs=[spec(VECTOR)] * len(shapes),
        scratch_shapes=list(scratch),
        cost_estimate=cost(flops),
    )(*vectors)


def start(arguments):
    shapes = (arguments[0].shape, SIDE, SIDE, FLAT, FLAT, (4, ROWS, HALF), SELECT)
    return pl.pallas_call(
        start_kernel,
        name="start",
        compiler_params=SMALL,
        out_shape=[shaped(shape) for shape in shapes],
        in_specs=[spec(pl.ANY)] * len(arguments),
        out_specs=[spec(VECTOR)] * len(shapes),
        scratch_shapes=[
            pltpu.VMEM(SPARE, jnp.float32),
            *(pltpu.SMEM(array.shape, jnp.int32) for array in arguments[1:]),
            pltpu.SemaphoreType.DMA((len(arguments) + 1,)),
        ],
    )(*(pltpu.with_memory_space_constraint(array, pltpu.HBM) for array in arguments))


def mask(flag):
    return jnp.broadcast_to(jnp.where(flag == 1, 1.0, 0.0).reshape(1, 1), FACE)


def body(fields, swap_dev, swap_grp, neighbors, orient):
    fields, low, high, faces, faces_dev, scale, select = start((fields, neighbors, orient))
    swap_dev, faces = lax.optimization_barrier((swap_dev, faces))
    faces = exchange(faces, "grp", 0)
    faces_dev = exchange(faces_dev, "dev", 0)
    mask_dev = mask(swap_dev)
    to_dev, to_grp = call(block_kernel, "blocks", [TO_DEV, TO_GRP], [mask_dev, fields, low, high], 1 << 24)
    swap_grp, to_grp = lax.optimization_barrier((swap_grp, to_grp))
    mask_grp = mask(swap_grp)
    block_grp = exchange(to_grp, "grp", 0)
    block_dev = exchange(to_dev, "dev", 0)
    new_low, new_high, *sends = call(
        faces_kernel,
        "faces",
        [SIDE, SIDE, SIDE, FLAT, FACE],
        [mask_dev, mask_grp, low, high, faces, faces_dev],
        1 << 24,
    )
    flat_a = exchange(sends[0], "dev", 0)
    flat_b = exchange(sends[1], "dev", 1)
    deep_b = exchange(sends[2], "grp", 1)
    partial, deep_a, relayed, z_low, z_high = call(
        first_inner_kernel,
        "inner_0",
        [STATE, FACE, FACE, FACE, FACE],
        [mask_dev, mask_grp, scale, fields, block_dev, block_grp, faces, low, high, new_low, new_high],
        4 << 20,
        [pltpu.VMEM(SPARE, jnp.float32)],
    )
    (partial,) = call(sides_kernel, "sides_0", [STATE], [scale, select, partial, new_low, new_high, flat_a, flat_b])
    state, *tables = call(
        finish_kernel,
        "finish_0",
        TABLES,
        [scale, select, partial, deep_a, deep_b, flat_a, relayed, z_low, z_high],
    )
    own, sends = tables[:2], tables[2:]
    flat_a = exchange(sends[0], "dev", 0)
    flat_b = exchange(sends[1], "dev", 1)
    deep_a = exchange(sends[2], "grp", 0)
    deep_b = exchange(sends[3], "grp", 1)
    (partial,) = call(inner_kernel, "inner_1", [STATE], [state, scale], 4 << 20)
    blocks, _ = call(sides_kernel, "sides_1", [fields.shape, SPARE], [scale, select, partial, *own, flat_a, flat_b])
    return pl.pallas_call(
        last_kernel,
        name="finish_1",
        compiler_params=SMALL,
        out_shape=shaped(fields.shape),
        in_specs=[spec(VECTOR)] * 7,
        out_specs=spec(pl.ANY),
        scratch_shapes=[
            pltpu.VMEM((2, 2, ROWS, HALF), jnp.float32),
            pltpu.VMEM(fields.shape, jnp.float32),
            pltpu.SemaphoreType.DMA((SLOTS,)),
        ],
    )(scale, select, blocks, *own, deep_a, deep_b)


def solution(mesh):
    in_specs = (
        P(("grp", "dev"), None, None, None),
        P(("grp", "dev")),
        P(("grp", "dev")),
        P(("grp", "dev"), None),
        P(("grp", "dev")),
    )
    out_specs = P(("grp", "dev"), None, None, None)
    return jax.shard_map(body, mesh=mesh, in_specs=in_specs, out_specs=out_specs, check_vma=False)
```

```python
import math

import jax
import jax.numpy as jnp
from jax import lax
from jax.experimental import pallas as pl
from jax.experimental.pallas import tpu as pltpu
from jax.sharding import PartitionSpec as P

NPHASE = 4
NCONC = 2
NFIELD = NPHASE + NCONC
EDGE = 16
PLANE = EDGE * EDGE
HALF = PLANE // 2
GROUPS = HALF // EDGE
SLOTS = 4
ROWS = NFIELD * SLOTS

phase_rate = 0.05
closure = 0.1
coupling = (0.5, -0.5, 1.0, -1.0)
conc_rates = (0.08, 0.04)

STATE = (2, EDGE * ROWS, HALF)
SPARE = (2, (EDGE + 1) * ROWS, HALF)
FACE = (ROWS, PLANE)
SIDE = (3, ROWS, PLANE)
SOURCES = 4
PARTS = 2
SELECT = (3, 2 * ROWS, PARTS * SOURCES * ROWS)


def partners(axis, offset):
    sizes = (lax.axis_size("grp"), lax.axis_size("dev"))
    along = ("grp", "dev").index(axis)
    route = []
    for grp in range(sizes[0]):
        for dev in range(sizes[1]):
            own = (grp, dev)
            step = 1 if (own[along] - offset) % 2 == 0 else -1
            partner = list(own)
            partner[along] += step
            if not 0 <= partner[along] < sizes[along]:
                partner = list(own)
                partner[1 - along] ^= 1
                if partner[1 - along] >= sizes[1 - along]:
                    partner = list(own)
            route.append((grp * sizes[1] + dev, partner[0] * sizes[1] + partner[1]))
    return route


def exchange(block, axis, offset):
    return lax.ppermute(block, ("grp", "dev"), partners(axis, offset))


def iota(shape, dim):
    return lax.broadcasted_iota(jnp.int32, shape, dim)


def plane_at(ref, x):
    rows = pl.ds(x * ROWS, ROWS)
    return ref[0, rows, :], ref[1, rows, :]


def turned(value, shift):
    shift %= HALF
    return pltpu.roll(value, shift, 1) if shift else value


class Packer:
    def __init__(self):
        lane = iota((ROWS, HALF), 1)
        self.lane, self.group, self.place = lane, lane // EDGE, lane % EDGE
        self.y = [[None, None], [None, None]]
        self.z = [[None, None], [None, None]]

    def add(self, x, left, right):
        odd, half, at = x % 2, x // GROUPS, x % GROUPS
        ends = turned(jnp.where(self.lane < EDGE, left, right), EDGE * at)
        taken = (self.group == at) | (self.group == (at + GROUPS - 1) % GROUPS)
        before = self.y[half][odd]
        self.y[half][odd] = ends if before is None else jnp.where(taken, ends, before)
        at = EDGE - 1 - x
        odd = at % 2
        taken = (self.place == at) | (self.place == (at + EDGE - 1) % EDGE)
        for h, value in enumerate((left, right)):
            moved = turned(value, at)
            before = self.z[h][odd]
            self.z[h][odd] = moved if before is None else jnp.where(taken, moved, before)

    def tables(self, h):
        even_group, even_place = self.group % 2 == 0, self.place % 2 == 0
        (y_even, y_odd), (z_even, z_odd) = self.y[h], self.z[h]
        low = (jnp.where(even_group, y_even, y_odd), jnp.where(even_place, z_even, z_odd))
        y_high, z_high = jnp.where(even_group, y_odd, y_even), jnp.where(even_place, z_odd, z_even)
        return low, (turned(y_high, EDGE), turned(z_high, 1 - EDGE))


def write_tables(packer, state, own):
    low, high = own
    for h in range(2):
        lanes = pl.ds(h * HALF, HALF)
        for ref, x in ((low, 0), (high, EDGE - 1)):
            ref[0, :, lanes] = state[h, pl.ds(x * ROWS, ROWS), :]
        for ref, (y_table, z_table) in zip(own, packer.tables(h)):
            ref[1, :, lanes] = y_table
            ref[2, :, lanes] = z_table


def emit_faces(packer, state, own, sends):
    write_tables(packer, state, own)
    low, high = own
    flat_a, flat_b, deep_a, deep_b = sends
    even = even_place("dev")
    for face in range(2):
        flat_a[face] = jnp.where(even, high[face], low[face])
        flat_b[face] = jnp.where(even, low[face], high[face])
    even = even_place("grp")
    deep_a[...] = jnp.where(even, high[2], low[2])
    deep_b[...] = jnp.where(even, low[2], high[2])


def fill_slot(state, slot, block, first=0, count=EDGE):
    for f in range(NFIELD):
        value = block(f)
        for h in range(2):
            rows = pl.ds(first * ROWS + f * SLOTS + slot, count, stride=ROWS)
            state[h, rows, :] = value[:, h * HALF : (h + 1) * HALF]


def slot_rows():
    return iota(FACE, 0) % SLOTS


def shifted(value, rows):
    rows %= ROWS
    return pltpu.roll(value, rows, 0) if rows else value


def gathered(tables, slot):
    rows = slot_rows()
    out = shifted(tables[0], -slot)
    for number in range(1, len(tables)):
        out = jnp.where(rows == number, shifted(tables[number], number - slot), out)
    return out


def scattered(table, number, slot):
    return shifted(table, slot - number)


def even_place(axis):
    return lax.rem(lax.axis_index(axis), 2) == 0


def block_kernel(mask_dev, fields, low, high, to_dev, to_grp):
    last, size = SLOTS - 1, NFIELD * EDGE
    for f in range(NFIELD):
        to_dev[f * EDGE : (f + 1) * EDGE] = fields[last, f]
        to_grp[f * EDGE : (f + 1) * EDGE] = fields[0, f]
    away = jnp.where(even_place("grp"), low[2], high[2])
    to_grp[size : size + ROWS] = jnp.where(slot_rows() == 0, away, mask_dev[...])


def faces_kernel(mask_dev, mask_grp, low, high, faces, faces_dev, *outs):
    new_low, new_high, flat_a, flat_b, deep_b = outs
    rows, last = slot_rows(), SLOTS - 1
    first_rows = (rows == 0) & (mask_grp[...] > 0.5)
    last_rows = (rows == last) & (mask_dev[...] > 0.5)
    even = even_place("grp")
    got_first, got_last, got_last_z = faces[0], faces_dev[0], faces_dev[1]
    for side, (raw, new) in enumerate(((low, new_low), (high, new_high))):
        for axis in range(2):
            number = 2 * axis + side
            table = jnp.where(first_rows, scattered(got_first, number, 0), raw[axis])
            new[axis] = jnp.where(last_rows, scattered(got_last, number, last), table)
        table = jnp.where(first_rows & (even if side == 0 else ~even), faces[1], raw[2])
        new[2] = jnp.where(last_rows, scattered(got_last_z, side, last), table)
    even_dev = even_place("dev")
    for axis in range(2):
        flat_a[axis] = jnp.where(even_dev, new_high[axis], new_low[axis])
        flat_b[axis] = jnp.where(even_dev, new_low[axis], new_high[axis])
    flat_a[2] = faces[1]
    deep_b[...] = jnp.where(even, new_low[2], new_high[2])


def cos_quarter(number):
    turn = number & 7
    size = jnp.where((turn & 3) == 0, 1.0, jnp.where((turn & 3) == 2, 0.0, math.sqrt(0.5)))
    return jnp.where((turn > 2) & (turn < 6), -size, size)


def plan_kernel(neighbors, orient, scale, select):
    shape = (ROWS, HALF)
    slot, field, column = iota(shape, 0) % SLOTS, iota(shape, 0) // SLOTS, iota(shape, 1)
    grp, dev = lax.axis_index("grp"), lax.axis_index("dev")
    rank = grp * lax.axis_size("dev") + dev

    def by_slot(values):
        rows = values[0]
        for number in range(1, SLOTS):
            rows = jnp.where(slot == number, values[number], rows)
        return rows

    spread = []
    for number in range(SLOTS):
        turn = 0.5 * cos_quarter(orient[number])
        lift = 0.5 * cos_quarter(orient[number] + 6)
        spread.append((1.0 + turn, 1.0 - turn, 1.0 + lift))
    conc = jnp.where(field == NPHASE, conc_rates[0], conc_rates[1])
    weights = [jnp.where(field < NPHASE, phase_rate * by_slot([own[axis] for own in spread]), conc) for axis in range(3)]
    for axis in range(3):
        scale[axis] = weights[axis]
    scale[3] = 1.0 - 2.0 * (weights[0] + weights[1] + weights[2])
    for face in range(6):
        first = []
        came = 2 + lax.rem(lax.rem(dev if face < 4 else grp, 2) + face % 2 + 1, 2)
        for number in range(SLOTS):
            target = neighbors[number, face]
            source = jnp.where(target < 0, face % 2, jnp.where(target // SLOTS == rank, 1 - face % 2, came))
            first.append(source * ROWS + jnp.where(target < 0, number, target & (SLOTS - 1)))
        chosen = jnp.where(column == by_slot(first) + field * SLOTS, 1.0, 0.0)[:, : SOURCES * ROWS]
        rows = pl.ds(face % 2 * ROWS, ROWS)
        for part in range(PARTS):
            select[face // 2, rows, pl.ds(part * SOURCES * ROWS, SOURCES * ROWS)] = chosen


def start_kernel(fields, neighbors, orient, *refs):
    fetched, low, high, faces_grp, faces_dev, scale, select = refs[:7]
    state, near, turn, arrived = refs[7:]
    scalars = ((neighbors, near), (orient, turn))
    parts = [pl.ds(first, EDGE // 2) for first in (0, EDGE // 2)]
    blocks = tuple((fields.at[:, :, part], fetched.at[:, :, part]) for part in parts)
    copies = [pltpu.make_async_copy(*pair, arrived.at[number]) for number, pair in enumerate((*scalars, *blocks))]
    for copy in copies:
        copy.start()
    for copy in copies[: len(scalars)]:
        copy.wait()
    plan_kernel(near, turn, scale, select)
    packer = Packer()
    for number, part in enumerate(parts):
        copies[len(scalars) + number].wait()
        first = number * (EDGE // 2)
        for slot in range(SLOTS):
            fill_slot(state, slot, lambda f: fetched[slot, f, part], first, EDGE // 2)
        for x in range(first, first + EDGE // 2):
            packer.add(x, *plane_at(state, x))
    write_tables(packer, state, (low, high))
    faces_grp[0] = gathered([low[0], high[0], low[1], high[1]], 0)
    faces_grp[1] = jnp.where(even_place("grp"), high[2], low[2])
    faces_dev[0] = gathered([low[0], high[0], low[1], high[1]], SLOTS - 1)
    faces_dev[1] = gathered([low[2], high[2]], SLOTS - 1)


def first_inner_kernel(mask_dev, mask_grp, scale, fields, block_dev, block_grp, faces, low, high, new_low, new_high, *refs):
    partial, got_deep, relayed, z_low, z_high, state = refs
    size = NFIELD * EDGE
    swap_dev, swap_grp = mask_dev[...] > 0.5, mask_grp[...] > 0.5

    def block(slot):
        def of(f):
            value = fields[slot, f]
            if slot == 0:
                value = jnp.where(swap_grp[:EDGE], block_grp[f * EDGE : (f + 1) * EDGE], value)
            if slot == SLOTS - 1:
                value = jnp.where(swap_dev[:EDGE], block_dev[f * EDGE : (f + 1) * EDGE], value)
            return value

        return of

    for slot in range(SLOTS):
        fill_slot(state, slot, block(slot))
    rows, even = slot_rows(), even_place("grp")
    first_rows = (rows == 0) & swap_grp
    got_deep[...] = jnp.where(first_rows, jnp.where(even, low[2], high[2]), faces[1])
    other = block_grp[size : size + ROWS]
    relayed[...] = jnp.where(rows == SLOTS - 1, jnp.broadcast_to(other[1:2], FACE), 0.0)
    z_low[...] = jnp.where(first_rows & ~even, other, new_low[2])
    z_high[...] = jnp.where(first_rows & even, other, new_high[2])
    inner_kernel(state, scale, partial)


def inner_kernel(state, scale, partial):
    lane = iota((ROWS, HALF), 1)
    start_y, end_y = lane < EDGE, lane >= HALF - EDGE
    start_z, end_z = lane % EDGE == 0, lane % EDGE == EDGE - 1
    weight_x, weight_y, weight_z, weight = (scale[number] for number in range(4))
    tile = 2 * SLOTS
    planes = {0: plane_at(state, 0)}
    for x in range(EDGE):
        if x + 1 < EDGE:
            planes[x + 1] = plane_at(state, x + 1)
        left, right = planes[x]
        up = [turned(half, EDGE) for half in (left, right)]
        down = [turned(half, -EDGE) for half in (left, right)]
        sum_y = (
            jnp.where(start_y, 0.0, up[0]) + jnp.where(end_y, down[1], down[0]),
            jnp.where(start_y, up[0], up[1]) + jnp.where(end_y, 0.0, down[1]),
        )
        for h, half in enumerate((left, right)):
            sum_z = jnp.where(start_z, 0.0, turned(half, 1)) + jnp.where(end_z, 0.0, turned(half, -1))
            if x == 0:
                sum_x = planes[1][h]
            elif x == EDGE - 1:
                sum_x = planes[x - 1][h]
            else:
                sum_x = planes[x - 1][h] + planes[x + 1][h]
            flow = weight * half + weight_x * sum_x + weight_y * sum_y[h] + weight_z * sum_z
            phases, conc = (half[:tile], half[tile : 2 * tile]), half[2 * tile :]
            drive = conc - pltpu.roll(conc, SLOTS, 0)
            total = phases[0] + phases[1]
            total = total + pltpu.roll(total, SLOTS, 0)
            tail = (phase_rate * closure) * (1.0 - total)
            rows = x * ROWS
            for number, value in enumerate(phases):
                gain = value * (1.0 - value) * (coupling[2 * number] * drive + (2.0 * value - 1.0))
                part = flow[number * tile : (number + 1) * tile]
                partial[h, pl.ds(rows + number * tile, tile), :] = part + (phase_rate * gain + tail)
            partial[h, pl.ds(rows + 2 * tile, tile), :] = flow[2 * tile :]


def ghosts_of(axis, scale, select, tables):
    tables = jnp.concatenate(tables, axis=0)
    near = tables.astype(jnp.bfloat16)
    rest = (tables - near.astype(jnp.float32)).astype(jnp.bfloat16)
    both = jnp.concatenate([near, rest], axis=0)
    pair = jnp.dot(select[axis].astype(jnp.bfloat16), both, preferred_element_type=jnp.float32)
    weight = jnp.concatenate([scale[axis]] * 2, axis=1)
    return weight * pair[:ROWS], weight * pair[ROWS:]


def side_by_side(low, high, even):
    return jnp.where(even, low, high), jnp.where(even, high, low)


def sides_kernel(scale, select, partial, low, high, flat_a, flat_b, *refs):
    done, blocks = refs[-1], refs[0] if len(refs) > 1 else None
    sources = (low, high, flat_a, flat_b)
    x_low, x_high = ghosts_of(0, scale, select, [ref[0] for ref in sources])
    y_low, y_high = ghosts_of(1, scale, select, [ref[1] for ref in sources])
    lane = iota((ROWS, HALF), 1)
    inside = (lane < EDGE, lane >= HALF - EDGE)
    even = (lane // EDGE) % 2 == 0
    pairs = []
    for h in range(2):
        lanes = slice(h * HALF, (h + 1) * HALF)
        pairs.append(side_by_side(y_low[:, lanes], turned(y_high[:, lanes], -EDGE), even))
    for x in range(EDGE):
        ends = turned(pairs[x // GROUPS][x % 2], -EDGE * (x % GROUPS))
        for h, value in enumerate(plane_at(partial, x)):
            value = value + jnp.where(inside[h], ends, 0.0)
            if x == 0:
                value = value + x_low[:, h * HALF : (h + 1) * HALF]
            if x == EDGE - 1:
                value = value + x_high[:, h * HALF : (h + 1) * HALF]
            done[h, pl.ds(x * ROWS, ROWS), :] = value
    if blocks is not None:
        for slot in range(SLOTS):
            for f in range(NFIELD):
                for h in range(2):
                    rows = pl.ds(f * SLOTS + slot, EDGE, stride=ROWS)
                    blocks[slot, f, :, h * HALF : (h + 1) * HALF] = done[h, rows, :]


def z_pairs(scale, select, tables):
    z_low, z_high = ghosts_of(2, scale, select, tables)
    even = iota((ROWS, HALF), 1) % 2 == 0
    halves = [slice(h * HALF, (h + 1) * HALF) for h in range(2)]
    return [side_by_side(z_low[:, lanes], turned(z_high[:, lanes], EDGE - 1), even) for lanes in halves]


def ends_of(shape):
    place = iota(shape, 1) % EDGE
    return (place == 0) | (place == EDGE - 1)


def finish_kernel(scale, select, partial, known, deep_b, flat_a, relayed, z_low, z_high, done, *outs):
    deep_a = jnp.where(relayed[...] > 0.5, flat_a[2], known[...])
    pairs = z_pairs(scale, select, [z_low[...], z_high[...], deep_a, deep_b[...]])
    ends = ends_of((ROWS, HALF))
    packer = Packer()
    for x in range(EDGE):
        halves, at = [], EDGE - 1 - x
        for h, value in enumerate(plane_at(partial, x)):
            value = value + jnp.where(ends, turned(pairs[h][at % 2], -at), 0.0)
            done[h, pl.ds(x * ROWS, ROWS), :] = value
            halves.append(value)
        packer.add(x, *halves)
    emit_faces(packer, done, outs[0:2], outs[2:6])


def last_kernel(scale, select, partial, low, high, deep_a, deep_b, result, rows_of, blocks, sent):
    for h, pair in enumerate(z_pairs(scale, select, [low[2], high[2], deep_a[...], deep_b[...]])):
        for odd in range(2):
            rows_of[h, odd] = pair[odd]
    shape = (EDGE, HALF)
    ends, even = ends_of(shape), iota(shape, 0) % 2 == 0
    copies = []
    for slot in range(SLOTS):
        for f in range(NFIELD):
            row = pl.ds(f * SLOTS + slot, 1)
            for h in range(2):
                both = [jnp.broadcast_to(rows_of[h, odd, row, :], shape) for odd in (1, 0)]
                ghost = pltpu.roll(jnp.where(even, *both), HALF - EDGE + 1, 1, stride=1, stride_axis=0)
                lanes = pl.ds(h * HALF, HALF)
                blocks[slot, f, :, lanes] = partial[slot, f, :, lanes] + jnp.where(ends, ghost, 0.0)
        copy = pltpu.make_async_copy(blocks.at[slot], result.at[slot], sent.at[slot])
        copy.start()
        copies.append(copy)
    for copy in copies:
        copy.wait()


def spec(space):
    return pl.BlockSpec(memory_space=space)


VECTOR = pltpu.VMEM
SMALL = pltpu.CompilerParams(vmem_limit_bytes=8 << 20)
FLAT = (2, ROWS, PLANE)
TABLES = (STATE, SIDE, SIDE, FLAT, FLAT, FACE, FACE)
TO_DEV = (NFIELD * EDGE, PLANE)
TO_GRP = (NFIELD * EDGE + ROWS, PLANE)


def shaped(shape):
    return jax.ShapeDtypeStruct(shape, jnp.float32)


def cost(flops):
    return pl.CostEstimate(flops=flops, bytes_accessed=min(flops, 2 << 20), transcendentals=0)


def call(kernel, name, shapes, vectors, flops=1 << 20, scratch=()):
    return pl.pallas_call(
        kernel,
        name=name,
        compiler_params=SMALL,
        out_shape=[shaped(shape) for shape in shapes],
        in_specs=[spec(VECTOR)] * len(vectors),
        out_specs=[spec(VECTOR)] * len(shapes),
        scratch_shapes=list(scratch),
        cost_estimate=cost(flops),
    )(*vectors)


def start(arguments):
    shapes = (arguments[0].shape, SIDE, SIDE, FLAT, FLAT, (4, ROWS, HALF), SELECT)
    return pl.pallas_call(
        start_kernel,
        name="start",
        compiler_params=SMALL,
        out_shape=[shaped(shape) for shape in shapes],
        in_specs=[spec(pl.ANY)] * len(arguments),
        out_specs=[spec(VECTOR)] * len(shapes),
        scratch_shapes=[
            pltpu.VMEM(SPARE, jnp.float32),
            *(pltpu.SMEM(array.shape, jnp.int32) for array in arguments[1:]),
            pltpu.SemaphoreType.DMA((len(arguments) + 1,)),
        ],
    )(*(pltpu.with_memory_space_constraint(array, pltpu.HBM) for array in arguments))


def mask(flag):
    return jnp.broadcast_to(jnp.where(flag == 1, 1.0, 0.0).reshape(1, 1), FACE)


def body(fields, swap_dev, swap_grp, neighbors, orient):
    fields, low, high, faces, faces_dev, scale, select = start((fields, neighbors, orient))
    swap_dev, faces = lax.optimization_barrier((swap_dev, faces))
    faces = exchange(faces, "grp", 0)
    faces_dev = exchange(faces_dev, "dev", 0)
    mask_dev = mask(swap_dev)
    to_dev, to_grp = call(block_kernel, "blocks", [TO_DEV, TO_GRP], [mask_dev, fields, low, high], 1 << 24)
    swap_grp, to_grp = lax.optimization_barrier((swap_grp, to_grp))
    mask_grp = mask(swap_grp)
    block_grp = exchange(to_grp, "grp", 0)
    block_dev = exchange(to_dev, "dev", 0)
    new_low, new_high, *sends = call(
        faces_kernel,
        "faces",
        [SIDE, SIDE, SIDE, FLAT, FACE],
        [mask_dev, mask_grp, low, high, faces, faces_dev],
        1 << 24,
    )
    flat_a = exchange(sends[0], "dev", 0)
    flat_b = exchange(sends[1], "dev", 1)
    deep_b = exchange(sends[2], "grp", 1)
    partial, deep_a, relayed, z_low, z_high = call(
        first_inner_kernel,
        "inner_0",
        [STATE, FACE, FACE, FACE, FACE],
        [mask_dev, mask_grp, scale, fields, block_dev, block_grp, faces, low, high, new_low, new_high],
        4 << 20,
        [pltpu.VMEM(SPARE, jnp.float32)],
    )
    (partial,) = call(sides_kernel, "sides_0", [STATE], [scale, select, partial, new_low, new_high, flat_a, flat_b])
    state, *tables = call(
        finish_kernel,
        "finish_0",
        TABLES,
        [scale, select, partial, deep_a, deep_b, flat_a, relayed, z_low, z_high],
    )
    own, sends = tables[:2], tables[2:]
    flat_a = exchange(sends[0], "dev", 0)
    flat_b = exchange(sends[1], "dev", 1)
    deep_a = exchange(sends[2], "grp", 0)
    deep_b = exchange(sends[3], "grp", 1)
    (partial,) = call(inner_kernel, "inner_1", [STATE], [state, scale], 4 << 20)
    (blocks,) = call(
        sides_kernel,
        "sides_1",
        [fields.shape],
        [scale, select, partial, *own, flat_a, flat_b],
        scratch=[pltpu.VMEM(SPARE, jnp.float32)],
    )
    return pl.pallas_call(
        last_kernel,
        name="finish_1",
        compiler_params=SMALL,
        out_shape=shaped(fields.shape),
        in_specs=[spec(VECTOR)] * 7,
        out_specs=spec(pl.ANY),
        scratch_shapes=[
            pltpu.VMEM((2, 2, ROWS, HALF), jnp.float32),
            pltpu.VMEM(fields.shape, jnp.float32),
            pltpu.SemaphoreType.DMA((SLOTS,)),
        ],
    )(scale, select, blocks, *own, deep_a, deep_b)


def solution(mesh):
    in_specs = (
        P(("grp", "dev"), None, None, None),
        P(("grp", "dev")),
        P(("grp", "dev")),
        P(("grp", "dev"), None),
        P(("grp", "dev")),
    )
    out_specs = P(("grp", "dev"), None, None, None)
    return jax.shard_map(body, mesh=mesh, in_specs=in_specs, out_specs=out_specs, check_vma=False)
```

```python
import math

import jax
import jax.numpy as jnp
from jax import lax
from jax.experimental import pallas as pl
from jax.experimental.pallas import tpu as pltpu
from jax.sharding import PartitionSpec as P

NPHASE = 4
NCONC = 2
NFIELD = NPHASE + NCONC
EDGE = 16
PLANE = EDGE * EDGE
HALF = PLANE // 2
GROUPS = HALF // EDGE
SLOTS = 4
ROWS = NFIELD * SLOTS

phase_rate = 0.05
closure = 0.1
coupling = (0.5, -0.5, 1.0, -1.0)
conc_rates = (0.08, 0.04)

STATE = (2, EDGE * ROWS, HALF)
SPARE = (2, (EDGE + 1) * ROWS, HALF)
FACE = (ROWS, PLANE)
SIDE = (3, ROWS, PLANE)
SOURCES = 4
PARTS = 2
SELECT = (3, 2 * ROWS, PARTS * SOURCES * ROWS)


def partners(axis, offset):
    sizes = (lax.axis_size("grp"), lax.axis_size("dev"))
    along = ("grp", "dev").index(axis)
    route = []
    for grp in range(sizes[0]):
        for dev in range(sizes[1]):
            own = (grp, dev)
            step = 1 if (own[along] - offset) % 2 == 0 else -1
            partner = list(own)
            partner[along] += step
            if not 0 <= partner[along] < sizes[along]:
                partner = list(own)
                partner[1 - along] ^= 1
                if partner[1 - along] >= sizes[1 - along]:
                    partner = list(own)
            route.append((grp * sizes[1] + dev, partner[0] * sizes[1] + partner[1]))
    return route


def exchange(block, axis, offset):
    return lax.ppermute(block, ("grp", "dev"), partners(axis, offset))


def iota(shape, dim):
    return lax.broadcasted_iota(jnp.int32, shape, dim)


def plane_at(ref, x):
    rows = pl.ds(x * ROWS, ROWS)
    return ref[0, rows, :], ref[1, rows, :]


def turned(value, shift):
    shift %= HALF
    return pltpu.roll(value, shift, 1) if shift else value


class Packer:
    def __init__(self):
        lane = iota((ROWS, HALF), 1)
        self.lane, self.group, self.place = lane, lane // EDGE, lane % EDGE
        self.y = [[None, None], [None, None]]
        self.z = [[None, None], [None, None]]

    def add(self, x, left, right):
        odd, half, at = x % 2, x // GROUPS, x % GROUPS
        ends = turned(jnp.where(self.lane < EDGE, left, right), EDGE * at)
        taken = (self.group == at) | (self.group == (at + GROUPS - 1) % GROUPS)
        before = self.y[half][odd]
        self.y[half][odd] = ends if before is None else jnp.where(taken, ends, before)
        at = EDGE - 1 - x
        odd = at % 2
        taken = (self.place == at) | (self.place == (at + EDGE - 1) % EDGE)
        for h, value in enumerate((left, right)):
            moved = turned(value, at)
            before = self.z[h][odd]
            self.z[h][odd] = moved if before is None else jnp.where(taken, moved, before)

    def tables(self, h):
        even_group, even_place = self.group % 2 == 0, self.place % 2 == 0
        (y_even, y_odd), (z_even, z_odd) = self.y[h], self.z[h]
        low = (jnp.where(even_group, y_even, y_odd), jnp.where(even_place, z_even, z_odd))
        y_high, z_high = jnp.where(even_group, y_odd, y_even), jnp.where(even_place, z_odd, z_even)
        return low, (turned(y_high, EDGE), turned(z_high, 1 - EDGE))


def write_tables(packer, state, own):
    low, high = own
    for h in range(2):
        lanes = pl.ds(h * HALF, HALF)
        for ref, x in ((low, 0), (high, EDGE - 1)):
            ref[0, :, lanes] = state[h, pl.ds(x * ROWS, ROWS), :]
        for ref, (y_table, z_table) in zip(own, packer.tables(h)):
            ref[1, :, lanes] = y_table
            ref[2, :, lanes] = z_table


def emit_faces(packer, state, own, sends):
    write_tables(packer, state, own)
    low, high = own
    flat_a, flat_b, deep_a, deep_b = sends
    even = even_place("dev")
    for face in range(2):
        flat_a[face] = jnp.where(even, high[face], low[face])
        flat_b[face] = jnp.where(even, low[face], high[face])
    even = even_place("grp")
    deep_a[...] = jnp.where(even, high[2], low[2])
    deep_b[...] = jnp.where(even, low[2], high[2])


def fill_slot(state, slot, block, first=0, count=EDGE):
    for f in range(NFIELD):
        value = block(f)
        for h in range(2):
            rows = pl.ds(first * ROWS + f * SLOTS + slot, count, stride=ROWS)
            state[h, rows, :] = value[:, h * HALF : (h + 1) * HALF]


def slot_rows():
    return iota(FACE, 0) % SLOTS


def shifted(value, rows):
    rows %= ROWS
    return pltpu.roll(value, rows, 0) if rows else value


def gathered(tables, slot):
    rows = slot_rows()
    out = shifted(tables[0], -slot)
    for number in range(1, len(tables)):
        out = jnp.where(rows == number, shifted(tables[number], number - slot), out)
    return out


def squeezed(table):
    tile = 2 * SLOTS
    rows = iota((tile, PLANE), 0) % SLOTS
    first, second, third = (table[number * tile : (number + 1) * tile] for number in range(3))
    between = jnp.where(rows == 1, pltpu.roll(second, 1, 0), pltpu.roll(second, tile - 1, 0))
    return jnp.concatenate([jnp.where((rows == 1) | (rows == 2), between, first), third], axis=0)


def stretched(value):
    tile = 2 * SLOTS
    rows = iota((tile, PLANE), 0) % SLOTS
    first, third = value[:tile], value[tile:]
    second = jnp.where(rows == 0, pltpu.roll(first, tile - 1, 0), pltpu.roll(first, 1, 0))
    return jnp.concatenate([first, second, third], axis=0)


def scattered(table, number, slot):
    return shifted(table, slot - number)


def even_place(axis):
    return lax.rem(lax.axis_index(axis), 2) == 0


def block_kernel(mask_dev, fields, low, high, to_dev, to_grp):
    last, size = SLOTS - 1, NFIELD * EDGE
    for f in range(NFIELD):
        to_dev[f * EDGE : (f + 1) * EDGE] = fields[last, f]
        to_grp[f * EDGE : (f + 1) * EDGE] = fields[0, f]
    rows, even = slot_rows(), even_place("grp")
    table = jnp.where(rows == 0, jnp.where(even, low[2], high[2]), jnp.where(even, high[2], low[2]))
    to_grp[size : size + ROWS] = jnp.where(rows == SLOTS - 1, mask_dev[...], table)


def faces_kernel(mask_dev, mask_grp, low, high, faces, faces_dev, *outs):
    new_low, new_high, flat_a, flat_b, deep_b = outs
    rows, last = slot_rows(), SLOTS - 1
    first_rows = (rows == 0) & (mask_grp[...] > 0.5)
    last_rows = (rows == last) & (mask_dev[...] > 0.5)
    even = even_place("grp")
    got_first, got_last = faces[:ROWS], faces_dev[:ROWS]
    got_z, got_last_z = stretched(faces[ROWS:]), stretched(faces_dev[ROWS:])
    for side, (raw, new) in enumerate(((low, new_low), (high, new_high))):
        for axis in range(2):
            number = 2 * axis + side
            table = jnp.where(first_rows, scattered(got_first, number, 0), raw[axis])
            new[axis] = jnp.where(last_rows, scattered(got_last, number, last), table)
        table = jnp.where(first_rows & (even if side == 0 else ~even), got_z, raw[2])
        new[2] = jnp.where(last_rows, scattered(got_last_z, side * last, last), table)
    even_dev = even_place("dev")
    for axis in range(2):
        flat_a[axis] = jnp.where(even_dev, new_high[axis], new_low[axis])
        flat_b[axis] = jnp.where(even_dev, new_low[axis], new_high[axis])
    flat_a[2] = got_z
    deep_b[...] = jnp.where(even, new_low[2], new_high[2])


def cos_quarter(number):
    turn = number & 7
    size = jnp.where((turn & 3) == 0, 1.0, jnp.where((turn & 3) == 2, 0.0, math.sqrt(0.5)))
    return jnp.where((turn > 2) & (turn < 6), -size, size)


def plan_kernel(neighbors, orient, scale, select):
    shape = (ROWS, HALF)
    slot, field, column = iota(shape, 0) % SLOTS, iota(shape, 0) // SLOTS, iota(shape, 1)
    grp, dev = lax.axis_index("grp"), lax.axis_index("dev")
    rank = grp * lax.axis_size("dev") + dev

    def by_slot(values):
        rows = values[0]
        for number in range(1, SLOTS):
            rows = jnp.where(slot == number, values[number], rows)
        return rows

    spread = []
    for number in range(SLOTS):
        turn = 0.5 * cos_quarter(orient[number])
        lift = 0.5 * cos_quarter(orient[number] + 6)
        spread.append((1.0 + turn, 1.0 - turn, 1.0 + lift))
    conc = jnp.where(field == NPHASE, conc_rates[0], conc_rates[1])
    weights = [jnp.where(field < NPHASE, phase_rate * by_slot([own[axis] for own in spread]), conc) for axis in range(3)]
    for axis in range(3):
        scale[axis] = weights[axis]
    scale[3] = 1.0 - 2.0 * (weights[0] + weights[1] + weights[2])
    for face in range(6):
        first = []
        came = 2 + lax.rem(lax.rem(dev if face < 4 else grp, 2) + face % 2 + 1, 2)
        for number in range(SLOTS):
            target = neighbors[number, face]
            source = jnp.where(target < 0, face % 2, jnp.where(target // SLOTS == rank, 1 - face % 2, came))
            first.append(source * ROWS + jnp.where(target < 0, number, target & (SLOTS - 1)))
        chosen = jnp.where(column == by_slot(first) + field * SLOTS, 1.0, 0.0)[:, : SOURCES * ROWS]
        rows = pl.ds(face % 2 * ROWS, ROWS)
        for part in range(PARTS):
            select[face // 2, rows, pl.ds(part * SOURCES * ROWS, SOURCES * ROWS)] = chosen


def start_kernel(fields, neighbors, orient, *refs):
    fetched, low, high, faces_grp, faces_dev, scale, select = refs[:7]
    state, near, turn, arrived = refs[7:]
    scalars = ((neighbors, near), (orient, turn))
    parts = [pl.ds(first, EDGE // 2) for first in (0, EDGE // 2)]
    blocks = tuple((fields.at[:, :, part], fetched.at[:, :, part]) for part in parts)
    copies = [pltpu.make_async_copy(*pair, arrived.at[number]) for number, pair in enumerate((*scalars, *blocks))]
    for copy in copies:
        copy.start()
    for copy in copies[: len(scalars)]:
        copy.wait()
    plan_kernel(near, turn, scale, select)
    packer = Packer()
    for number, part in enumerate(parts):
        copies[len(scalars) + number].wait()
        first = number * (EDGE // 2)
        for slot in range(SLOTS):
            fill_slot(state, slot, lambda f: fetched[slot, f, part], first, EDGE // 2)
        for x in range(first, first + EDGE // 2):
            packer.add(x, *plane_at(state, x))
    write_tables(packer, state, (low, high))
    faces_grp[:ROWS] = gathered([low[0], high[0], low[1], high[1]], 0)
    faces_grp[ROWS:] = squeezed(jnp.where(even_place("grp"), high[2], low[2]))
    faces_dev[:ROWS] = gathered([low[0], high[0], low[1], high[1]], SLOTS - 1)
    faces_dev[ROWS:] = squeezed(gathered([low[2], low[2], low[2], high[2]], SLOTS - 1))


def first_inner_kernel(mask_dev, mask_grp, scale, fields, block_dev, block_grp, faces, low, high, new_low, new_high, *refs):
    partial, got_deep, relayed, z_low, z_high, state = refs
    size = NFIELD * EDGE
    swap_dev, swap_grp = mask_dev[...] > 0.5, mask_grp[...] > 0.5

    def block(slot):
        def of(f):
            value = fields[slot, f]
            if slot == 0:
                value = jnp.where(swap_grp[:EDGE], block_grp[f * EDGE : (f + 1) * EDGE], value)
            if slot == SLOTS - 1:
                value = jnp.where(swap_dev[:EDGE], block_dev[f * EDGE : (f + 1) * EDGE], value)
            return value

        return of

    for slot in range(SLOTS):
        fill_slot(state, slot, block(slot))
    rows, even = slot_rows(), even_place("grp")
    first_rows = (rows == 0) & swap_grp
    other = block_grp[size : size + ROWS]
    got = jnp.where((rows == 0) | (rows == SLOTS - 1), stretched(faces[ROWS:]), other)
    got_deep[...] = jnp.where(first_rows, jnp.where(even, low[2], high[2]), got)
    relayed[...] = jnp.where(rows == SLOTS - 1, jnp.broadcast_to(other[SLOTS - 1 : SLOTS], FACE), 0.0)
    z_low[...] = jnp.where(first_rows & ~even, other, new_low[2])
    z_high[...] = jnp.where(first_rows & even, other, new_high[2])
    inner_kernel(state, scale, partial)


def inner_kernel(state, scale, partial):
    lane = iota((ROWS, HALF), 1)
    start_y, end_y = lane < EDGE, lane >= HALF - EDGE
    start_z, end_z = lane % EDGE == 0, lane % EDGE == EDGE - 1
    weight_x, weight_y, weight_z, weight = (scale[number] for number in range(4))
    tile = 2 * SLOTS
    planes = {0: plane_at(state, 0)}
    for x in range(EDGE):
        if x + 1 < EDGE:
            planes[x + 1] = plane_at(state, x + 1)
        left, right = planes[x]
        up = [turned(half, EDGE) for half in (left, right)]
        down = [turned(half, -EDGE) for half in (left, right)]
        sum_y = (
            jnp.where(start_y, 0.0, up[0]) + jnp.where(end_y, down[1], down[0]),
            jnp.where(start_y, up[0], up[1]) + jnp.where(end_y, 0.0, down[1]),
        )
        for h, half in enumerate((left, right)):
            sum_z = jnp.where(start_z, 0.0, turned(half, 1)) + jnp.where(end_z, 0.0, turned(half, -1))
            if x == 0:
                sum_x = planes[1][h]
            elif x == EDGE - 1:
                sum_x = planes[x - 1][h]
            else:
                sum_x = planes[x - 1][h] + planes[x + 1][h]
            flow = weight * half + weight_x * sum_x + weight_y * sum_y[h] + weight_z * sum_z
            phases, conc = (half[:tile], half[tile : 2 * tile]), half[2 * tile :]
            drive = conc - pltpu.roll(conc, SLOTS, 0)
            total = phases[0] + phases[1]
            total = total + pltpu.roll(total, SLOTS, 0)
            tail = (phase_rate * closure) * (1.0 - total)
            rows = x * ROWS
            for number, value in enumerate(phases):
                gain = value * (1.0 - value) * (coupling[2 * number] * drive + (2.0 * value - 1.0))
                part = flow[number * tile : (number + 1) * tile]
                partial[h, pl.ds(rows + number * tile, tile), :] = part + (phase_rate * gain + tail)
            partial[h, pl.ds(rows + 2 * tile, tile), :] = flow[2 * tile :]


def ghosts_of(axis, scale, select, tables):
    tables = jnp.concatenate(tables, axis=0)
    near = tables.astype(jnp.bfloat16)
    rest = (tables - near.astype(jnp.float32)).astype(jnp.bfloat16)
    both = jnp.concatenate([near, rest], axis=0)
    pair = jnp.dot(select[axis].astype(jnp.bfloat16), both, preferred_element_type=jnp.float32)
    weight = jnp.concatenate([scale[axis]] * 2, axis=1)
    return weight * pair[:ROWS], weight * pair[ROWS:]


def side_by_side(low, high, even):
    return jnp.where(even, low, high), jnp.where(even, high, low)


def sides_kernel(scale, select, partial, low, high, flat_a, flat_b, *refs):
    done, blocks = refs[-1], refs[0] if len(refs) > 1 else None
    sources = (low, high, flat_a, flat_b)
    x_low, x_high = ghosts_of(0, scale, select, [ref[0] for ref in sources])
    y_low, y_high = ghosts_of(1, scale, select, [ref[1] for ref in sources])
    lane = iota((ROWS, HALF), 1)
    inside = (lane < EDGE, lane >= HALF - EDGE)
    even = (lane // EDGE) % 2 == 0
    pairs = []
    for h in range(2):
        lanes = slice(h * HALF, (h + 1) * HALF)
        pairs.append(side_by_side(y_low[:, lanes], turned(y_high[:, lanes], -EDGE), even))
    for x in range(EDGE):
        ends = turned(pairs[x // GROUPS][x % 2], -EDGE * (x % GROUPS))
        for h, value in enumerate(plane_at(partial, x)):
            value = value + jnp.where(inside[h], ends, 0.0)
            if x == 0:
                value = value + x_low[:, h * HALF : (h + 1) * HALF]
            if x == EDGE - 1:
                value = value + x_high[:, h * HALF : (h + 1) * HALF]
            done[h, pl.ds(x * ROWS, ROWS), :] = value
    if blocks is not None:
        for slot in range(SLOTS):
            for f in range(NFIELD):
                for h in range(2):
                    rows = pl.ds(f * SLOTS + slot, EDGE, stride=ROWS)
                    blocks[slot, f, :, h * HALF : (h + 1) * HALF] = done[h, rows, :]


def z_pairs(scale, select, tables):
    z_low, z_high = ghosts_of(2, scale, select, tables)
    even = iota((ROWS, HALF), 1) % 2 == 0
    halves = [slice(h * HALF, (h + 1) * HALF) for h in range(2)]
    return [side_by_side(z_low[:, lanes], turned(z_high[:, lanes], EDGE - 1), even) for lanes in halves]


def ends_of(shape):
    place = iota(shape, 1) % EDGE
    return (place == 0) | (place == EDGE - 1)


def finish_kernel(scale, select, partial, known, deep_b, flat_a, relayed, z_low, z_high, done, *outs):
    deep_a = jnp.where(relayed[...] > 0.5, flat_a[2], known[...])
    pairs = z_pairs(scale, select, [z_low[...], z_high[...], deep_a, deep_b[...]])
    ends = ends_of((ROWS, HALF))
    packer = Packer()
    for x in range(EDGE):
        halves, at = [], EDGE - 1 - x
        for h, value in enumerate(plane_at(partial, x)):
            value = value + jnp.where(ends, turned(pairs[h][at % 2], -at), 0.0)
            done[h, pl.ds(x * ROWS, ROWS), :] = value
            halves.append(value)
        packer.add(x, *halves)
    emit_faces(packer, done, outs[0:2], outs[2:6])


def last_kernel(scale, select, partial, low, high, deep_a, deep_b, result, rows_of, blocks, sent):
    for h, pair in enumerate(z_pairs(scale, select, [low[2], high[2], deep_a[...], deep_b[...]])):
        for odd in range(2):
            rows_of[h, odd] = pair[odd]
    shape = (EDGE, HALF)
    ends, even = ends_of(shape), iota(shape, 0) % 2 == 0
    copies = []
    for slot in range(SLOTS):
        for f in range(NFIELD):
            row = pl.ds(f * SLOTS + slot, 1)
            for h in range(2):
                both = [jnp.broadcast_to(rows_of[h, odd, row, :], shape) for odd in (1, 0)]
                ghost = pltpu.roll(jnp.where(even, *both), HALF - EDGE + 1, 1, stride=1, stride_axis=0)
                lanes = pl.ds(h * HALF, HALF)
                blocks[slot, f, :, lanes] = partial[slot, f, :, lanes] + jnp.where(ends, ghost, 0.0)
        copy = pltpu.make_async_copy(blocks.at[slot], result.at[slot], sent.at[slot])
        copy.start()
        copies.append(copy)
    for copy in copies:
        copy.wait()


def spec(space):
    return pl.BlockSpec(memory_space=space)


VECTOR = pltpu.VMEM
SMALL = pltpu.CompilerParams(vmem_limit_bytes=8 << 20)
FLAT = (2, ROWS, PLANE)
TABLES = (STATE, SIDE, SIDE, FLAT, FLAT, FACE, FACE)
EARLY = (ROWS + 4 * SLOTS, PLANE)
TO_DEV = (NFIELD * EDGE, PLANE)
TO_GRP = (NFIELD * EDGE + ROWS, PLANE)


def shaped(shape):
    return jax.ShapeDtypeStruct(shape, jnp.float32)


def cost(flops):
    return pl.CostEstimate(flops=flops, bytes_accessed=min(flops, 2 << 20), transcendentals=0)


def call(kernel, name, shapes, vectors, flops=1 << 20, scratch=()):
    return pl.pallas_call(
        kernel,
        name=name,
        compiler_params=SMALL,
        out_shape=[shaped(shape) for shape in shapes],
        in_specs=[spec(VECTOR)] * len(vectors),
        out_specs=[spec(VECTOR)] * len(shapes),
        scratch_shapes=list(scratch),
        cost_estimate=cost(flops),
    )(*vectors)


def start(arguments):
    shapes = (arguments[0].shape, SIDE, SIDE, EARLY, EARLY, (4, ROWS, HALF), SELECT)
    return pl.pallas_call(
        start_kernel,
        name="start",
        compiler_params=SMALL,
        out_shape=[shaped(shape) for shape in shapes],
        in_specs=[spec(pl.ANY)] * len(arguments),
        out_specs=[spec(VECTOR)] * len(shapes),
        scratch_shapes=[
            pltpu.VMEM(SPARE, jnp.float32),
            *(pltpu.SMEM(array.shape, jnp.int32) for array in arguments[1:]),
            pltpu.SemaphoreType.DMA((len(arguments) + 1,)),
        ],
    )(*(pltpu.with_memory_space_constraint(array, pltpu.HBM) for array in arguments))


def mask(flag):
    return jnp.broadcast_to(jnp.where(flag == 1, 1.0, 0.0).reshape(1, 1), FACE)


def body(fields, swap_dev, swap_grp, neighbors, orient):
    fields, low, high, faces, faces_dev, scale, select = start((fields, neighbors, orient))
    swap_dev, faces = lax.optimization_barrier((swap_dev, faces))
    faces = exchange(faces, "grp", 0)
    faces_dev = exchange(faces_dev, "dev", 0)
    mask_dev = mask(swap_dev)
    to_dev, to_grp = call(block_kernel, "blocks", [TO_DEV, TO_GRP], [mask_dev, fields, low, high], 1 << 28)
    swap_grp, to_grp = lax.optimization_barrier((swap_grp, to_grp))
    mask_grp = mask(swap_grp)
    block_grp = exchange(to_grp, "grp", 0)
    block_dev = exchange(to_dev, "dev", 0)
    new_low, new_high, *sends = call(
        faces_kernel,
        "faces",
        [SIDE, SIDE, SIDE, FLAT, FACE],
        [mask_dev, mask_grp, low, high, faces, faces_dev],
        1 << 28,
    )
    flat_a = exchange(sends[0], "dev", 0)
    flat_b = exchange(sends[1], "dev", 1)
    deep_b = exchange(sends[2], "grp", 1)
    partial, deep_a, relayed, z_low, z_high = call(
        first_inner_kernel,
        "inner_0",
        [STATE, FACE, FACE, FACE, FACE],
        [mask_dev, mask_grp, scale, fields, block_dev, block_grp, faces, low, high, new_low, new_high],
        4 << 20,
        [pltpu.VMEM(SPARE, jnp.float32)],
    )
    (partial,) = call(sides_kernel, "sides_0", [STATE], [scale, select, partial, new_low, new_high, flat_a, flat_b])
    state, *tables = call(
        finish_kernel,
        "finish_0",
        TABLES,
        [scale, select, partial, deep_a, deep_b, flat_a, relayed, z_low, z_high],
    )
    own, sends = tables[:2], tables[2:]
    flat_a = exchange(sends[0], "dev", 0)
    flat_b = exchange(sends[1], "dev", 1)
    deep_a = exchange(sends[2], "grp", 0)
    deep_b = exchange(sends[3], "grp", 1)
    (partial,) = call(inner_kernel, "inner_1", [STATE], [state, scale], 4 << 20)
    (blocks,) = call(
        sides_kernel,
        "sides_1",
        [fields.shape],
        [scale, select, partial, *own, flat_a, flat_b],
        scratch=[pltpu.VMEM(SPARE, jnp.float32)],
    )
    return pl.pallas_call(
        last_kernel,
        name="finish_1",
        compiler_params=SMALL,
        out_shape=shaped(fields.shape),
        in_specs=[spec(VECTOR)] * 7,
        out_specs=spec(pl.ANY),
        scratch_shapes=[
            pltpu.VMEM((2, 2, ROWS, HALF), jnp.float32),
            pltpu.VMEM(fields.shape, jnp.float32),
            pltpu.SemaphoreType.DMA((SLOTS,)),
        ],
    )(scale, select, blocks, *own, deep_a, deep_b)


def solution(mesh):
    in_specs = (
        P(("grp", "dev"), None, None, None),
        P(("grp", "dev")),
        P(("grp", "dev")),
        P(("grp", "dev"), None),
        P(("grp", "dev")),
    )
    out_specs = P(("grp", "dev"), None, None, None)
    return jax.shard_map(body, mesh=mesh, in_specs=in_specs, out_specs=out_specs, check_vma=False)
```

```python
import math

import jax
import jax.numpy as jnp
from jax import lax
from jax.experimental import pallas as pl
from jax.experimental.pallas import tpu as pltpu
from jax.sharding import PartitionSpec as P

NPHASE = 4
NCONC = 2
NFIELD = NPHASE + NCONC
EDGE = 16
PLANE = EDGE * EDGE
HALF = PLANE // 2
GROUPS = HALF // EDGE
SLOTS = 4
ROWS = NFIELD * SLOTS

phase_rate = 0.05
closure = 0.1
coupling = (0.5, -0.5, 1.0, -1.0)
conc_rates = (0.08, 0.04)

STATE = (2, EDGE * ROWS, HALF)
SPARE = (2, (EDGE + 1) * ROWS, HALF)
FACE = (ROWS, PLANE)
SIDE = (3, ROWS, PLANE)
SOURCES = 4
PARTS = 2
SELECT = (3, 2 * ROWS, PARTS * SOURCES * ROWS)


def partners(axis, offset):
    sizes = (lax.axis_size("grp"), lax.axis_size("dev"))
    along = ("grp", "dev").index(axis)
    route = []
    for grp in range(sizes[0]):
        for dev in range(sizes[1]):
            own = (grp, dev)
            step = 1 if (own[along] - offset) % 2 == 0 else -1
            partner = list(own)
            partner[along] += step
            if not 0 <= partner[along] < sizes[along]:
                partner = list(own)
                partner[1 - along] ^= 1
                if partner[1 - along] >= sizes[1 - along]:
                    partner = list(own)
            route.append((grp * sizes[1] + dev, partner[0] * sizes[1] + partner[1]))
    return route


def exchange(block, axis, offset):
    return lax.ppermute(block, ("grp", "dev"), partners(axis, offset))


def iota(shape, dim):
    return lax.broadcasted_iota(jnp.int32, shape, dim)


def plane_at(ref, x):
    rows = pl.ds(x * ROWS, ROWS)
    return ref[0, rows, :], ref[1, rows, :]


def turned(value, shift):
    shift %= HALF
    return pltpu.roll(value, shift, 1) if shift else value


class Packer:
    def __init__(self):
        lane = iota((ROWS, HALF), 1)
        self.lane, self.group, self.place = lane, lane // EDGE, lane % EDGE
        self.y = [[None, None], [None, None]]
        self.z = [[None, None], [None, None]]

    def add(self, x, left, right):
        odd, half, at = x % 2, x // GROUPS, x % GROUPS
        ends = turned(jnp.where(self.lane < EDGE, left, right), EDGE * at)
        taken = (self.group == at) | (self.group == (at + GROUPS - 1) % GROUPS)
        before = self.y[half][odd]
        self.y[half][odd] = ends if before is None else jnp.where(taken, ends, before)
        at = EDGE - 1 - x
        odd = at % 2
        taken = (self.place == at) | (self.place == (at + EDGE - 1) % EDGE)
        for h, value in enumerate((left, right)):
            moved = turned(value, at)
            before = self.z[h][odd]
            self.z[h][odd] = moved if before is None else jnp.where(taken, moved, before)

    def tables(self, h):
        even_group, even_place = self.group % 2 == 0, self.place % 2 == 0
        (y_even, y_odd), (z_even, z_odd) = self.y[h], self.z[h]
        low = (jnp.where(even_group, y_even, y_odd), jnp.where(even_place, z_even, z_odd))
        y_high, z_high = jnp.where(even_group, y_odd, y_even), jnp.where(even_place, z_odd, z_even)
        return low, (turned(y_high, EDGE), turned(z_high, 1 - EDGE))


def write_tables(packer, state, own):
    low, high = own
    for h in range(2):
        lanes = pl.ds(h * HALF, HALF)
        for ref, x in ((low, 0), (high, EDGE - 1)):
            ref[0, :, lanes] = state[h, pl.ds(x * ROWS, ROWS), :]
        for ref, (y_table, z_table) in zip(own, packer.tables(h)):
            ref[1, :, lanes] = y_table
            ref[2, :, lanes] = z_table


def emit_faces(packer, state, own, sends):
    write_tables(packer, state, own)
    low, high = own
    flat_a, flat_b, deep_a, deep_b = sends
    even = even_place("dev")
    for face in range(2):
        flat_a[face] = jnp.where(even, high[face], low[face])
        flat_b[face] = jnp.where(even, low[face], high[face])
    even = even_place("grp")
    deep_a[...] = jnp.where(even, high[2], low[2])
    deep_b[...] = jnp.where(even, low[2], high[2])


def fill_slot(state, slot, block, first=0, count=EDGE):
    for f in range(NFIELD):
        value = block(f)
        for h in range(2):
            rows = pl.ds(first * ROWS + f * SLOTS + slot, count, stride=ROWS)
            state[h, rows, :] = value[:, h * HALF : (h + 1) * HALF]


def slot_rows():
    return iota(FACE, 0) % SLOTS


def shifted(value, rows):
    rows %= ROWS
    return pltpu.roll(value, rows, 0) if rows else value


def gathered(tables, slot):
    rows = slot_rows()
    out = shifted(tables[0], -slot)
    for number in range(1, len(tables)):
        out = jnp.where(rows == number, shifted(tables[number], number - slot), out)
    return out


def squeezed(table):
    tile = 2 * SLOTS
    rows = iota((tile, PLANE), 0) % SLOTS
    first, second, third = (table[number * tile : (number + 1) * tile] for number in range(3))
    between = jnp.where(rows == 1, pltpu.roll(second, 1, 0), pltpu.roll(second, tile - 1, 0))
    return jnp.concatenate([jnp.where((rows == 1) | (rows == 2), between, first), third], axis=0)


def stretched(value):
    tile = 2 * SLOTS
    rows = iota((tile, PLANE), 0) % SLOTS
    first, third = value[:tile], value[tile:]
    second = jnp.where(rows == 0, pltpu.roll(first, tile - 1, 0), pltpu.roll(first, 1, 0))
    return jnp.concatenate([first, second, third], axis=0)


def scattered(table, number, slot):
    return shifted(table, slot - number)


def even_place(axis):
    return lax.rem(lax.axis_index(axis), 2) == 0


def block_kernel(mask_dev, fields, low, high, to_dev, to_grp):
    last, size = SLOTS - 1, NFIELD * EDGE
    for f in range(NFIELD):
        to_dev[f * EDGE : (f + 1) * EDGE] = fields[last, f]
        to_grp[f * EDGE : (f + 1) * EDGE] = fields[0, f]
    rows, even = slot_rows(), even_place("grp")
    table = jnp.where(rows == 0, jnp.where(even, low[2], high[2]), jnp.where(even, high[2], low[2]))
    to_grp[size : size + ROWS] = jnp.where(rows == SLOTS - 1, mask_dev[...], table)


def faces_kernel(mask_dev, mask_grp, low, high, faces, faces_dev, *outs):
    new_low, new_high, flat_a, flat_b, deep_b = outs
    rows, last = slot_rows(), SLOTS - 1
    first_rows = (rows == 0) & (mask_grp[...] > 0.5)
    last_rows = (rows == last) & (mask_dev[...] > 0.5)
    even = even_place("grp")
    got_first, got_last = faces[:ROWS], faces_dev[:ROWS]
    got_z, got_last_z = stretched(faces[ROWS:]), stretched(faces_dev[ROWS:])
    for side, (raw, new) in enumerate(((low, new_low), (high, new_high))):
        for axis in range(2):
            number = 2 * axis + side
            table = jnp.where(first_rows, scattered(got_first, number, 0), raw[axis])
            new[axis] = jnp.where(last_rows, scattered(got_last, number, last), table)
        table = jnp.where(first_rows & (even if side == 0 else ~even), got_z, raw[2])
        new[2] = jnp.where(last_rows, scattered(got_last_z, side * last, last), table)
    even_dev = even_place("dev")
    for axis in range(2):
        flat_a[axis] = jnp.where(even_dev, new_high[axis], new_low[axis])
        flat_b[axis] = jnp.where(even_dev, new_low[axis], new_high[axis])
    flat_a[2] = got_z
    deep_b[...] = jnp.where(even, new_low[2], new_high[2])


def cos_quarter(number):
    turn = number & 7
    size = jnp.where((turn & 3) == 0, 1.0, jnp.where((turn & 3) == 2, 0.0, math.sqrt(0.5)))
    return jnp.where((turn > 2) & (turn < 6), -size, size)


def plan_kernel(neighbors, orient, scale, select):
    shape = (ROWS, HALF)
    slot, field, column = iota(shape, 0) % SLOTS, iota(shape, 0) // SLOTS, iota(shape, 1)
    grp, dev = lax.axis_index("grp"), lax.axis_index("dev")
    rank = grp * lax.axis_size("dev") + dev

    def by_slot(values):
        rows = values[0]
        for number in range(1, SLOTS):
            rows = jnp.where(slot == number, values[number], rows)
        return rows

    spread = []
    for number in range(SLOTS):
        turn = 0.5 * cos_quarter(orient[number])
        lift = 0.5 * cos_quarter(orient[number] + 6)
        spread.append((1.0 + turn, 1.0 - turn, 1.0 + lift))
    conc = jnp.where(field == NPHASE, conc_rates[0], conc_rates[1])
    weights = [jnp.where(field < NPHASE, phase_rate * by_slot([own[axis] for own in spread]), conc) for axis in range(3)]
    for axis in range(3):
        scale[axis] = weights[axis]
    scale[3] = 1.0 - 2.0 * (weights[0] + weights[1] + weights[2])
    for face in range(6):
        first = []
        came = 2 + lax.rem(lax.rem(dev if face < 4 else grp, 2) + face % 2 + 1, 2)
        for number in range(SLOTS):
            target = neighbors[number, face]
            source = jnp.where(target < 0, face % 2, jnp.where(target // SLOTS == rank, 1 - face % 2, came))
            first.append(source * ROWS + jnp.where(target < 0, number, target & (SLOTS - 1)))
        chosen = jnp.where(column == by_slot(first) + field * SLOTS, 1.0, 0.0)[:, : SOURCES * ROWS]
        rows = pl.ds(face % 2 * ROWS, ROWS)
        for part in range(PARTS):
            select[face // 2, rows, pl.ds(part * SOURCES * ROWS, SOURCES * ROWS)] = chosen


def start_kernel(fields, neighbors, orient, *refs):
    fetched, low, high, faces_grp, faces_dev, scale, select = refs[:7]
    state, near, turn, arrived = refs[7:]
    scalars = ((neighbors, near), (orient, turn))
    parts = [pl.ds(first, EDGE // 2) for first in (0, EDGE // 2)]
    blocks = tuple((fields.at[:, :, part], fetched.at[:, :, part]) for part in parts)
    copies = [pltpu.make_async_copy(*pair, arrived.at[number]) for number, pair in enumerate((*scalars, *blocks))]
    for copy in copies:
        copy.start()
    for copy in copies[: len(scalars)]:
        copy.wait()
    plan_kernel(near, turn, scale, select)
    packer = Packer()
    for number, part in enumerate(parts):
        copies[len(scalars) + number].wait()
        first = number * (EDGE // 2)
        for slot in range(SLOTS):
            fill_slot(state, slot, lambda f: fetched[slot, f, part], first, EDGE // 2)
        for x in range(first, first + EDGE // 2):
            packer.add(x, *plane_at(state, x))
    write_tables(packer, state, (low, high))
    faces_grp[:ROWS] = gathered([low[0], high[0], low[1], high[1]], 0)
    faces_grp[ROWS:] = squeezed(jnp.where(even_place("grp"), high[2], low[2]))
    faces_dev[:ROWS] = gathered([low[0], high[0], low[1], high[1]], SLOTS - 1)
    faces_dev[ROWS:] = squeezed(gathered([low[2], low[2], low[2], high[2]], SLOTS - 1))


def first_inner_kernel(mask_dev, mask_grp, scale, fields, block_dev, block_grp, faces, low, high, new_low, new_high, *refs):
    partial, got_deep, relayed, z_low, z_high, state = refs
    size = NFIELD * EDGE
    swap_dev, swap_grp = mask_dev[...] > 0.5, mask_grp[...] > 0.5

    def block(slot):
        def of(f):
            value = fields[slot, f]
            if slot == 0:
                value = jnp.where(swap_grp[:EDGE], block_grp[f * EDGE : (f + 1) * EDGE], value)
            if slot == SLOTS - 1:
                value = jnp.where(swap_dev[:EDGE], block_dev[f * EDGE : (f + 1) * EDGE], value)
            return value

        return of

    for slot in range(SLOTS):
        fill_slot(state, slot, block(slot))
    rows, even = slot_rows(), even_place("grp")
    first_rows = (rows == 0) & swap_grp
    other = block_grp[size : size + ROWS]
    got = jnp.where((rows == 0) | (rows == SLOTS - 1), stretched(faces[ROWS:]), other)
    got_deep[...] = jnp.where(first_rows, jnp.where(even, low[2], high[2]), got)
    relayed[...] = jnp.where(rows == SLOTS - 1, jnp.broadcast_to(other[SLOTS - 1 : SLOTS], FACE), 0.0)
    z_low[...] = jnp.where(first_rows & ~even, other, new_low[2])
    z_high[...] = jnp.where(first_rows & even, other, new_high[2])
    inner_kernel(state, scale, partial)


def inner_kernel(state, scale, partial):
    lane = iota((ROWS, HALF), 1)
    start_y, end_y = lane < EDGE, lane >= HALF - EDGE
    start_z, end_z = lane % EDGE == 0, lane % EDGE == EDGE - 1
    weight_x, weight_y, weight_z, weight = (scale[number] for number in range(4))
    tile = 2 * SLOTS
    planes = {0: plane_at(state, 0)}
    for x in range(EDGE):
        if x + 1 < EDGE:
            planes[x + 1] = plane_at(state, x + 1)
        left, right = planes[x]
        up = [turned(half, EDGE) for half in (left, right)]
        down = [turned(half, -EDGE) for half in (left, right)]
        sum_y = (
            jnp.where(start_y, 0.0, up[0]) + jnp.where(end_y, down[1], down[0]),
            jnp.where(start_y, up[0], up[1]) + jnp.where(end_y, 0.0, down[1]),
        )
        for h, half in enumerate((left, right)):
            sum_z = jnp.where(start_z, 0.0, turned(half, 1)) + jnp.where(end_z, 0.0, turned(half, -1))
            if x == 0:
                sum_x = planes[1][h]
            elif x == EDGE - 1:
                sum_x = planes[x - 1][h]
            else:
                sum_x = planes[x - 1][h] + planes[x + 1][h]
            flow = weight * half + weight_x * sum_x + weight_y * sum_y[h] + weight_z * sum_z
            phases, conc = (half[:tile], half[tile : 2 * tile]), half[2 * tile :]
            drive = conc - pltpu.roll(conc, SLOTS, 0)
            total = phases[0] + phases[1]
            total = total + pltpu.roll(total, SLOTS, 0)
            tail = (phase_rate * closure) * (1.0 - total)
            rows = x * ROWS
            for number, value in enumerate(phases):
                gain = value * (1.0 - value) * (coupling[2 * number] * drive + (2.0 * value - 1.0))
                part = flow[number * tile : (number + 1) * tile]
                partial[h, pl.ds(rows + number * tile, tile), :] = part + (phase_rate * gain + tail)
            partial[h, pl.ds(rows + 2 * tile, tile), :] = flow[2 * tile :]


def ghosts_of(axis, scale, select, tables):
    tables = jnp.concatenate(tables, axis=0)
    near = tables.astype(jnp.bfloat16)
    rest = (tables - near.astype(jnp.float32)).astype(jnp.bfloat16)
    both = jnp.concatenate([near, rest], axis=0)
    pair = jnp.dot(select[axis].astype(jnp.bfloat16), both, preferred_element_type=jnp.float32)
    weight = jnp.concatenate([scale[axis]] * 2, axis=1)
    return weight * pair[:ROWS], weight * pair[ROWS:]


def side_by_side(low, high, even):
    return jnp.where(even, low, high), jnp.where(even, high, low)


def sides_kernel(scale, select, partial, low, high, flat_a, flat_b, *refs):
    done, blocks = refs[-1], refs[0] if len(refs) > 1 else None
    sources = (low, high, flat_a, flat_b)
    x_low, x_high = ghosts_of(0, scale, select, [ref[0] for ref in sources])
    y_low, y_high = ghosts_of(1, scale, select, [ref[1] for ref in sources])
    lane = iota((ROWS, HALF), 1)
    inside = (lane < EDGE, lane >= HALF - EDGE)
    even = (lane // EDGE) % 2 == 0
    pairs = []
    for h in range(2):
        lanes = slice(h * HALF, (h + 1) * HALF)
        pairs.append(side_by_side(y_low[:, lanes], turned(y_high[:, lanes], -EDGE), even))
    for x in range(EDGE):
        ends = turned(pairs[x // GROUPS][x % 2], -EDGE * (x % GROUPS))
        for h, value in enumerate(plane_at(partial, x)):
            value = value + jnp.where(inside[h], ends, 0.0)
            if x == 0:
                value = value + x_low[:, h * HALF : (h + 1) * HALF]
            if x == EDGE - 1:
                value = value + x_high[:, h * HALF : (h + 1) * HALF]
            done[h, pl.ds(x * ROWS, ROWS), :] = value
    if blocks is not None:
        for slot in range(SLOTS):
            for f in range(NFIELD):
                for h in range(2):
                    rows = pl.ds(f * SLOTS + slot, EDGE, stride=ROWS)
                    blocks[slot, f, :, h * HALF : (h + 1) * HALF] = done[h, rows, :]


def z_pairs(scale, select, tables):
    z_low, z_high = ghosts_of(2, scale, select, tables)
    even = iota((ROWS, HALF), 1) % 2 == 0
    halves = [slice(h * HALF, (h + 1) * HALF) for h in range(2)]
    return [side_by_side(z_low[:, lanes], turned(z_high[:, lanes], EDGE - 1), even) for lanes in halves]


def ends_of(shape):
    place = iota(shape, 1) % EDGE
    return (place == 0) | (place == EDGE - 1)


def finish_kernel(scale, select, partial, known, deep_b, flat_a, relayed, z_low, z_high, done, *outs):
    deep_a = jnp.where(relayed[...] > 0.5, flat_a[2], known[...])
    pairs = z_pairs(scale, select, [z_low[...], z_high[...], deep_a, deep_b[...]])
    ends = ends_of((ROWS, HALF))
    packer = Packer()
    for x in range(EDGE):
        halves, at = [], EDGE - 1 - x
        for h, value in enumerate(plane_at(partial, x)):
            value = value + jnp.where(ends, turned(pairs[h][at % 2], -at), 0.0)
            done[h, pl.ds(x * ROWS, ROWS), :] = value
            halves.append(value)
        packer.add(x, *halves)
    emit_faces(packer, done, outs[0:2], outs[2:6])


def last_kernel(scale, select, partial, low, high, deep_b, deep_a, result, rows_of, blocks, sent):
    for h, pair in enumerate(z_pairs(scale, select, [low[2], high[2], deep_a[...], deep_b[...]])):
        for odd in range(2):
            rows_of[h, odd] = pair[odd]
    shape = (EDGE, HALF)
    ends, even = ends_of(shape), iota(shape, 0) % 2 == 0
    copies = []
    for slot in range(SLOTS):
        for f in range(NFIELD):
            row = pl.ds(f * SLOTS + slot, 1)
            for h in range(2):
                both = [jnp.broadcast_to(rows_of[h, odd, row, :], shape) for odd in (1, 0)]
                ghost = pltpu.roll(jnp.where(even, *both), HALF - EDGE + 1, 1, stride=1, stride_axis=0)
                lanes = pl.ds(h * HALF, HALF)
                blocks[slot, f, :, lanes] = partial[slot, f, :, lanes] + jnp.where(ends, ghost, 0.0)
        copy = pltpu.make_async_copy(blocks.at[slot], result.at[slot], sent.at[slot])
        copy.start()
        copies.append(copy)
    for copy in copies:
        copy.wait()


def spec(space):
    return pl.BlockSpec(memory_space=space)


VECTOR = pltpu.VMEM
SMALL = pltpu.CompilerParams(vmem_limit_bytes=8 << 20)
FLAT = (2, ROWS, PLANE)
TABLES = (STATE, SIDE, SIDE, FLAT, FLAT, FACE, FACE)
EARLY = (ROWS + 4 * SLOTS, PLANE)
TO_DEV = (NFIELD * EDGE, PLANE)
TO_GRP = (NFIELD * EDGE + ROWS, PLANE)


def shaped(shape):
    return jax.ShapeDtypeStruct(shape, jnp.float32)


def cost(flops):
    return pl.CostEstimate(flops=flops, bytes_accessed=min(flops, 2 << 20), transcendentals=0)


def call(kernel, name, shapes, vectors, flops=1 << 20, scratch=()):
    return pl.pallas_call(
        kernel,
        name=name,
        compiler_params=SMALL,
        out_shape=[shaped(shape) for shape in shapes],
        in_specs=[spec(VECTOR)] * len(vectors),
        out_specs=[spec(VECTOR)] * len(shapes),
        scratch_shapes=list(scratch),
        cost_estimate=cost(flops),
    )(*vectors)


def start(arguments):
    shapes = (arguments[0].shape, SIDE, SIDE, EARLY, EARLY, (4, ROWS, HALF), SELECT)
    return pl.pallas_call(
        start_kernel,
        name="start",
        compiler_params=SMALL,
        out_shape=[shaped(shape) for shape in shapes],
        in_specs=[spec(pl.ANY)] * len(arguments),
        out_specs=[spec(VECTOR)] * len(shapes),
        scratch_shapes=[
            pltpu.VMEM(SPARE, jnp.float32),
            *(pltpu.SMEM(array.shape, jnp.int32) for array in arguments[1:]),
            pltpu.SemaphoreType.DMA((len(arguments) + 1,)),
        ],
    )(*(pltpu.with_memory_space_constraint(array, pltpu.HBM) for array in arguments))


def mask(flag):
    return jnp.broadcast_to(jnp.where(flag == 1, 1.0, 0.0).reshape(1, 1), FACE)


def body(fields, swap_dev, swap_grp, neighbors, orient):
    fields, low, high, faces, faces_dev, scale, select = start((fields, neighbors, orient))
    swap_dev, faces = lax.optimization_barrier((swap_dev, faces))
    faces = exchange(faces, "grp", 0)
    faces_dev = exchange(faces_dev, "dev", 0)
    mask_dev = mask(swap_dev)
    to_dev, to_grp = call(block_kernel, "blocks", [TO_DEV, TO_GRP], [mask_dev, fields, low, high], 1 << 28)
    swap_grp, to_grp = lax.optimization_barrier((swap_grp, to_grp))
    mask_grp = mask(swap_grp)
    block_grp = exchange(to_grp, "grp", 0)
    block_dev = exchange(to_dev, "dev", 0)
    new_low, new_high, *sends = call(
        faces_kernel,
        "faces",
        [SIDE, SIDE, SIDE, FLAT, FACE],
        [mask_dev, mask_grp, low, high, faces, faces_dev],
        1 << 28,
    )
    flat_a = exchange(sends[0], "dev", 0)
    flat_b = exchange(sends[1], "dev", 1)
    deep_b = exchange(sends[2], "grp", 1)
    partial, deep_a, relayed, z_low, z_high = call(
        first_inner_kernel,
        "inner_0",
        [STATE, FACE, FACE, FACE, FACE],
        [mask_dev, mask_grp, scale, fields, block_dev, block_grp, faces, low, high, new_low, new_high],
        4 << 20,
        [pltpu.VMEM(SPARE, jnp.float32)],
    )
    (partial,) = call(sides_kernel, "sides_0", [STATE], [scale, select, partial, new_low, new_high, flat_a, flat_b])
    state, *tables = call(
        finish_kernel,
        "finish_0",
        TABLES,
        [scale, select, partial, deep_a, deep_b, flat_a, relayed, z_low, z_high],
    )
    own, sends = tables[:2], tables[2:]
    flat_a = exchange(sends[0], "dev", 0)
    flat_b = exchange(sends[1], "dev", 1)
    deep_a = exchange(sends[2], "grp", 0)
    deep_b = exchange(sends[3], "grp", 1)
    (partial,) = call(inner_kernel, "inner_1", [STATE], [state, scale], 4 << 20)
    (blocks,) = call(
        sides_kernel,
        "sides_1",
        [fields.shape],
        [scale, select, partial, *own, flat_a, flat_b],
        scratch=[pltpu.VMEM(SPARE, jnp.float32)],
    )
    return pl.pallas_call(
        last_kernel,
        name="finish_1",
        compiler_params=SMALL,
        out_shape=shaped(fields.shape),
        in_specs=[spec(VECTOR)] * 7,
        out_specs=spec(pl.ANY),
        scratch_shapes=[
            pltpu.VMEM((2, 2, ROWS, HALF), jnp.float32),
            pltpu.VMEM(fields.shape, jnp.float32),
            pltpu.SemaphoreType.DMA((SLOTS,)),
        ],
    )(scale, select, blocks, *own, deep_b, deep_a)


def solution(mesh):
    in_specs = (
        P(("grp", "dev"), None, None, None),
        P(("grp", "dev")),
        P(("grp", "dev")),
        P(("grp", "dev"), None),
        P(("grp", "dev")),
    )
    out_specs = P(("grp", "dev"), None, None, None)
    return jax.shard_map(body, mesh=mesh, in_specs=in_specs, out_specs=out_specs, check_vma=False)
```

```python
import math

import jax
import jax.numpy as jnp
from jax import lax
from jax.experimental import pallas as pl
from jax.experimental.pallas import tpu as pltpu
from jax.sharding import PartitionSpec as P

NPHASE = 4
NCONC = 2
NFIELD = NPHASE + NCONC
EDGE = 16
PLANE = EDGE * EDGE
HALF = PLANE // 2
GROUPS = HALF // EDGE
SLOTS = 4
ROWS = NFIELD * SLOTS

phase_rate = 0.05
closure = 0.1
coupling = (0.5, -0.5, 1.0, -1.0)
conc_rates = (0.08, 0.04)

STATE = (2, EDGE * ROWS, HALF)
SPARE = (2, (EDGE + 1) * ROWS, HALF)
FACE = (ROWS, PLANE)
SIDE = (3, ROWS, PLANE)
SOURCES = 4
PARTS = 2
SELECT = (3, 2 * ROWS, PARTS * SOURCES * ROWS)


def partners(axis, offset):
    sizes = (lax.axis_size("grp"), lax.axis_size("dev"))
    along = ("grp", "dev").index(axis)
    route = []
    for grp in range(sizes[0]):
        for dev in range(sizes[1]):
            own = (grp, dev)
            step = 1 if (own[along] - offset) % 2 == 0 else -1
            partner = list(own)
            partner[along] += step
            if not 0 <= partner[along] < sizes[along]:
                partner = list(own)
                partner[1 - along] ^= 1
                if partner[1 - along] >= sizes[1 - along]:
                    partner = list(own)
            route.append((grp * sizes[1] + dev, partner[0] * sizes[1] + partner[1]))
    return route


def exchange(block, axis, offset):
    return lax.ppermute(block, ("grp", "dev"), partners(axis, offset))


def iota(shape, dim):
    return lax.broadcasted_iota(jnp.int32, shape, dim)


def plane_at(ref, x):
    rows = pl.ds(x * ROWS, ROWS)
    return ref[0, rows, :], ref[1, rows, :]


def turned(value, shift):
    shift %= HALF
    return pltpu.roll(value, shift, 1) if shift else value


class Packer:
    def __init__(self):
        lane = iota((ROWS, HALF), 1)
        self.lane, self.group, self.place = lane, lane // EDGE, lane % EDGE
        self.y = [[None, None], [None, None]]
        self.z = [[None, None], [None, None]]

    def add_y(self, x, left, right):
        odd, half, at = x % 2, x // GROUPS, x % GROUPS
        ends = turned(jnp.where(self.lane < EDGE, left, right), EDGE * at)
        taken = (self.group == at) | (self.group == (at + GROUPS - 1) % GROUPS)
        before = self.y[half][odd]
        self.y[half][odd] = ends if before is None else jnp.where(taken, ends, before)

    def add_z(self, x, left, right):
        at = EDGE - 1 - x
        odd = at % 2
        taken = (self.place == at) | (self.place == (at + EDGE - 1) % EDGE)
        for h, value in enumerate((left, right)):
            moved = turned(value, at)
            before = self.z[h][odd]
            self.z[h][odd] = moved if before is None else jnp.where(taken, moved, before)

    def y_tables(self, h):
        even, (first, second) = self.group % 2 == 0, self.y[h]
        return jnp.where(even, first, second), turned(jnp.where(even, second, first), EDGE)

    def z_tables(self, h):
        even, (first, second) = self.place % 2 == 0, self.z[h]
        return jnp.where(even, first, second), turned(jnp.where(even, second, first), 1 - EDGE)


def write_tables(packer, state, own):
    low, high = own
    for h in range(2):
        lanes = pl.ds(h * HALF, HALF)
        for ref, x in ((low, 0), (high, EDGE - 1)):
            ref[0, :, lanes] = state[h, pl.ds(x * ROWS, ROWS), :]
        for ref, table in zip(own, packer.y_tables(h)):
            ref[1, :, lanes] = table


def emit_faces(own, sends):
    low, high = own
    flat_a, flat_b, deep_a, deep_b = sends
    even = even_place("dev")
    for face in range(2):
        flat_a[face] = jnp.where(even, high[face], low[face])
        flat_b[face] = jnp.where(even, low[face], high[face])
    even = even_place("grp")
    deep_a[...] = jnp.where(even, high[2], low[2])
    deep_b[...] = jnp.where(even, low[2], high[2])


def fill_slot(state, slot, block, first=0, count=EDGE):
    for f in range(NFIELD):
        value = block(f)
        for h in range(2):
            rows = pl.ds(first * ROWS + f * SLOTS + slot, count, stride=ROWS)
            state[h, rows, :] = value[:, h * HALF : (h + 1) * HALF]


def slot_rows():
    return iota(FACE, 0) % SLOTS


def shifted(value, rows):
    rows %= ROWS
    return pltpu.roll(value, rows, 0) if rows else value


def gathered(tables, slot):
    rows = slot_rows()
    out = shifted(tables[0], -slot)
    for number in range(1, len(tables)):
        out = jnp.where(rows == number, shifted(tables[number], number - slot), out)
    return out


def squeezed(table):
    tile = 2 * SLOTS
    rows = iota((tile, PLANE), 0) % SLOTS
    first, second, third = (table[number * tile : (number + 1) * tile] for number in range(3))
    between = jnp.where(rows == 1, pltpu.roll(second, 1, 0), pltpu.roll(second, tile - 1, 0))
    return jnp.concatenate([jnp.where((rows == 1) | (rows == 2), between, first), third], axis=0)


def stretched(value):
    tile = 2 * SLOTS
    rows = iota((tile, PLANE), 0) % SLOTS
    first, third = value[:tile], value[tile:]
    second = jnp.where(rows == 0, pltpu.roll(first, tile - 1, 0), pltpu.roll(first, 1, 0))
    return jnp.concatenate([first, second, third], axis=0)


def scattered(table, number, slot):
    return shifted(table, slot - number)


def even_place(axis):
    return lax.rem(lax.axis_index(axis), 2) == 0


def block_kernel(mask_dev, fields, low, high, to_dev, to_grp):
    last, size = SLOTS - 1, NFIELD * EDGE
    for f in range(NFIELD):
        to_dev[f * EDGE : (f + 1) * EDGE] = fields[last, f]
        to_grp[f * EDGE : (f + 1) * EDGE] = fields[0, f]
    rows, even = slot_rows(), even_place("grp")
    table = jnp.where(rows == 0, jnp.where(even, low[2], high[2]), jnp.where(even, high[2], low[2]))
    to_grp[size : size + ROWS] = jnp.where(rows == SLOTS - 1, mask_dev[...], table)


def faces_kernel(mask_dev, mask_grp, low, high, faces, faces_dev, *outs):
    new_low, new_high, flat_a, flat_b, deep_b = outs
    rows, last = slot_rows(), SLOTS - 1
    first_rows = (rows == 0) & (mask_grp[...] > 0.5)
    last_rows = (rows == last) & (mask_dev[...] > 0.5)
    even = even_place("grp")
    got_first, got_last = faces[:ROWS], faces_dev[:ROWS]
    got_z, got_last_z = stretched(faces[ROWS:]), stretched(faces_dev[ROWS:])
    for side, (raw, new) in enumerate(((low, new_low), (high, new_high))):
        for axis in range(2):
            number = 2 * axis + side
            table = jnp.where(first_rows, scattered(got_first, number, 0), raw[axis])
            new[axis] = jnp.where(last_rows, scattered(got_last, number, last), table)
        table = jnp.where(first_rows & (even if side == 0 else ~even), got_z, raw[2])
        new[2] = jnp.where(last_rows, scattered(got_last_z, side * last, last), table)
    even_dev = even_place("dev")
    for axis in range(2):
        flat_a[axis] = jnp.where(even_dev, new_high[axis], new_low[axis])
        flat_b[axis] = jnp.where(even_dev, new_low[axis], new_high[axis])
    flat_a[2] = got_z
    deep_b[...] = jnp.where(even, new_low[2], new_high[2])


def cos_quarter(number):
    turn = number & 7
    size = jnp.where((turn & 3) == 0, 1.0, jnp.where((turn & 3) == 2, 0.0, math.sqrt(0.5)))
    return jnp.where((turn > 2) & (turn < 6), -size, size)


def plan_kernel(neighbors, orient, scale, select):
    shape = (ROWS, HALF)
    slot, field, column = iota(shape, 0) % SLOTS, iota(shape, 0) // SLOTS, iota(shape, 1)
    grp, dev = lax.axis_index("grp"), lax.axis_index("dev")
    rank = grp * lax.axis_size("dev") + dev

    def by_slot(values):
        rows = values[0]
        for number in range(1, SLOTS):
            rows = jnp.where(slot == number, values[number], rows)
        return rows

    spread = []
    for number in range(SLOTS):
        turn = 0.5 * cos_quarter(orient[number])
        lift = 0.5 * cos_quarter(orient[number] + 6)
        spread.append((1.0 + turn, 1.0 - turn, 1.0 + lift))
    conc = jnp.where(field == NPHASE, conc_rates[0], conc_rates[1])
    weights = [jnp.where(field < NPHASE, phase_rate * by_slot([own[axis] for own in spread]), conc) for axis in range(3)]
    for axis in range(3):
        scale[axis] = weights[axis]
    scale[3] = 1.0 - 2.0 * (weights[0] + weights[1] + weights[2])
    for face in range(6):
        first = []
        came = 2 + lax.rem(lax.rem(dev if face < 4 else grp, 2) + face % 2 + 1, 2)
        for number in range(SLOTS):
            target = neighbors[number, face]
            source = jnp.where(target < 0, face % 2, jnp.where(target // SLOTS == rank, 1 - face % 2, came))
            first.append(source * ROWS + jnp.where(target < 0, number, target & (SLOTS - 1)))
        chosen = jnp.where(column == by_slot(first) + field * SLOTS, 1.0, 0.0)[:, : SOURCES * ROWS]
        rows = pl.ds(face % 2 * ROWS, ROWS)
        for part in range(PARTS):
            select[face // 2, rows, pl.ds(part * SOURCES * ROWS, SOURCES * ROWS)] = chosen


def start_kernel(fields, neighbors, orient, *refs):
    fetched, low, high, faces_grp, faces_dev, scale, select = refs[:7]
    state, near, turn, arrived = refs[7:]
    scalars = ((neighbors, near), (orient, turn))
    parts = [pl.ds(first, EDGE // 2) for first in (0, EDGE // 2)]
    blocks = tuple((fields.at[:, :, part], fetched.at[:, :, part]) for part in parts)
    copies = [pltpu.make_async_copy(*pair, arrived.at[number]) for number, pair in enumerate((*scalars, *blocks))]
    for copy in copies:
        copy.start()
    for copy in copies[: len(scalars)]:
        copy.wait()
    plan_kernel(near, turn, scale, select)
    packer = Packer()
    for number, part in enumerate(parts):
        copies[len(scalars) + number].wait()
        first = number * (EDGE // 2)
        for slot in range(SLOTS):
            fill_slot(state, slot, lambda f: fetched[slot, f, part], first, EDGE // 2)
        for x in range(first, first + EDGE // 2):
            packer.add_y(x, *plane_at(state, x))
            packer.add_z(x, *plane_at(state, x))
    write_tables(packer, state, (low, high))
    for h in range(2):
        for ref, table in zip((low, high), packer.z_tables(h)):
            ref[2, :, h * HALF : (h + 1) * HALF] = table
    faces_grp[:ROWS] = gathered([low[0], high[0], low[1], high[1]], 0)
    faces_grp[ROWS:] = squeezed(jnp.where(even_place("grp"), high[2], low[2]))
    faces_dev[:ROWS] = gathered([low[0], high[0], low[1], high[1]], SLOTS - 1)
    faces_dev[ROWS:] = squeezed(gathered([low[2], low[2], low[2], high[2]], SLOTS - 1))


def first_inner_kernel(mask_dev, mask_grp, scale, fields, block_dev, block_grp, faces, low, high, new_low, new_high, *refs):
    partial, got_deep, relayed, z_low, z_high, state = refs
    size = NFIELD * EDGE
    swap_dev, swap_grp = mask_dev[...] > 0.5, mask_grp[...] > 0.5

    def block(slot):
        def of(f):
            value = fields[slot, f]
            if slot == 0:
                value = jnp.where(swap_grp[:EDGE], block_grp[f * EDGE : (f + 1) * EDGE], value)
            if slot == SLOTS - 1:
                value = jnp.where(swap_dev[:EDGE], block_dev[f * EDGE : (f + 1) * EDGE], value)
            return value

        return of

    for slot in range(SLOTS):
        fill_slot(state, slot, block(slot))
    rows, even = slot_rows(), even_place("grp")
    first_rows = (rows == 0) & swap_grp
    other = block_grp[size : size + ROWS]
    got = jnp.where((rows == 0) | (rows == SLOTS - 1), stretched(faces[ROWS:]), other)
    got_deep[...] = jnp.where(first_rows, jnp.where(even, low[2], high[2]), got)
    relayed[...] = jnp.where(rows == SLOTS - 1, jnp.broadcast_to(other[SLOTS - 1 : SLOTS], FACE), 0.0)
    z_low[...] = jnp.where(first_rows & ~even, other, new_low[2])
    z_high[...] = jnp.where(first_rows & even, other, new_high[2])
    inner_kernel(state, scale, partial)


def inner_kernel(state, scale, partial):
    lane = iota((ROWS, HALF), 1)
    start_y, end_y = lane < EDGE, lane >= HALF - EDGE
    start_z, end_z = lane % EDGE == 0, lane % EDGE == EDGE - 1
    weight_x, weight_y, weight_z, weight = (scale[number] for number in range(4))
    tile = 2 * SLOTS
    planes = {0: plane_at(state, 0)}
    for x in range(EDGE):
        if x + 1 < EDGE:
            planes[x + 1] = plane_at(state, x + 1)
        left, right = planes[x]
        up = [turned(half, EDGE) for half in (left, right)]
        down = [turned(half, -EDGE) for half in (left, right)]
        sum_y = (
            jnp.where(start_y, 0.0, up[0]) + jnp.where(end_y, down[1], down[0]),
            jnp.where(start_y, up[0], up[1]) + jnp.where(end_y, 0.0, down[1]),
        )
        for h, half in enumerate((left, right)):
            sum_z = jnp.where(start_z, 0.0, turned(half, 1)) + jnp.where(end_z, 0.0, turned(half, -1))
            if x == 0:
                sum_x = planes[1][h]
            elif x == EDGE - 1:
                sum_x = planes[x - 1][h]
            else:
                sum_x = planes[x - 1][h] + planes[x + 1][h]
            flow = weight * half + weight_x * sum_x + weight_y * sum_y[h] + weight_z * sum_z
            phases, conc = (half[:tile], half[tile : 2 * tile]), half[2 * tile :]
            drive = conc - pltpu.roll(conc, SLOTS, 0)
            total = phases[0] + phases[1]
            total = total + pltpu.roll(total, SLOTS, 0)
            tail = (phase_rate * closure) * (1.0 - total)
            rows = x * ROWS
            for number, value in enumerate(phases):
                gain = value * (1.0 - value) * (coupling[2 * number] * drive + (2.0 * value - 1.0))
                part = flow[number * tile : (number + 1) * tile]
                partial[h, pl.ds(rows + number * tile, tile), :] = part + (phase_rate * gain + tail)
            partial[h, pl.ds(rows + 2 * tile, tile), :] = flow[2 * tile :]


def ghosts_of(axis, scale, select, tables):
    tables = jnp.concatenate(tables, axis=0)
    near = tables.astype(jnp.bfloat16)
    rest = (tables - near.astype(jnp.float32)).astype(jnp.bfloat16)
    both = jnp.concatenate([near, rest], axis=0)
    pair = jnp.dot(select[axis].astype(jnp.bfloat16), both, preferred_element_type=jnp.float32)
    weight = jnp.concatenate([scale[axis]] * 2, axis=1)
    return weight * pair[:ROWS], weight * pair[ROWS:]


def side_by_side(low, high, even):
    return jnp.where(even, low, high), jnp.where(even, high, low)


def sides_kernel(scale, select, partial, low, high, flat_a, flat_b, *refs):
    first_step = len(refs) == 3
    done = refs[0] if first_step else refs[1]
    packer = Packer()
    sources = (low, high, flat_a, flat_b)
    x_low, x_high = ghosts_of(0, scale, select, [ref[0] for ref in sources])
    y_low, y_high = ghosts_of(1, scale, select, [ref[1] for ref in sources])
    lane = iota((ROWS, HALF), 1)
    inside = (lane < EDGE, lane >= HALF - EDGE)
    even = (lane // EDGE) % 2 == 0
    pairs = []
    for h in range(2):
        lanes = slice(h * HALF, (h + 1) * HALF)
        pairs.append(side_by_side(y_low[:, lanes], turned(y_high[:, lanes], -EDGE), even))
    for x in range(EDGE):
        ends = turned(pairs[x // GROUPS][x % 2], -EDGE * (x % GROUPS))
        halves = []
        for h, value in enumerate(plane_at(partial, x)):
            value = value + jnp.where(inside[h], ends, 0.0)
            if x == 0:
                value = value + x_low[:, h * HALF : (h + 1) * HALF]
            if x == EDGE - 1:
                value = value + x_high[:, h * HALF : (h + 1) * HALF]
            done[h, pl.ds(x * ROWS, ROWS), :] = value
            halves.append(value)
        if first_step:
            packer.add_z(x, *halves)
    if first_step:
        for h in range(2):
            for ref, table in zip(refs[1:], packer.z_tables(h)):
                ref[:, h * HALF : (h + 1) * HALF] = table
    else:
        blocks = refs[0]
        for slot in range(SLOTS):
            for f in range(NFIELD):
                for h in range(2):
                    rows = pl.ds(f * SLOTS + slot, EDGE, stride=ROWS)
                    blocks[slot, f, :, h * HALF : (h + 1) * HALF] = done[h, rows, :]


def z_pairs(z_low, z_high):
    even = iota((ROWS, HALF), 1) % 2 == 0
    halves = [slice(h * HALF, (h + 1) * HALF) for h in range(2)]
    return [side_by_side(z_low[:, lanes], turned(z_high[:, lanes], EDGE - 1), even) for lanes in halves]


def ends_of(shape):
    place = iota(shape, 1) % EDGE
    return (place == 0) | (place == EDGE - 1)


def finish_kernel(
    scale, select, partial, packed_low, packed_high, known, deep_b, flat_a, relayed, z_low, z_high, done, low, high, *sends
):
    deep_a = jnp.where(relayed[...] > 0.5, flat_a[2], known[...])
    ghosts = ghosts_of(2, scale, select, [z_low[...], z_high[...], deep_a, deep_b[...]])
    pairs = z_pairs(*ghosts)
    ends = ends_of((ROWS, HALF))
    packer = Packer()
    for x in range(EDGE):
        halves, at = [], EDGE - 1 - x
        for h, value in enumerate(plane_at(partial, x)):
            value = value + jnp.where(ends, turned(pairs[h][at % 2], -at), 0.0)
            done[h, pl.ds(x * ROWS, ROWS), :] = value
            halves.append(value)
        packer.add_y(x, *halves)
    write_tables(packer, done, (low, high))
    low[2] = packed_low[...] + ghosts[0]
    high[2] = packed_high[...] + ghosts[1]
    emit_faces((low, high), sends)


def last_kernel(scale, select, partial, low, high, deep_a, deep_b, result, rows_of, blocks, sent):
    for h, pair in enumerate(z_pairs(*ghosts_of(2, scale, select, [low[2], high[2], deep_a[...], deep_b[...]]))):
        for odd in range(2):
            rows_of[h, odd] = pair[odd]
    shape = (EDGE, HALF)
    ends, even = ends_of(shape), iota(shape, 0) % 2 == 0
    copies = []
    for slot in range(SLOTS):
        for f in range(NFIELD):
            row = pl.ds(f * SLOTS + slot, 1)
            for h in range(2):
                both = [jnp.broadcast_to(rows_of[h, odd, row, :], shape) for odd in (1, 0)]
                ghost = pltpu.roll(jnp.where(even, *both), HALF - EDGE + 1, 1, stride=1, stride_axis=0)
                lanes = pl.ds(h * HALF, HALF)
                blocks[slot, f, :, lanes] = partial[slot, f, :, lanes] + jnp.where(ends, ghost, 0.0)
        copy = pltpu.make_async_copy(blocks.at[slot], result.at[slot], sent.at[slot])
        copy.start()
        copies.append(copy)
    for copy in copies:
        copy.wait()


def spec(space):
    return pl.BlockSpec(memory_space=space)


VECTOR = pltpu.VMEM
SMALL = pltpu.CompilerParams(vmem_limit_bytes=8 << 20)
FLAT = (2, ROWS, PLANE)
TABLES = (STATE, SIDE, SIDE, FLAT, FLAT, FACE, FACE)
EARLY = (ROWS + 4 * SLOTS, PLANE)
TO_DEV = (NFIELD * EDGE, PLANE)
TO_GRP = (NFIELD * EDGE + ROWS, PLANE)


def shaped(shape):
    return jax.ShapeDtypeStruct(shape, jnp.float32)


def cost(flops):
    return pl.CostEstimate(flops=flops, bytes_accessed=min(flops, 2 << 20), transcendentals=0)


def call(kernel, name, shapes, vectors, flops=1 << 20, scratch=()):
    return pl.pallas_call(
        kernel,
        name=name,
        compiler_params=SMALL,
        out_shape=[shaped(shape) for shape in shapes],
        in_specs=[spec(VECTOR)] * len(vectors),
        out_specs=[spec(VECTOR)] * len(shapes),
        scratch_shapes=list(scratch),
        cost_estimate=cost(flops),
    )(*vectors)


def start(arguments):
    shapes = (arguments[0].shape, SIDE, SIDE, EARLY, EARLY, (4, ROWS, HALF), SELECT)
    return pl.pallas_call(
        start_kernel,
        name="start",
        compiler_params=SMALL,
        out_shape=[shaped(shape) for shape in shapes],
        in_specs=[spec(pl.ANY)] * len(arguments),
        out_specs=[spec(VECTOR)] * len(shapes),
        scratch_shapes=[
            pltpu.VMEM(SPARE, jnp.float32),
            *(pltpu.SMEM(array.shape, jnp.int32) for array in arguments[1:]),
            pltpu.SemaphoreType.DMA((len(arguments) + 1,)),
        ],
    )(*(pltpu.with_memory_space_constraint(array, pltpu.HBM) for array in arguments))


def mask(flag):
    return jnp.broadcast_to(jnp.where(flag == 1, 1.0, 0.0).reshape(1, 1), FACE)


def body(fields, swap_dev, swap_grp, neighbors, orient):
    fields, low, high, faces, faces_dev, scale, select = start((fields, neighbors, orient))
    swap_dev, faces = lax.optimization_barrier((swap_dev, faces))
    faces = exchange(faces, "grp", 0)
    faces_dev = exchange(faces_dev, "dev", 0)
    mask_dev = mask(swap_dev)
    to_dev, to_grp = call(block_kernel, "blocks", [TO_DEV, TO_GRP], [mask_dev, fields, low, high], 1 << 28)
    swap_grp, to_grp = lax.optimization_barrier((swap_grp, to_grp))
    mask_grp = mask(swap_grp)
    block_grp = exchange(to_grp, "grp", 0)
    block_dev = exchange(to_dev, "dev", 0)
    new_low, new_high, *sends = call(
        faces_kernel,
        "faces",
        [SIDE, SIDE, SIDE, FLAT, FACE],
        [mask_dev, mask_grp, low, high, faces, faces_dev],
        1 << 28,
    )
    flat_a = exchange(sends[0], "dev", 0)
    flat_b = exchange(sends[1], "dev", 1)
    deep_b = exchange(sends[2], "grp", 1)
    partial, deep_a, relayed, z_low, z_high = call(
        first_inner_kernel,
        "inner_0",
        [STATE, FACE, FACE, FACE, FACE],
        [mask_dev, mask_grp, scale, fields, block_dev, block_grp, faces, low, high, new_low, new_high],
        4 << 20,
        [pltpu.VMEM(SPARE, jnp.float32)],
    )
    partial, packed_low, packed_high = call(
        sides_kernel,
        "sides_0",
        [STATE, FACE, FACE],
        [scale, select, partial, new_low, new_high, flat_a, flat_b],
    )
    state, *tables = call(
        finish_kernel,
        "finish_0",
        TABLES,
        [scale, select, partial, packed_low, packed_high, deep_a, deep_b, flat_a, relayed, z_low, z_high],
    )
    own, sends = tables[:2], tables[2:]
    flat_a = exchange(sends[0], "dev", 0)
    flat_b = exchange(sends[1], "dev", 1)
    deep_a = exchange(sends[2], "grp", 0)
    deep_b = exchange(sends[3], "grp", 1)
    (partial,) = call(inner_kernel, "inner_1", [STATE], [state, scale], 4 << 20)
    (blocks,) = call(
        sides_kernel,
        "sides_1",
        [fields.shape],
        [scale, select, partial, *own, flat_a, flat_b],
        scratch=[pltpu.VMEM(SPARE, jnp.float32)],
    )
    return pl.pallas_call(
        last_kernel,
        name="finish_1",
        compiler_params=SMALL,
        out_shape=shaped(fields.shape),
        in_specs=[spec(VECTOR)] * 7,
        out_specs=spec(pl.ANY),
        scratch_shapes=[
            pltpu.VMEM((2, 2, ROWS, HALF), jnp.float32),
            pltpu.VMEM(fields.shape, jnp.float32),
            pltpu.SemaphoreType.DMA((SLOTS,)),
        ],
    )(scale, select, blocks, *own, deep_a, deep_b)


def solution(mesh):
    in_specs = (
        P(("grp", "dev"), None, None, None),
        P(("grp", "dev")),
        P(("grp", "dev")),
        P(("grp", "dev"), None),
        P(("grp", "dev")),
    )
    out_specs = P(("grp", "dev"), None, None, None)
    return jax.shard_map(body, mesh=mesh, in_specs=in_specs, out_specs=out_specs, check_vma=False)
```

```python
import math

import jax
import jax.numpy as jnp
from jax import lax
from jax.experimental import pallas as pl
from jax.experimental.pallas import tpu as pltpu
from jax.sharding import PartitionSpec as P

NPHASE = 4
NCONC = 2
NFIELD = NPHASE + NCONC
EDGE = 16
PLANE = EDGE * EDGE
HALF = PLANE // 2
GROUPS = HALF // EDGE
SLOTS = 4
ROWS = NFIELD * SLOTS

phase_rate = 0.05
closure = 0.1
coupling = (0.5, -0.5, 1.0, -1.0)
conc_rates = (0.08, 0.04)

STATE = (2, EDGE * ROWS, HALF)
SPARE = (2, (EDGE + 1) * ROWS, HALF)
FACE = (ROWS, PLANE)
SIDE = (3, ROWS, PLANE)
SOURCES = 4
PARTS = 2
SELECT = (3, 2 * ROWS, PARTS * SOURCES * ROWS)


def swapped_order(dev):
    return dev // 4 % 2 == 1


def partners(axis, offset):
    sizes = (lax.axis_size("grp"), lax.axis_size("dev"))
    along = ("grp", "dev").index(axis)
    route = []
    for grp in range(sizes[0]):
        for dev in range(sizes[1]):
            own = (grp, dev)
            start = offset(dev) if callable(offset) else offset
            partner = list(own)
            partner[along] += 1 if (own[along] - start) % 2 == 0 else -1
            if not 0 <= partner[along] < sizes[along]:
                partner = list(own)
                partner[1 - along] ^= 1
                if partner[1 - along] >= sizes[1 - along]:
                    partner = list(own)
            route.append((grp * sizes[1] + dev, partner[0] * sizes[1] + partner[1]))
    return route


def exchange(block, axis, offset):
    return lax.ppermute(block, ("grp", "dev"), partners(axis, offset))


def iota(shape, dim):
    return lax.broadcasted_iota(jnp.int32, shape, dim)


def plane_at(ref, x):
    rows = pl.ds(x * ROWS, ROWS)
    return ref[0, rows, :], ref[1, rows, :]


def turned(value, shift):
    shift %= HALF
    return pltpu.roll(value, shift, 1) if shift else value


class Packer:
    def __init__(self):
        lane = iota((ROWS, HALF), 1)
        self.lane, self.group, self.place = lane, lane // EDGE, lane % EDGE
        self.y = [[None, None], [None, None]]
        self.z = [[None, None], [None, None]]

    def add_y(self, x, left, right):
        odd, half, at = x % 2, x // GROUPS, x % GROUPS
        ends = turned(jnp.where(self.lane < EDGE, left, right), EDGE * at)
        taken = (self.group == at) | (self.group == (at + GROUPS - 1) % GROUPS)
        before = self.y[half][odd]
        self.y[half][odd] = ends if before is None else jnp.where(taken, ends, before)

    def add_z(self, x, left, right):
        at = EDGE - 1 - x
        odd = at % 2
        taken = (self.place == at) | (self.place == (at + EDGE - 1) % EDGE)
        for h, value in enumerate((left, right)):
            moved = turned(value, at)
            before = self.z[h][odd]
            self.z[h][odd] = moved if before is None else jnp.where(taken, moved, before)

    def y_tables(self, h):
        even, (first, second) = self.group % 2 == 0, self.y[h]
        return jnp.where(even, first, second), turned(jnp.where(even, second, first), EDGE)

    def z_tables(self, h):
        even, (first, second) = self.place % 2 == 0, self.z[h]
        return jnp.where(even, first, second), turned(jnp.where(even, second, first), 1 - EDGE)


def write_tables(packer, state, own):
    low, high = own
    for h in range(2):
        lanes = pl.ds(h * HALF, HALF)
        for ref, x in ((low, 0), (high, EDGE - 1)):
            ref[0, :, lanes] = state[h, pl.ds(x * ROWS, ROWS), :]
        for ref, table in zip(own, packer.y_tables(h)):
            ref[1, :, lanes] = table


def emit_faces(own, sends):
    low, high = own
    flat_a, flat_b, deep_first, deep_second = sends
    even = even_place("dev")
    for face in range(2):
        flat_a[face] = jnp.where(even, high[face], low[face])
        flat_b[face] = jnp.where(even, low[face], high[face])
    upper = even_place("grp") != swapped_order(lax.axis_index("dev"))
    deep_first[...] = jnp.where(upper, high[2], low[2])
    deep_second[...] = jnp.where(upper, low[2], high[2])


def fill_slot(state, slot, block, first=0, count=EDGE):
    for f in range(NFIELD):
        value = block(f)
        for h in range(2):
            rows = pl.ds(first * ROWS + f * SLOTS + slot, count, stride=ROWS)
            state[h, rows, :] = value[:, h * HALF : (h + 1) * HALF]


def slot_rows():
    return iota(FACE, 0) % SLOTS


def shifted(value, rows):
    rows %= ROWS
    return pltpu.roll(value, rows, 0) if rows else value


def gathered(tables, slot):
    rows = slot_rows()
    out = shifted(tables[0], -slot)
    for number in range(1, len(tables)):
        out = jnp.where(rows == number, shifted(tables[number], number - slot), out)
    return out


def squeezed(table):
    tile = 2 * SLOTS
    rows = iota((tile, PLANE), 0) % SLOTS
    first, second, third = (table[number * tile : (number + 1) * tile] for number in range(3))
    between = jnp.where(rows == 1, pltpu.roll(second, 1, 0), pltpu.roll(second, tile - 1, 0))
    return jnp.concatenate([jnp.where((rows == 1) | (rows == 2), between, first), third], axis=0)


def stretched(value):
    tile = 2 * SLOTS
    rows = iota((tile, PLANE), 0) % SLOTS
    first, third = value[:tile], value[tile:]
    second = jnp.where(rows == 0, pltpu.roll(first, tile - 1, 0), pltpu.roll(first, 1, 0))
    return jnp.concatenate([first, second, third], axis=0)


def scattered(table, number, slot):
    return shifted(table, slot - number)


def even_place(axis):
    return lax.rem(lax.axis_index(axis), 2) == 0


def block_kernel(mask_dev, fields, low, high, to_dev, to_grp):
    last, size = SLOTS - 1, NFIELD * EDGE
    for f in range(NFIELD):
        to_dev[f * EDGE : (f + 1) * EDGE] = fields[last, f]
        to_grp[f * EDGE : (f + 1) * EDGE] = fields[0, f]
    rows, even = slot_rows(), even_place("grp")
    table = jnp.where(rows == 0, jnp.where(even, low[2], high[2]), jnp.where(even, high[2], low[2]))
    to_grp[size : size + ROWS] = jnp.where(rows == SLOTS - 1, mask_dev[...], table)


def faces_kernel(mask_dev, mask_grp, low, high, faces, faces_dev, *outs):
    new_low, new_high, flat_a, flat_b, deep_b = outs
    rows, last = slot_rows(), SLOTS - 1
    first_rows = (rows == 0) & (mask_grp[...] > 0.5)
    last_rows = (rows == last) & (mask_dev[...] > 0.5)
    even = even_place("grp")
    got_first, got_last = faces[:ROWS], faces_dev[:ROWS]
    got_z, got_last_z = stretched(faces[ROWS:]), stretched(faces_dev[ROWS:])
    for side, (raw, new) in enumerate(((low, new_low), (high, new_high))):
        for axis in range(2):
            number = 2 * axis + side
            table = jnp.where(first_rows, scattered(got_first, number, 0), raw[axis])
            new[axis] = jnp.where(last_rows, scattered(got_last, number, last), table)
        table = jnp.where(first_rows & (even if side == 0 else ~even), got_z, raw[2])
        new[2] = jnp.where(last_rows, scattered(got_last_z, side * last, last), table)
    even_dev = even_place("dev")
    for axis in range(2):
        flat_a[axis] = jnp.where(even_dev, new_high[axis], new_low[axis])
        flat_b[axis] = jnp.where(even_dev, new_low[axis], new_high[axis])
    flat_a[2] = got_z
    deep_b[...] = jnp.where(even, new_low[2], new_high[2])


def cos_quarter(number):
    turn = number & 7
    size = jnp.where((turn & 3) == 0, 1.0, jnp.where((turn & 3) == 2, 0.0, math.sqrt(0.5)))
    return jnp.where((turn > 2) & (turn < 6), -size, size)


def plan_kernel(neighbors, orient, scale, select):
    shape = (ROWS, HALF)
    slot, field, column = iota(shape, 0) % SLOTS, iota(shape, 0) // SLOTS, iota(shape, 1)
    grp, dev = lax.axis_index("grp"), lax.axis_index("dev")
    rank = grp * lax.axis_size("dev") + dev

    def by_slot(values):
        rows = values[0]
        for number in range(1, SLOTS):
            rows = jnp.where(slot == number, values[number], rows)
        return rows

    spread = []
    for number in range(SLOTS):
        turn = 0.5 * cos_quarter(orient[number])
        lift = 0.5 * cos_quarter(orient[number] + 6)
        spread.append((1.0 + turn, 1.0 - turn, 1.0 + lift))
    conc = jnp.where(field == NPHASE, conc_rates[0], conc_rates[1])
    weights = [jnp.where(field < NPHASE, phase_rate * by_slot([own[axis] for own in spread]), conc) for axis in range(3)]
    for axis in range(3):
        scale[axis] = weights[axis]
    scale[3] = 1.0 - 2.0 * (weights[0] + weights[1] + weights[2])
    for face in range(6):
        first = []
        came = 2 + lax.rem(lax.rem(dev if face < 4 else grp, 2) + face % 2 + 1, 2)
        for number in range(SLOTS):
            target = neighbors[number, face]
            source = jnp.where(target < 0, face % 2, jnp.where(target // SLOTS == rank, 1 - face % 2, came))
            first.append(source * ROWS + jnp.where(target < 0, number, target & (SLOTS - 1)))
        chosen = jnp.where(column == by_slot(first) + field * SLOTS, 1.0, 0.0)[:, : SOURCES * ROWS]
        rows = pl.ds(face % 2 * ROWS, ROWS)
        for part in range(PARTS):
            select[face // 2, rows, pl.ds(part * SOURCES * ROWS, SOURCES * ROWS)] = chosen


def start_kernel(fields, neighbors, orient, *refs):
    fetched, low, high, faces_grp, faces_dev, scale, select = refs[:7]
    state, near, turn, arrived = refs[7:]
    scalars = ((neighbors, near), (orient, turn))
    parts = [pl.ds(first, EDGE // 2) for first in (0, EDGE // 2)]
    blocks = tuple((fields.at[:, :, part], fetched.at[:, :, part]) for part in parts)
    copies = [pltpu.make_async_copy(*pair, arrived.at[number]) for number, pair in enumerate((*scalars, *blocks))]
    for copy in copies:
        copy.start()
    for copy in copies[: len(scalars)]:
        copy.wait()
    plan_kernel(near, turn, scale, select)
    packer = Packer()
    for number, part in enumerate(parts):
        copies[len(scalars) + number].wait()
        first = number * (EDGE // 2)
        for slot in range(SLOTS):
            fill_slot(state, slot, lambda f: fetched[slot, f, part], first, EDGE // 2)
        for x in range(first, first + EDGE // 2):
            packer.add_y(x, *plane_at(state, x))
            packer.add_z(x, *plane_at(state, x))
    write_tables(packer, state, (low, high))
    for h in range(2):
        for ref, table in zip((low, high), packer.z_tables(h)):
            ref[2, :, h * HALF : (h + 1) * HALF] = table
    faces_grp[:ROWS] = gathered([low[0], high[0], low[1], high[1]], 0)
    faces_grp[ROWS:] = squeezed(jnp.where(even_place("grp"), high[2], low[2]))
    faces_dev[:ROWS] = gathered([low[0], high[0], low[1], high[1]], SLOTS - 1)
    faces_dev[ROWS:] = squeezed(gathered([low[2], low[2], low[2], high[2]], SLOTS - 1))


def first_inner_kernel(mask_dev, mask_grp, scale, fields, block_dev, block_grp, faces, low, high, new_low, new_high, *refs):
    partial, got_deep, relayed, z_low, z_high, state = refs
    size = NFIELD * EDGE
    swap_dev, swap_grp = mask_dev[...] > 0.5, mask_grp[...] > 0.5

    def block(slot):
        def of(f):
            value = fields[slot, f]
            if slot == 0:
                value = jnp.where(swap_grp[:EDGE], block_grp[f * EDGE : (f + 1) * EDGE], value)
            if slot == SLOTS - 1:
                value = jnp.where(swap_dev[:EDGE], block_dev[f * EDGE : (f + 1) * EDGE], value)
            return value

        return of

    for slot in range(SLOTS):
        fill_slot(state, slot, block(slot))
    rows, even = slot_rows(), even_place("grp")
    first_rows = (rows == 0) & swap_grp
    other = block_grp[size : size + ROWS]
    got = jnp.where((rows == 0) | (rows == SLOTS - 1), stretched(faces[ROWS:]), other)
    got_deep[...] = jnp.where(first_rows, jnp.where(even, low[2], high[2]), got)
    relayed[...] = jnp.where(rows == SLOTS - 1, jnp.broadcast_to(other[SLOTS - 1 : SLOTS], FACE), 0.0)
    z_low[...] = jnp.where(first_rows & ~even, other, new_low[2])
    z_high[...] = jnp.where(first_rows & even, other, new_high[2])
    inner_kernel(state, scale, partial)


def inner_kernel(state, scale, partial):
    lane = iota((ROWS, HALF), 1)
    start_y, end_y = lane < EDGE, lane >= HALF - EDGE
    start_z, end_z = lane % EDGE == 0, lane % EDGE == EDGE - 1
    weight_x, weight_y, weight_z, weight = (scale[number] for number in range(4))
    tile = 2 * SLOTS
    planes = {0: plane_at(state, 0)}
    for x in range(EDGE):
        if x + 1 < EDGE:
            planes[x + 1] = plane_at(state, x + 1)
        left, right = planes[x]
        up = [turned(half, EDGE) for half in (left, right)]
        down = [turned(half, -EDGE) for half in (left, right)]
        sum_y = (
            jnp.where(start_y, 0.0, up[0]) + jnp.where(end_y, down[1], down[0]),
            jnp.where(start_y, up[0], up[1]) + jnp.where(end_y, 0.0, down[1]),
        )
        for h, half in enumerate((left, right)):
            sum_z = jnp.where(start_z, 0.0, turned(half, 1)) + jnp.where(end_z, 0.0, turned(half, -1))
            if x == 0:
                sum_x = planes[1][h]
            elif x == EDGE - 1:
                sum_x = planes[x - 1][h]
            else:
                sum_x = planes[x - 1][h] + planes[x + 1][h]
            flow = weight * half + weight_x * sum_x + weight_y * sum_y[h] + weight_z * sum_z
            phases, conc = (half[:tile], half[tile : 2 * tile]), half[2 * tile :]
            drive = conc - pltpu.roll(conc, SLOTS, 0)
            total = phases[0] + phases[1]
            total = total + pltpu.roll(total, SLOTS, 0)
            tail = (phase_rate * closure) * (1.0 - total)
            rows = x * ROWS
            for number, value in enumerate(phases):
                gain = value * (1.0 - value) * (coupling[2 * number] * drive + (2.0 * value - 1.0))
                part = flow[number * tile : (number + 1) * tile]
                partial[h, pl.ds(rows + number * tile, tile), :] = part + (phase_rate * gain + tail)
            partial[h, pl.ds(rows + 2 * tile, tile), :] = flow[2 * tile :]


def ghosts_of(axis, scale, select, tables):
    tables = jnp.concatenate(tables, axis=0)
    near = tables.astype(jnp.bfloat16)
    rest = (tables - near.astype(jnp.float32)).astype(jnp.bfloat16)
    both = jnp.concatenate([near, rest], axis=0)
    pair = jnp.dot(select[axis].astype(jnp.bfloat16), both, preferred_element_type=jnp.float32)
    weight = jnp.concatenate([scale[axis]] * 2, axis=1)
    return weight * pair[:ROWS], weight * pair[ROWS:]


def side_by_side(low, high, even):
    return jnp.where(even, low, high), jnp.where(even, high, low)


def sides_kernel(scale, select, partial, low, high, flat_a, flat_b, *refs):
    first_step = len(refs) == 3
    done = refs[0] if first_step else refs[1]
    packer = Packer()
    sources = (low, high, flat_a, flat_b)
    x_low, x_high = ghosts_of(0, scale, select, [ref[0] for ref in sources])
    y_low, y_high = ghosts_of(1, scale, select, [ref[1] for ref in sources])
    lane = iota((ROWS, HALF), 1)
    inside = (lane < EDGE, lane >= HALF - EDGE)
    even = (lane // EDGE) % 2 == 0
    pairs = []
    for h in range(2):
        lanes = slice(h * HALF, (h + 1) * HALF)
        pairs.append(side_by_side(y_low[:, lanes], turned(y_high[:, lanes], -EDGE), even))
    for x in range(EDGE):
        ends = turned(pairs[x // GROUPS][x % 2], -EDGE * (x % GROUPS))
        halves = []
        for h, value in enumerate(plane_at(partial, x)):
            value = value + jnp.where(inside[h], ends, 0.0)
            if x == 0:
                value = value + x_low[:, h * HALF : (h + 1) * HALF]
            if x == EDGE - 1:
                value = value + x_high[:, h * HALF : (h + 1) * HALF]
            done[h, pl.ds(x * ROWS, ROWS), :] = value
            halves.append(value)
        if first_step:
            packer.add_z(x, *halves)
    if first_step:
        for h in range(2):
            for ref, table in zip(refs[1:], packer.z_tables(h)):
                ref[:, h * HALF : (h + 1) * HALF] = table
    else:
        blocks = refs[0]
        for slot in range(SLOTS):
            for f in range(NFIELD):
                for h in range(2):
                    rows = pl.ds(f * SLOTS + slot, EDGE, stride=ROWS)
                    blocks[slot, f, :, h * HALF : (h + 1) * HALF] = done[h, rows, :]


def z_pairs(z_low, z_high):
    even = iota((ROWS, HALF), 1) % 2 == 0
    halves = [slice(h * HALF, (h + 1) * HALF) for h in range(2)]
    return [side_by_side(z_low[:, lanes], turned(z_high[:, lanes], EDGE - 1), even) for lanes in halves]


def ends_of(shape):
    place = iota(shape, 1) % EDGE
    return (place == 0) | (place == EDGE - 1)


def finish_kernel(
    scale, select, partial, packed_low, packed_high, known, deep_b, flat_a, relayed, z_low, z_high, done, low, high, *sends
):
    deep_a = jnp.where(relayed[...] > 0.5, flat_a[2], known[...])
    ghosts = ghosts_of(2, scale, select, [z_low[...], z_high[...], deep_a, deep_b[...]])
    pairs = z_pairs(*ghosts)
    ends = ends_of((ROWS, HALF))
    packer = Packer()
    for x in range(EDGE):
        halves, at = [], EDGE - 1 - x
        for h, value in enumerate(plane_at(partial, x)):
            value = value + jnp.where(ends, turned(pairs[h][at % 2], -at), 0.0)
            done[h, pl.ds(x * ROWS, ROWS), :] = value
            halves.append(value)
        packer.add_y(x, *halves)
    write_tables(packer, done, (low, high))
    low[2] = packed_low[...] + ghosts[0]
    high[2] = packed_high[...] + ghosts[1]
    emit_faces((low, high), sends)


def last_kernel(scale, select, partial, low, high, deep_first, deep_second, result, rows_of, blocks, sent):
    first, second, swapped = deep_first[...], deep_second[...], swapped_order(lax.axis_index("dev"))
    tables = [low[2], high[2], jnp.where(swapped, second, first), jnp.where(swapped, first, second)]
    for h, pair in enumerate(z_pairs(*ghosts_of(2, scale, select, tables))):
        for odd in range(2):
            rows_of[h, odd] = pair[odd]
    shape = (EDGE, HALF)
    ends, even = ends_of(shape), iota(shape, 0) % 2 == 0
    copies = []
    for slot in range(SLOTS):
        for f in range(NFIELD):
            row = pl.ds(f * SLOTS + slot, 1)
            for h in range(2):
                both = [jnp.broadcast_to(rows_of[h, odd, row, :], shape) for odd in (1, 0)]
                ghost = pltpu.roll(jnp.where(even, *both), HALF - EDGE + 1, 1, stride=1, stride_axis=0)
                lanes = pl.ds(h * HALF, HALF)
                blocks[slot, f, :, lanes] = partial[slot, f, :, lanes] + jnp.where(ends, ghost, 0.0)
        copy = pltpu.make_async_copy(blocks.at[slot], result.at[slot], sent.at[slot])
        copy.start()
        copies.append(copy)
    for copy in copies:
        copy.wait()


def spec(space):
    return pl.BlockSpec(memory_space=space)


VECTOR = pltpu.VMEM
SMALL = pltpu.CompilerParams(vmem_limit_bytes=8 << 20)
FLAT = (2, ROWS, PLANE)
TABLES = (STATE, SIDE, SIDE, FLAT, FLAT, FACE, FACE)
EARLY = (ROWS + 4 * SLOTS, PLANE)
TO_DEV = (NFIELD * EDGE, PLANE)
TO_GRP = (NFIELD * EDGE + ROWS, PLANE)


def shaped(shape):
    return jax.ShapeDtypeStruct(shape, jnp.float32)


def cost(flops):
    return pl.CostEstimate(flops=flops, bytes_accessed=min(flops, 2 << 20), transcendentals=0)


def call(kernel, name, shapes, vectors, flops=1 << 20, scratch=()):
    return pl.pallas_call(
        kernel,
        name=name,
        compiler_params=SMALL,
        out_shape=[shaped(shape) for shape in shapes],
        in_specs=[spec(VECTOR)] * len(vectors),
        out_specs=[spec(VECTOR)] * len(shapes),
        scratch_shapes=list(scratch),
        cost_estimate=cost(flops),
    )(*vectors)


def start(arguments):
    shapes = (arguments[0].shape, SIDE, SIDE, EARLY, EARLY, (4, ROWS, HALF), SELECT)
    return pl.pallas_call(
        start_kernel,
        name="start",
        compiler_params=SMALL,
        out_shape=[shaped(shape) for shape in shapes],
        in_specs=[spec(pl.ANY)] * len(arguments),
        out_specs=[spec(VECTOR)] * len(shapes),
        scratch_shapes=[
            pltpu.VMEM(SPARE, jnp.float32),
            *(pltpu.SMEM(array.shape, jnp.int32) for array in arguments[1:]),
            pltpu.SemaphoreType.DMA((len(arguments) + 1,)),
        ],
    )(*(pltpu.with_memory_space_constraint(array, pltpu.HBM) for array in arguments))


def mask(flag):
    return jnp.broadcast_to(jnp.where(flag == 1, 1.0, 0.0).reshape(1, 1), FACE)


def body(fields, swap_dev, swap_grp, neighbors, orient):
    fields, low, high, faces, faces_dev, scale, select = start((fields, neighbors, orient))
    swap_dev, faces = lax.optimization_barrier((swap_dev, faces))
    faces = exchange(faces, "grp", 0)
    faces_dev = exchange(faces_dev, "dev", 0)
    mask_dev = mask(swap_dev)
    to_dev, to_grp = call(block_kernel, "blocks", [TO_DEV, TO_GRP], [mask_dev, fields, low, high], 1 << 28)
    swap_grp, to_grp = lax.optimization_barrier((swap_grp, to_grp))
    mask_grp = mask(swap_grp)
    block_grp = exchange(to_grp, "grp", 0)
    block_dev = exchange(to_dev, "dev", 0)
    new_low, new_high, *sends = call(
        faces_kernel,
        "faces",
        [SIDE, SIDE, SIDE, FLAT, FACE],
        [mask_dev, mask_grp, low, high, faces, faces_dev],
        1 << 28,
    )
    flat_a = exchange(sends[0], "dev", 0)
    flat_b = exchange(sends[1], "dev", 1)
    deep_b = exchange(sends[2], "grp", 1)
    partial, deep_a, relayed, z_low, z_high = call(
        first_inner_kernel,
        "inner_0",
        [STATE, FACE, FACE, FACE, FACE],
        [mask_dev, mask_grp, scale, fields, block_dev, block_grp, faces, low, high, new_low, new_high],
        4 << 20,
        [pltpu.VMEM(SPARE, jnp.float32)],
    )
    partial, packed_low, packed_high = call(
        sides_kernel,
        "sides_0",
        [STATE, FACE, FACE],
        [scale, select, partial, new_low, new_high, flat_a, flat_b],
    )
    state, *tables = call(
        finish_kernel,
        "finish_0",
        TABLES,
        [scale, select, partial, packed_low, packed_high, deep_a, deep_b, flat_a, relayed, z_low, z_high],
    )
    own, sends = tables[:2], tables[2:]
    flat_a = exchange(sends[0], "dev", 0)
    flat_b = exchange(sends[1], "dev", 1)
    deep_first = exchange(sends[2], "grp", lambda dev: 1 if swapped_order(dev) else 0)
    deep_second = exchange(sends[3], "grp", lambda dev: 0 if swapped_order(dev) else 1)
    (partial,) = call(inner_kernel, "inner_1", [STATE], [state, scale], 4 << 20)
    (blocks,) = call(
        sides_kernel,
        "sides_1",
        [fields.shape],
        [scale, select, partial, *own, flat_a, flat_b],
        scratch=[pltpu.VMEM(SPARE, jnp.float32)],
    )
    return pl.pallas_call(
        last_kernel,
        name="finish_1",
        compiler_params=SMALL,
        out_shape=shaped(fields.shape),
        in_specs=[spec(VECTOR)] * 7,
        out_specs=spec(pl.ANY),
        scratch_shapes=[
            pltpu.VMEM((2, 2, ROWS, HALF), jnp.float32),
            pltpu.VMEM(fields.shape, jnp.float32),
            pltpu.SemaphoreType.DMA((SLOTS,)),
        ],
    )(scale, select, blocks, *own, deep_first, deep_second)


def solution(mesh):
    in_specs = (
        P(("grp", "dev"), None, None, None),
        P(("grp", "dev")),
        P(("grp", "dev")),
        P(("grp", "dev"), None),
        P(("grp", "dev")),
    )
    out_specs = P(("grp", "dev"), None, None, None)
    return jax.shard_map(body, mesh=mesh, in_specs=in_specs, out_specs=out_specs, check_vma=False)
```

```python
import math

import jax
import jax.numpy as jnp
from jax import lax
from jax.experimental import pallas as pl
from jax.experimental.pallas import tpu as pltpu
from jax.sharding import PartitionSpec as P

NPHASE = 4
NCONC = 2
NFIELD = NPHASE + NCONC
EDGE = 16
PLANE = EDGE * EDGE
HALF = PLANE // 2
GROUPS = HALF // EDGE
SLOTS = 4
ROWS = NFIELD * SLOTS

phase_rate = 0.05
closure = 0.1
coupling = (0.5, -0.5, 1.0, -1.0)
conc_rates = (0.08, 0.04)

STATE = (2, EDGE * ROWS, HALF)
SPARE = (2, (EDGE + 1) * ROWS, HALF)
FACE = (ROWS, PLANE)
SIDE = (3, ROWS, PLANE)
SOURCES = 4
PARTS = 2
SELECT = (3, 2 * ROWS, PARTS * SOURCES * ROWS)


def swapped_order(dev):
    return dev // 4 % 2 == 1


def partners(axis, offset):
    sizes = (lax.axis_size("grp"), lax.axis_size("dev"))
    along = ("grp", "dev").index(axis)
    route = []
    for grp in range(sizes[0]):
        for dev in range(sizes[1]):
            own = (grp, dev)
            start = offset(dev) if callable(offset) else offset
            partner = list(own)
            partner[along] += 1 if (own[along] - start) % 2 == 0 else -1
            if not 0 <= partner[along] < sizes[along]:
                partner = list(own)
                partner[1 - along] ^= 1
                if partner[1 - along] >= sizes[1 - along]:
                    partner = list(own)
            route.append((grp * sizes[1] + dev, partner[0] * sizes[1] + partner[1]))
    return route


def exchange(block, axis, offset):
    return lax.ppermute(block, ("grp", "dev"), partners(axis, offset))


def iota(shape, dim):
    return lax.broadcasted_iota(jnp.int32, shape, dim)


def plane_at(ref, x):
    rows = pl.ds(x * ROWS, ROWS)
    return ref[0, rows, :], ref[1, rows, :]


def turned(value, shift):
    shift %= HALF
    return pltpu.roll(value, shift, 1) if shift else value


class Packer:
    def __init__(self):
        lane = iota((ROWS, HALF), 1)
        self.lane, self.group, self.place = lane, lane // EDGE, lane % EDGE
        self.y = [[None, None], [None, None]]
        self.z = [[None, None], [None, None]]

    def add_y(self, x, left, right):
        odd, half, at = x % 2, x // GROUPS, x % GROUPS
        ends = turned(jnp.where(self.lane < EDGE, left, right), EDGE * at)
        taken = (self.group == at) | (self.group == (at + GROUPS - 1) % GROUPS)
        before = self.y[half][odd]
        self.y[half][odd] = ends if before is None else jnp.where(taken, ends, before)

    def add_z(self, x, left, right):
        at = EDGE - 1 - x
        odd = at % 2
        taken = (self.place == at) | (self.place == (at + EDGE - 1) % EDGE)
        for h, value in enumerate((left, right)):
            moved = turned(value, at)
            before = self.z[h][odd]
            self.z[h][odd] = moved if before is None else jnp.where(taken, moved, before)

    def y_tables(self, h):
        even, (first, second) = self.group % 2 == 0, self.y[h]
        return jnp.where(even, first, second), turned(jnp.where(even, second, first), EDGE)

    def z_tables(self, h):
        even, (first, second) = self.place % 2 == 0, self.z[h]
        return jnp.where(even, first, second), turned(jnp.where(even, second, first), 1 - EDGE)


def write_tables(packer, state, own):
    low, high = own
    for h in range(2):
        lanes = pl.ds(h * HALF, HALF)
        for ref, x in ((low, 0), (high, EDGE - 1)):
            ref[0, :, lanes] = state[h, pl.ds(x * ROWS, ROWS), :]
        for ref, table in zip(own, packer.y_tables(h)):
            ref[1, :, lanes] = table


def emit_faces(own, sends):
    low, high = own
    flat_a, flat_b, deep_first, deep_second = sends
    even = even_place("dev")
    for face in range(2):
        flat_a[face] = jnp.where(even, high[face], low[face])
        flat_b[face] = jnp.where(even, low[face], high[face])
    upper = even_place("grp") != swapped_order(lax.axis_index("dev"))
    deep_first[...] = jnp.where(upper, high[2], low[2])
    deep_second[...] = jnp.where(upper, low[2], high[2])


def fill_slot(state, slot, block, first=0, count=EDGE):
    for f in range(NFIELD):
        value = block(f)
        for h in range(2):
            rows = pl.ds(first * ROWS + f * SLOTS + slot, count, stride=ROWS)
            state[h, rows, :] = value[:, h * HALF : (h + 1) * HALF]


def slot_rows():
    return iota(FACE, 0) % SLOTS


def shifted(value, rows):
    rows %= ROWS
    return pltpu.roll(value, rows, 0) if rows else value


def gathered(tables, slot):
    rows = slot_rows()
    out = shifted(tables[0], -slot)
    for number in range(1, len(tables)):
        out = jnp.where(rows == number, shifted(tables[number], number - slot), out)
    return out


def squeezed(table):
    tile = 2 * SLOTS
    rows = iota((tile, PLANE), 0) % SLOTS
    first, second, third = (table[number * tile : (number + 1) * tile] for number in range(3))
    between = jnp.where(rows == 1, pltpu.roll(second, 1, 0), pltpu.roll(second, tile - 1, 0))
    return jnp.concatenate([jnp.where((rows == 1) | (rows == 2), between, first), third], axis=0)


def stretched(value):
    tile = 2 * SLOTS
    rows = iota((tile, PLANE), 0) % SLOTS
    first, third = value[:tile], value[tile:]
    second = jnp.where(rows == 0, pltpu.roll(first, tile - 1, 0), pltpu.roll(first, 1, 0))
    return jnp.concatenate([first, second, third], axis=0)


def scattered(table, number, slot):
    return shifted(table, slot - number)


def even_place(axis):
    return lax.rem(lax.axis_index(axis), 2) == 0


def block_kernel(mask_dev, fields, low, high, to_dev, to_grp):
    last, size = SLOTS - 1, NFIELD * EDGE
    for f in range(NFIELD):
        to_dev[f * EDGE : (f + 1) * EDGE] = fields[last, f]
        to_grp[f * EDGE : (f + 1) * EDGE] = fields[0, f]
    rows, even = slot_rows(), even_place("grp")
    table = jnp.where(rows == 0, jnp.where(even, low[2], high[2]), jnp.where(even, high[2], low[2]))
    to_grp[size : size + ROWS] = jnp.where(rows == SLOTS - 1, mask_dev[...], table)


def faces_kernel(mask_dev, mask_grp, low, high, faces, faces_dev, *outs):
    new_low, new_high, flat_a, flat_b, deep_b = outs
    rows, last = slot_rows(), SLOTS - 1
    first_rows = (rows == 0) & (mask_grp[...] > 0.5)
    last_rows = (rows == last) & (mask_dev[...] > 0.5)
    even = even_place("grp")
    got_first, got_last = faces[:ROWS], faces_dev[:ROWS]
    got_z, got_last_z = stretched(faces[ROWS:]), stretched(faces_dev[ROWS:])
    for side, (raw, new) in enumerate(((low, new_low), (high, new_high))):
        for axis in range(2):
            number = 2 * axis + side
            table = jnp.where(first_rows, scattered(got_first, number, 0), raw[axis])
            new[axis] = jnp.where(last_rows, scattered(got_last, number, last), table)
        table = jnp.where(first_rows & (even if side == 0 else ~even), got_z, raw[2])
        new[2] = jnp.where(last_rows, scattered(got_last_z, side * last, last), table)
    even_dev = even_place("dev")
    for axis in range(2):
        flat_a[axis] = jnp.where(even_dev, new_high[axis], new_low[axis])
        flat_b[axis] = jnp.where(even_dev, new_low[axis], new_high[axis])
    flat_a[2] = got_z
    deep_b[...] = jnp.where(even, new_low[2], new_high[2])


def cos_quarter(number):
    turn = number & 7
    size = jnp.where((turn & 3) == 0, 1.0, jnp.where((turn & 3) == 2, 0.0, math.sqrt(0.5)))
    return jnp.where((turn > 2) & (turn < 6), -size, size)


def plan_kernel(neighbors, orient, scale, select):
    shape = (ROWS, HALF)
    slot, field, column = iota(shape, 0) % SLOTS, iota(shape, 0) // SLOTS, iota(shape, 1)
    grp, dev = lax.axis_index("grp"), lax.axis_index("dev")
    rank = grp * lax.axis_size("dev") + dev

    def by_slot(values):
        rows = values[0]
        for number in range(1, SLOTS):
            rows = jnp.where(slot == number, values[number], rows)
        return rows

    spread = []
    for number in range(SLOTS):
        turn = 0.5 * cos_quarter(orient[number])
        lift = 0.5 * cos_quarter(orient[number] + 6)
        spread.append((1.0 + turn, 1.0 - turn, 1.0 + lift))
    conc = jnp.where(field == NPHASE, conc_rates[0], conc_rates[1])
    weights = [jnp.where(field < NPHASE, phase_rate * by_slot([own[axis] for own in spread]), conc) for axis in range(3)]
    for axis in range(3):
        scale[axis] = weights[axis]
    scale[3] = 1.0 - 2.0 * (weights[0] + weights[1] + weights[2])
    for face in range(6):
        first = []
        came = 2 + lax.rem(lax.rem(dev if face < 4 else grp, 2) + face % 2 + 1, 2)
        for number in range(SLOTS):
            target = neighbors[number, face]
            source = jnp.where(target < 0, face % 2, jnp.where(target // SLOTS == rank, 1 - face % 2, came))
            first.append(source * ROWS + jnp.where(target < 0, number, target & (SLOTS - 1)))
        chosen = jnp.where(column == by_slot(first) + field * SLOTS, 1.0, 0.0)[:, : SOURCES * ROWS]
        rows = pl.ds(face % 2 * ROWS, ROWS)
        for part in range(PARTS):
            select[face // 2, rows, pl.ds(part * SOURCES * ROWS, SOURCES * ROWS)] = chosen


def start_kernel(fields, neighbors, orient, *refs):
    fetched, low, high, faces_grp, faces_dev, scale, select = refs[:7]
    state, near, turn, arrived = refs[7:]
    scalars = ((neighbors, near), (orient, turn))
    parts = [pl.ds(first, EDGE // 2) for first in (0, EDGE // 2)]
    pairs = [pl.ds(first, SLOTS // 2) for first in (0, SLOTS // 2)]
    blocks = [(fields.at[pair, :, part], fetched.at[pair, :, part]) for part in parts for pair in pairs]
    copies = [pltpu.make_async_copy(*ends, arrived.at[number]) for number, ends in enumerate((*scalars, *blocks))]
    for number, copy in enumerate(copies):
        copy.start(priority=number % 2)
    for copy in copies[: len(scalars)]:
        copy.wait()
    plan_kernel(near, turn, scale, select)
    packer = Packer()
    for number, part in enumerate(parts):
        for copy in copies[len(scalars) + 2 * number :][:2]:
            copy.wait()
        first = number * (EDGE // 2)
        for slot in range(SLOTS):
            fill_slot(state, slot, lambda f: fetched[slot, f, part], first, EDGE // 2)
        for x in range(first, first + EDGE // 2):
            packer.add_y(x, *plane_at(state, x))
            packer.add_z(x, *plane_at(state, x))
    write_tables(packer, state, (low, high))
    for h in range(2):
        for ref, table in zip((low, high), packer.z_tables(h)):
            ref[2, :, h * HALF : (h + 1) * HALF] = table
    faces_grp[:ROWS] = gathered([low[0], high[0], low[1], high[1]], 0)
    faces_grp[ROWS:] = squeezed(jnp.where(even_place("grp"), high[2], low[2]))
    faces_dev[:ROWS] = gathered([low[0], high[0], low[1], high[1]], SLOTS - 1)
    faces_dev[ROWS:] = squeezed(gathered([low[2], low[2], low[2], high[2]], SLOTS - 1))


def first_inner_kernel(mask_dev, mask_grp, scale, fields, block_dev, block_grp, faces, low, high, new_low, new_high, *refs):
    partial, got_deep, relayed, z_low, z_high, state = refs
    size = NFIELD * EDGE
    swap_dev, swap_grp = mask_dev[...] > 0.5, mask_grp[...] > 0.5

    def block(slot):
        def of(f):
            value = fields[slot, f]
            if slot == 0:
                value = jnp.where(swap_grp[:EDGE], block_grp[f * EDGE : (f + 1) * EDGE], value)
            if slot == SLOTS - 1:
                value = jnp.where(swap_dev[:EDGE], block_dev[f * EDGE : (f + 1) * EDGE], value)
            return value

        return of

    for slot in range(SLOTS):
        fill_slot(state, slot, block(slot))
    rows, even = slot_rows(), even_place("grp")
    first_rows = (rows == 0) & swap_grp
    other = block_grp[size : size + ROWS]
    got = jnp.where((rows == 0) | (rows == SLOTS - 1), stretched(faces[ROWS:]), other)
    got_deep[...] = jnp.where(first_rows, jnp.where(even, low[2], high[2]), got)
    relayed[...] = jnp.where(rows == SLOTS - 1, jnp.broadcast_to(other[SLOTS - 1 : SLOTS], FACE), 0.0)
    z_low[...] = jnp.where(first_rows & ~even, other, new_low[2])
    z_high[...] = jnp.where(first_rows & even, other, new_high[2])
    inner_kernel(state, scale, partial)


def inner_kernel(state, scale, partial):
    lane = iota((ROWS, HALF), 1)
    start_y, end_y = lane < EDGE, lane >= HALF - EDGE
    start_z, end_z = lane % EDGE == 0, lane % EDGE == EDGE - 1
    weight_x, weight_y, weight_z, weight = (scale[number] for number in range(4))
    tile = 2 * SLOTS
    planes = {0: plane_at(state, 0)}
    for x in range(EDGE):
        if x + 1 < EDGE:
            planes[x + 1] = plane_at(state, x + 1)
        left, right = planes[x]
        up = [turned(half, EDGE) for half in (left, right)]
        down = [turned(half, -EDGE) for half in (left, right)]
        sum_y = (
            jnp.where(start_y, 0.0, up[0]) + jnp.where(end_y, down[1], down[0]),
            jnp.where(start_y, up[0], up[1]) + jnp.where(end_y, 0.0, down[1]),
        )
        for h, half in enumerate((left, right)):
            sum_z = jnp.where(start_z, 0.0, turned(half, 1)) + jnp.where(end_z, 0.0, turned(half, -1))
            if x == 0:
                sum_x = planes[1][h]
            elif x == EDGE - 1:
                sum_x = planes[x - 1][h]
            else:
                sum_x = planes[x - 1][h] + planes[x + 1][h]
            flow = weight * half + weight_x * sum_x + weight_y * sum_y[h] + weight_z * sum_z
            phases, conc = (half[:tile], half[tile : 2 * tile]), half[2 * tile :]
            drive = conc - pltpu.roll(conc, SLOTS, 0)
            total = phases[0] + phases[1]
            total = total + pltpu.roll(total, SLOTS, 0)
            tail = (phase_rate * closure) * (1.0 - total)
            rows = x * ROWS
            for number, value in enumerate(phases):
                gain = value * (1.0 - value) * (coupling[2 * number] * drive + (2.0 * value - 1.0))
                part = flow[number * tile : (number + 1) * tile]
                partial[h, pl.ds(rows + number * tile, tile), :] = part + (phase_rate * gain + tail)
            partial[h, pl.ds(rows + 2 * tile, tile), :] = flow[2 * tile :]


def ghosts_of(axis, scale, select, tables):
    tables = jnp.concatenate(tables, axis=0)
    near = tables.astype(jnp.bfloat16)
    rest = (tables - near.astype(jnp.float32)).astype(jnp.bfloat16)
    both = jnp.concatenate([near, rest], axis=0)
    pair = jnp.dot(select[axis].astype(jnp.bfloat16), both, preferred_element_type=jnp.float32)
    weight = jnp.concatenate([scale[axis]] * 2, axis=1)
    return weight * pair[:ROWS], weight * pair[ROWS:]


def side_by_side(low, high, even):
    return jnp.where(even, low, high), jnp.where(even, high, low)


def sides_kernel(scale, select, partial, low, high, flat_a, flat_b, *refs):
    first_step = len(refs) == 3
    done = refs[0] if first_step else refs[1]
    packer = Packer()
    sources = (low, high, flat_a, flat_b)
    x_low, x_high = ghosts_of(0, scale, select, [ref[0] for ref in sources])
    y_low, y_high = ghosts_of(1, scale, select, [ref[1] for ref in sources])
    lane = iota((ROWS, HALF), 1)
    inside = (lane < EDGE, lane >= HALF - EDGE)
    even = (lane // EDGE) % 2 == 0
    pairs = []
    for h in range(2):
        lanes = slice(h * HALF, (h + 1) * HALF)
        pairs.append(side_by_side(y_low[:, lanes], turned(y_high[:, lanes], -EDGE), even))
    for x in range(EDGE):
        ends = turned(pairs[x // GROUPS][x % 2], -EDGE * (x % GROUPS))
        halves = []
        for h, value in enumerate(plane_at(partial, x)):
            value = value + jnp.where(inside[h], ends, 0.0)
            if x == 0:
                value = value + x_low[:, h * HALF : (h + 1) * HALF]
            if x == EDGE - 1:
                value = value + x_high[:, h * HALF : (h + 1) * HALF]
            done[h, pl.ds(x * ROWS, ROWS), :] = value
            halves.append(value)
        if first_step:
            packer.add_z(x, *halves)
    if first_step:
        for h in range(2):
            for ref, table in zip(refs[1:], packer.z_tables(h)):
                ref[:, h * HALF : (h + 1) * HALF] = table
    else:
        blocks = refs[0]
        for slot in range(SLOTS):
            for f in range(NFIELD):
                for h in range(2):
                    rows = pl.ds(f * SLOTS + slot, EDGE, stride=ROWS)
                    blocks[slot, f, :, h * HALF : (h + 1) * HALF] = done[h, rows, :]


def z_pairs(z_low, z_high):
    even = iota((ROWS, HALF), 1) % 2 == 0
    halves = [slice(h * HALF, (h + 1) * HALF) for h in range(2)]
    return [side_by_side(z_low[:, lanes], turned(z_high[:, lanes], EDGE - 1), even) for lanes in halves]


def ends_of(shape):
    place = iota(shape, 1) % EDGE
    return (place == 0) | (place == EDGE - 1)


def finish_kernel(
    scale, select, partial, packed_low, packed_high, known, deep_b, flat_a, relayed, z_low, z_high, done, low, high, *sends
):
    deep_a = jnp.where(relayed[...] > 0.5, flat_a[2], known[...])
    ghosts = ghosts_of(2, scale, select, [z_low[...], z_high[...], deep_a, deep_b[...]])
    pairs = z_pairs(*ghosts)
    ends = ends_of((ROWS, HALF))
    packer = Packer()
    for x in range(EDGE):
        halves, at = [], EDGE - 1 - x
        for h, value in enumerate(plane_at(partial, x)):
            value = value + jnp.where(ends, turned(pairs[h][at % 2], -at), 0.0)
            done[h, pl.ds(x * ROWS, ROWS), :] = value
            halves.append(value)
        packer.add_y(x, *halves)
    write_tables(packer, done, (low, high))
    low[2] = packed_low[...] + ghosts[0]
    high[2] = packed_high[...] + ghosts[1]
    emit_faces((low, high), sends)


def last_kernel(scale, select, partial, low, high, deep_first, deep_second, result, rows_of, blocks, sent):
    first, second, swapped = deep_first[...], deep_second[...], swapped_order(lax.axis_index("dev"))
    tables = [low[2], high[2], jnp.where(swapped, second, first), jnp.where(swapped, first, second)]
    for h, pair in enumerate(z_pairs(*ghosts_of(2, scale, select, tables))):
        for odd in range(2):
            rows_of[h, odd] = pair[odd]
    shape = (EDGE, HALF)
    ends, even = ends_of(shape), iota(shape, 0) % 2 == 0
    copies = []
    for slot in range(SLOTS):
        for f in range(NFIELD):
            row = pl.ds(f * SLOTS + slot, 1)
            for h in range(2):
                both = [jnp.broadcast_to(rows_of[h, odd, row, :], shape) for odd in (1, 0)]
                ghost = pltpu.roll(jnp.where(even, *both), HALF - EDGE + 1, 1, stride=1, stride_axis=0)
                lanes = pl.ds(h * HALF, HALF)
                blocks[slot, f, :, lanes] = partial[slot, f, :, lanes] + jnp.where(ends, ghost, 0.0)
        copy = pltpu.make_async_copy(blocks.at[slot], result.at[slot], sent.at[slot])
        copy.start(priority=slot % 2)
        copies.append(copy)
    for copy in copies:
        copy.wait()


def spec(space):
    return pl.BlockSpec(memory_space=space)


VECTOR = pltpu.VMEM
SMALL = pltpu.CompilerParams(vmem_limit_bytes=8 << 20)
FLAT = (2, ROWS, PLANE)
TABLES = (STATE, SIDE, SIDE, FLAT, FLAT, FACE, FACE)
EARLY = (ROWS + 4 * SLOTS, PLANE)
TO_DEV = (NFIELD * EDGE, PLANE)
TO_GRP = (NFIELD * EDGE + ROWS, PLANE)


def shaped(shape):
    return jax.ShapeDtypeStruct(shape, jnp.float32)


def cost(flops):
    return pl.CostEstimate(flops=flops, bytes_accessed=min(flops, 2 << 20), transcendentals=0)


def call(kernel, name, shapes, vectors, flops=1 << 20, scratch=()):
    return pl.pallas_call(
        kernel,
        name=name,
        compiler_params=SMALL,
        out_shape=[shaped(shape) for shape in shapes],
        in_specs=[spec(VECTOR)] * len(vectors),
        out_specs=[spec(VECTOR)] * len(shapes),
        scratch_shapes=list(scratch),
        cost_estimate=cost(flops),
    )(*vectors)


def start(arguments):
    shapes = (arguments[0].shape, SIDE, SIDE, EARLY, EARLY, (4, ROWS, HALF), SELECT)
    return pl.pallas_call(
        start_kernel,
        name="start",
        compiler_params=SMALL,
        out_shape=[shaped(shape) for shape in shapes],
        in_specs=[spec(pl.ANY)] * len(arguments),
        out_specs=[spec(VECTOR)] * len(shapes),
        scratch_shapes=[
            pltpu.VMEM(SPARE, jnp.float32),
            *(pltpu.SMEM(array.shape, jnp.int32) for array in arguments[1:]),
            pltpu.SemaphoreType.DMA((len(arguments) + 3,)),
        ],
    )(*(pltpu.with_memory_space_constraint(array, pltpu.HBM) for array in arguments))


def mask(flag):
    return jnp.broadcast_to(jnp.where(flag == 1, 1.0, 0.0).reshape(1, 1), FACE)


def body(fields, swap_dev, swap_grp, neighbors, orient):
    fields, low, high, faces, faces_dev, scale, select = start((fields, neighbors, orient))
    swap_dev, faces = lax.optimization_barrier((swap_dev, faces))
    faces = exchange(faces, "grp", 0)
    faces_dev = exchange(faces_dev, "dev", 0)
    mask_dev = mask(swap_dev)
    to_dev, to_grp = call(block_kernel, "blocks", [TO_DEV, TO_GRP], [mask_dev, fields, low, high], 1 << 28)
    swap_grp, to_grp = lax.optimization_barrier((swap_grp, to_grp))
    mask_grp = mask(swap_grp)
    block_grp = exchange(to_grp, "grp", 0)
    block_dev = exchange(to_dev, "dev", 0)
    new_low, new_high, *sends = call(
        faces_kernel,
        "faces",
        [SIDE, SIDE, SIDE, FLAT, FACE],
        [mask_dev, mask_grp, low, high, faces, faces_dev],
        1 << 28,
    )
    flat_a = exchange(sends[0], "dev", 0)
    flat_b = exchange(sends[1], "dev", 1)
    deep_b = exchange(sends[2], "grp", 1)
    partial, deep_a, relayed, z_low, z_high = call(
        first_inner_kernel,
        "inner_0",
        [STATE, FACE, FACE, FACE, FACE],
        [mask_dev, mask_grp, scale, fields, block_dev, block_grp, faces, low, high, new_low, new_high],
        4 << 20,
        [pltpu.VMEM(SPARE, jnp.float32)],
    )
    partial, packed_low, packed_high = call(
        sides_kernel,
        "sides_0",
        [STATE, FACE, FACE],
        [scale, select, partial, new_low, new_high, flat_a, flat_b],
    )
    state, *tables = call(
        finish_kernel,
        "finish_0",
        TABLES,
        [scale, select, partial, packed_low, packed_high, deep_a, deep_b, flat_a, relayed, z_low, z_high],
    )
    own, sends = tables[:2], tables[2:]
    flat_a = exchange(sends[0], "dev", 0)
    flat_b = exchange(sends[1], "dev", 1)
    deep_first = exchange(sends[2], "grp", lambda dev: 1 if swapped_order(dev) else 0)
    deep_second = exchange(sends[3], "grp", lambda dev: 0 if swapped_order(dev) else 1)
    (partial,) = call(inner_kernel, "inner_1", [STATE], [state, scale], 4 << 20)
    (blocks,) = call(
        sides_kernel,
        "sides_1",
        [fields.shape],
        [scale, select, partial, *own, flat_a, flat_b],
        scratch=[pltpu.VMEM(SPARE, jnp.float32)],
    )
    return pl.pallas_call(
        last_kernel,
        name="finish_1",
        compiler_params=SMALL,
        out_shape=shaped(fields.shape),
        in_specs=[spec(VECTOR)] * 7,
        out_specs=spec(pl.ANY),
        scratch_shapes=[
            pltpu.VMEM((2, 2, ROWS, HALF), jnp.float32),
            pltpu.VMEM(fields.shape, jnp.float32),
            pltpu.SemaphoreType.DMA((SLOTS,)),
        ],
    )(scale, select, blocks, *own, deep_first, deep_second)


def solution(mesh):
    in_specs = (
        P(("grp", "dev"), None, None, None),
        P(("grp", "dev")),
        P(("grp", "dev")),
        P(("grp", "dev"), None),
        P(("grp", "dev")),
    )
    out_specs = P(("grp", "dev"), None, None, None)
    return jax.shard_map(body, mesh=mesh, in_specs=in_specs, out_specs=out_specs, check_vma=False)
```

```python
import math

import jax
import jax.numpy as jnp
from jax import lax
from jax.experimental import pallas as pl
from jax.experimental.pallas import tpu as pltpu
from jax.sharding import PartitionSpec as P

NPHASE = 4
NCONC = 2
NFIELD = NPHASE + NCONC
EDGE = 16
PLANE = EDGE * EDGE
HALF = PLANE // 2
GROUPS = HALF // EDGE
SLOTS = 4
ROWS = NFIELD * SLOTS

phase_rate = 0.05
closure = 0.1
coupling = (0.5, -0.5, 1.0, -1.0)
conc_rates = (0.08, 0.04)

STATE = (2, EDGE * ROWS, HALF)
SPARE = (2, (EDGE + 1) * ROWS, HALF)
FACE = (ROWS, PLANE)
SIDE = (3, ROWS, PLANE)
SOURCES = 4
PARTS = 2
SELECT = (2, 2 * ROWS, PARTS * SOURCES * ROWS)
TURNS = (2, 2 * SLOTS, ROWS, HALF)


def swapped_order(dev):
    return dev // 4 % 2 == 1


def partners(axis, offset):
    sizes = (lax.axis_size("grp"), lax.axis_size("dev"))
    along = ("grp", "dev").index(axis)
    route = []
    for grp in range(sizes[0]):
        for dev in range(sizes[1]):
            own = (grp, dev)
            start = offset(dev) if callable(offset) else offset
            partner = list(own)
            partner[along] += 1 if (own[along] - start) % 2 == 0 else -1
            if not 0 <= partner[along] < sizes[along]:
                partner = list(own)
                partner[1 - along] ^= 1
                if partner[1 - along] >= sizes[1 - along]:
                    partner = list(own)
            route.append((grp * sizes[1] + dev, partner[0] * sizes[1] + partner[1]))
    return route


def exchange(block, axis, offset):
    return lax.ppermute(block, ("grp", "dev"), partners(axis, offset))


def iota(shape, dim):
    return lax.broadcasted_iota(jnp.int32, shape, dim)


def plane_at(ref, x):
    rows = pl.ds(x * ROWS, ROWS)
    return ref[0, rows, :], ref[1, rows, :]


def turned(value, shift):
    shift %= HALF
    return pltpu.roll(value, shift, 1) if shift else value


class Packer:
    def __init__(self):
        lane = iota((ROWS, HALF), 1)
        self.lane, self.group, self.place = lane, lane // EDGE, lane % EDGE
        self.y = [[None, None], [None, None]]
        self.z = [[None, None], [None, None]]

    def add_y(self, x, left, right):
        odd, half, at = x % 2, x // GROUPS, x % GROUPS
        ends = turned(jnp.where(self.lane < EDGE, left, right), EDGE * at)
        taken = (self.group == at) | (self.group == (at + GROUPS - 1) % GROUPS)
        before = self.y[half][odd]
        self.y[half][odd] = ends if before is None else jnp.where(taken, ends, before)

    def add_z(self, x, left, right):
        at = EDGE - 1 - x
        odd = at % 2
        taken = (self.place == at) | (self.place == (at + EDGE - 1) % EDGE)
        for h, value in enumerate((left, right)):
            moved = turned(value, at)
            before = self.z[h][odd]
            self.z[h][odd] = moved if before is None else jnp.where(taken, moved, before)

    def y_tables(self, h):
        even, (first, second) = self.group % 2 == 0, self.y[h]
        return jnp.where(even, first, second), turned(jnp.where(even, second, first), EDGE)

    def z_tables(self, h):
        even, (first, second) = self.place % 2 == 0, self.z[h]
        return jnp.where(even, first, second), turned(jnp.where(even, second, first), 1 - EDGE)


def write_tables(packer, state, own):
    low, high = own
    for h in range(2):
        lanes = pl.ds(h * HALF, HALF)
        for ref, x in ((low, 0), (high, EDGE - 1)):
            ref[0, :, lanes] = state[h, pl.ds(x * ROWS, ROWS), :]
        for ref, table in zip(own, packer.y_tables(h)):
            ref[1, :, lanes] = table


def emit_faces(own, sends):
    low, high = own
    flat_a, flat_b, deep_first, deep_second = sends
    even = even_place("dev")
    for face in range(2):
        flat_a[face] = jnp.where(even, high[face], low[face])
        flat_b[face] = jnp.where(even, low[face], high[face])
    upper = even_place("grp") != swapped_order(lax.axis_index("dev"))
    deep_first[...] = jnp.where(upper, high[2], low[2])
    deep_second[...] = jnp.where(upper, low[2], high[2])


def fill_slot(state, slot, block, first=0, count=EDGE):
    for f in range(NFIELD):
        value = block(f)
        for h in range(2):
            rows = pl.ds(first * ROWS + f * SLOTS + slot, count, stride=ROWS)
            state[h, rows, :] = value[:, h * HALF : (h + 1) * HALF]


def slot_rows():
    return iota(FACE, 0) % SLOTS


def shifted(value, rows):
    rows %= ROWS
    return pltpu.roll(value, rows, 0) if rows else value


def gathered(tables, slot):
    rows = slot_rows()
    out = shifted(tables[0], -slot)
    for number in range(1, len(tables)):
        out = jnp.where(rows == number, shifted(tables[number], number - slot), out)
    return out


def squeezed(table):
    tile = 2 * SLOTS
    rows = iota((tile, PLANE), 0) % SLOTS
    first, second, third = (table[number * tile : (number + 1) * tile] for number in range(3))
    between = jnp.where(rows == 1, pltpu.roll(second, 1, 0), pltpu.roll(second, tile - 1, 0))
    return jnp.concatenate([jnp.where((rows == 1) | (rows == 2), between, first), third], axis=0)


def stretched(value):
    tile = 2 * SLOTS
    rows = iota((tile, PLANE), 0) % SLOTS
    first, third = value[:tile], value[tile:]
    second = jnp.where(rows == 0, pltpu.roll(first, tile - 1, 0), pltpu.roll(first, 1, 0))
    return jnp.concatenate([first, second, third], axis=0)


def scattered(table, number, slot):
    return shifted(table, slot - number)


def even_place(axis):
    return lax.rem(lax.axis_index(axis), 2) == 0


def block_kernel(mask_dev, fields, low, high, to_dev, to_grp):
    last, size = SLOTS - 1, NFIELD * EDGE
    for f in range(NFIELD):
        to_dev[f * EDGE : (f + 1) * EDGE] = fields[last, f]
        to_grp[f * EDGE : (f + 1) * EDGE] = fields[0, f]
    rows, even = slot_rows(), even_place("grp")
    table = jnp.where(rows == 0, jnp.where(even, low[2], high[2]), jnp.where(even, high[2], low[2]))
    to_grp[size : size + ROWS] = jnp.where(rows == SLOTS - 1, mask_dev[...], table)


def faces_kernel(mask_dev, mask_grp, low, high, faces, faces_dev, *outs):
    new_low, new_high, flat_a, flat_b, deep_b = outs
    rows, last = slot_rows(), SLOTS - 1
    first_rows = (rows == 0) & (mask_grp[...] > 0.5)
    last_rows = (rows == last) & (mask_dev[...] > 0.5)
    even = even_place("grp")
    got_first, got_last = faces[:ROWS], faces_dev[:ROWS]
    got_z, got_last_z = stretched(faces[ROWS:]), stretched(faces_dev[ROWS:])
    for side, (raw, new) in enumerate(((low, new_low), (high, new_high))):
        for axis in range(2):
            number = 2 * axis + side
            table = jnp.where(first_rows, scattered(got_first, number, 0), raw[axis])
            new[axis] = jnp.where(last_rows, scattered(got_last, number, last), table)
        table = jnp.where(first_rows & (even if side == 0 else ~even), got_z, raw[2])
        new[2] = jnp.where(last_rows, scattered(got_last_z, side * last, last), table)
    even_dev = even_place("dev")
    for axis in range(2):
        flat_a[axis] = jnp.where(even_dev, new_high[axis], new_low[axis])
        flat_b[axis] = jnp.where(even_dev, new_low[axis], new_high[axis])
    flat_a[2] = got_z
    deep_b[...] = jnp.where(even, new_low[2], new_high[2])


def cos_quarter(number):
    turn = number & 7
    size = jnp.where((turn & 3) == 0, 1.0, jnp.where((turn & 3) == 2, 0.0, math.sqrt(0.5)))
    return jnp.where((turn > 2) & (turn < 6), -size, size)


def plan_kernel(neighbors, orient, scale, select, turns):
    shape = (ROWS, HALF)
    slot, field, column = iota(shape, 0) % SLOTS, iota(shape, 0) // SLOTS, iota(shape, 1)
    grp, dev = lax.axis_index("grp"), lax.axis_index("dev")
    rank = grp * lax.axis_size("dev") + dev

    def by_slot(values):
        rows = values[0]
        for number in range(1, SLOTS):
            rows = jnp.where(slot == number, values[number], rows)
        return rows

    spread = []
    for number in range(SLOTS):
        turn = 0.5 * cos_quarter(orient[number])
        lift = 0.5 * cos_quarter(orient[number] + 6)
        spread.append((1.0 + turn, 1.0 - turn, 1.0 + lift))
    conc = jnp.where(field == NPHASE, conc_rates[0], conc_rates[1])
    weights = [jnp.where(field < NPHASE, phase_rate * by_slot([own[axis] for own in spread]), conc) for axis in range(3)]
    for axis in range(3):
        scale[axis] = weights[axis]
    scale[3] = 1.0 - 2.0 * (weights[0] + weights[1] + weights[2])
    for face in range(4, 6):
        where_from = []
        for number in range(SLOTS):
            target = neighbors[number, face]
            where_from.append(jnp.where(target < 0, 2 * SLOTS - 1, number - (target & (SLOTS - 1)) + SLOTS - 1))
        rows = by_slot(where_from)
        for term in range(2 * SLOTS):
            turns[face - 4, term] = jnp.where(rows == term, weights[2], 0.0)
    for face in range(4):
        first = []
        came = 2 + lax.rem(lax.rem(dev, 2) + face % 2 + 1, 2)
        for number in range(SLOTS):
            target = neighbors[number, face]
            source = jnp.where(target < 0, face % 2, jnp.where(target // SLOTS == rank, 1 - face % 2, came))
            first.append(source * ROWS + jnp.where(target < 0, number, target & (SLOTS - 1)))
        chosen = jnp.where(column == by_slot(first) + field * SLOTS, 1.0, 0.0)[:, : SOURCES * ROWS]
        rows = pl.ds(face % 2 * ROWS, ROWS)
        for part in range(PARTS):
            select[face // 2, rows, pl.ds(part * SOURCES * ROWS, SOURCES * ROWS)] = chosen


def start_kernel(fields, neighbors, orient, *refs):
    fetched, low, high, faces_grp, faces_dev, scale, select, turns = refs[:8]
    state, near, turn, arrived = refs[8:]
    scalars = ((neighbors, near), (orient, turn))
    parts = [pl.ds(first, EDGE // 2) for first in (0, EDGE // 2)]
    blocks = tuple((fields.at[:, :, part], fetched.at[:, :, part]) for part in parts)
    copies = [pltpu.make_async_copy(*pair, arrived.at[number]) for number, pair in enumerate((*scalars, *blocks))]
    for copy in copies:
        copy.start()
    for copy in copies[: len(scalars)]:
        copy.wait()
    plan_kernel(near, turn, scale, select, turns)
    packer = Packer()
    for number, part in enumerate(parts):
        copies[len(scalars) + number].wait()
        first = number * (EDGE // 2)
        for slot in range(SLOTS):
            fill_slot(state, slot, lambda f: fetched[slot, f, part], first, EDGE // 2)
        for x in range(first, first + EDGE // 2):
            packer.add_y(x, *plane_at(state, x))
            packer.add_z(x, *plane_at(state, x))
    write_tables(packer, state, (low, high))
    for h in range(2):
        for ref, table in zip((low, high), packer.z_tables(h)):
            ref[2, :, h * HALF : (h + 1) * HALF] = table
    faces_grp[:ROWS] = gathered([low[0], high[0], low[1], high[1]], 0)
    faces_grp[ROWS:] = squeezed(jnp.where(even_place("grp"), high[2], low[2]))
    faces_dev[:ROWS] = gathered([low[0], high[0], low[1], high[1]], SLOTS - 1)
    faces_dev[ROWS:] = squeezed(gathered([low[2], low[2], low[2], high[2]], SLOTS - 1))


def first_inner_kernel(mask_dev, mask_grp, scale, fields, block_dev, block_grp, faces, low, high, new_low, new_high, *refs):
    partial, got_deep, relayed, z_low, z_high, state = refs
    size = NFIELD * EDGE
    swap_dev, swap_grp = mask_dev[...] > 0.5, mask_grp[...] > 0.5

    def block(slot):
        def of(f):
            value = fields[slot, f]
            if slot == 0:
                value = jnp.where(swap_grp[:EDGE], block_grp[f * EDGE : (f + 1) * EDGE], value)
            if slot == SLOTS - 1:
                value = jnp.where(swap_dev[:EDGE], block_dev[f * EDGE : (f + 1) * EDGE], value)
            return value

        return of

    for slot in range(SLOTS):
        fill_slot(state, slot, block(slot))
    rows, even = slot_rows(), even_place("grp")
    first_rows = (rows == 0) & swap_grp
    other = block_grp[size : size + ROWS]
    got = jnp.where((rows == 0) | (rows == SLOTS - 1), stretched(faces[ROWS:]), other)
    got_deep[...] = jnp.where(first_rows, jnp.where(even, low[2], high[2]), got)
    relayed[...] = jnp.where(rows == SLOTS - 1, jnp.broadcast_to(other[SLOTS - 1 : SLOTS], FACE), 0.0)
    z_low[...] = jnp.where(first_rows & ~even, other, new_low[2])
    z_high[...] = jnp.where(first_rows & even, other, new_high[2])
    inner_kernel(state, scale, partial)


def inner_kernel(state, scale, partial):
    lane = iota((ROWS, HALF), 1)
    start_y, end_y = lane < EDGE, lane >= HALF - EDGE
    start_z, end_z = lane % EDGE == 0, lane % EDGE == EDGE - 1
    weight_x, weight_y, weight_z, weight = (scale[number] for number in range(4))
    tile = 2 * SLOTS
    planes = {0: plane_at(state, 0)}
    for x in range(EDGE):
        if x + 1 < EDGE:
            planes[x + 1] = plane_at(state, x + 1)
        left, right = planes[x]
        up = [turned(half, EDGE) for half in (left, right)]
        down = [turned(half, -EDGE) for half in (left, right)]
        sum_y = (
            jnp.where(start_y, 0.0, up[0]) + jnp.where(end_y, down[1], down[0]),
            jnp.where(start_y, up[0], up[1]) + jnp.where(end_y, 0.0, down[1]),
        )
        for h, half in enumerate((left, right)):
            sum_z = jnp.where(start_z, 0.0, turned(half, 1)) + jnp.where(end_z, 0.0, turned(half, -1))
            if x == 0:
                sum_x = planes[1][h]
            elif x == EDGE - 1:
                sum_x = planes[x - 1][h]
            else:
                sum_x = planes[x - 1][h] + planes[x + 1][h]
            flow = weight * half + weight_x * sum_x + weight_y * sum_y[h] + weight_z * sum_z
            phases, conc = (half[:tile], half[tile : 2 * tile]), half[2 * tile :]
            drive = conc - pltpu.roll(conc, SLOTS, 0)
            total = phases[0] + phases[1]
            total = total + pltpu.roll(total, SLOTS, 0)
            tail = (phase_rate * closure) * (1.0 - total)
            rows = x * ROWS
            for number, value in enumerate(phases):
                gain = value * (1.0 - value) * (coupling[2 * number] * drive + (2.0 * value - 1.0))
                part = flow[number * tile : (number + 1) * tile]
                partial[h, pl.ds(rows + number * tile, tile), :] = part + (phase_rate * gain + tail)
            partial[h, pl.ds(rows + 2 * tile, tile), :] = flow[2 * tile :]


def ghosts_of(axis, scale, select, tables):
    tables = jnp.concatenate(tables, axis=0)
    near = tables.astype(jnp.bfloat16)
    rest = (tables - near.astype(jnp.float32)).astype(jnp.bfloat16)
    both = jnp.concatenate([near, rest], axis=0)
    pair = jnp.dot(select[axis].astype(jnp.bfloat16), both, preferred_element_type=jnp.float32)
    weight = jnp.concatenate([scale[axis]] * 2, axis=1)
    return weight * pair[:ROWS], weight * pair[ROWS:]


def side_by_side(low, high, even):
    return jnp.where(even, low, high), jnp.where(even, high, low)


def sides_kernel(scale, select, partial, low, high, flat_a, flat_b, *refs):
    first_step = len(refs) == 3
    done = refs[0] if first_step else refs[1]
    packer = Packer()
    sources = (low, high, flat_a, flat_b)
    x_low, x_high = ghosts_of(0, scale, select, [ref[0] for ref in sources])
    y_low, y_high = ghosts_of(1, scale, select, [ref[1] for ref in sources])
    lane = iota((ROWS, HALF), 1)
    inside = (lane < EDGE, lane >= HALF - EDGE)
    even = (lane // EDGE) % 2 == 0
    pairs = []
    for h in range(2):
        lanes = slice(h * HALF, (h + 1) * HALF)
        pairs.append(side_by_side(y_low[:, lanes], turned(y_high[:, lanes], -EDGE), even))
    for x in range(EDGE):
        ends = turned(pairs[x // GROUPS][x % 2], -EDGE * (x % GROUPS))
        halves = []
        for h, value in enumerate(plane_at(partial, x)):
            value = value + jnp.where(inside[h], ends, 0.0)
            if x == 0:
                value = value + x_low[:, h * HALF : (h + 1) * HALF]
            if x == EDGE - 1:
                value = value + x_high[:, h * HALF : (h + 1) * HALF]
            done[h, pl.ds(x * ROWS, ROWS), :] = value
            halves.append(value)
        if first_step:
            packer.add_z(x, *halves)
    if first_step:
        for h in range(2):
            for ref, table in zip(refs[1:], packer.z_tables(h)):
                ref[:, h * HALF : (h + 1) * HALF] = table
    else:
        blocks = refs[0]
        for slot in range(SLOTS):
            for f in range(NFIELD):
                for h in range(2):
                    rows = pl.ds(f * SLOTS + slot, EDGE, stride=ROWS)
                    blocks[slot, f, :, h * HALF : (h + 1) * HALF] = done[h, rows, :]


def z_ghosts(turns, own, deep_a, deep_b):
    even = even_place("grp")
    came = (jnp.where(even, deep_b, deep_a), jnp.where(even, deep_a, deep_b))
    ghosts = []
    for side in range(2):
        halves = []
        for h in range(2):
            lanes = slice(h * HALF, (h + 1) * HALF)
            table = came[side][:, lanes].reshape(NFIELD // 2, 2 * SLOTS, HALF)
            total = turns[side, 2 * SLOTS - 1] * own[side][:, lanes]
            for term in range(2 * SLOTS - 1):
                shift = (term - SLOTS + 1) % (2 * SLOTS)
                moved = pltpu.roll(table, shift, 1) if shift else table
                total = total + turns[side, term] * moved.reshape(ROWS, HALF)
            halves.append(total)
        ghosts.append(jnp.concatenate(halves, axis=1))
    return ghosts


def z_pairs(z_low, z_high):
    even = iota((ROWS, HALF), 1) % 2 == 0
    halves = [slice(h * HALF, (h + 1) * HALF) for h in range(2)]
    return [side_by_side(z_low[:, lanes], turned(z_high[:, lanes], EDGE - 1), even) for lanes in halves]


def ends_of(shape):
    place = iota(shape, 1) % EDGE
    return (place == 0) | (place == EDGE - 1)


def finish_kernel(
    turns, partial, packed_low, packed_high, known, deep_b, flat_a, relayed, z_low, z_high, done, low, high, *sends
):
    deep_a = jnp.where(relayed[...] > 0.5, flat_a[2], known[...])
    ghosts = z_ghosts(turns, (z_low[...], z_high[...]), deep_a, deep_b[...])
    pairs = z_pairs(*ghosts)
    ends = ends_of((ROWS, HALF))
    packer = Packer()
    for x in range(EDGE):
        halves, at = [], EDGE - 1 - x
        for h, value in enumerate(plane_at(partial, x)):
            value = value + jnp.where(ends, turned(pairs[h][at % 2], -at), 0.0)
            done[h, pl.ds(x * ROWS, ROWS), :] = value
            halves.append(value)
        packer.add_y(x, *halves)
    write_tables(packer, done, (low, high))
    low[2] = packed_low[...] + ghosts[0]
    high[2] = packed_high[...] + ghosts[1]
    emit_faces((low, high), sends)


def last_kernel(turns, partial, low, high, deep_first, deep_second, result, rows_of, blocks, sent):
    first, second, swapped = deep_first[...], deep_second[...], swapped_order(lax.axis_index("dev"))
    came = jnp.where(swapped, second, first), jnp.where(swapped, first, second)
    for h, pair in enumerate(z_pairs(*z_ghosts(turns, (low[2], high[2]), *came))):
        for odd in range(2):
            rows_of[h, odd] = pair[odd]
    shape = (EDGE, HALF)
    ends, even = ends_of(shape), iota(shape, 0) % 2 == 0
    copies = []
    for slot in range(SLOTS):
        for f in range(NFIELD):
            row = pl.ds(f * SLOTS + slot, 1)
            for h in range(2):
                both = [jnp.broadcast_to(rows_of[h, odd, row, :], shape) for odd in (1, 0)]
                ghost = pltpu.roll(jnp.where(even, *both), HALF - EDGE + 1, 1, stride=1, stride_axis=0)
                lanes = pl.ds(h * HALF, HALF)
                blocks[slot, f, :, lanes] = partial[slot, f, :, lanes] + jnp.where(ends, ghost, 0.0)
        copy = pltpu.make_async_copy(blocks.at[slot], result.at[slot], sent.at[slot])
        copy.start()
        copies.append(copy)
    for copy in copies:
        copy.wait()


def spec(space):
    return pl.BlockSpec(memory_space=space)


VECTOR = pltpu.VMEM
SMALL = pltpu.CompilerParams(vmem_limit_bytes=8 << 20)
FLAT = (2, ROWS, PLANE)
TABLES = (STATE, SIDE, SIDE, FLAT, FLAT, FACE, FACE)
EARLY = (ROWS + 4 * SLOTS, PLANE)
TO_DEV = (NFIELD * EDGE, PLANE)
TO_GRP = (NFIELD * EDGE + ROWS, PLANE)


def shaped(shape):
    return jax.ShapeDtypeStruct(shape, jnp.float32)


def cost(flops):
    return pl.CostEstimate(flops=flops, bytes_accessed=min(flops, 2 << 20), transcendentals=0)


def call(kernel, name, shapes, vectors, flops=1 << 20, scratch=()):
    return pl.pallas_call(
        kernel,
        name=name,
        compiler_params=SMALL,
        out_shape=[shaped(shape) for shape in shapes],
        in_specs=[spec(VECTOR)] * len(vectors),
        out_specs=[spec(VECTOR)] * len(shapes),
        scratch_shapes=list(scratch),
        cost_estimate=cost(flops),
    )(*vectors)


def start(arguments):
    shapes = (arguments[0].shape, SIDE, SIDE, EARLY, EARLY, (4, ROWS, HALF), SELECT, TURNS)
    return pl.pallas_call(
        start_kernel,
        name="start",
        compiler_params=SMALL,
        out_shape=[shaped(shape) for shape in shapes],
        in_specs=[spec(pl.ANY)] * len(arguments),
        out_specs=[spec(VECTOR)] * len(shapes),
        scratch_shapes=[
            pltpu.VMEM(SPARE, jnp.float32),
            *(pltpu.SMEM(array.shape, jnp.int32) for array in arguments[1:]),
            pltpu.SemaphoreType.DMA((len(arguments) + 1,)),
        ],
    )(*(pltpu.with_memory_space_constraint(array, pltpu.HBM) for array in arguments))


def mask(flag):
    return jnp.broadcast_to(jnp.where(flag == 1, 1.0, 0.0).reshape(1, 1), FACE)


def body(fields, swap_dev, swap_grp, neighbors, orient):
    fields, low, high, faces, faces_dev, scale, select, turns = start((fields, neighbors, orient))
    swap_dev, faces = lax.optimization_barrier((swap_dev, faces))
    faces = exchange(faces, "grp", 0)
    faces_dev = exchange(faces_dev, "dev", 0)
    mask_dev = mask(swap_dev)
    to_dev, to_grp = call(block_kernel, "blocks", [TO_DEV, TO_GRP], [mask_dev, fields, low, high], 1 << 28)
    swap_grp, to_grp = lax.optimization_barrier((swap_grp, to_grp))
    mask_grp = mask(swap_grp)
    block_grp = exchange(to_grp, "grp", 0)
    block_dev = exchange(to_dev, "dev", 0)
    new_low, new_high, *sends = call(
        faces_kernel,
        "faces",
        [SIDE, SIDE, SIDE, FLAT, FACE],
        [mask_dev, mask_grp, low, high, faces, faces_dev],
        1 << 28,
    )
    flat_a = exchange(sends[0], "dev", 0)
    flat_b = exchange(sends[1], "dev", 1)
    deep_b = exchange(sends[2], "grp", 1)
    partial, deep_a, relayed, z_low, z_high = call(
        first_inner_kernel,
        "inner_0",
        [STATE, FACE, FACE, FACE, FACE],
        [mask_dev, mask_grp, scale, fields, block_dev, block_grp, faces, low, high, new_low, new_high],
        4 << 20,
        [pltpu.VMEM(SPARE, jnp.float32)],
    )
    partial, packed_low, packed_high = call(
        sides_kernel,
        "sides_0",
        [STATE, FACE, FACE],
        [scale, select, partial, new_low, new_high, flat_a, flat_b],
    )
    state, *tables = call(
        finish_kernel,
        "finish_0",
        TABLES,
        [turns, partial, packed_low, packed_high, deep_a, deep_b, flat_a, relayed, z_low, z_high],
    )
    own, sends = tables[:2], tables[2:]
    flat_a = exchange(sends[0], "dev", 0)
    flat_b = exchange(sends[1], "dev", 1)
    deep_first = exchange(sends[2], "grp", lambda dev: 1 if swapped_order(dev) else 0)
    deep_second = exchange(sends[3], "grp", lambda dev: 0 if swapped_order(dev) else 1)
    (partial,) = call(inner_kernel, "inner_1", [STATE], [state, scale], 4 << 20)
    (blocks,) = call(
        sides_kernel,
        "sides_1",
        [fields.shape],
        [scale, select, partial, *own, flat_a, flat_b],
        scratch=[pltpu.VMEM(SPARE, jnp.float32)],
    )
    return pl.pallas_call(
        last_kernel,
        name="finish_1",
        compiler_params=SMALL,
        out_shape=shaped(fields.shape),
        in_specs=[spec(VECTOR)] * 6,
        out_specs=spec(pl.ANY),
        scratch_shapes=[
            pltpu.VMEM((2, 2, ROWS, HALF), jnp.float32),
            pltpu.VMEM(fields.shape, jnp.float32),
            pltpu.SemaphoreType.DMA((SLOTS,)),
        ],
    )(turns, blocks, *own, deep_first, deep_second)


def solution(mesh):
    in_specs = (
        P(("grp", "dev"), None, None, None),
        P(("grp", "dev")),
        P(("grp", "dev")),
        P(("grp", "dev"), None),
        P(("grp", "dev")),
    )
    out_specs = P(("grp", "dev"), None, None, None)
    return jax.shard_map(body, mesh=mesh, in_specs=in_specs, out_specs=out_specs, check_vma=False)
```

```python
import math

import jax
import jax.numpy as jnp
from jax import lax
from jax.experimental import pallas as pl
from jax.experimental.pallas import tpu as pltpu
from jax.sharding import PartitionSpec as P

NPHASE = 4
NCONC = 2
NFIELD = NPHASE + NCONC
EDGE = 16
PLANE = EDGE * EDGE
HALF = PLANE // 2
GROUPS = HALF // EDGE
SLOTS = 4
ROWS = NFIELD * SLOTS

phase_rate = 0.05
closure = 0.1
coupling = (0.5, -0.5, 1.0, -1.0)
conc_rates = (0.08, 0.04)

STATE = (2, EDGE * ROWS, HALF)
SPARE = (2, (EDGE + 1) * ROWS, HALF)
FACE = (ROWS, PLANE)
SIDE = (3, ROWS, PLANE)
SOURCES = 4
PARTS = 2
SELECT = (2, 2 * ROWS, PARTS * SOURCES * ROWS)
TURNS = (2, 2 * SLOTS, ROWS, HALF)


def swapped_order(dev):
    return dev // 4 % 2 == 1


def partners(axis, offset):
    sizes = (lax.axis_size("grp"), lax.axis_size("dev"))
    along = ("grp", "dev").index(axis)
    route = []
    for grp in range(sizes[0]):
        for dev in range(sizes[1]):
            own = (grp, dev)
            start = offset(dev) if callable(offset) else offset
            partner = list(own)
            partner[along] += 1 if (own[along] - start) % 2 == 0 else -1
            if not 0 <= partner[along] < sizes[along]:
                partner = list(own)
                partner[1 - along] ^= 1
                if partner[1 - along] >= sizes[1 - along]:
                    partner = list(own)
            route.append((grp * sizes[1] + dev, partner[0] * sizes[1] + partner[1]))
    return route


def exchange(block, axis, offset):
    return lax.ppermute(block, ("grp", "dev"), partners(axis, offset))


def iota(shape, dim):
    return lax.broadcasted_iota(jnp.int32, shape, dim)


def plane_at(ref, x):
    rows = pl.ds(x * ROWS, ROWS)
    return ref[0, rows, :], ref[1, rows, :]


def turned(value, shift):
    shift %= HALF
    return pltpu.roll(value, shift, 1) if shift else value


class Packer:
    def __init__(self):
        lane = iota((ROWS, HALF), 1)
        self.lane, self.group, self.place = lane, lane // EDGE, lane % EDGE
        self.y = [[None, None], [None, None]]
        self.z = [[None, None], [None, None]]

    def add_y(self, x, left, right):
        odd, half, at = x % 2, x // GROUPS, x % GROUPS
        ends = turned(jnp.where(self.lane < EDGE, left, right), EDGE * at)
        taken = (self.group == at) | (self.group == (at + GROUPS - 1) % GROUPS)
        before = self.y[half][odd]
        self.y[half][odd] = ends if before is None else jnp.where(taken, ends, before)

    def add_z(self, x, left, right):
        at = EDGE - 1 - x
        odd = at % 2
        taken = (self.place == at) | (self.place == (at + EDGE - 1) % EDGE)
        for h, value in enumerate((left, right)):
            moved = turned(value, at)
            before = self.z[h][odd]
            self.z[h][odd] = moved if before is None else jnp.where(taken, moved, before)

    def y_tables(self, h):
        even, (first, second) = self.group % 2 == 0, self.y[h]
        return jnp.where(even, first, second), turned(jnp.where(even, second, first), EDGE)

    def z_tables(self, h):
        even, (first, second) = self.place % 2 == 0, self.z[h]
        return jnp.where(even, first, second), turned(jnp.where(even, second, first), 1 - EDGE)


def write_tables(packer, state, own):
    low, high = own
    for h in range(2):
        lanes = pl.ds(h * HALF, HALF)
        for ref, x in ((low, 0), (high, EDGE - 1)):
            ref[0, :, lanes] = state[h, pl.ds(x * ROWS, ROWS), :]
        for ref, table in zip(own, packer.y_tables(h)):
            ref[1, :, lanes] = table


def emit_faces(own, sends):
    low, high = own
    flat_a, flat_b, deep_first, deep_second = sends
    even = even_place("dev")
    for face in range(2):
        flat_a[face] = jnp.where(even, high[face], low[face])
        flat_b[face] = jnp.where(even, low[face], high[face])
    upper = even_place("grp") != swapped_order(lax.axis_index("dev"))
    deep_first[...] = jnp.where(upper, high[2], low[2])
    deep_second[...] = jnp.where(upper, low[2], high[2])


def fill_slot(state, slot, block, first=0, count=EDGE):
    for f in range(NFIELD):
        value = block(f)
        for h in range(2):
            rows = pl.ds(first * ROWS + f * SLOTS + slot, count, stride=ROWS)
            state[h, rows, :] = value[:, h * HALF : (h + 1) * HALF]


def slot_rows():
    return iota(FACE, 0) % SLOTS


def shifted(value, rows):
    rows %= ROWS
    return pltpu.roll(value, rows, 0) if rows else value


def gathered(tables, slot):
    rows = slot_rows()
    out = shifted(tables[0], -slot)
    for number in range(1, len(tables)):
        out = jnp.where(rows == number, shifted(tables[number], number - slot), out)
    return out


def squeezed(table):
    tile = 2 * SLOTS
    rows = iota((tile, PLANE), 0) % SLOTS
    first, second, third = (table[number * tile : (number + 1) * tile] for number in range(3))
    between = jnp.where(rows == 1, pltpu.roll(second, 1, 0), pltpu.roll(second, tile - 1, 0))
    return jnp.concatenate([jnp.where((rows == 1) | (rows == 2), between, first), third], axis=0)


def stretched(value):
    tile = 2 * SLOTS
    rows = iota((tile, PLANE), 0) % SLOTS
    first, third = value[:tile], value[tile:]
    second = jnp.where(rows == 0, pltpu.roll(first, tile - 1, 0), pltpu.roll(first, 1, 0))
    return jnp.concatenate([first, second, third], axis=0)


def scattered(table, number, slot):
    return shifted(table, slot - number)


def even_place(axis):
    return lax.rem(lax.axis_index(axis), 2) == 0


def block_kernel(mask_dev, fields, low, high, to_dev, to_grp):
    last, size = SLOTS - 1, NFIELD * EDGE
    for f in range(NFIELD):
        to_dev[f * EDGE : (f + 1) * EDGE] = fields[last, f]
        to_grp[f * EDGE : (f + 1) * EDGE] = fields[0, f]
    rows, even = slot_rows(), even_place("grp")
    table = jnp.where(rows == 0, jnp.where(even, low[2], high[2]), jnp.where(even, high[2], low[2]))
    to_grp[size : size + ROWS] = jnp.where(rows == SLOTS - 1, mask_dev[...], table)


def faces_kernel(mask_dev, mask_grp, low, high, faces, faces_dev, *outs):
    new_low, new_high, flat_a, flat_b, deep_b = outs
    rows, last = slot_rows(), SLOTS - 1
    first_rows = (rows == 0) & (mask_grp[...] > 0.5)
    last_rows = (rows == last) & (mask_dev[...] > 0.5)
    even = even_place("grp")
    got_first, got_last = faces[:ROWS], faces_dev[:ROWS]
    got_z, got_last_z = stretched(faces[ROWS:]), stretched(faces_dev[ROWS:])
    for side, (raw, new) in enumerate(((low, new_low), (high, new_high))):
        for axis in range(2):
            number = 2 * axis + side
            table = jnp.where(first_rows, scattered(got_first, number, 0), raw[axis])
            new[axis] = jnp.where(last_rows, scattered(got_last, number, last), table)
        table = jnp.where(first_rows & (even if side == 0 else ~even), got_z, raw[2])
        new[2] = jnp.where(last_rows, scattered(got_last_z, side * last, last), table)
    even_dev = even_place("dev")
    for axis in range(2):
        flat_a[axis] = jnp.where(even_dev, new_high[axis], new_low[axis])
        flat_b[axis] = jnp.where(even_dev, new_low[axis], new_high[axis])
    flat_a[2] = got_z
    deep_b[...] = jnp.where(even, new_low[2], new_high[2])


def cos_quarter(number):
    turn = number & 7
    size = jnp.where((turn & 3) == 0, 1.0, jnp.where((turn & 3) == 2, 0.0, math.sqrt(0.5)))
    return jnp.where((turn > 2) & (turn < 6), -size, size)


def plan_kernel(neighbors, orient, scale, select, turns):
    shape = (ROWS, HALF)
    slot, field, column = iota(shape, 0) % SLOTS, iota(shape, 0) // SLOTS, iota(shape, 1)
    grp, dev = lax.axis_index("grp"), lax.axis_index("dev")
    rank = grp * lax.axis_size("dev") + dev

    def by_slot(values):
        rows = values[0]
        for number in range(1, SLOTS):
            rows = jnp.where(slot == number, values[number], rows)
        return rows

    spread = []
    for number in range(SLOTS):
        turn = 0.5 * cos_quarter(orient[number])
        lift = 0.5 * cos_quarter(orient[number] + 6)
        spread.append((1.0 + turn, 1.0 - turn, 1.0 + lift))
    conc = jnp.where(field == NPHASE, conc_rates[0], conc_rates[1])
    weights = [jnp.where(field < NPHASE, phase_rate * by_slot([own[axis] for own in spread]), conc) for axis in range(3)]
    for axis in range(3):
        scale[axis] = weights[axis]
    scale[3] = 1.0 - 2.0 * (weights[0] + weights[1] + weights[2])
    for face in range(4, 6):
        where_from = []
        for number in range(SLOTS):
            target = neighbors[number, face]
            where_from.append(jnp.where(target < 0, 2 * SLOTS - 1, number - (target & (SLOTS - 1)) + SLOTS - 1))
        rows = by_slot(where_from)
        for term in range(2 * SLOTS):
            turns[face - 4, term] = jnp.where(rows == term, weights[2], 0.0)
    for face in range(4):
        first = []
        came = 2 + lax.rem(lax.rem(dev, 2) + face % 2 + 1, 2)
        for number in range(SLOTS):
            target = neighbors[number, face]
            source = jnp.where(target < 0, face % 2, jnp.where(target // SLOTS == rank, 1 - face % 2, came))
            first.append(source * ROWS + jnp.where(target < 0, number, target & (SLOTS - 1)))
        chosen = jnp.where(column == by_slot(first) + field * SLOTS, 1.0, 0.0)[:, : SOURCES * ROWS]
        rows = pl.ds(face % 2 * ROWS, ROWS)
        for part in range(PARTS):
            select[face // 2, rows, pl.ds(part * SOURCES * ROWS, SOURCES * ROWS)] = chosen


def start_kernel(fields, neighbors, orient, *refs):
    fetched, low, high, faces_grp, faces_dev, scale, select, turns = refs[:8]
    state, near, turn, arrived = refs[8:]
    scalars = ((neighbors, near), (orient, turn))
    parts = [pl.ds(first, EDGE // 2) for first in (0, EDGE // 2)]
    blocks = tuple((fields.at[:, :, part], fetched.at[:, :, part]) for part in parts)
    copies = [pltpu.make_async_copy(*pair, arrived.at[number]) for number, pair in enumerate((*scalars, *blocks))]
    for copy in copies:
        copy.start()
    for copy in copies[: len(scalars)]:
        copy.wait()
    plan_kernel(near, turn, scale, select, turns)
    packer = Packer()
    for number, part in enumerate(parts):
        copies[len(scalars) + number].wait()
        first = number * (EDGE // 2)
        for slot in range(SLOTS):
            fill_slot(state, slot, lambda f: fetched[slot, f, part], first, EDGE // 2)
        for x in range(first, first + EDGE // 2):
            packer.add_y(x, *plane_at(state, x))
            packer.add_z(x, *plane_at(state, x))
    write_tables(packer, state, (low, high))
    for h in range(2):
        for ref, table in zip((low, high), packer.z_tables(h)):
            ref[2, :, h * HALF : (h + 1) * HALF] = table
    faces_grp[:ROWS] = gathered([low[0], high[0], low[1], high[1]], 0)
    faces_grp[ROWS:] = squeezed(jnp.where(even_place("grp"), high[2], low[2]))
    faces_dev[:ROWS] = gathered([low[0], high[0], low[1], high[1]], SLOTS - 1)
    faces_dev[ROWS:] = squeezed(gathered([low[2], low[2], low[2], high[2]], SLOTS - 1))


def first_inner_kernel(mask_dev, mask_grp, scale, fields, block_dev, block_grp, faces, low, high, new_low, new_high, *refs):
    partial, got_deep, relayed, z_low, z_high, state = refs
    size = NFIELD * EDGE
    swap_dev, swap_grp = mask_dev[...] > 0.5, mask_grp[...] > 0.5

    def block(slot):
        def of(f):
            value = fields[slot, f]
            if slot == 0:
                value = jnp.where(swap_grp[:EDGE], block_grp[f * EDGE : (f + 1) * EDGE], value)
            if slot == SLOTS - 1:
                value = jnp.where(swap_dev[:EDGE], block_dev[f * EDGE : (f + 1) * EDGE], value)
            return value

        return of

    for slot in range(SLOTS):
        fill_slot(state, slot, block(slot))
    rows, even = slot_rows(), even_place("grp")
    first_rows = (rows == 0) & swap_grp
    other = block_grp[size : size + ROWS]
    got = jnp.where((rows == 0) | (rows == SLOTS - 1), stretched(faces[ROWS:]), other)
    got_deep[...] = jnp.where(first_rows, jnp.where(even, low[2], high[2]), got)
    relayed[...] = jnp.where(rows == SLOTS - 1, jnp.broadcast_to(other[SLOTS - 1 : SLOTS], FACE), 0.0)
    z_low[...] = jnp.where(first_rows & ~even, other, new_low[2])
    z_high[...] = jnp.where(first_rows & even, other, new_high[2])
    inner_kernel(state, scale, partial)


def later_inner_kernel(state, ghosts, scale, partial):
    inner_kernel(state, scale, partial, z_pairs(ghosts[0], ghosts[1]))


def inner_kernel(state, scale, partial, pairs=None):
    ends = ends_of((ROWS, HALF))

    def plane(x):
        halves, at = plane_at(state, x), EDGE - 1 - x
        if pairs is None:
            return halves
        return [half + jnp.where(ends, turned(pairs[h][at % 2], -at), 0.0) for h, half in enumerate(halves)]

    lane = iota((ROWS, HALF), 1)
    start_y, end_y = lane < EDGE, lane >= HALF - EDGE
    start_z, end_z = lane % EDGE == 0, lane % EDGE == EDGE - 1
    weight_x, weight_y, weight_z, weight = (scale[number] for number in range(4))
    tile = 2 * SLOTS
    planes = {0: plane(0)}
    for x in range(EDGE):
        if x + 1 < EDGE:
            planes[x + 1] = plane(x + 1)
        left, right = planes[x]
        up = [turned(half, EDGE) for half in (left, right)]
        down = [turned(half, -EDGE) for half in (left, right)]
        sum_y = (
            jnp.where(start_y, 0.0, up[0]) + jnp.where(end_y, down[1], down[0]),
            jnp.where(start_y, up[0], up[1]) + jnp.where(end_y, 0.0, down[1]),
        )
        for h, half in enumerate((left, right)):
            sum_z = jnp.where(start_z, 0.0, turned(half, 1)) + jnp.where(end_z, 0.0, turned(half, -1))
            if x == 0:
                sum_x = planes[1][h]
            elif x == EDGE - 1:
                sum_x = planes[x - 1][h]
            else:
                sum_x = planes[x - 1][h] + planes[x + 1][h]
            flow = weight * half + weight_x * sum_x + weight_y * sum_y[h] + weight_z * sum_z
            phases, conc = (half[:tile], half[tile : 2 * tile]), half[2 * tile :]
            drive = conc - pltpu.roll(conc, SLOTS, 0)
            total = phases[0] + phases[1]
            total = total + pltpu.roll(total, SLOTS, 0)
            tail = (phase_rate * closure) * (1.0 - total)
            rows = x * ROWS
            for number, value in enumerate(phases):
                gain = value * (1.0 - value) * (coupling[2 * number] * drive + (2.0 * value - 1.0))
                part = flow[number * tile : (number + 1) * tile]
                partial[h, pl.ds(rows + number * tile, tile), :] = part + (phase_rate * gain + tail)
            partial[h, pl.ds(rows + 2 * tile, tile), :] = flow[2 * tile :]


def ghosts_of(axis, scale, select, tables):
    tables = jnp.concatenate(tables, axis=0)
    near = tables.astype(jnp.bfloat16)
    rest = (tables - near.astype(jnp.float32)).astype(jnp.bfloat16)
    both = jnp.concatenate([near, rest], axis=0)
    pair = jnp.dot(select[axis].astype(jnp.bfloat16), both, preferred_element_type=jnp.float32)
    weight = jnp.concatenate([scale[axis]] * 2, axis=1)
    return weight * pair[:ROWS], weight * pair[ROWS:]


def side_by_side(low, high, even):
    return jnp.where(even, low, high), jnp.where(even, high, low)


def sides_kernel(scale, select, partial, low, high, flat_a, flat_b, *refs):
    first_step = len(refs) == 5
    done = refs[0] if first_step else refs[1]
    packer = Packer()
    sources = (low, high, flat_a, flat_b)
    x_low, x_high = ghosts_of(0, scale, select, [ref[0] for ref in sources])
    y_low, y_high = ghosts_of(1, scale, select, [ref[1] for ref in sources])
    lane = iota((ROWS, HALF), 1)
    inside = (lane < EDGE, lane >= HALF - EDGE)
    even = (lane // EDGE) % 2 == 0
    pairs = []
    for h in range(2):
        lanes = slice(h * HALF, (h + 1) * HALF)
        pairs.append(side_by_side(y_low[:, lanes], turned(y_high[:, lanes], -EDGE), even))
    for x in range(EDGE):
        ends = turned(pairs[x // GROUPS][x % 2], -EDGE * (x % GROUPS))
        halves = []
        for h, value in enumerate(plane_at(partial, x)):
            value = value + jnp.where(inside[h], ends, 0.0)
            if x == 0:
                value = value + x_low[:, h * HALF : (h + 1) * HALF]
            if x == EDGE - 1:
                value = value + x_high[:, h * HALF : (h + 1) * HALF]
            done[h, pl.ds(x * ROWS, ROWS), :] = value
            halves.append(value)
        if first_step:
            packer.add_z(x, *halves)
            packer.add_y(x, *halves)
    if first_step:
        for h in range(2):
            for ref, table in zip(refs[1:], (*packer.z_tables(h), *packer.y_tables(h))):
                ref[:, h * HALF : (h + 1) * HALF] = table
    else:
        blocks = refs[0]
        for slot in range(SLOTS):
            for f in range(NFIELD):
                for h in range(2):
                    rows = pl.ds(f * SLOTS + slot, EDGE, stride=ROWS)
                    blocks[slot, f, :, h * HALF : (h + 1) * HALF] = done[h, rows, :]


def z_ghosts(turns, own, deep_a, deep_b):
    even = even_place("grp")
    came = (jnp.where(even, deep_b, deep_a), jnp.where(even, deep_a, deep_b))
    ghosts = []
    for side in range(2):
        halves = []
        for h in range(2):
            lanes = slice(h * HALF, (h + 1) * HALF)
            table = came[side][:, lanes].reshape(NFIELD // 2, 2 * SLOTS, HALF)
            total = turns[side, 2 * SLOTS - 1] * own[side][:, lanes]
            for term in range(2 * SLOTS - 1):
                shift = (term - SLOTS + 1) % (2 * SLOTS)
                moved = pltpu.roll(table, shift, 1) if shift else table
                total = total + turns[side, term] * moved.reshape(ROWS, HALF)
            halves.append(total)
        ghosts.append(jnp.concatenate(halves, axis=1))
    return ghosts


def z_pairs(z_low, z_high):
    even = iota((ROWS, HALF), 1) % 2 == 0
    halves = [slice(h * HALF, (h + 1) * HALF) for h in range(2)]
    return [side_by_side(z_low[:, lanes], turned(z_high[:, lanes], EDGE - 1), even) for lanes in halves]


def ends_of(shape):
    place = iota(shape, 1) % EDGE
    return (place == 0) | (place == EDGE - 1)


def finish_kernel(turns, partial, packed_z, packed_y, known, deep_b, flat_a, relayed, own_z, outs):
    low, high, *sends, ghosts = outs
    deep_a = jnp.where(relayed[...] > 0.5, flat_a[2], known[...])
    both = z_ghosts(turns, [ref[...] for ref in own_z], deep_a, deep_b[...])
    pairs = z_pairs(*both)
    lane = iota((ROWS, HALF), 1)
    ends, group = ends_of((ROWS, HALF)), lane // EDGE
    for side, ref in enumerate((low, high)):
        ghosts[side] = both[side]
        x = side * (EDGE - 1)
        at = EDGE - 1 - x
        for h, half in enumerate(plane_at(partial, x)):
            lanes = slice(h * HALF, (h + 1) * HALF)
            ref[0, :, lanes] = half + jnp.where(ends, turned(pairs[h][at % 2], -at), 0.0)
        ref[2] = packed_z[side][...] + both[side]
        for h in range(2):
            total = jnp.zeros((ROWS, HALF), jnp.float32)
            for number in range(GROUPS):
                at = EDGE - 1 - (h * GROUPS + number)
                moved = turned(pairs[side][at % 2], EDGE * number - at - side * (HALF - EDGE))
                total = jnp.where(ends & (group == number), moved, total)
            lanes = slice(h * HALF, (h + 1) * HALF)
            ref[1, :, lanes] = packed_y[side][:, lanes] + total
    emit_faces((low, high), sends)


def finish_0_kernel(turns, partial, *refs):
    packed, (known, deep_b, flat_a, relayed), own_z, outs = refs[:4], refs[4:8], refs[8:10], refs[10:]
    finish_kernel(turns, partial, packed[:2], packed[2:], known, deep_b, flat_a, relayed, own_z, outs)


def last_kernel(turns, partial, low, high, deep_first, deep_second, result, rows_of, blocks, sent):
    first, second, swapped = deep_first[...], deep_second[...], swapped_order(lax.axis_index("dev"))
    came = jnp.where(swapped, second, first), jnp.where(swapped, first, second)
    for h, pair in enumerate(z_pairs(*z_ghosts(turns, (low[2], high[2]), *came))):
        for odd in range(2):
            rows_of[h, odd] = pair[odd]
    shape = (EDGE, HALF)
    ends, even = ends_of(shape), iota(shape, 0) % 2 == 0
    copies = []
    for slot in range(SLOTS):
        for f in range(NFIELD):
            row = pl.ds(f * SLOTS + slot, 1)
            for h in range(2):
                both = [jnp.broadcast_to(rows_of[h, odd, row, :], shape) for odd in (1, 0)]
                ghost = pltpu.roll(jnp.where(even, *both), HALF - EDGE + 1, 1, stride=1, stride_axis=0)
                lanes = pl.ds(h * HALF, HALF)
                blocks[slot, f, :, lanes] = partial[slot, f, :, lanes] + jnp.where(ends, ghost, 0.0)
        copy = pltpu.make_async_copy(blocks.at[slot], result.at[slot], sent.at[slot])
        copy.start()
        copies.append(copy)
    for copy in copies:
        copy.wait()


def spec(space):
    return pl.BlockSpec(memory_space=space)


VECTOR = pltpu.VMEM
SMALL = pltpu.CompilerParams(vmem_limit_bytes=8 << 20)
FLAT = (2, ROWS, PLANE)
TABLES = (SIDE, SIDE, FLAT, FLAT, FACE, FACE, (2, *FACE))
EARLY = (ROWS + 4 * SLOTS, PLANE)
TO_DEV = (NFIELD * EDGE, PLANE)
TO_GRP = (NFIELD * EDGE + ROWS, PLANE)


def shaped(shape):
    return jax.ShapeDtypeStruct(shape, jnp.float32)


def cost(flops):
    return pl.CostEstimate(flops=flops, bytes_accessed=min(flops, 2 << 20), transcendentals=0)


def call(kernel, name, shapes, vectors, flops=1 << 20, scratch=()):
    return pl.pallas_call(
        kernel,
        name=name,
        compiler_params=SMALL,
        out_shape=[shaped(shape) for shape in shapes],
        in_specs=[spec(VECTOR)] * len(vectors),
        out_specs=[spec(VECTOR)] * len(shapes),
        scratch_shapes=list(scratch),
        cost_estimate=cost(flops),
    )(*vectors)


def start(arguments):
    shapes = (arguments[0].shape, SIDE, SIDE, EARLY, EARLY, (4, ROWS, HALF), SELECT, TURNS)
    return pl.pallas_call(
        start_kernel,
        name="start",
        compiler_params=SMALL,
        out_shape=[shaped(shape) for shape in shapes],
        in_specs=[spec(pl.ANY)] * len(arguments),
        out_specs=[spec(VECTOR)] * len(shapes),
        scratch_shapes=[
            pltpu.VMEM(SPARE, jnp.float32),
            *(pltpu.SMEM(array.shape, jnp.int32) for array in arguments[1:]),
            pltpu.SemaphoreType.DMA((len(arguments) + 1,)),
        ],
    )(*(pltpu.with_memory_space_constraint(array, pltpu.HBM) for array in arguments))


def mask(flag):
    return jnp.broadcast_to(jnp.where(flag == 1, 1.0, 0.0).reshape(1, 1), FACE)


def body(fields, swap_dev, swap_grp, neighbors, orient):
    fields, low, high, faces, faces_dev, scale, select, turns = start((fields, neighbors, orient))
    swap_dev, faces = lax.optimization_barrier((swap_dev, faces))
    faces = exchange(faces, "grp", 0)
    faces_dev = exchange(faces_dev, "dev", 0)
    mask_dev = mask(swap_dev)
    to_dev, to_grp = call(block_kernel, "blocks", [TO_DEV, TO_GRP], [mask_dev, fields, low, high], 1 << 28)
    swap_grp, to_grp = lax.optimization_barrier((swap_grp, to_grp))
    mask_grp = mask(swap_grp)
    block_grp = exchange(to_grp, "grp", 0)
    block_dev = exchange(to_dev, "dev", 0)
    new_low, new_high, *sends = call(
        faces_kernel,
        "faces",
        [SIDE, SIDE, SIDE, FLAT, FACE],
        [mask_dev, mask_grp, low, high, faces, faces_dev],
        1 << 28,
    )
    flat_a = exchange(sends[0], "dev", 0)
    flat_b = exchange(sends[1], "dev", 1)
    deep_b = exchange(sends[2], "grp", 1)
    partial, deep_a, relayed, z_low, z_high = call(
        first_inner_kernel,
        "inner_0",
        [STATE, FACE, FACE, FACE, FACE],
        [mask_dev, mask_grp, scale, fields, block_dev, block_grp, faces, low, high, new_low, new_high],
        4 << 20,
        [pltpu.VMEM(SPARE, jnp.float32)],
    )
    partial, *packed = call(
        sides_kernel,
        "sides_0",
        [STATE, FACE, FACE, FACE, FACE],
        [scale, select, partial, new_low, new_high, flat_a, flat_b],
    )
    *tables, ghosts = call(
        finish_0_kernel,
        "finish_0",
        TABLES,
        [turns, partial, *packed, deep_a, deep_b, flat_a, relayed, z_low, z_high],
    )
    own, sends = tables[:2], tables[2:]
    flat_a = exchange(sends[0], "dev", 0)
    flat_b = exchange(sends[1], "dev", 1)
    deep_first = exchange(sends[2], "grp", lambda dev: 1 if swapped_order(dev) else 0)
    deep_second = exchange(sends[3], "grp", lambda dev: 0 if swapped_order(dev) else 1)
    (partial,) = call(later_inner_kernel, "inner_1", [STATE], [partial, ghosts, scale], 4 << 20)
    (blocks,) = call(
        sides_kernel,
        "sides_1",
        [fields.shape],
        [scale, select, partial, *own, flat_a, flat_b],
        scratch=[pltpu.VMEM(SPARE, jnp.float32)],
    )
    return pl.pallas_call(
        last_kernel,
        name="finish_1",
        compiler_params=SMALL,
        out_shape=shaped(fields.shape),
        in_specs=[spec(VECTOR)] * 6,
        out_specs=spec(pl.ANY),
        scratch_shapes=[
            pltpu.VMEM((2, 2, ROWS, HALF), jnp.float32),
            pltpu.VMEM(fields.shape, jnp.float32),
            pltpu.SemaphoreType.DMA((SLOTS,)),
        ],
    )(turns, blocks, *own, deep_first, deep_second)


def solution(mesh):
    in_specs = (
        P(("grp", "dev"), None, None, None),
        P(("grp", "dev")),
        P(("grp", "dev")),
        P(("grp", "dev"), None),
        P(("grp", "dev")),
    )
    out_specs = P(("grp", "dev"), None, None, None)
    return jax.shard_map(body, mesh=mesh, in_specs=in_specs, out_specs=out_specs, check_vma=False)
```

```python
import math

import jax
import jax.numpy as jnp
from jax import lax
from jax.experimental import pallas as pl
from jax.experimental.pallas import tpu as pltpu
from jax.sharding import PartitionSpec as P

NPHASE = 4
NCONC = 2
NFIELD = NPHASE + NCONC
EDGE = 16
PLANE = EDGE * EDGE
HALF = PLANE // 2
GROUPS = HALF // EDGE
SLOTS = 4
ROWS = NFIELD * SLOTS

phase_rate = 0.05
closure = 0.1
coupling = (0.5, -0.5, 1.0, -1.0)
conc_rates = (0.08, 0.04)

STATE = (2, EDGE * ROWS, HALF)
SPARE = (2, (EDGE + 1) * ROWS, HALF)
FACE = (ROWS, PLANE)
SIDE = (3, ROWS, PLANE)
SOURCES = 4
PARTS = 2
SELECT = (2, 2 * ROWS, PARTS * SOURCES * ROWS)
PIECE = 3
TURNS = (2, 2 * SLOTS, ROWS, HALF)


def swapped_order(dev):
    return dev // 4 % 2 == 1


def partners(axis, offset):
    sizes = (lax.axis_size("grp"), lax.axis_size("dev"))
    along = ("grp", "dev").index(axis)
    route = []
    for grp in range(sizes[0]):
        for dev in range(sizes[1]):
            own = (grp, dev)
            start = offset(dev) if callable(offset) else offset
            partner = list(own)
            partner[along] += 1 if (own[along] - start) % 2 == 0 else -1
            if not 0 <= partner[along] < sizes[along]:
                partner = list(own)
                partner[1 - along] ^= 1
                if partner[1 - along] >= sizes[1 - along]:
                    partner = list(own)
            route.append((grp * sizes[1] + dev, partner[0] * sizes[1] + partner[1]))
    return route


def exchange(block, axis, offset):
    return lax.ppermute(block, ("grp", "dev"), partners(axis, offset))


def iota(shape, dim):
    return lax.broadcasted_iota(jnp.int32, shape, dim)


def plane_at(ref, x):
    rows = pl.ds(x * ROWS, ROWS)
    return ref[0, rows, :], ref[1, rows, :]


def turned(value, shift):
    shift %= HALF
    return pltpu.roll(value, shift, 1) if shift else value


class Packer:
    def __init__(self):
        lane = iota((ROWS, HALF), 1)
        self.lane, self.group, self.place = lane, lane // EDGE, lane % EDGE
        self.y = [[None, None], [None, None]]
        self.z = [[None, None], [None, None]]

    def add_y(self, x, left, right):
        odd, half, at = x % 2, x // GROUPS, x % GROUPS
        ends = turned(jnp.where(self.lane < EDGE, left, right), EDGE * at)
        taken = (self.group == at) | (self.group == (at + GROUPS - 1) % GROUPS)
        before = self.y[half][odd]
        self.y[half][odd] = ends if before is None else jnp.where(taken, ends, before)

    def add_z(self, x, left, right):
        at = EDGE - 1 - x
        odd = at % 2
        taken = (self.place == at) | (self.place == (at + EDGE - 1) % EDGE)
        for h, value in enumerate((left, right)):
            moved = turned(value, at)
            before = self.z[h][odd]
            self.z[h][odd] = moved if before is None else jnp.where(taken, moved, before)

    def y_tables(self, h):
        even, (first, second) = self.group % 2 == 0, self.y[h]
        return jnp.where(even, first, second), turned(jnp.where(even, second, first), EDGE)

    def z_tables(self, h):
        even, (first, second) = self.place % 2 == 0, self.z[h]
        return jnp.where(even, first, second), turned(jnp.where(even, second, first), 1 - EDGE)


def write_tables(packer, state, own):
    low, high = own
    for h in range(2):
        lanes = pl.ds(h * HALF, HALF)
        for ref, x in ((low, 0), (high, EDGE - 1)):
            ref[0, :, lanes] = state[h, pl.ds(x * ROWS, ROWS), :]
        for ref, table in zip(own, packer.y_tables(h)):
            ref[1, :, lanes] = table


def emit_faces(own, sends):
    low, high = own
    flat_a, flat_b, deep_first, deep_second = sends
    even = even_place("dev")
    for face in range(2):
        flat_a[face] = jnp.where(even, high[face], low[face])
        flat_b[face] = jnp.where(even, low[face], high[face])
    upper = even_place("grp") != swapped_order(lax.axis_index("dev"))
    deep_first[...] = jnp.where(upper, high[2], low[2])
    deep_second[...] = jnp.where(upper, low[2], high[2])


def fill_slot(state, slot, block, first=0, count=EDGE):
    for f in range(NFIELD):
        value = block(f)
        for h in range(2):
            rows = pl.ds(first * ROWS + f * SLOTS + slot, count, stride=ROWS)
            state[h, rows, :] = value[:, h * HALF : (h + 1) * HALF]


def slot_rows():
    return iota(FACE, 0) % SLOTS


def shifted(value, rows):
    rows %= ROWS
    return pltpu.roll(value, rows, 0) if rows else value


def gathered(tables, slot):
    rows = slot_rows()
    out = shifted(tables[0], -slot)
    for number in range(1, len(tables)):
        out = jnp.where(rows == number, shifted(tables[number], number - slot), out)
    return out


def squeezed(table):
    tile = 2 * SLOTS
    rows = iota((tile, PLANE), 0) % SLOTS
    first, second, third = (table[number * tile : (number + 1) * tile] for number in range(3))
    between = jnp.where(rows == 1, pltpu.roll(second, 1, 0), pltpu.roll(second, tile - 1, 0))
    return jnp.concatenate([jnp.where((rows == 1) | (rows == 2), between, first), third], axis=0)


def stretched(value):
    tile = 2 * SLOTS
    rows = iota((tile, PLANE), 0) % SLOTS
    first, third = value[:tile], value[tile:]
    second = jnp.where(rows == 0, pltpu.roll(first, tile - 1, 0), pltpu.roll(first, 1, 0))
    return jnp.concatenate([first, second, third], axis=0)


def scattered(table, number, slot):
    return shifted(table, slot - number)


def even_place(axis):
    return lax.rem(lax.axis_index(axis), 2) == 0


def block_kernel(mask_dev, fields, low, high, to_dev, to_grp):
    last, size = SLOTS - 1, NFIELD * EDGE
    for f in range(NFIELD):
        to_dev[f * EDGE : (f + 1) * EDGE] = fields[last, f]
        to_grp[f * EDGE : (f + 1) * EDGE] = fields[0, f]
    rows, even = slot_rows(), even_place("grp")
    table = jnp.where(rows == 0, jnp.where(even, low[2], high[2]), jnp.where(even, high[2], low[2]))
    to_grp[size : size + ROWS] = jnp.where(rows == SLOTS - 1, mask_dev[...], table)


def faces_kernel(mask_dev, mask_grp, low, high, faces, faces_dev, *outs):
    new_low, new_high, flat_a, flat_b, deep_b = outs
    rows, last = slot_rows(), SLOTS - 1
    first_rows = (rows == 0) & (mask_grp[...] > 0.5)
    last_rows = (rows == last) & (mask_dev[...] > 0.5)
    even = even_place("grp")
    got_first, got_last = faces[:ROWS], faces_dev[:ROWS]
    got_z, got_last_z = stretched(faces[ROWS:]), stretched(faces_dev[ROWS:])
    for side, (raw, new) in enumerate(((low, new_low), (high, new_high))):
        for axis in range(2):
            number = 2 * axis + side
            table = jnp.where(first_rows, scattered(got_first, number, 0), raw[axis])
            new[axis] = jnp.where(last_rows, scattered(got_last, number, last), table)
        table = jnp.where(first_rows & (even if side == 0 else ~even), got_z, raw[2])
        new[2] = jnp.where(last_rows, scattered(got_last_z, side * last, last), table)
    even_dev = even_place("dev")
    for axis in range(2):
        flat_a[axis] = jnp.where(even_dev, new_high[axis], new_low[axis])
        flat_b[axis] = jnp.where(even_dev, new_low[axis], new_high[axis])
    flat_a[2] = got_z
    deep_b[...] = jnp.where(even, new_low[2], new_high[2])


def cos_quarter(number):
    turn = number & 7
    size = jnp.where((turn & 3) == 0, 1.0, jnp.where((turn & 3) == 2, 0.0, math.sqrt(0.5)))
    return jnp.where((turn > 2) & (turn < 6), -size, size)


def plan_kernel(neighbors, orient, scale, select, turns):
    shape = (ROWS, HALF)
    slot, field, column = iota(shape, 0) % SLOTS, iota(shape, 0) // SLOTS, iota(shape, 1)
    grp, dev = lax.axis_index("grp"), lax.axis_index("dev")
    rank = grp * lax.axis_size("dev") + dev

    def by_slot(values):
        rows = values[0]
        for number in range(1, SLOTS):
            rows = jnp.where(slot == number, values[number], rows)
        return rows

    spread = []
    for number in range(SLOTS):
        turn = 0.5 * cos_quarter(orient[number])
        lift = 0.5 * cos_quarter(orient[number] + 6)
        spread.append((1.0 + turn, 1.0 - turn, 1.0 + lift))
    conc = jnp.where(field == NPHASE, conc_rates[0], conc_rates[1])
    weights = [jnp.where(field < NPHASE, phase_rate * by_slot([own[axis] for own in spread]), conc) for axis in range(3)]
    for axis in range(3):
        scale[axis] = weights[axis]
    scale[3] = 1.0 - 2.0 * (weights[0] + weights[1] + weights[2])
    for face in range(4, 6):
        where_from = []
        for number in range(SLOTS):
            target = neighbors[number, face]
            where_from.append(jnp.where(target < 0, 2 * SLOTS - 1, number - (target & (SLOTS - 1)) + SLOTS - 1))
        rows = by_slot(where_from)
        for term in range(2 * SLOTS):
            turns[face - 4, term] = jnp.where(rows == term, weights[2], 0.0)
    for face in range(4):
        first = []
        came = 2 + lax.rem(lax.rem(dev, 2) + face % 2 + 1, 2)
        for number in range(SLOTS):
            target = neighbors[number, face]
            source = jnp.where(target < 0, face % 2, jnp.where(target // SLOTS == rank, 1 - face % 2, came))
            first.append(source * ROWS + jnp.where(target < 0, number, target & (SLOTS - 1)))
        chosen = jnp.where(column == by_slot(first) + field * SLOTS, 1.0, 0.0)[:, : SOURCES * ROWS]
        rows = pl.ds(face % 2 * ROWS, ROWS)
        for part in range(PARTS):
            select[face // 2, rows, pl.ds(part * SOURCES * ROWS, SOURCES * ROWS)] = chosen


def start_kernel(fields, neighbors, orient, *refs):
    fetched, low, high, faces_grp, faces_dev, scale, select, turns = refs[:8]
    state, near, turn, arrived = refs[8:]
    scalars = ((neighbors, near), (orient, turn))
    parts = [pl.ds(first, EDGE // 2) for first in (0, EDGE // 2)]
    blocks = tuple((fields.at[:, :, part], fetched.at[:, :, part]) for part in parts)
    copies = [pltpu.make_async_copy(*pair, arrived.at[number]) for number, pair in enumerate((*scalars, *blocks))]
    for copy in copies:
        copy.start()
    for copy in copies[: len(scalars)]:
        copy.wait()
    plan_kernel(near, turn, scale, select, turns)
    packer = Packer()
    for number, part in enumerate(parts):
        copies[len(scalars) + number].wait()
        first = number * (EDGE // 2)
        for slot in range(SLOTS):
            fill_slot(state, slot, lambda f: fetched[slot, f, part], first, EDGE // 2)
        for x in range(first, first + EDGE // 2):
            packer.add_y(x, *plane_at(state, x))
            packer.add_z(x, *plane_at(state, x))
    write_tables(packer, state, (low, high))
    for h in range(2):
        for ref, table in zip((low, high), packer.z_tables(h)):
            ref[2, :, h * HALF : (h + 1) * HALF] = table
    faces_grp[:ROWS] = gathered([low[0], high[0], low[1], high[1]], 0)
    faces_grp[ROWS:] = squeezed(jnp.where(even_place("grp"), high[2], low[2]))
    faces_dev[:ROWS] = gathered([low[0], high[0], low[1], high[1]], SLOTS - 1)
    faces_dev[ROWS:] = squeezed(gathered([low[2], low[2], low[2], high[2]], SLOTS - 1))


def first_inner_kernel(mask_dev, mask_grp, scale, fields, block_dev, block_grp, faces, low, high, new_low, new_high, *refs):
    partial, got_deep, relayed, z_low, z_high, state = refs
    size = NFIELD * EDGE
    swap_dev, swap_grp = mask_dev[...] > 0.5, mask_grp[...] > 0.5

    def block(slot):
        def of(f):
            value = fields[slot, f]
            if slot == 0:
                value = jnp.where(swap_grp[:EDGE], block_grp[f * EDGE : (f + 1) * EDGE], value)
            if slot == SLOTS - 1:
                value = jnp.where(swap_dev[:EDGE], block_dev[f * EDGE : (f + 1) * EDGE], value)
            return value

        return of

    for slot in range(SLOTS):
        fill_slot(state, slot, block(slot))
    rows, even = slot_rows(), even_place("grp")
    first_rows = (rows == 0) & swap_grp
    other = block_grp[size : size + ROWS]
    got = jnp.where((rows == 0) | (rows == SLOTS - 1), stretched(faces[ROWS:]), other)
    got_deep[...] = jnp.where(first_rows, jnp.where(even, low[2], high[2]), got)
    relayed[...] = jnp.where(rows == SLOTS - 1, jnp.broadcast_to(other[SLOTS - 1 : SLOTS], FACE), 0.0)
    z_low[...] = jnp.where(first_rows & ~even, other, new_low[2])
    z_high[...] = jnp.where(first_rows & even, other, new_high[2])
    inner_kernel(state, scale, partial)


def later_inner_kernel(state, ghosts, scale, partial):
    inner_kernel(state, scale, partial, z_pairs(ghosts[0], ghosts[1]))


def inner_kernel(state, scale, partial, pairs=None):
    ends = ends_of((ROWS, HALF))

    def plane(x):
        halves, at = plane_at(state, x), EDGE - 1 - x
        if pairs is None:
            return halves
        return [half + jnp.where(ends, turned(pairs[h][at % 2], -at), 0.0) for h, half in enumerate(halves)]

    lane = iota((ROWS, HALF), 1)
    start_y, end_y = lane < EDGE, lane >= HALF - EDGE
    start_z, end_z = lane % EDGE == 0, lane % EDGE == EDGE - 1
    weight_x, weight_y, weight_z, weight = (scale[number] for number in range(4))
    tile = 2 * SLOTS
    planes = {0: plane(0)}
    for x in range(EDGE):
        if x + 1 < EDGE:
            planes[x + 1] = plane(x + 1)
        left, right = planes[x]
        up = [turned(half, EDGE) for half in (left, right)]
        down = [turned(half, -EDGE) for half in (left, right)]
        sum_y = (
            jnp.where(start_y, 0.0, up[0]) + jnp.where(end_y, down[1], down[0]),
            jnp.where(start_y, up[0], up[1]) + jnp.where(end_y, 0.0, down[1]),
        )
        for h, half in enumerate((left, right)):
            sum_z = jnp.where(start_z, 0.0, turned(half, 1)) + jnp.where(end_z, 0.0, turned(half, -1))
            if x == 0:
                sum_x = planes[1][h]
            elif x == EDGE - 1:
                sum_x = planes[x - 1][h]
            else:
                sum_x = planes[x - 1][h] + planes[x + 1][h]
            flow = weight * half + weight_x * sum_x + weight_y * sum_y[h] + weight_z * sum_z
            phases, conc = (half[:tile], half[tile : 2 * tile]), half[2 * tile :]
            drive = conc - pltpu.roll(conc, SLOTS, 0)
            total = phases[0] + phases[1]
            total = total + pltpu.roll(total, SLOTS, 0)
            tail = (phase_rate * closure) * (1.0 - total)
            rows = x * ROWS
            for number, value in enumerate(phases):
                gain = value * (1.0 - value) * (coupling[2 * number] * drive + (2.0 * value - 1.0))
                part = flow[number * tile : (number + 1) * tile]
                partial[h, pl.ds(rows + number * tile, tile), :] = part + (phase_rate * gain + tail)
            partial[h, pl.ds(rows + 2 * tile, tile), :] = flow[2 * tile :]


def ghosts_of(axis, scale, select, tables):
    tables = jnp.concatenate(tables, axis=0)
    near = tables.astype(jnp.bfloat16)
    rest = (tables - near.astype(jnp.float32)).astype(jnp.bfloat16)
    both = jnp.concatenate([near, rest], axis=0)
    pair = jnp.dot(select[axis].astype(jnp.bfloat16), both, preferred_element_type=jnp.float32)
    weight = jnp.concatenate([scale[axis]] * 2, axis=1)
    return weight * pair[:ROWS], weight * pair[ROWS:]


def side_by_side(low, high, even):
    return jnp.where(even, low, high), jnp.where(even, high, low)


def sides_kernel(scale, select, partial, low, high, flat_a, flat_b, *refs):
    first_step = len(refs) == 5
    done = refs[0] if first_step else refs[1]
    packer = Packer()
    sources = (low, high, flat_a, flat_b)
    x_low, x_high = ghosts_of(0, scale, select, [ref[0] for ref in sources])
    y_low, y_high = ghosts_of(1, scale, select, [ref[1] for ref in sources])
    lane = iota((ROWS, HALF), 1)
    inside = (lane < EDGE, lane >= HALF - EDGE)
    even = (lane // EDGE) % 2 == 0
    pairs = []
    for h in range(2):
        lanes = slice(h * HALF, (h + 1) * HALF)
        pairs.append(side_by_side(y_low[:, lanes], turned(y_high[:, lanes], -EDGE), even))
    for x in range(EDGE):
        ends = turned(pairs[x // GROUPS][x % 2], -EDGE * (x % GROUPS))
        halves = []
        for h, value in enumerate(plane_at(partial, x)):
            value = value + jnp.where(inside[h], ends, 0.0)
            if x == 0:
                value = value + x_low[:, h * HALF : (h + 1) * HALF]
            if x == EDGE - 1:
                value = value + x_high[:, h * HALF : (h + 1) * HALF]
            done[h, pl.ds(x * ROWS, ROWS), :] = value
            halves.append(value)
        if first_step:
            packer.add_z(x, *halves)
            packer.add_y(x, *halves)
    if first_step:
        for h in range(2):
            for ref, table in zip(refs[1:], (*packer.z_tables(h), *packer.y_tables(h))):
                ref[:, h * HALF : (h + 1) * HALF] = table
    else:
        blocks = refs[0]
        for slot in range(SLOTS):
            for f in range(NFIELD):
                for h in range(2):
                    rows = pl.ds(f * SLOTS + slot, EDGE, stride=ROWS)
                    blocks[slot, f, :, h * HALF : (h + 1) * HALF] = done[h, rows, :]


def z_ghosts(turns, own, deep_a, deep_b):
    even = even_place("grp")
    came = (jnp.where(even, deep_b, deep_a), jnp.where(even, deep_a, deep_b))
    ghosts = []
    for side in range(2):
        halves = []
        for h in range(2):
            lanes = slice(h * HALF, (h + 1) * HALF)
            table = came[side][:, lanes].reshape(NFIELD // 2, 2 * SLOTS, HALF)
            total = turns[side, 2 * SLOTS - 1] * own[side][:, lanes]
            for term in range(2 * SLOTS - 1):
                shift = (term - SLOTS + 1) % (2 * SLOTS)
                moved = pltpu.roll(table, shift, 1) if shift else table
                total = total + turns[side, term] * moved.reshape(ROWS, HALF)
            halves.append(total)
        ghosts.append(jnp.concatenate(halves, axis=1))
    return ghosts


def z_pairs(z_low, z_high):
    even = iota((ROWS, HALF), 1) % 2 == 0
    halves = [slice(h * HALF, (h + 1) * HALF) for h in range(2)]
    return [side_by_side(z_low[:, lanes], turned(z_high[:, lanes], EDGE - 1), even) for lanes in halves]


def ends_of(shape):
    place = iota(shape, 1) % EDGE
    return (place == 0) | (place == EDGE - 1)


def finish_kernel(turns, partial, packed_z, packed_y, known, deep_b, flat_a, relayed, own_z, outs):
    low, high, *sends, ghosts = outs
    deep_a = jnp.where(relayed[...] > 0.5, flat_a[2], known[...])
    both = z_ghosts(turns, [ref[...] for ref in own_z], deep_a, deep_b[...])
    pairs = z_pairs(*both)
    lane = iota((ROWS, HALF), 1)
    ends, group = ends_of((ROWS, HALF)), lane // EDGE
    for side, ref in enumerate((low, high)):
        ghosts[side] = both[side]
        x = side * (EDGE - 1)
        at = EDGE - 1 - x
        for h, half in enumerate(plane_at(partial, x)):
            lanes = slice(h * HALF, (h + 1) * HALF)
            ref[0, :, lanes] = half + jnp.where(ends, turned(pairs[h][at % 2], -at), 0.0)
        ref[2] = packed_z[side][...] + both[side]
        for h in range(2):
            total = jnp.zeros((ROWS, HALF), jnp.float32)
            for number in range(GROUPS):
                at = EDGE - 1 - (h * GROUPS + number)
                moved = turned(pairs[side][at % 2], EDGE * number - at - side * (HALF - EDGE))
                total = jnp.where(ends & (group == number), moved, total)
            lanes = slice(h * HALF, (h + 1) * HALF)
            ref[1, :, lanes] = packed_y[side][:, lanes] + total
    emit_faces((low, high), sends)


def finish_0_kernel(turns, partial, *refs):
    packed, (known, deep_b, flat_a, relayed), own_z, outs = refs[:4], refs[4:8], refs[8:10], refs[10:]
    finish_kernel(turns, partial, packed[:2], packed[2:], known, deep_b, flat_a, relayed, own_z, outs)


def last_kernel(turns, partial, low, high, deep_first, deep_second, result, rows_of, blocks, sent):
    first, second, swapped = deep_first[...], deep_second[...], swapped_order(lax.axis_index("dev"))
    came = jnp.where(swapped, second, first), jnp.where(swapped, first, second)
    for h, pair in enumerate(z_pairs(*z_ghosts(turns, (low[2], high[2]), *came))):
        for odd in range(2):
            rows_of[h, odd] = pair[odd]
    shape = (EDGE, HALF)
    ends, even = ends_of(shape), iota(shape, 0) % 2 == 0
    copies = []
    for slot in range(SLOTS):
        for f in range(NFIELD):
            row = pl.ds(f * SLOTS + slot, 1)
            for h in range(2):
                both = [jnp.broadcast_to(rows_of[h, odd, row, :], shape) for odd in (1, 0)]
                ghost = pltpu.roll(jnp.where(even, *both), HALF - EDGE + 1, 1, stride=1, stride_axis=0)
                lanes = pl.ds(h * HALF, HALF)
                blocks[slot, f, :, lanes] = partial[slot, f, :, lanes] + jnp.where(ends, ghost, 0.0)
            if f % PIECE == PIECE - 1:
                part = (slot, pl.ds(f + 1 - PIECE, PIECE))
                copy = pltpu.make_async_copy(blocks.at[part], result.at[part], sent.at[len(copies)])
                copy.start()
                copies.append(copy)
    for copy in copies:
        copy.wait()


def spec(space):
    return pl.BlockSpec(memory_space=space)


VECTOR = pltpu.VMEM
SMALL = pltpu.CompilerParams(vmem_limit_bytes=8 << 20)
FLAT = (2, ROWS, PLANE)
TABLES = (SIDE, SIDE, FLAT, FLAT, FACE, FACE, (2, *FACE))
EARLY = (ROWS + 4 * SLOTS, PLANE)
TO_DEV = (NFIELD * EDGE, PLANE)
TO_GRP = (NFIELD * EDGE + ROWS, PLANE)


def shaped(shape):
    return jax.ShapeDtypeStruct(shape, jnp.float32)


def cost(flops):
    return pl.CostEstimate(flops=flops, bytes_accessed=min(flops, 2 << 20), transcendentals=0)


def call(kernel, name, shapes, vectors, flops=1 << 20, scratch=()):
    return pl.pallas_call(
        kernel,
        name=name,
        compiler_params=SMALL,
        out_shape=[shaped(shape) for shape in shapes],
        in_specs=[spec(VECTOR)] * len(vectors),
        out_specs=[spec(VECTOR)] * len(shapes),
        scratch_shapes=list(scratch),
        cost_estimate=cost(flops),
    )(*vectors)


def start(arguments):
    shapes = (arguments[0].shape, SIDE, SIDE, EARLY, EARLY, (4, ROWS, HALF), SELECT, TURNS)
    return pl.pallas_call(
        start_kernel,
        name="start",
        compiler_params=SMALL,
        out_shape=[shaped(shape) for shape in shapes],
        in_specs=[spec(pl.ANY)] * len(arguments),
        out_specs=[spec(VECTOR)] * len(shapes),
        scratch_shapes=[
            pltpu.VMEM(SPARE, jnp.float32),
            *(pltpu.SMEM(array.shape, jnp.int32) for array in arguments[1:]),
            pltpu.SemaphoreType.DMA((len(arguments) + 1,)),
        ],
    )(*(pltpu.with_memory_space_constraint(array, pltpu.HBM) for array in arguments))


def mask(flag):
    return jnp.broadcast_to(jnp.where(flag == 1, 1.0, 0.0).reshape(1, 1), FACE)


def body(fields, swap_dev, swap_grp, neighbors, orient):
    fields, low, high, faces, faces_dev, scale, select, turns = start((fields, neighbors, orient))
    swap_dev, faces = lax.optimization_barrier((swap_dev, faces))
    faces = exchange(faces, "grp", 0)
    faces_dev = exchange(faces_dev, "dev", 0)
    mask_dev = mask(swap_dev)
    to_dev, to_grp = call(block_kernel, "blocks", [TO_DEV, TO_GRP], [mask_dev, fields, low, high], 1 << 28)
    swap_grp, to_grp = lax.optimization_barrier((swap_grp, to_grp))
    mask_grp = mask(swap_grp)
    block_grp = exchange(to_grp, "grp", 0)
    block_dev = exchange(to_dev, "dev", 0)
    new_low, new_high, *sends = call(
        faces_kernel,
        "faces",
        [SIDE, SIDE, SIDE, FLAT, FACE],
        [mask_dev, mask_grp, low, high, faces, faces_dev],
        1 << 28,
    )
    flat_a = exchange(sends[0], "dev", 0)
    flat_b = exchange(sends[1], "dev", 1)
    deep_b = exchange(sends[2], "grp", 1)
    partial, deep_a, relayed, z_low, z_high = call(
        first_inner_kernel,
        "inner_0",
        [STATE, FACE, FACE, FACE, FACE],
        [mask_dev, mask_grp, scale, fields, block_dev, block_grp, faces, low, high, new_low, new_high],
        4 << 20,
        [pltpu.VMEM(SPARE, jnp.float32)],
    )
    partial, *packed = call(
        sides_kernel,
        "sides_0",
        [STATE, FACE, FACE, FACE, FACE],
        [scale, select, partial, new_low, new_high, flat_a, flat_b],
    )
    *tables, ghosts = call(
        finish_0_kernel,
        "finish_0",
        TABLES,
        [turns, partial, *packed, deep_a, deep_b, flat_a, relayed, z_low, z_high],
    )
    own, sends = tables[:2], tables[2:]
    flat_a = exchange(sends[0], "dev", 0)
    flat_b = exchange(sends[1], "dev", 1)
    deep_first = exchange(sends[2], "grp", lambda dev: 1 if swapped_order(dev) else 0)
    deep_second = exchange(sends[3], "grp", lambda dev: 0 if swapped_order(dev) else 1)
    (partial,) = call(later_inner_kernel, "inner_1", [STATE], [partial, ghosts, scale], 4 << 20)
    (blocks,) = call(
        sides_kernel,
        "sides_1",
        [fields.shape],
        [scale, select, partial, *own, flat_a, flat_b],
        scratch=[pltpu.VMEM(SPARE, jnp.float32)],
    )
    return pl.pallas_call(
        last_kernel,
        name="finish_1",
        compiler_params=SMALL,
        out_shape=shaped(fields.shape),
        in_specs=[spec(VECTOR)] * 6,
        out_specs=spec(pl.ANY),
        scratch_shapes=[
            pltpu.VMEM((2, 2, ROWS, HALF), jnp.float32),
            pltpu.VMEM(fields.shape, jnp.float32),
            pltpu.SemaphoreType.DMA((SLOTS * NFIELD // PIECE,)),
        ],
    )(turns, blocks, *own, deep_first, deep_second)


def solution(mesh):
    in_specs = (
        P(("grp", "dev"), None, None, None),
        P(("grp", "dev")),
        P(("grp", "dev")),
        P(("grp", "dev"), None),
        P(("grp", "dev")),
    )
    out_specs = P(("grp", "dev"), None, None, None)
    return jax.shard_map(body, mesh=mesh, in_specs=in_specs, out_specs=out_specs, check_vma=False)
```

```python
import math

import jax
import jax.numpy as jnp
from jax import lax
from jax.experimental import pallas as pl
from jax.experimental.pallas import tpu as pltpu
from jax.sharding import PartitionSpec as P

NPHASE = 4
NCONC = 2
NFIELD = NPHASE + NCONC
EDGE = 16
PLANE = EDGE * EDGE
HALF = PLANE // 2
GROUPS = HALF // EDGE
SLOTS = 4
ROWS = NFIELD * SLOTS

phase_rate = 0.05
closure = 0.1
coupling = (0.5, -0.5, 1.0, -1.0)
conc_rates = (0.08, 0.04)

STATE = (2, EDGE * ROWS, HALF)
SPARE = (2, (EDGE + 1) * ROWS, HALF)
FACE = (ROWS, PLANE)
SIDE = (3, ROWS, PLANE)
SOURCES = 4
PARTS = 2
SELECT = (2, 2 * ROWS, PARTS * SOURCES * ROWS)
PIECE = 3
TURNS = (2, 2 * SLOTS, ROWS, HALF)


def swapped_order(dev):
    return dev // 4 % 2 == 1


def partners(axis, offset):
    sizes = (lax.axis_size("grp"), lax.axis_size("dev"))
    along = ("grp", "dev").index(axis)
    route = []
    for grp in range(sizes[0]):
        for dev in range(sizes[1]):
            own = (grp, dev)
            start = offset(dev) if callable(offset) else offset
            partner = list(own)
            partner[along] += 1 if (own[along] - start) % 2 == 0 else -1
            if not 0 <= partner[along] < sizes[along]:
                partner = list(own)
                partner[1 - along] ^= 1
                if partner[1 - along] >= sizes[1 - along]:
                    partner = list(own)
            route.append((grp * sizes[1] + dev, partner[0] * sizes[1] + partner[1]))
    return route


def exchange(block, axis, offset):
    return lax.ppermute(block, ("grp", "dev"), partners(axis, offset))


def iota(shape, dim):
    return lax.broadcasted_iota(jnp.int32, shape, dim)


def plane_at(ref, x):
    rows = pl.ds(x * ROWS, ROWS)
    return ref[0, rows, :], ref[1, rows, :]


def turned(value, shift):
    shift %= HALF
    return pltpu.roll(value, shift, 1) if shift else value


class Packer:
    def __init__(self):
        lane = iota((ROWS, HALF), 1)
        self.lane, self.group, self.place = lane, lane // EDGE, lane % EDGE
        self.y = [[None, None], [None, None]]
        self.z = [[None, None], [None, None]]

    def add_y(self, x, left, right):
        odd, half, at = x % 2, x // GROUPS, x % GROUPS
        ends = turned(jnp.where(self.lane < EDGE, left, right), EDGE * at)
        taken = (self.group == at) | (self.group == (at + GROUPS - 1) % GROUPS)
        before = self.y[half][odd]
        self.y[half][odd] = ends if before is None else jnp.where(taken, ends, before)

    def add_z(self, x, left, right):
        at = EDGE - 1 - x
        odd = at % 2
        taken = (self.place == at) | (self.place == (at + EDGE - 1) % EDGE)
        for h, value in enumerate((left, right)):
            moved = turned(value, at)
            before = self.z[h][odd]
            self.z[h][odd] = moved if before is None else jnp.where(taken, moved, before)

    def y_tables(self, h):
        even, (first, second) = self.group % 2 == 0, self.y[h]
        return jnp.where(even, first, second), turned(jnp.where(even, second, first), EDGE)

    def z_tables(self, h):
        even, (first, second) = self.place % 2 == 0, self.z[h]
        return jnp.where(even, first, second), turned(jnp.where(even, second, first), 1 - EDGE)


def write_tables(packer, state, own):
    low, high = own
    for h in range(2):
        lanes = pl.ds(h * HALF, HALF)
        for ref, x in ((low, 0), (high, EDGE - 1)):
            ref[0, :, lanes] = state[h, pl.ds(x * ROWS, ROWS), :]
        for ref, table in zip(own, packer.y_tables(h)):
            ref[1, :, lanes] = table


def emit_faces(own, sends):
    low, high = own
    flat_a, flat_b, deep_first, deep_second = sends
    even = even_place("dev")
    for face in range(2):
        flat_a[face] = jnp.where(even, high[face], low[face])
        flat_b[face] = jnp.where(even, low[face], high[face])
    upper = even_place("grp") != swapped_order(lax.axis_index("dev"))
    deep_first[...] = jnp.where(upper, high[2], low[2])
    deep_second[...] = jnp.where(upper, low[2], high[2])


def fill_slot(state, slot, block, first=0, count=EDGE):
    for f in range(NFIELD):
        value = block(f)
        for h in range(2):
            rows = pl.ds(first * ROWS + f * SLOTS + slot, count, stride=ROWS)
            state[h, rows, :] = value[:, h * HALF : (h + 1) * HALF]


def slot_rows():
    return iota(FACE, 0) % SLOTS


def shifted(value, rows):
    rows %= ROWS
    return pltpu.roll(value, rows, 0) if rows else value


def gathered(tables, slot):
    rows = slot_rows()
    out = shifted(tables[0], -slot)
    for number in range(1, len(tables)):
        out = jnp.where(rows == number, shifted(tables[number], number - slot), out)
    return out


def squeezed(table):
    tile = 2 * SLOTS
    rows = iota((tile, PLANE), 0) % SLOTS
    first, second, third = (table[number * tile : (number + 1) * tile] for number in range(3))
    between = jnp.where(rows == 1, pltpu.roll(second, 1, 0), pltpu.roll(second, tile - 1, 0))
    return jnp.concatenate([jnp.where((rows == 1) | (rows == 2), between, first), third], axis=0)


def stretched(value):
    tile = 2 * SLOTS
    rows = iota((tile, PLANE), 0) % SLOTS
    first, third = value[:tile], value[tile:]
    second = jnp.where(rows == 0, pltpu.roll(first, tile - 1, 0), pltpu.roll(first, 1, 0))
    return jnp.concatenate([first, second, third], axis=0)


def scattered(table, number, slot):
    return shifted(table, slot - number)


def even_place(axis):
    return lax.rem(lax.axis_index(axis), 2) == 0


def block_kernel(mask_dev, fields, low, high, to_dev, to_grp):
    last, size = SLOTS - 1, NFIELD * EDGE
    for f in range(NFIELD):
        to_dev[f * EDGE : (f + 1) * EDGE] = fields[last, f]
        to_grp[f * EDGE : (f + 1) * EDGE] = fields[0, f]
    rows, even = slot_rows(), even_place("grp")
    table = jnp.where(rows == 0, jnp.where(even, low[2], high[2]), jnp.where(even, high[2], low[2]))
    to_grp[size : size + ROWS] = jnp.where(rows == SLOTS - 1, mask_dev[...], table)


def faces_kernel(mask_dev, mask_grp, low, high, faces, faces_dev, *outs):
    new_low, new_high, flat_a, flat_b, deep_b = outs
    rows, last = slot_rows(), SLOTS - 1
    first_rows = (rows == 0) & (mask_grp[...] > 0.5)
    last_rows = (rows == last) & (mask_dev[...] > 0.5)
    even = even_place("grp")
    got_first, got_last = faces[:ROWS], faces_dev[:ROWS]
    got_z, got_last_z = stretched(faces[ROWS:]), stretched(faces_dev[ROWS:])
    for side, (raw, new) in enumerate(((low, new_low), (high, new_high))):
        for axis in range(2):
            number = 2 * axis + side
            table = jnp.where(first_rows, scattered(got_first, number, 0), raw[axis])
            new[axis] = jnp.where(last_rows, scattered(got_last, number, last), table)
        table = jnp.where(first_rows & (even if side == 0 else ~even), got_z, raw[2])
        new[2] = jnp.where(last_rows, scattered(got_last_z, side * last, last), table)
    even_dev = even_place("dev")
    for axis in range(2):
        flat_a[axis] = jnp.where(even_dev, new_high[axis], new_low[axis])
        flat_b[axis] = jnp.where(even_dev, new_low[axis], new_high[axis])
    flat_a[2] = got_z
    deep_b[...] = jnp.where(even, new_low[2], new_high[2])


def cos_quarter(number):
    turn = number & 7
    size = jnp.where((turn & 3) == 0, 1.0, jnp.where((turn & 3) == 2, 0.0, math.sqrt(0.5)))
    return jnp.where((turn > 2) & (turn < 6), -size, size)


def plan_kernel(neighbors, orient, sent, scale, select, turns):
    del sent
    shape = (ROWS, HALF)
    slot, field, column = iota(shape, 0) % SLOTS, iota(shape, 0) // SLOTS, iota(shape, 1)
    grp, dev = lax.axis_index("grp"), lax.axis_index("dev")
    rank = grp * lax.axis_size("dev") + dev

    def by_slot(values):
        rows = values[0]
        for number in range(1, SLOTS):
            rows = jnp.where(slot == number, values[number], rows)
        return rows

    spread = []
    for number in range(SLOTS):
        turn = 0.5 * cos_quarter(orient[number])
        lift = 0.5 * cos_quarter(orient[number] + 6)
        spread.append((1.0 + turn, 1.0 - turn, 1.0 + lift))
    conc = jnp.where(field == NPHASE, conc_rates[0], conc_rates[1])
    weights = [jnp.where(field < NPHASE, phase_rate * by_slot([own[axis] for own in spread]), conc) for axis in range(3)]
    for axis in range(3):
        scale[axis] = weights[axis]
    scale[3] = 1.0 - 2.0 * (weights[0] + weights[1] + weights[2])
    for face in range(4, 6):
        where_from = []
        for number in range(SLOTS):
            target = neighbors[number, face]
            where_from.append(jnp.where(target < 0, 2 * SLOTS - 1, number - (target & (SLOTS - 1)) + SLOTS - 1))
        rows = by_slot(where_from)
        for term in range(2 * SLOTS):
            turns[face - 4, term] = jnp.where(rows == term, weights[2], 0.0)
    for face in range(4):
        first = []
        came = 2 + lax.rem(lax.rem(dev, 2) + face % 2 + 1, 2)
        for number in range(SLOTS):
            target = neighbors[number, face]
            source = jnp.where(target < 0, face % 2, jnp.where(target // SLOTS == rank, 1 - face % 2, came))
            first.append(source * ROWS + jnp.where(target < 0, number, target & (SLOTS - 1)))
        chosen = jnp.where(column == by_slot(first) + field * SLOTS, 1.0, 0.0)[:, : SOURCES * ROWS]
        rows = pl.ds(face % 2 * ROWS, ROWS)
        for part in range(PARTS):
            select[face // 2, rows, pl.ds(part * SOURCES * ROWS, SOURCES * ROWS)] = chosen


def start_kernel(fields, fetched, low, high, faces_grp, faces_dev, state, arrived):
    parts = [pl.ds(first, EDGE // 2) for first in (0, EDGE // 2)]
    copies = [
        pltpu.make_async_copy(fields.at[:, :, part], fetched.at[:, :, part], arrived.at[number])
        for number, part in enumerate(parts)
    ]
    for copy in copies:
        copy.start()
    packer = Packer()
    for number, part in enumerate(parts):
        copies[number].wait()
        first = number * (EDGE // 2)
        for slot in range(SLOTS):
            fill_slot(state, slot, lambda f: fetched[slot, f, part], first, EDGE // 2)
        for x in range(first, first + EDGE // 2):
            packer.add_y(x, *plane_at(state, x))
            packer.add_z(x, *plane_at(state, x))
    write_tables(packer, state, (low, high))
    for h in range(2):
        for ref, table in zip((low, high), packer.z_tables(h)):
            ref[2, :, h * HALF : (h + 1) * HALF] = table
    faces_grp[:ROWS] = gathered([low[0], high[0], low[1], high[1]], 0)
    faces_grp[ROWS:] = squeezed(jnp.where(even_place("grp"), high[2], low[2]))
    faces_dev[:ROWS] = gathered([low[0], high[0], low[1], high[1]], SLOTS - 1)
    faces_dev[ROWS:] = squeezed(gathered([low[2], low[2], low[2], high[2]], SLOTS - 1))


def first_inner_kernel(mask_dev, mask_grp, scale, fields, block_dev, block_grp, faces, low, high, new_low, new_high, *refs):
    partial, got_deep, relayed, z_low, z_high, state = refs
    size = NFIELD * EDGE
    swap_dev, swap_grp = mask_dev[...] > 0.5, mask_grp[...] > 0.5

    def block(slot):
        def of(f):
            value = fields[slot, f]
            if slot == 0:
                value = jnp.where(swap_grp[:EDGE], block_grp[f * EDGE : (f + 1) * EDGE], value)
            if slot == SLOTS - 1:
                value = jnp.where(swap_dev[:EDGE], block_dev[f * EDGE : (f + 1) * EDGE], value)
            return value

        return of

    for slot in range(SLOTS):
        fill_slot(state, slot, block(slot))
    rows, even = slot_rows(), even_place("grp")
    first_rows = (rows == 0) & swap_grp
    other = block_grp[size : size + ROWS]
    got = jnp.where((rows == 0) | (rows == SLOTS - 1), stretched(faces[ROWS:]), other)
    got_deep[...] = jnp.where(first_rows, jnp.where(even, low[2], high[2]), got)
    relayed[...] = jnp.where(rows == SLOTS - 1, jnp.broadcast_to(other[SLOTS - 1 : SLOTS], FACE), 0.0)
    z_low[...] = jnp.where(first_rows & ~even, other, new_low[2])
    z_high[...] = jnp.where(first_rows & even, other, new_high[2])
    inner_kernel(state, scale, partial)


def later_inner_kernel(state, ghosts, scale, partial):
    inner_kernel(state, scale, partial, z_pairs(ghosts[0], ghosts[1]))


def inner_kernel(state, scale, partial, pairs=None):
    ends = ends_of((ROWS, HALF))

    def plane(x):
        halves, at = plane_at(state, x), EDGE - 1 - x
        if pairs is None:
            return halves
        return [half + jnp.where(ends, turned(pairs[h][at % 2], -at), 0.0) for h, half in enumerate(halves)]

    lane = iota((ROWS, HALF), 1)
    start_y, end_y = lane < EDGE, lane >= HALF - EDGE
    start_z, end_z = lane % EDGE == 0, lane % EDGE == EDGE - 1
    weight_x, weight_y, weight_z, weight = (scale[number] for number in range(4))
    tile = 2 * SLOTS
    planes = {0: plane(0)}
    for x in range(EDGE):
        if x + 1 < EDGE:
            planes[x + 1] = plane(x + 1)
        left, right = planes[x]
        up = [turned(half, EDGE) for half in (left, right)]
        down = [turned(half, -EDGE) for half in (left, right)]
        sum_y = (
            jnp.where(start_y, 0.0, up[0]) + jnp.where(end_y, down[1], down[0]),
            jnp.where(start_y, up[0], up[1]) + jnp.where(end_y, 0.0, down[1]),
        )
        for h, half in enumerate((left, right)):
            sum_z = jnp.where(start_z, 0.0, turned(half, 1)) + jnp.where(end_z, 0.0, turned(half, -1))
            if x == 0:
                sum_x = planes[1][h]
            elif x == EDGE - 1:
                sum_x = planes[x - 1][h]
            else:
                sum_x = planes[x - 1][h] + planes[x + 1][h]
            flow = weight * half + weight_x * sum_x + weight_y * sum_y[h] + weight_z * sum_z
            phases, conc = (half[:tile], half[tile : 2 * tile]), half[2 * tile :]
            drive = conc - pltpu.roll(conc, SLOTS, 0)
            total = phases[0] + phases[1]
            total = total + pltpu.roll(total, SLOTS, 0)
            tail = (phase_rate * closure) * (1.0 - total)
            rows = x * ROWS
            for number, value in enumerate(phases):
                gain = value * (1.0 - value) * (coupling[2 * number] * drive + (2.0 * value - 1.0))
                part = flow[number * tile : (number + 1) * tile]
                partial[h, pl.ds(rows + number * tile, tile), :] = part + (phase_rate * gain + tail)
            partial[h, pl.ds(rows + 2 * tile, tile), :] = flow[2 * tile :]


def ghosts_of(axis, scale, select, tables):
    tables = jnp.concatenate(tables, axis=0)
    near = tables.astype(jnp.bfloat16)
    rest = (tables - near.astype(jnp.float32)).astype(jnp.bfloat16)
    both = jnp.concatenate([near, rest], axis=0)
    pair = jnp.dot(select[axis].astype(jnp.bfloat16), both, preferred_element_type=jnp.float32)
    weight = jnp.concatenate([scale[axis]] * 2, axis=1)
    return weight * pair[:ROWS], weight * pair[ROWS:]


def side_by_side(low, high, even):
    return jnp.where(even, low, high), jnp.where(even, high, low)


def sides_kernel(scale, select, partial, low, high, flat_a, flat_b, *refs):
    first_step = len(refs) == 5
    done = refs[0] if first_step else refs[1]
    packer = Packer()
    sources = (low, high, flat_a, flat_b)
    x_low, x_high = ghosts_of(0, scale, select, [ref[0] for ref in sources])
    y_low, y_high = ghosts_of(1, scale, select, [ref[1] for ref in sources])
    lane = iota((ROWS, HALF), 1)
    inside = (lane < EDGE, lane >= HALF - EDGE)
    even = (lane // EDGE) % 2 == 0
    pairs = []
    for h in range(2):
        lanes = slice(h * HALF, (h + 1) * HALF)
        pairs.append(side_by_side(y_low[:, lanes], turned(y_high[:, lanes], -EDGE), even))
    for x in range(EDGE):
        ends = turned(pairs[x // GROUPS][x % 2], -EDGE * (x % GROUPS))
        halves = []
        for h, value in enumerate(plane_at(partial, x)):
            value = value + jnp.where(inside[h], ends, 0.0)
            if x == 0:
                value = value + x_low[:, h * HALF : (h + 1) * HALF]
            if x == EDGE - 1:
                value = value + x_high[:, h * HALF : (h + 1) * HALF]
            done[h, pl.ds(x * ROWS, ROWS), :] = value
            halves.append(value)
        if first_step:
            packer.add_z(x, *halves)
            packer.add_y(x, *halves)
    if first_step:
        for h in range(2):
            for ref, table in zip(refs[1:], (*packer.z_tables(h), *packer.y_tables(h))):
                ref[:, h * HALF : (h + 1) * HALF] = table
    else:
        blocks = refs[0]
        for slot in range(SLOTS):
            for f in range(NFIELD):
                for h in range(2):
                    rows = pl.ds(f * SLOTS + slot, EDGE, stride=ROWS)
                    blocks[slot, f, :, h * HALF : (h + 1) * HALF] = done[h, rows, :]


def z_ghosts(turns, own, deep_a, deep_b):
    even = even_place("grp")
    came = (jnp.where(even, deep_b, deep_a), jnp.where(even, deep_a, deep_b))
    ghosts = []
    for side in range(2):
        halves = []
        for h in range(2):
            lanes = slice(h * HALF, (h + 1) * HALF)
            table = came[side][:, lanes].reshape(NFIELD // 2, 2 * SLOTS, HALF)
            total = turns[side, 2 * SLOTS - 1] * own[side][:, lanes]
            for term in range(2 * SLOTS - 1):
                shift = (term - SLOTS + 1) % (2 * SLOTS)
                moved = pltpu.roll(table, shift, 1) if shift else table
                total = total + turns[side, term] * moved.reshape(ROWS, HALF)
            halves.append(total)
        ghosts.append(jnp.concatenate(halves, axis=1))
    return ghosts


def z_pairs(z_low, z_high):
    even = iota((ROWS, HALF), 1) % 2 == 0
    halves = [slice(h * HALF, (h + 1) * HALF) for h in range(2)]
    return [side_by_side(z_low[:, lanes], turned(z_high[:, lanes], EDGE - 1), even) for lanes in halves]


def ends_of(shape):
    place = iota(shape, 1) % EDGE
    return (place == 0) | (place == EDGE - 1)


def finish_kernel(turns, partial, packed_z, packed_y, known, deep_b, flat_a, relayed, own_z, outs):
    low, high, *sends, ghosts = outs
    deep_a = jnp.where(relayed[...] > 0.5, flat_a[2], known[...])
    both = z_ghosts(turns, [ref[...] for ref in own_z], deep_a, deep_b[...])
    pairs = z_pairs(*both)
    lane = iota((ROWS, HALF), 1)
    ends, group = ends_of((ROWS, HALF)), lane // EDGE
    for side, ref in enumerate((low, high)):
        ghosts[side] = both[side]
        x = side * (EDGE - 1)
        at = EDGE - 1 - x
        for h, half in enumerate(plane_at(partial, x)):
            lanes = slice(h * HALF, (h + 1) * HALF)
            ref[0, :, lanes] = half + jnp.where(ends, turned(pairs[h][at % 2], -at), 0.0)
        ref[2] = packed_z[side][...] + both[side]
        for h in range(2):
            total = jnp.zeros((ROWS, HALF), jnp.float32)
            for number in range(GROUPS):
                at = EDGE - 1 - (h * GROUPS + number)
                moved = turned(pairs[side][at % 2], EDGE * number - at - side * (HALF - EDGE))
                total = jnp.where(ends & (group == number), moved, total)
            lanes = slice(h * HALF, (h + 1) * HALF)
            ref[1, :, lanes] = packed_y[side][:, lanes] + total
    emit_faces((low, high), sends)


def finish_0_kernel(turns, partial, *refs):
    packed, (known, deep_b, flat_a, relayed), own_z, outs = refs[:4], refs[4:8], refs[8:10], refs[10:]
    finish_kernel(turns, partial, packed[:2], packed[2:], known, deep_b, flat_a, relayed, own_z, outs)


def last_kernel(turns, partial, low, high, deep_first, deep_second, result, rows_of, blocks, sent):
    first, second, swapped = deep_first[...], deep_second[...], swapped_order(lax.axis_index("dev"))
    came = jnp.where(swapped, second, first), jnp.where(swapped, first, second)
    for h, pair in enumerate(z_pairs(*z_ghosts(turns, (low[2], high[2]), *came))):
        for odd in range(2):
            rows_of[h, odd] = pair[odd]
    shape = (EDGE, HALF)
    ends, even = ends_of(shape), iota(shape, 0) % 2 == 0
    copies = []
    for slot in range(SLOTS):
        for f in range(NFIELD):
            row = pl.ds(f * SLOTS + slot, 1)
            for h in range(2):
                both = [jnp.broadcast_to(rows_of[h, odd, row, :], shape) for odd in (1, 0)]
                ghost = pltpu.roll(jnp.where(even, *both), HALF - EDGE + 1, 1, stride=1, stride_axis=0)
                lanes = pl.ds(h * HALF, HALF)
                blocks[slot, f, :, lanes] = partial[slot, f, :, lanes] + jnp.where(ends, ghost, 0.0)
            if f % PIECE == PIECE - 1:
                part = (slot, pl.ds(f + 1 - PIECE, PIECE))
                copy = pltpu.make_async_copy(blocks.at[part], result.at[part], sent.at[len(copies)])
                copy.start()
                copies.append(copy)
    for copy in copies:
        copy.wait()


def spec(space):
    return pl.BlockSpec(memory_space=space)


VECTOR = pltpu.VMEM
SMALL = pltpu.CompilerParams(vmem_limit_bytes=8 << 20)
FLAT = (2, ROWS, PLANE)
TABLES = (SIDE, SIDE, FLAT, FLAT, FACE, FACE, (2, *FACE))
EARLY = (ROWS + 4 * SLOTS, PLANE)
TO_DEV = (NFIELD * EDGE, PLANE)
TO_GRP = (NFIELD * EDGE + ROWS, PLANE)


def shaped(shape):
    return jax.ShapeDtypeStruct(shape, jnp.float32)


def cost(flops):
    return pl.CostEstimate(flops=flops, bytes_accessed=min(flops, 2 << 20), transcendentals=0)


def call(kernel, name, shapes, vectors, flops=1 << 20, scratch=()):
    return pl.pallas_call(
        kernel,
        name=name,
        compiler_params=SMALL,
        out_shape=[shaped(shape) for shape in shapes],
        in_specs=[spec(VECTOR)] * len(vectors),
        out_specs=[spec(VECTOR)] * len(shapes),
        scratch_shapes=list(scratch),
        cost_estimate=cost(flops),
    )(*vectors)


def start(fields):
    shapes = (fields.shape, SIDE, SIDE, EARLY, EARLY)
    return pl.pallas_call(
        start_kernel,
        name="start",
        compiler_params=SMALL,
        out_shape=[shaped(shape) for shape in shapes],
        in_specs=[spec(pl.ANY)],
        out_specs=[spec(VECTOR)] * len(shapes),
        scratch_shapes=[pltpu.VMEM(SPARE, jnp.float32), pltpu.SemaphoreType.DMA((2,))],
    )(pltpu.with_memory_space_constraint(fields, pltpu.HBM))


def plan(neighbors, orient, sent):
    return pl.pallas_call(
        plan_kernel,
        name="plan",
        compiler_params=SMALL,
        out_shape=[shaped((4, ROWS, HALF)), shaped(SELECT), shaped(TURNS)],
        in_specs=[spec(pltpu.SMEM)] * 2 + [spec(VECTOR)],
        out_specs=[spec(VECTOR)] * 3,
        cost_estimate=cost(1 << 20),
    )(neighbors, orient, sent)


def mask(flag):
    return jnp.broadcast_to(jnp.where(flag == 1, 1.0, 0.0).reshape(1, 1), FACE)


def body(fields, swap_dev, swap_grp, neighbors, orient):
    fields, low, high, faces, faces_dev = start(fields)
    swap_dev, faces = lax.optimization_barrier((swap_dev, faces))
    faces = exchange(faces, "grp", 0)
    faces_dev = exchange(faces_dev, "dev", 0)
    mask_dev = mask(swap_dev)
    to_dev, to_grp = call(block_kernel, "blocks", [TO_DEV, TO_GRP], [mask_dev, fields, low, high], 1 << 28)
    swap_grp, to_grp = lax.optimization_barrier((swap_grp, to_grp))
    mask_grp = mask(swap_grp)
    block_grp = exchange(to_grp, "grp", 0)
    block_dev = exchange(to_dev, "dev", 0)
    new_low, new_high, *sends = call(
        faces_kernel,
        "faces",
        [SIDE, SIDE, SIDE, FLAT, FACE],
        [mask_dev, mask_grp, low, high, faces, faces_dev],
        1 << 28,
    )
    flat_a = exchange(sends[0], "dev", 0)
    flat_b = exchange(sends[1], "dev", 1)
    deep_b = exchange(sends[2], "grp", 1)
    scale, select, turns = plan(neighbors, orient, sends[2])
    partial, deep_a, relayed, z_low, z_high = call(
        first_inner_kernel,
        "inner_0",
        [STATE, FACE, FACE, FACE, FACE],
        [mask_dev, mask_grp, scale, fields, block_dev, block_grp, faces, low, high, new_low, new_high],
        4 << 20,
        [pltpu.VMEM(SPARE, jnp.float32)],
    )
    partial, *packed = call(
        sides_kernel,
        "sides_0",
        [STATE, FACE, FACE, FACE, FACE],
        [scale, select, partial, new_low, new_high, flat_a, flat_b],
    )
    *tables, ghosts = call(
        finish_0_kernel,
        "finish_0",
        TABLES,
        [turns, partial, *packed, deep_a, deep_b, flat_a, relayed, z_low, z_high],
    )
    own, sends = tables[:2], tables[2:]
    flat_a = exchange(sends[0], "dev", 0)
    flat_b = exchange(sends[1], "dev", 1)
    deep_first = exchange(sends[2], "grp", lambda dev: 1 if swapped_order(dev) else 0)
    deep_second = exchange(sends[3], "grp", lambda dev: 0 if swapped_order(dev) else 1)
    (partial,) = call(later_inner_kernel, "inner_1", [STATE], [partial, ghosts, scale], 4 << 20)
    (blocks,) = call(
        sides_kernel,
        "sides_1",
        [fields.shape],
        [scale, select, partial, *own, flat_a, flat_b],
        scratch=[pltpu.VMEM(SPARE, jnp.float32)],
    )
    return pl.pallas_call(
        last_kernel,
        name="finish_1",
        compiler_params=SMALL,
        out_shape=shaped(fields.shape),
        in_specs=[spec(VECTOR)] * 6,
        out_specs=spec(pl.ANY),
        scratch_shapes=[
            pltpu.VMEM((2, 2, ROWS, HALF), jnp.float32),
            pltpu.VMEM(fields.shape, jnp.float32),
            pltpu.SemaphoreType.DMA((SLOTS * NFIELD // PIECE,)),
        ],
    )(turns, blocks, *own, deep_first, deep_second)


def solution(mesh):
    in_specs = (
        P(("grp", "dev"), None, None, None),
        P(("grp", "dev")),
        P(("grp", "dev")),
        P(("grp", "dev"), None),
        P(("grp", "dev")),
    )
    out_specs = P(("grp", "dev"), None, None, None)
    return jax.shard_map(body, mesh=mesh, in_specs=in_specs, out_specs=out_specs, check_vma=False)
```

```python
import math

import jax
import jax.numpy as jnp
from jax import lax
from jax.experimental import pallas as pl
from jax.experimental.pallas import tpu as pltpu
from jax.sharding import PartitionSpec as P

NPHASE = 4
NCONC = 2
NFIELD = NPHASE + NCONC
EDGE = 16
PLANE = EDGE * EDGE
HALF = PLANE // 2
GROUPS = HALF // EDGE
SLOTS = 4
ROWS = NFIELD * SLOTS

phase_rate = 0.05
closure = 0.1
coupling = (0.5, -0.5, 1.0, -1.0)
conc_rates = (0.08, 0.04)

STATE = (2, EDGE * ROWS, HALF)
SPARE = (2, (EDGE + 1) * ROWS, HALF)
FACE = (ROWS, PLANE)
SIDE = (3, ROWS, PLANE)
SOURCES = 4
PARTS = 2
SELECT = (2, 2 * ROWS, PARTS * SOURCES * ROWS)
PIECE = 3
TURNS = (2, 2 * SLOTS, ROWS, HALF)


def swapped_order(dev):
    return dev // 4 % 2 == 1


def partners(axis, offset):
    sizes = (lax.axis_size("grp"), lax.axis_size("dev"))
    along = ("grp", "dev").index(axis)
    route = []
    for grp in range(sizes[0]):
        for dev in range(sizes[1]):
            own = (grp, dev)
            start = offset(dev) if callable(offset) else offset
            partner = list(own)
            partner[along] += 1 if (own[along] - start) % 2 == 0 else -1
            if not 0 <= partner[along] < sizes[along]:
                partner = list(own)
                partner[1 - along] ^= 1
                if partner[1 - along] >= sizes[1 - along]:
                    partner = list(own)
            route.append((grp * sizes[1] + dev, partner[0] * sizes[1] + partner[1]))
    return route


def exchange(block, axis, offset):
    return lax.ppermute(block, ("grp", "dev"), partners(axis, offset))


def iota(shape, dim):
    return lax.broadcasted_iota(jnp.int32, shape, dim)


def plane_at(ref, x):
    rows = pl.ds(x * ROWS, ROWS)
    return ref[0, rows, :], ref[1, rows, :]


def turned(value, shift):
    shift %= HALF
    return pltpu.roll(value, shift, 1) if shift else value


class Packer:
    def __init__(self):
        lane = iota((ROWS, HALF), 1)
        self.lane, self.group, self.place = lane, lane // EDGE, lane % EDGE
        self.y = [[None, None], [None, None]]
        self.z = [[None, None], [None, None]]

    def add_y(self, x, left, right):
        odd, half, at = x % 2, x // GROUPS, x % GROUPS
        ends = turned(jnp.where(self.lane < EDGE, left, right), EDGE * at)
        taken = (self.group == at) | (self.group == (at + GROUPS - 1) % GROUPS)
        before = self.y[half][odd]
        self.y[half][odd] = ends if before is None else jnp.where(taken, ends, before)

    def add_z(self, x, left, right):
        at = EDGE - 1 - x
        odd = at % 2
        taken = (self.place == at) | (self.place == (at + EDGE - 1) % EDGE)
        for h, value in enumerate((left, right)):
            moved = turned(value, at)
            before = self.z[h][odd]
            self.z[h][odd] = moved if before is None else jnp.where(taken, moved, before)

    def y_tables(self, h):
        even, (first, second) = self.group % 2 == 0, self.y[h]
        return jnp.where(even, first, second), turned(jnp.where(even, second, first), EDGE)

    def z_tables(self, h):
        even, (first, second) = self.place % 2 == 0, self.z[h]
        return jnp.where(even, first, second), turned(jnp.where(even, second, first), 1 - EDGE)


def write_tables(packer, state, own):
    low, high = own
    for h in range(2):
        lanes = pl.ds(h * HALF, HALF)
        for ref, x in ((low, 0), (high, EDGE - 1)):
            ref[0, :, lanes] = state[h, pl.ds(x * ROWS, ROWS), :]
        for ref, table in zip(own, packer.y_tables(h)):
            ref[1, :, lanes] = table


def emit_faces(own, sends):
    low, high = own
    flat_a, flat_b, deep_first, deep_second = sends
    even = even_place("dev")
    for face in range(2):
        flat_a[face] = jnp.where(even, high[face], low[face])
        flat_b[face] = jnp.where(even, low[face], high[face])
    upper = even_place("grp") != swapped_order(lax.axis_index("dev"))
    deep_first[...] = jnp.where(upper, high[2], low[2])
    deep_second[...] = jnp.where(upper, low[2], high[2])


def fill_slot(state, slot, block, first=0, count=EDGE):
    for f in range(NFIELD):
        value = block(f)
        for h in range(2):
            rows = pl.ds(first * ROWS + f * SLOTS + slot, count, stride=ROWS)
            state[h, rows, :] = value[:, h * HALF : (h + 1) * HALF]


def slot_rows():
    return iota(FACE, 0) % SLOTS


def shifted(value, rows):
    rows %= ROWS
    return pltpu.roll(value, rows, 0) if rows else value


def gathered(tables, slot):
    rows = slot_rows()
    out = shifted(tables[0], -slot)
    for number in range(1, len(tables)):
        out = jnp.where(rows == number, shifted(tables[number], number - slot), out)
    return out


def squeezed(table):
    tile = 2 * SLOTS
    rows = iota((tile, PLANE), 0) % SLOTS
    first, second, third = (table[number * tile : (number + 1) * tile] for number in range(3))
    between = jnp.where(rows == 1, pltpu.roll(second, 1, 0), pltpu.roll(second, tile - 1, 0))
    return jnp.concatenate([jnp.where((rows == 1) | (rows == 2), between, first), third], axis=0)


def stretched(value):
    tile = 2 * SLOTS
    rows = iota((tile, PLANE), 0) % SLOTS
    first, third = value[:tile], value[tile:]
    second = jnp.where(rows == 0, pltpu.roll(first, tile - 1, 0), pltpu.roll(first, 1, 0))
    return jnp.concatenate([first, second, third], axis=0)


def scattered(table, number, slot):
    return shifted(table, slot - number)


def even_place(axis):
    return lax.rem(lax.axis_index(axis), 2) == 0


def block_kernel(mask_dev, fields, low, high, to_dev, to_grp):
    last, size = SLOTS - 1, NFIELD * EDGE
    for f in range(NFIELD):
        to_dev[f * EDGE : (f + 1) * EDGE] = fields[last, f]
        to_grp[f * EDGE : (f + 1) * EDGE] = fields[0, f]
    rows, even = slot_rows(), even_place("grp")
    table = jnp.where(rows == 0, jnp.where(even, low[2], high[2]), jnp.where(even, high[2], low[2]))
    to_grp[size : size + ROWS] = jnp.where(rows == SLOTS - 1, mask_dev[...], table)


def faces_kernel(mask_dev, mask_grp, low, high, faces, faces_dev, *outs):
    new_low, new_high, flat_a, flat_b, deep_b = outs
    rows, last = slot_rows(), SLOTS - 1
    first_rows = (rows == 0) & (mask_grp[...] > 0.5)
    last_rows = (rows == last) & (mask_dev[...] > 0.5)
    even = even_place("grp")
    got_first, got_last = faces[:ROWS], faces_dev[:ROWS]
    got_z, got_last_z = stretched(faces[ROWS:]), stretched(faces_dev[ROWS:])
    for side, (raw, new) in enumerate(((low, new_low), (high, new_high))):
        for axis in range(2):
            number = 2 * axis + side
            table = jnp.where(first_rows, scattered(got_first, number, 0), raw[axis])
            new[axis] = jnp.where(last_rows, scattered(got_last, number, last), table)
        table = jnp.where(first_rows & (even if side == 0 else ~even), got_z, raw[2])
        new[2] = jnp.where(last_rows, scattered(got_last_z, side * last, last), table)
    even_dev = even_place("dev")
    for axis in range(2):
        flat_a[axis] = jnp.where(even_dev, new_high[axis], new_low[axis])
        flat_b[axis] = jnp.where(even_dev, new_low[axis], new_high[axis])
    flat_a[2] = got_z
    deep_b[...] = jnp.where(even, new_low[2], new_high[2])


def cos_quarter(number):
    turn = number & 7
    size = jnp.where((turn & 3) == 0, 1.0, jnp.where((turn & 3) == 2, 0.0, math.sqrt(0.5)))
    return jnp.where((turn > 2) & (turn < 6), -size, size)


def plan_kernel(neighbors, orient, scale, select, turns):
    shape = (ROWS, HALF)
    slot, field, column = iota(shape, 0) % SLOTS, iota(shape, 0) // SLOTS, iota(shape, 1)
    grp, dev = lax.axis_index("grp"), lax.axis_index("dev")
    rank = grp * lax.axis_size("dev") + dev

    def by_slot(values):
        rows = values[0]
        for number in range(1, SLOTS):
            rows = jnp.where(slot == number, values[number], rows)
        return rows

    spread = []
    for number in range(SLOTS):
        turn = 0.5 * cos_quarter(orient[number])
        lift = 0.5 * cos_quarter(orient[number] + 6)
        spread.append((1.0 + turn, 1.0 - turn, 1.0 + lift))
    conc = jnp.where(field == NPHASE, conc_rates[0], conc_rates[1])
    weights = [jnp.where(field < NPHASE, phase_rate * by_slot([own[axis] for own in spread]), conc) for axis in range(3)]
    for axis in range(3):
        scale[axis] = weights[axis]
    scale[3] = 1.0 - 2.0 * (weights[0] + weights[1] + weights[2])
    for face in range(4, 6):
        where_from = []
        for number in range(SLOTS):
            target = neighbors[number, face]
            where_from.append(jnp.where(target < 0, 2 * SLOTS - 1, number - (target & (SLOTS - 1)) + SLOTS - 1))
        rows = by_slot(where_from)
        for term in range(2 * SLOTS):
            turns[face - 4, term] = jnp.where(rows == term, weights[2], 0.0)
    for face in range(4):
        first = []
        came = 2 + lax.rem(lax.rem(dev, 2) + face % 2 + 1, 2)
        for number in range(SLOTS):
            target = neighbors[number, face]
            source = jnp.where(target < 0, face % 2, jnp.where(target // SLOTS == rank, 1 - face % 2, came))
            first.append(source * ROWS + jnp.where(target < 0, number, target & (SLOTS - 1)))
        chosen = jnp.where(column == by_slot(first) + field * SLOTS, 1.0, 0.0)[:, : SOURCES * ROWS]
        rows = pl.ds(face % 2 * ROWS, ROWS)
        for part in range(PARTS):
            select[face // 2, rows, pl.ds(part * SOURCES * ROWS, SOURCES * ROWS)] = chosen


def start_kernel(fields, neighbors, orient, *refs):
    fetched, low, high, faces_grp, faces_dev, scale, select, turns = refs[:8]
    state, near, turn, arrived = refs[8:]
    scalars = ((neighbors, near), (orient, turn))
    parts = [pl.ds(first, EDGE // 2) for first in (0, EDGE // 2)]
    blocks = tuple((fields.at[:, :, part], fetched.at[:, :, part]) for part in parts)
    copies = [pltpu.make_async_copy(*pair, arrived.at[number]) for number, pair in enumerate((*scalars, *blocks))]
    for copy in copies:
        copy.start()
    for copy in copies[: len(scalars)]:
        copy.wait()
    plan_kernel(near, turn, scale, select, turns)
    packer = Packer()
    for number, part in enumerate(parts):
        copies[len(scalars) + number].wait()
        first = number * (EDGE // 2)
        for slot in range(SLOTS):
            fill_slot(state, slot, lambda f: fetched[slot, f, part], first, EDGE // 2)
        for x in range(first, first + EDGE // 2):
            packer.add_y(x, *plane_at(state, x))
            packer.add_z(x, *plane_at(state, x))
    write_tables(packer, state, (low, high))
    for h in range(2):
        for ref, table in zip((low, high), packer.z_tables(h)):
            ref[2, :, h * HALF : (h + 1) * HALF] = table
    faces_grp[:ROWS] = gathered([low[0], high[0], low[1], high[1]], 0)
    faces_grp[ROWS:] = squeezed(jnp.where(even_place("grp"), high[2], low[2]))
    faces_dev[:ROWS] = gathered([low[0], high[0], low[1], high[1]], SLOTS - 1)
    faces_dev[ROWS:] = squeezed(gathered([low[2], low[2], low[2], high[2]], SLOTS - 1))


def first_inner_kernel(mask_dev, mask_grp, scale, fields, block_dev, block_grp, faces, low, high, new_low, new_high, *refs):
    partial, got_deep, relayed, z_low, z_high, state = refs
    size = NFIELD * EDGE
    swap_dev, swap_grp = mask_dev[...] > 0.5, mask_grp[...] > 0.5

    def block(slot):
        def of(f):
            value = fields[slot, f]
            if slot == 0:
                value = jnp.where(swap_grp[:EDGE], block_grp[f * EDGE : (f + 1) * EDGE], value)
            if slot == SLOTS - 1:
                value = jnp.where(swap_dev[:EDGE], block_dev[f * EDGE : (f + 1) * EDGE], value)
            return value

        return of

    for slot in range(SLOTS):
        fill_slot(state, slot, block(slot))
    rows, even = slot_rows(), even_place("grp")
    first_rows = (rows == 0) & swap_grp
    other = block_grp[size : size + ROWS]
    got = jnp.where((rows == 0) | (rows == SLOTS - 1), stretched(faces[ROWS:]), other)
    got_deep[...] = jnp.where(first_rows, jnp.where(even, low[2], high[2]), got)
    relayed[...] = jnp.where(rows == SLOTS - 1, jnp.broadcast_to(other[SLOTS - 1 : SLOTS], FACE), 0.0)
    z_low[...] = jnp.where(first_rows & ~even, other, new_low[2])
    z_high[...] = jnp.where(first_rows & even, other, new_high[2])
    inner_kernel(state, scale, partial)


def later_inner_kernel(state, ghosts, scale, partial):
    inner_kernel(state, scale, partial, z_pairs(ghosts[0], ghosts[1]))


def inner_kernel(state, scale, partial, pairs=None):
    ends = ends_of((ROWS, HALF))

    def plane(x):
        halves, at = plane_at(state, x), EDGE - 1 - x
        if pairs is None:
            return halves
        return [half + jnp.where(ends, turned(pairs[h][at % 2], -at), 0.0) for h, half in enumerate(halves)]

    lane = iota((ROWS, HALF), 1)
    start_y, end_y = lane < EDGE, lane >= HALF - EDGE
    start_z, end_z = lane % EDGE == 0, lane % EDGE == EDGE - 1
    weight_x, weight_y, weight_z, weight = (scale[number] for number in range(4))
    tile = 2 * SLOTS
    planes = {0: plane(0)}
    for x in range(EDGE):
        if x + 1 < EDGE:
            planes[x + 1] = plane(x + 1)
        left, right = planes[x]
        up = [turned(half, EDGE) for half in (left, right)]
        down = [turned(half, -EDGE) for half in (left, right)]
        sum_y = (
            jnp.where(start_y, 0.0, up[0]) + jnp.where(end_y, down[1], down[0]),
            jnp.where(start_y, up[0], up[1]) + jnp.where(end_y, 0.0, down[1]),
        )
        for h, half in enumerate((left, right)):
            sum_z = jnp.where(start_z, 0.0, turned(half, 1)) + jnp.where(end_z, 0.0, turned(half, -1))
            if x == 0:
                sum_x = planes[1][h]
            elif x == EDGE - 1:
                sum_x = planes[x - 1][h]
            else:
                sum_x = planes[x - 1][h] + planes[x + 1][h]
            flow = weight * half + weight_x * sum_x + weight_y * sum_y[h] + weight_z * sum_z
            phases, conc = (half[:tile], half[tile : 2 * tile]), half[2 * tile :]
            drive = conc - pltpu.roll(conc, SLOTS, 0)
            total = phases[0] + phases[1]
            total = total + pltpu.roll(total, SLOTS, 0)
            tail = (phase_rate * closure) * (1.0 - total)
            rows = x * ROWS
            for number, value in enumerate(phases):
                gain = value * (1.0 - value) * (coupling[2 * number] * drive + (2.0 * value - 1.0))
                part = flow[number * tile : (number + 1) * tile]
                partial[h, pl.ds(rows + number * tile, tile), :] = part + (phase_rate * gain + tail)
            partial[h, pl.ds(rows + 2 * tile, tile), :] = flow[2 * tile :]


def ghosts_of(axis, scale, select, tables):
    tables = jnp.concatenate(tables, axis=0)
    near = tables.astype(jnp.bfloat16)
    rest = (tables - near.astype(jnp.float32)).astype(jnp.bfloat16)
    both = jnp.concatenate([near, rest], axis=0)
    pair = jnp.dot(select[axis].astype(jnp.bfloat16), both, preferred_element_type=jnp.float32)
    weight = jnp.concatenate([scale[axis]] * 2, axis=1)
    return weight * pair[:ROWS], weight * pair[ROWS:]


def side_by_side(low, high, even):
    return jnp.where(even, low, high), jnp.where(even, high, low)


def sides_kernel(scale, select, partial, low, high, flat_a, flat_b, *refs):
    first_step = len(refs) == 5
    done = refs[0] if first_step else refs[1]
    packer = Packer()
    sources = (low, high, flat_a, flat_b)
    x_low, x_high = ghosts_of(0, scale, select, [ref[0] for ref in sources])
    y_low, y_high = ghosts_of(1, scale, select, [ref[1] for ref in sources])
    lane = iota((ROWS, HALF), 1)
    inside = (lane < EDGE, lane >= HALF - EDGE)
    even = (lane // EDGE) % 2 == 0
    pairs = []
    for h in range(2):
        lanes = slice(h * HALF, (h + 1) * HALF)
        pairs.append(side_by_side(y_low[:, lanes], turned(y_high[:, lanes], -EDGE), even))
    for x in range(EDGE):
        ends = turned(pairs[x // GROUPS][x % 2], -EDGE * (x % GROUPS))
        halves = []
        for h, value in enumerate(plane_at(partial, x)):
            value = value + jnp.where(inside[h], ends, 0.0)
            if x == 0:
                value = value + x_low[:, h * HALF : (h + 1) * HALF]
            if x == EDGE - 1:
                value = value + x_high[:, h * HALF : (h + 1) * HALF]
            done[h, pl.ds(x * ROWS, ROWS), :] = value
            halves.append(value)
        if first_step:
            packer.add_z(x, *halves)
            packer.add_y(x, *halves)
    if first_step:
        for h in range(2):
            for ref, table in zip(refs[1:], (*packer.z_tables(h), *packer.y_tables(h))):
                ref[:, h * HALF : (h + 1) * HALF] = table
    else:
        blocks = refs[0]
        for slot in range(SLOTS):
            for f in range(NFIELD):
                for h in range(2):
                    rows = pl.ds(f * SLOTS + slot, EDGE, stride=ROWS)
                    blocks[slot, f, :, h * HALF : (h + 1) * HALF] = done[h, rows, :]


def z_ghosts(turns, own, deep_a, deep_b):
    even = even_place("grp")
    came = (jnp.where(even, deep_b, deep_a), jnp.where(even, deep_a, deep_b))
    ghosts = []
    for side in range(2):
        halves = []
        for h in range(2):
            lanes = slice(h * HALF, (h + 1) * HALF)
            table = came[side][:, lanes].reshape(NFIELD // 2, 2 * SLOTS, HALF)
            total = turns[side, 2 * SLOTS - 1] * own[side][:, lanes]
            for term in range(2 * SLOTS - 1):
                shift = (term - SLOTS + 1) % (2 * SLOTS)
                moved = pltpu.roll(table, shift, 1) if shift else table
                total = total + turns[side, term] * moved.reshape(ROWS, HALF)
            halves.append(total)
        ghosts.append(jnp.concatenate(halves, axis=1))
    return ghosts


def z_pairs(z_low, z_high):
    even = iota((ROWS, HALF), 1) % 2 == 0
    halves = [slice(h * HALF, (h + 1) * HALF) for h in range(2)]
    return [side_by_side(z_low[:, lanes], turned(z_high[:, lanes], EDGE - 1), even) for lanes in halves]


def ends_of(shape):
    place = iota(shape, 1) % EDGE
    return (place == 0) | (place == EDGE - 1)


def finish_kernel(turns, partial, packed_z, packed_y, known, deep_b, flat_a, relayed, own_z, outs):
    low, high, *sends, ghosts = outs
    deep_a = jnp.where(relayed[...] > 0.5, flat_a[2], known[...])
    both = z_ghosts(turns, [ref[...] for ref in own_z], deep_a, deep_b[...])
    pairs = z_pairs(*both)
    lane = iota((ROWS, HALF), 1)
    ends, group = ends_of((ROWS, HALF)), lane // EDGE
    made = [[], []]
    for side, ref in enumerate((low, high)):
        ghosts[side] = both[side]
        x_halves, y_halves = [], []
        x = side * (EDGE - 1)
        at = EDGE - 1 - x
        for h, half in enumerate(plane_at(partial, x)):
            x_halves.append(half + jnp.where(ends, turned(pairs[h][at % 2], -at), 0.0))
        for h in range(2):
            total = jnp.zeros((ROWS, HALF), jnp.float32)
            for number in range(GROUPS):
                at = EDGE - 1 - (h * GROUPS + number)
                moved = turned(pairs[side][at % 2], EDGE * number - at - side * (HALF - EDGE))
                total = jnp.where(ends & (group == number), moved, total)
            lanes = slice(h * HALF, (h + 1) * HALF)
            y_halves.append(packed_y[side][:, lanes] + total)
        z_face = packed_z[side][...] + both[side]
        made[side] = [jnp.concatenate(x_halves, axis=1), jnp.concatenate(y_halves, axis=1), z_face]
        for axis in range(3):
            ref[axis] = made[side][axis]
    emit_faces(made, sends)


def finish_0_kernel(turns, partial, *refs):
    packed, (known, deep_b, flat_a, relayed), own_z, outs = refs[:4], refs[4:8], refs[8:10], refs[10:]
    finish_kernel(turns, partial, packed[:2], packed[2:], known, deep_b, flat_a, relayed, own_z, outs)


def last_kernel(turns, partial, low, high, deep_first, deep_second, result, rows_of, blocks, sent):
    first, second, swapped = deep_first[...], deep_second[...], swapped_order(lax.axis_index("dev"))
    came = jnp.where(swapped, second, first), jnp.where(swapped, first, second)
    for h, pair in enumerate(z_pairs(*z_ghosts(turns, (low[2], high[2]), *came))):
        for odd in range(2):
            rows_of[h, odd] = pair[odd]
    shape = (EDGE, HALF)
    ends, even = ends_of(shape), iota(shape, 0) % 2 == 0
    copies = []
    for slot in range(SLOTS):
        for f in range(NFIELD):
            row = pl.ds(f * SLOTS + slot, 1)
            for h in range(2):
                both = [jnp.broadcast_to(rows_of[h, odd, row, :], shape) for odd in (1, 0)]
                ghost = pltpu.roll(jnp.where(even, *both), HALF - EDGE + 1, 1, stride=1, stride_axis=0)
                lanes = pl.ds(h * HALF, HALF)
                blocks[slot, f, :, lanes] = partial[slot, f, :, lanes] + jnp.where(ends, ghost, 0.0)
            if f % PIECE == PIECE - 1:
                part = (slot, pl.ds(f + 1 - PIECE, PIECE))
                copy = pltpu.make_async_copy(blocks.at[part], result.at[part], sent.at[len(copies)])
                copy.start()
                copies.append(copy)
    for copy in copies:
        copy.wait()


def spec(space):
    return pl.BlockSpec(memory_space=space)


VECTOR = pltpu.VMEM
SMALL = pltpu.CompilerParams(vmem_limit_bytes=8 << 20)
FLAT = (2, ROWS, PLANE)
TABLES = (SIDE, SIDE, FLAT, FLAT, FACE, FACE, (2, *FACE))
EARLY = (ROWS + 4 * SLOTS, PLANE)
TO_DEV = (NFIELD * EDGE, PLANE)
TO_GRP = (NFIELD * EDGE + ROWS, PLANE)


def shaped(shape):
    return jax.ShapeDtypeStruct(shape, jnp.float32)


def cost(flops):
    return pl.CostEstimate(flops=flops, bytes_accessed=min(flops, 2 << 20), transcendentals=0)


def call(kernel, name, shapes, vectors, flops=1 << 20, scratch=()):
    return pl.pallas_call(
        kernel,
        name=name,
        compiler_params=SMALL,
        out_shape=[shaped(shape) for shape in shapes],
        in_specs=[spec(VECTOR)] * len(vectors),
        out_specs=[spec(VECTOR)] * len(shapes),
        scratch_shapes=list(scratch),
        cost_estimate=cost(flops),
    )(*vectors)


def start(arguments):
    shapes = (arguments[0].shape, SIDE, SIDE, EARLY, EARLY, (4, ROWS, HALF), SELECT, TURNS)
    return pl.pallas_call(
        start_kernel,
        name="start",
        compiler_params=SMALL,
        out_shape=[shaped(shape) for shape in shapes],
        in_specs=[spec(pl.ANY)] * len(arguments),
        out_specs=[spec(VECTOR)] * len(shapes),
        scratch_shapes=[
            pltpu.VMEM(SPARE, jnp.float32),
            *(pltpu.SMEM(array.shape, jnp.int32) for array in arguments[1:]),
            pltpu.SemaphoreType.DMA((len(arguments) + 1,)),
        ],
    )(*(pltpu.with_memory_space_constraint(array, pltpu.HBM) for array in arguments))


def mask(flag):
    return jnp.broadcast_to(jnp.where(flag == 1, 1.0, 0.0).reshape(1, 1), FACE)


def body(fields, swap_dev, swap_grp, neighbors, orient):
    fields, low, high, faces, faces_dev, scale, select, turns = start((fields, neighbors, orient))
    swap_dev, faces = lax.optimization_barrier((swap_dev, faces))
    faces = exchange(faces, "grp", 0)
    faces_dev = exchange(faces_dev, "dev", 0)
    mask_dev = mask(swap_dev)
    to_dev, to_grp = call(block_kernel, "blocks", [TO_DEV, TO_GRP], [mask_dev, fields, low, high], 1 << 28)
    swap_grp, to_grp = lax.optimization_barrier((swap_grp, to_grp))
    mask_grp = mask(swap_grp)
    block_grp = exchange(to_grp, "grp", 0)
    block_dev = exchange(to_dev, "dev", 0)
    new_low, new_high, *sends = call(
        faces_kernel,
        "faces",
        [SIDE, SIDE, SIDE, FLAT, FACE],
        [mask_dev, mask_grp, low, high, faces, faces_dev],
        1 << 28,
    )
    flat_a = exchange(sends[0], "dev", 0)
    flat_b = exchange(sends[1], "dev", 1)
    deep_b = exchange(sends[2], "grp", 1)
    partial, deep_a, relayed, z_low, z_high = call(
        first_inner_kernel,
        "inner_0",
        [STATE, FACE, FACE, FACE, FACE],
        [mask_dev, mask_grp, scale, fields, block_dev, block_grp, faces, low, high, new_low, new_high],
        4 << 20,
        [pltpu.VMEM(SPARE, jnp.float32)],
    )
    partial, *packed = call(
        sides_kernel,
        "sides_0",
        [STATE, FACE, FACE, FACE, FACE],
        [scale, select, partial, new_low, new_high, flat_a, flat_b],
    )
    *tables, ghosts = call(
        finish_0_kernel,
        "finish_0",
        TABLES,
        [turns, partial, *packed, deep_a, deep_b, flat_a, relayed, z_low, z_high],
    )
    own, sends = tables[:2], tables[2:]
    flat_a = exchange(sends[0], "dev", 0)
    flat_b = exchange(sends[1], "dev", 1)
    deep_first = exchange(sends[2], "grp", lambda dev: 1 if swapped_order(dev) else 0)
    deep_second = exchange(sends[3], "grp", lambda dev: 0 if swapped_order(dev) else 1)
    (partial,) = call(later_inner_kernel, "inner_1", [STATE], [partial, ghosts, scale], 4 << 20)
    (blocks,) = call(
        sides_kernel,
        "sides_1",
        [fields.shape],
        [scale, select, partial, *own, flat_a, flat_b],
        scratch=[pltpu.VMEM(SPARE, jnp.float32)],
    )
    return pl.pallas_call(
        last_kernel,
        name="finish_1",
        compiler_params=SMALL,
        out_shape=shaped(fields.shape),
        in_specs=[spec(VECTOR)] * 6,
        out_specs=spec(pl.ANY),
        scratch_shapes=[
            pltpu.VMEM((2, 2, ROWS, HALF), jnp.float32),
            pltpu.VMEM(fields.shape, jnp.float32),
            pltpu.SemaphoreType.DMA((SLOTS * NFIELD // PIECE,)),
        ],
    )(turns, blocks, *own, deep_first, deep_second)


def solution(mesh):
    in_specs = (
        P(("grp", "dev"), None, None, None),
        P(("grp", "dev")),
        P(("grp", "dev")),
        P(("grp", "dev"), None),
        P(("grp", "dev")),
    )
    out_specs = P(("grp", "dev"), None, None, None)
    return jax.shard_map(body, mesh=mesh, in_specs=in_specs, out_specs=out_specs, check_vma=False)
```

```python
import math

import jax
import jax.numpy as jnp
from jax import lax
from jax.experimental import pallas as pl
from jax.experimental.pallas import tpu as pltpu
from jax.sharding import PartitionSpec as P

NPHASE = 4
NCONC = 2
NFIELD = NPHASE + NCONC
EDGE = 16
PLANE = EDGE * EDGE
HALF = PLANE // 2
GROUPS = HALF // EDGE
SLOTS = 4
ROWS = NFIELD * SLOTS

phase_rate = 0.05
closure = 0.1
coupling = (0.5, -0.5, 1.0, -1.0)
conc_rates = (0.08, 0.04)

STATE = (2, EDGE * ROWS, HALF)
SPARE = (2, (EDGE + 1) * ROWS, HALF)
FACE = (ROWS, PLANE)
SIDE = (3, ROWS, PLANE)
SOURCES = 4
PARTS = 2
SELECT = (2, 2 * ROWS, PARTS * SOURCES * ROWS)
PIECE = 2
TURNS = (2, 2 * SLOTS, ROWS, HALF)


def swapped_order(dev):
    return dev // 4 % 2 == 1


def partners(axis, offset):
    sizes = (lax.axis_size("grp"), lax.axis_size("dev"))
    along = ("grp", "dev").index(axis)
    route = []
    for grp in range(sizes[0]):
        for dev in range(sizes[1]):
            own = (grp, dev)
            start = offset(dev) if callable(offset) else offset
            partner = list(own)
            partner[along] += 1 if (own[along] - start) % 2 == 0 else -1
            if not 0 <= partner[along] < sizes[along]:
                partner = list(own)
                partner[1 - along] ^= 1
                if partner[1 - along] >= sizes[1 - along]:
                    partner = list(own)
            route.append((grp * sizes[1] + dev, partner[0] * sizes[1] + partner[1]))
    return route


def exchange(block, axis, offset):
    return lax.ppermute(block, ("grp", "dev"), partners(axis, offset))


def iota(shape, dim):
    return lax.broadcasted_iota(jnp.int32, shape, dim)


def plane_at(ref, x):
    rows = pl.ds(x * ROWS, ROWS)
    return ref[0, rows, :], ref[1, rows, :]


def turned(value, shift):
    shift %= HALF
    return pltpu.roll(value, shift, 1) if shift else value


class Packer:
    def __init__(self):
        lane = iota((ROWS, HALF), 1)
        self.lane, self.group, self.place = lane, lane // EDGE, lane % EDGE
        self.y = [[None, None], [None, None]]
        self.z = [[None, None], [None, None]]

    def add_y(self, x, left, right):
        odd, half, at = x % 2, x // GROUPS, x % GROUPS
        ends = turned(jnp.where(self.lane < EDGE, left, right), EDGE * at)
        taken = (self.group == at) | (self.group == (at + GROUPS - 1) % GROUPS)
        before = self.y[half][odd]
        self.y[half][odd] = ends if before is None else jnp.where(taken, ends, before)

    def add_z(self, x, left, right):
        at = EDGE - 1 - x
        odd = at % 2
        taken = (self.place == at) | (self.place == (at + EDGE - 1) % EDGE)
        for h, value in enumerate((left, right)):
            moved = turned(value, at)
            before = self.z[h][odd]
            self.z[h][odd] = moved if before is None else jnp.where(taken, moved, before)

    def y_tables(self, h):
        even, (first, second) = self.group % 2 == 0, self.y[h]
        return jnp.where(even, first, second), turned(jnp.where(even, second, first), EDGE)

    def z_tables(self, h):
        even, (first, second) = self.place % 2 == 0, self.z[h]
        return jnp.where(even, first, second), turned(jnp.where(even, second, first), 1 - EDGE)


def write_tables(packer, state, own):
    low, high = own
    for h in range(2):
        lanes = pl.ds(h * HALF, HALF)
        for ref, x in ((low, 0), (high, EDGE - 1)):
            ref[0, :, lanes] = state[h, pl.ds(x * ROWS, ROWS), :]
        for ref, table in zip(own, packer.y_tables(h)):
            ref[1, :, lanes] = table


def emit_faces(own, sends):
    low, high = own
    flat_a, flat_b, deep_first, deep_second = sends
    even = even_place("dev")
    for face in range(2):
        flat_a[face] = jnp.where(even, high[face], low[face])
        flat_b[face] = jnp.where(even, low[face], high[face])
    upper = even_place("grp") != swapped_order(lax.axis_index("dev"))
    deep_first[...] = jnp.where(upper, high[2], low[2])
    deep_second[...] = jnp.where(upper, low[2], high[2])


def fill_slot(state, slot, block, first=0, count=EDGE):
    for f in range(NFIELD):
        value = block(f)
        for h in range(2):
            rows = pl.ds(first * ROWS + f * SLOTS + slot, count, stride=ROWS)
            state[h, rows, :] = value[:, h * HALF : (h + 1) * HALF]


def slot_rows():
    return iota(FACE, 0) % SLOTS


def shifted(value, rows):
    rows %= ROWS
    return pltpu.roll(value, rows, 0) if rows else value


def gathered(tables, slot):
    rows = slot_rows()
    out = shifted(tables[0], -slot)
    for number in range(1, len(tables)):
        out = jnp.where(rows == number, shifted(tables[number], number - slot), out)
    return out


def squeezed(table):
    tile = 2 * SLOTS
    rows = iota((tile, PLANE), 0) % SLOTS
    first, second, third = (table[number * tile : (number + 1) * tile] for number in range(3))
    between = jnp.where(rows == 1, pltpu.roll(second, 1, 0), pltpu.roll(second, tile - 1, 0))
    return jnp.concatenate([jnp.where((rows == 1) | (rows == 2), between, first), third], axis=0)


def stretched(value):
    tile = 2 * SLOTS
    rows = iota((tile, PLANE), 0) % SLOTS
    first, third = value[:tile], value[tile:]
    second = jnp.where(rows == 0, pltpu.roll(first, tile - 1, 0), pltpu.roll(first, 1, 0))
    return jnp.concatenate([first, second, third], axis=0)


def scattered(table, number, slot):
    return shifted(table, slot - number)


def even_place(axis):
    return lax.rem(lax.axis_index(axis), 2) == 0


def block_kernel(mask_dev, fields, low, high, to_dev, to_grp):
    last, size = SLOTS - 1, NFIELD * EDGE
    for f in range(NFIELD):
        to_dev[f * EDGE : (f + 1) * EDGE] = fields[last, f]
        to_grp[f * EDGE : (f + 1) * EDGE] = fields[0, f]
    rows, even = slot_rows(), even_place("grp")
    table = jnp.where(rows == 0, jnp.where(even, low[2], high[2]), jnp.where(even, high[2], low[2]))
    to_grp[size : size + ROWS] = jnp.where(rows == SLOTS - 1, mask_dev[...], table)


def faces_kernel(mask_dev, mask_grp, low, high, faces, faces_dev, *outs):
    new_low, new_high, flat_a, flat_b, deep_b = outs
    rows, last = slot_rows(), SLOTS - 1
    first_rows = (rows == 0) & (mask_grp[...] > 0.5)
    last_rows = (rows == last) & (mask_dev[...] > 0.5)
    even = even_place("grp")
    got_first, got_last = faces[:ROWS], faces_dev[:ROWS]
    got_z, got_last_z = stretched(faces[ROWS:]), stretched(faces_dev[ROWS:])
    for side, (raw, new) in enumerate(((low, new_low), (high, new_high))):
        for axis in range(2):
            number = 2 * axis + side
            table = jnp.where(first_rows, scattered(got_first, number, 0), raw[axis])
            new[axis] = jnp.where(last_rows, scattered(got_last, number, last), table)
        table = jnp.where(first_rows & (even if side == 0 else ~even), got_z, raw[2])
        new[2] = jnp.where(last_rows, scattered(got_last_z, side * last, last), table)
    even_dev = even_place("dev")
    for axis in range(2):
        flat_a[axis] = jnp.where(even_dev, new_high[axis], new_low[axis])
        flat_b[axis] = jnp.where(even_dev, new_low[axis], new_high[axis])
    flat_a[2] = got_z
    deep_b[...] = jnp.where(even, new_low[2], new_high[2])


def cos_quarter(number):
    turn = number & 7
    size = jnp.where((turn & 3) == 0, 1.0, jnp.where((turn & 3) == 2, 0.0, math.sqrt(0.5)))
    return jnp.where((turn > 2) & (turn < 6), -size, size)


def plan_kernel(neighbors, orient, scale, select, turns):
    shape = (ROWS, HALF)
    slot, field, column = iota(shape, 0) % SLOTS, iota(shape, 0) // SLOTS, iota(shape, 1)
    grp, dev = lax.axis_index("grp"), lax.axis_index("dev")
    rank = grp * lax.axis_size("dev") + dev

    def by_slot(values):
        rows = values[0]
        for number in range(1, SLOTS):
            rows = jnp.where(slot == number, values[number], rows)
        return rows

    spread = []
    for number in range(SLOTS):
        turn = 0.5 * cos_quarter(orient[number])
        lift = 0.5 * cos_quarter(orient[number] + 6)
        spread.append((1.0 + turn, 1.0 - turn, 1.0 + lift))
    conc = jnp.where(field == NPHASE, conc_rates[0], conc_rates[1])
    weights = [jnp.where(field < NPHASE, phase_rate * by_slot([own[axis] for own in spread]), conc) for axis in range(3)]
    for axis in range(3):
        scale[axis] = weights[axis]
    scale[3] = 1.0 - 2.0 * (weights[0] + weights[1] + weights[2])
    for face in range(4, 6):
        where_from = []
        for number in range(SLOTS):
            target = neighbors[number, face]
            where_from.append(jnp.where(target < 0, 2 * SLOTS - 1, number - (target & (SLOTS - 1)) + SLOTS - 1))
        rows = by_slot(where_from)
        for term in range(2 * SLOTS):
            turns[face - 4, term] = jnp.where(rows == term, weights[2], 0.0)
    for face in range(4):
        first = []
        came = 2 + lax.rem(lax.rem(dev, 2) + face % 2 + 1, 2)
        for number in range(SLOTS):
            target = neighbors[number, face]
            source = jnp.where(target < 0, face % 2, jnp.where(target // SLOTS == rank, 1 - face % 2, came))
            first.append(source * ROWS + jnp.where(target < 0, number, target & (SLOTS - 1)))
        chosen = jnp.where(column == by_slot(first) + field * SLOTS, 1.0, 0.0)[:, : SOURCES * ROWS]
        rows = pl.ds(face % 2 * ROWS, ROWS)
        for part in range(PARTS):
            select[face // 2, rows, pl.ds(part * SOURCES * ROWS, SOURCES * ROWS)] = chosen


def start_kernel(fields, neighbors, orient, *refs):
    fetched, low, high, faces_grp, faces_dev, scale, select, turns = refs[:8]
    state, near, turn, arrived = refs[8:]
    scalars = ((neighbors, near), (orient, turn))
    parts = [pl.ds(first, EDGE // 2) for first in (0, EDGE // 2)]
    blocks = tuple((fields.at[:, :, part], fetched.at[:, :, part]) for part in parts)
    copies = [pltpu.make_async_copy(*pair, arrived.at[number]) for number, pair in enumerate((*scalars, *blocks))]
    for copy in copies:
        copy.start()
    for copy in copies[: len(scalars)]:
        copy.wait()
    plan_kernel(near, turn, scale, select, turns)
    packer = Packer()
    for number, part in enumerate(parts):
        copies[len(scalars) + number].wait()
        first = number * (EDGE // 2)
        for slot in range(SLOTS):
            fill_slot(state, slot, lambda f: fetched[slot, f, part], first, EDGE // 2)
        for x in range(first, first + EDGE // 2):
            packer.add_y(x, *plane_at(state, x))
            packer.add_z(x, *plane_at(state, x))
    write_tables(packer, state, (low, high))
    for h in range(2):
        for ref, table in zip((low, high), packer.z_tables(h)):
            ref[2, :, h * HALF : (h + 1) * HALF] = table
    faces_grp[:ROWS] = gathered([low[0], high[0], low[1], high[1]], 0)
    faces_grp[ROWS:] = squeezed(jnp.where(even_place("grp"), high[2], low[2]))
    faces_dev[:ROWS] = gathered([low[0], high[0], low[1], high[1]], SLOTS - 1)
    faces_dev[ROWS:] = squeezed(gathered([low[2], low[2], low[2], high[2]], SLOTS - 1))


def first_inner_kernel(mask_dev, mask_grp, scale, fields, block_dev, block_grp, faces, low, high, new_low, new_high, *refs):
    partial, got_deep, relayed, z_low, z_high, state = refs
    size = NFIELD * EDGE
    swap_dev, swap_grp = mask_dev[...] > 0.5, mask_grp[...] > 0.5

    def block(slot):
        def of(f):
            value = fields[slot, f]
            if slot == 0:
                value = jnp.where(swap_grp[:EDGE], block_grp[f * EDGE : (f + 1) * EDGE], value)
            if slot == SLOTS - 1:
                value = jnp.where(swap_dev[:EDGE], block_dev[f * EDGE : (f + 1) * EDGE], value)
            return value

        return of

    for slot in range(SLOTS):
        fill_slot(state, slot, block(slot))
    rows, even = slot_rows(), even_place("grp")
    first_rows = (rows == 0) & swap_grp
    other = block_grp[size : size + ROWS]
    got = jnp.where((rows == 0) | (rows == SLOTS - 1), stretched(faces[ROWS:]), other)
    got_deep[...] = jnp.where(first_rows, jnp.where(even, low[2], high[2]), got)
    relayed[...] = jnp.where(rows == SLOTS - 1, jnp.broadcast_to(other[SLOTS - 1 : SLOTS], FACE), 0.0)
    z_low[...] = jnp.where(first_rows & ~even, other, new_low[2])
    z_high[...] = jnp.where(first_rows & even, other, new_high[2])
    inner_kernel(state, scale, partial)


def later_inner_kernel(state, ghosts, scale, partial):
    inner_kernel(state, scale, partial, z_pairs(ghosts[0], ghosts[1]))


def inner_kernel(state, scale, partial, pairs=None):
    ends = ends_of((ROWS, HALF))

    def plane(x):
        halves, at = plane_at(state, x), EDGE - 1 - x
        if pairs is None:
            return halves
        return [half + jnp.where(ends, turned(pairs[h][at % 2], -at), 0.0) for h, half in enumerate(halves)]

    lane = iota((ROWS, HALF), 1)
    start_y, end_y = lane < EDGE, lane >= HALF - EDGE
    start_z, end_z = lane % EDGE == 0, lane % EDGE == EDGE - 1
    weight_x, weight_y, weight_z, weight = (scale[number] for number in range(4))
    tile = 2 * SLOTS
    planes = {0: plane(0)}
    for x in range(EDGE):
        if x + 1 < EDGE:
            planes[x + 1] = plane(x + 1)
        left, right = planes[x]
        up = [turned(half, EDGE) for half in (left, right)]
        down = [turned(half, -EDGE) for half in (left, right)]
        sum_y = (
            jnp.where(start_y, 0.0, up[0]) + jnp.where(end_y, down[1], down[0]),
            jnp.where(start_y, up[0], up[1]) + jnp.where(end_y, 0.0, down[1]),
        )
        for h, half in enumerate((left, right)):
            sum_z = jnp.where(start_z, 0.0, turned(half, 1)) + jnp.where(end_z, 0.0, turned(half, -1))
            if x == 0:
                sum_x = planes[1][h]
            elif x == EDGE - 1:
                sum_x = planes[x - 1][h]
            else:
                sum_x = planes[x - 1][h] + planes[x + 1][h]
            flow = weight * half + weight_x * sum_x + weight_y * sum_y[h] + weight_z * sum_z
            phases, conc = (half[:tile], half[tile : 2 * tile]), half[2 * tile :]
            drive = conc - pltpu.roll(conc, SLOTS, 0)
            total = phases[0] + phases[1]
            total = total + pltpu.roll(total, SLOTS, 0)
            tail = (phase_rate * closure) * (1.0 - total)
            rows = x * ROWS
            for number, value in enumerate(phases):
                gain = value * (1.0 - value) * (coupling[2 * number] * drive + (2.0 * value - 1.0))
                part = flow[number * tile : (number + 1) * tile]
                partial[h, pl.ds(rows + number * tile, tile), :] = part + (phase_rate * gain + tail)
            partial[h, pl.ds(rows + 2 * tile, tile), :] = flow[2 * tile :]


def ghosts_of(axis, scale, select, tables):
    tables = jnp.concatenate(tables, axis=0)
    near = tables.astype(jnp.bfloat16)
    rest = (tables - near.astype(jnp.float32)).astype(jnp.bfloat16)
    both = jnp.concatenate([near, rest], axis=0)
    pair = jnp.dot(select[axis].astype(jnp.bfloat16), both, preferred_element_type=jnp.float32)
    weight = jnp.concatenate([scale[axis]] * 2, axis=1)
    return weight * pair[:ROWS], weight * pair[ROWS:]


def side_by_side(low, high, even):
    return jnp.where(even, low, high), jnp.where(even, high, low)


def sides_kernel(scale, select, partial, low, high, flat_a, flat_b, *refs):
    first_step = len(refs) == 5
    done = refs[0] if first_step else refs[1]
    packer = Packer()
    sources = (low, high, flat_a, flat_b)
    x_low, x_high = ghosts_of(0, scale, select, [ref[0] for ref in sources])
    y_low, y_high = ghosts_of(1, scale, select, [ref[1] for ref in sources])
    lane = iota((ROWS, HALF), 1)
    inside = (lane < EDGE, lane >= HALF - EDGE)
    even = (lane // EDGE) % 2 == 0
    pairs = []
    for h in range(2):
        lanes = slice(h * HALF, (h + 1) * HALF)
        pairs.append(side_by_side(y_low[:, lanes], turned(y_high[:, lanes], -EDGE), even))
    for x in range(EDGE):
        ends = turned(pairs[x // GROUPS][x % 2], -EDGE * (x % GROUPS))
        halves = []
        for h, value in enumerate(plane_at(partial, x)):
            value = value + jnp.where(inside[h], ends, 0.0)
            if x == 0:
                value = value + x_low[:, h * HALF : (h + 1) * HALF]
            if x == EDGE - 1:
                value = value + x_high[:, h * HALF : (h + 1) * HALF]
            done[h, pl.ds(x * ROWS, ROWS), :] = value
            halves.append(value)
        if first_step:
            packer.add_z(x, *halves)
            packer.add_y(x, *halves)
    if first_step:
        for h in range(2):
            for ref, table in zip(refs[1:], (*packer.z_tables(h), *packer.y_tables(h))):
                ref[:, h * HALF : (h + 1) * HALF] = table
    else:
        blocks = refs[0]
        for slot in range(SLOTS):
            for f in range(NFIELD):
                for h in range(2):
                    rows = pl.ds(f * SLOTS + slot, EDGE, stride=ROWS)
                    blocks[slot, f, :, h * HALF : (h + 1) * HALF] = done[h, rows, :]


def z_ghosts(turns, own, deep_a, deep_b):
    even = even_place("grp")
    came = (jnp.where(even, deep_b, deep_a), jnp.where(even, deep_a, deep_b))
    ghosts = []
    for side in range(2):
        halves = []
        for h in range(2):
            lanes = slice(h * HALF, (h + 1) * HALF)
            table = came[side][:, lanes].reshape(NFIELD // 2, 2 * SLOTS, HALF)
            total = turns[side, 2 * SLOTS - 1] * own[side][:, lanes]
            for term in range(2 * SLOTS - 1):
                shift = (term - SLOTS + 1) % (2 * SLOTS)
                moved = pltpu.roll(table, shift, 1) if shift else table
                total = total + turns[side, term] * moved.reshape(ROWS, HALF)
            halves.append(total)
        ghosts.append(jnp.concatenate(halves, axis=1))
    return ghosts


def z_pairs(z_low, z_high):
    even = iota((ROWS, HALF), 1) % 2 == 0
    halves = [slice(h * HALF, (h + 1) * HALF) for h in range(2)]
    return [side_by_side(z_low[:, lanes], turned(z_high[:, lanes], EDGE - 1), even) for lanes in halves]


def ends_of(shape):
    place = iota(shape, 1) % EDGE
    return (place == 0) | (place == EDGE - 1)


def finish_kernel(turns, partial, packed_z, packed_y, known, deep_b, flat_a, relayed, own_z, outs):
    low, high, *sends, ghosts = outs
    deep_a = jnp.where(relayed[...] > 0.5, flat_a[2], known[...])
    both = z_ghosts(turns, [ref[...] for ref in own_z], deep_a, deep_b[...])
    pairs = z_pairs(*both)
    lane = iota((ROWS, HALF), 1)
    ends, group = ends_of((ROWS, HALF)), lane // EDGE
    for side, ref in enumerate((low, high)):
        ghosts[side] = both[side]
        x = side * (EDGE - 1)
        at = EDGE - 1 - x
        for h, half in enumerate(plane_at(partial, x)):
            lanes = slice(h * HALF, (h + 1) * HALF)
            ref[0, :, lanes] = half + jnp.where(ends, turned(pairs[h][at % 2], -at), 0.0)
        ref[2] = packed_z[side][...] + both[side]
        for h in range(2):
            total = jnp.zeros((ROWS, HALF), jnp.float32)
            for number in range(GROUPS):
                at = EDGE - 1 - (h * GROUPS + number)
                moved = turned(pairs[side][at % 2], EDGE * number - at - side * (HALF - EDGE))
                total = jnp.where(ends & (group == number), moved, total)
            lanes = slice(h * HALF, (h + 1) * HALF)
            ref[1, :, lanes] = packed_y[side][:, lanes] + total
    emit_faces((low, high), sends)


def finish_0_kernel(turns, partial, *refs):
    packed, (known, deep_b, flat_a, relayed), own_z, outs = refs[:4], refs[4:8], refs[8:10], refs[10:]
    finish_kernel(turns, partial, packed[:2], packed[2:], known, deep_b, flat_a, relayed, own_z, outs)


def last_kernel(turns, partial, low, high, deep_first, deep_second, result, rows_of, blocks, sent):
    first, second, swapped = deep_first[...], deep_second[...], swapped_order(lax.axis_index("dev"))
    came = jnp.where(swapped, second, first), jnp.where(swapped, first, second)
    for h, pair in enumerate(z_pairs(*z_ghosts(turns, (low[2], high[2]), *came))):
        for odd in range(2):
            rows_of[h, odd] = pair[odd]
    shape = (EDGE, HALF)
    ends, even = ends_of(shape), iota(shape, 0) % 2 == 0
    copies = []
    for slot in range(SLOTS):
        for f in range(NFIELD):
            row = pl.ds(f * SLOTS + slot, 1)
            for h in range(2):
                both = [jnp.broadcast_to(rows_of[h, odd, row, :], shape) for odd in (1, 0)]
                ghost = pltpu.roll(jnp.where(even, *both), HALF - EDGE + 1, 1, stride=1, stride_axis=0)
                lanes = pl.ds(h * HALF, HALF)
                blocks[slot, f, :, lanes] = partial[slot, f, :, lanes] + jnp.where(ends, ghost, 0.0)
            if f % PIECE == PIECE - 1:
                part = (slot, pl.ds(f + 1 - PIECE, PIECE))
                copy = pltpu.make_async_copy(blocks.at[part], result.at[part], sent.at[len(copies)])
                copy.start()
                copies.append(copy)
    for copy in copies:
        copy.wait()


def spec(space):
    return pl.BlockSpec(memory_space=space)


VECTOR = pltpu.VMEM
SMALL = pltpu.CompilerParams(vmem_limit_bytes=8 << 20)
FLAT = (2, ROWS, PLANE)
TABLES = (SIDE, SIDE, FLAT, FLAT, FACE, FACE, (2, *FACE))
EARLY = (ROWS + 4 * SLOTS, PLANE)
TO_DEV = (NFIELD * EDGE, PLANE)
TO_GRP = (NFIELD * EDGE + ROWS, PLANE)


def shaped(shape):
    return jax.ShapeDtypeStruct(shape, jnp.float32)


def cost(flops):
    return pl.CostEstimate(flops=flops, bytes_accessed=min(flops, 2 << 20), transcendentals=0)


def call(kernel, name, shapes, vectors, flops=1 << 20, scratch=()):
    return pl.pallas_call(
        kernel,
        name=name,
        compiler_params=SMALL,
        out_shape=[shaped(shape) for shape in shapes],
        in_specs=[spec(VECTOR)] * len(vectors),
        out_specs=[spec(VECTOR)] * len(shapes),
        scratch_shapes=list(scratch),
        cost_estimate=cost(flops),
    )(*vectors)


def start(arguments):
    shapes = (arguments[0].shape, SIDE, SIDE, EARLY, EARLY, (4, ROWS, HALF), SELECT, TURNS)
    return pl.pallas_call(
        start_kernel,
        name="start",
        compiler_params=SMALL,
        out_shape=[shaped(shape) for shape in shapes],
        in_specs=[spec(pl.ANY)] * len(arguments),
        out_specs=[spec(VECTOR)] * len(shapes),
        scratch_shapes=[
            pltpu.VMEM(SPARE, jnp.float32),
            *(pltpu.SMEM(array.shape, jnp.int32) for array in arguments[1:]),
            pltpu.SemaphoreType.DMA((len(arguments) + 1,)),
        ],
    )(*(pltpu.with_memory_space_constraint(array, pltpu.HBM) for array in arguments))


def mask(flag):
    return jnp.broadcast_to(jnp.where(flag == 1, 1.0, 0.0).reshape(1, 1), FACE)


def body(fields, swap_dev, swap_grp, neighbors, orient):
    fields, low, high, faces, faces_dev, scale, select, turns = start((fields, neighbors, orient))
    swap_dev, faces = lax.optimization_barrier((swap_dev, faces))
    faces = exchange(faces, "grp", 0)
    faces_dev = exchange(faces_dev, "dev", 0)
    mask_dev = mask(swap_dev)
    to_dev, to_grp = call(block_kernel, "blocks", [TO_DEV, TO_GRP], [mask_dev, fields, low, high], 1 << 28)
    swap_grp, to_grp = lax.optimization_barrier((swap_grp, to_grp))
    mask_grp = mask(swap_grp)
    block_grp = exchange(to_grp, "grp", 0)
    block_dev = exchange(to_dev, "dev", 0)
    new_low, new_high, *sends = call(
        faces_kernel,
        "faces",
        [SIDE, SIDE, SIDE, FLAT, FACE],
        [mask_dev, mask_grp, low, high, faces, faces_dev],
        1 << 28,
    )
    flat_a = exchange(sends[0], "dev", 0)
    flat_b = exchange(sends[1], "dev", 1)
    deep_b = exchange(sends[2], "grp", 1)
    partial, deep_a, relayed, z_low, z_high = call(
        first_inner_kernel,
        "inner_0",
        [STATE, FACE, FACE, FACE, FACE],
        [mask_dev, mask_grp, scale, fields, block_dev, block_grp, faces, low, high, new_low, new_high],
        4 << 20,
        [pltpu.VMEM(SPARE, jnp.float32)],
    )
    partial, *packed = call(
        sides_kernel,
        "sides_0",
        [STATE, FACE, FACE, FACE, FACE],
        [scale, select, partial, new_low, new_high, flat_a, flat_b],
    )
    *tables, ghosts = call(
        finish_0_kernel,
        "finish_0",
        TABLES,
        [turns, partial, *packed, deep_a, deep_b, flat_a, relayed, z_low, z_high],
    )
    own, sends = tables[:2], tables[2:]
    flat_a = exchange(sends[0], "dev", 0)
    flat_b = exchange(sends[1], "dev", 1)
    deep_first = exchange(sends[2], "grp", lambda dev: 1 if swapped_order(dev) else 0)
    deep_second = exchange(sends[3], "grp", lambda dev: 0 if swapped_order(dev) else 1)
    (partial,) = call(later_inner_kernel, "inner_1", [STATE], [partial, ghosts, scale], 4 << 20)
    (blocks,) = call(
        sides_kernel,
        "sides_1",
        [fields.shape],
        [scale, select, partial, *own, flat_a, flat_b],
        scratch=[pltpu.VMEM(SPARE, jnp.float32)],
    )
    return pl.pallas_call(
        last_kernel,
        name="finish_1",
        compiler_params=SMALL,
        out_shape=shaped(fields.shape),
        in_specs=[spec(VECTOR)] * 6,
        out_specs=spec(pl.ANY),
        scratch_shapes=[
            pltpu.VMEM((2, 2, ROWS, HALF), jnp.float32),
            pltpu.VMEM(fields.shape, jnp.float32),
            pltpu.SemaphoreType.DMA((SLOTS * NFIELD // PIECE,)),
        ],
    )(turns, blocks, *own, deep_first, deep_second)


def solution(mesh):
    in_specs = (
        P(("grp", "dev"), None, None, None),
        P(("grp", "dev")),
        P(("grp", "dev")),
        P(("grp", "dev"), None),
        P(("grp", "dev")),
    )
    out_specs = P(("grp", "dev"), None, None, None)
    return jax.shard_map(body, mesh=mesh, in_specs=in_specs, out_specs=out_specs, check_vma=False)
```
